32 devices in a mesh: dp: 8 (over z, x), rep: 4 (over y, core).
Axes of the slice: x: 2, y: 2, z: 4, core: 2. Of those that a mesh axis runs over, the one named last changes fastest.
Arguments:
- deter_states: bfloat16 [64, 64, 1024], P(('dp', 'rep')), may hold values from -6 to 6
- embed: bfloat16 [64, 64, 1536], P(('dp', 'rep')), may hold values from -6 to 6
- lengths: int32 [64], P(('dp', 'rep')), may hold values from 8 to 64, as said below
- resets: int32 [64, 64], P(('dp', 'rep')), may hold values 0 or 1
- terminal: int32 [64, 64], P(('dp', 'rep')), may hold values 0 or 1
- rewards: float32 [64, 64], P(('dp', 'rep')), may hold values from -6 to 6
- prev_stoch: int32 [64, 64, 32], P(('dp', 'rep')), may hold values from 0 to 31
- prev_action: int32 [64, 64], P(('dp', 'rep')), may hold values from 0 to 16
- regroup: int32 [32, 128], P(('dp', 'rep')), may hold values from 0 to 127, each once within a row
- goal_codes: int32 [4096, 8], P(('dp', 'rep')), may hold values from 0 to 7
- samples: int32 [4096, 16, 32], P(('dp', 'rep')), may hold values from 0 to 31
- actions: int32 [4096, 16], P(('dp', 'rep')), may hold values from 0 to 16
- obs_gain: bfloat16 [1024], P('rep'), may hold values from 0.5 to 1.5
- manager_in: bfloat16 [1024, 512], P('rep'), may hold values from -0.1875 to 0.1875
- manager_gain: bfloat16 [512], P('rep'), may hold values from 0.5 to 1.5
- manager_out: bfloat16 [512], P('rep'), may hold values from -0.25 to 0.25
- goal_in: bfloat16 [64, 512], P('rep'), may hold values from -2 to 2
- goal_gain: bfloat16 [512], P('rep'), may hold values from 0.5 to 1.5
- goal_out: bfloat16 [512, 1024], P('rep'), may hold values from -0.25 to 0.25
- actor_in: bfloat16 [3072, 512], P('rep'), may hold values from -0.125 to 0.125
- actor_gain: bfloat16 [512], P('rep'), may hold values from 0.5 to 1.5
- actor_out: bfloat16 [512, 17], P('rep'), may hold values from -0.25 to 0.25
- critic_in: bfloat16 [3072, 512], P('rep'), may hold values from -0.125 to 0.125
- critic_gain: bfloat16 [512], P('rep'), may hold values from 0.5 to 1.5
- critic_out: bfloat16 [512], P('rep'), may hold values from -0.25 to 0.25
- img_stoch: bfloat16 [1024, 1024], P('rep'), may hold values from -1 to 1
- img_action: bfloat16 [17, 1024], P(None, 'rep'), may hold values from -6 to 6
- img_gain: bfloat16 [1024], P('rep'), may hold values from 0.5 to 1.5
- gru_weight: bfloat16 [2048, 3072], P('rep'), may hold values from -0.125 to 0.125
- gru_gain: bfloat16 [3072], P('rep'), may hold values from 0.5 to 1.5
- post_in: bfloat16 [2560, 1024], P('rep'), may hold values from -0.125 to 0.125
- post_gain: bfloat16 [1024], P('rep'), may hold values from 0.5 to 1.5
- post_out: bfloat16 [1024, 1024], P('rep'), may hold values from -0.1875 to 0.1875
- prior_in: bfloat16 [1024, 1024], P('rep'), may hold values from -0.1875 to 0.1875
- prior_gain: bfloat16 [1024], P('rep'), may hold values from 0.5 to 1.5
- prior_out: bfloat16 [1024, 1024], P('rep'), may hold values from -0.1875 to 0.1875
- enc_in: bfloat16 [1024, 512], P('rep'), may hold values from -0.1875 to 0.1875
- enc_gain: bfloat16 [512], P('rep'), may hold values from 0.5 to 1.5
- enc_out: bfloat16 [512, 64], P('rep'), may hold values from -0.25 to 0.25
Outputs:
- total_loss: float32 [], replicated
- deter_grad: float32 [64, 64, 1024], P(('dp', 'rep'))
- embed_grad: float32 [64, 64, 1536], P(('dp', 'rep'))
- obs_gain_grad: float32 [1024], P('rep')
- manager_in_grad: float32 [1024, 512], P('rep', 'dp')
- manager_gain_grad: float32 [512], P('rep')
- manager_out_grad: float32 [512], P('rep')
- goal_in_grad: float32 [64, 512], P('rep', 'dp')
- goal_gain_grad: float32 [512], P('rep')
- goal_out_grad: float32 [512, 1024], P('rep', 'dp')
- actor_in_grad: float32 [3072, 512], P('rep', 'dp')
- actor_gain_grad: float32 [512], P('rep')
- actor_out_grad: float32 [512, 17], P('rep')
- critic_in_grad: float32 [3072, 512], P('rep', 'dp')
- critic_gain_grad: float32 [512], P('rep')
- critic_out_grad: float32 [512], P('rep')
- img_stoch_grad: float32 [1024, 1024], P('rep', 'dp')
- img_action_grad: float32 [17, 1024], P(None, 'rep')
- img_gain_grad: float32 [1024], P('rep')
- gru_weight_grad: float32 [2048, 3072], P('rep', 'dp')
- gru_gain_grad: float32 [3072], P('rep')
- post_in_grad: float32 [2560, 1024], P('rep', 'dp')
- post_gain_grad: float32 [1024], P('rep')
- post_out_grad: float32 [1024, 1024], P('rep', 'dp')
- prior_in_grad: float32 [1024, 1024], P('rep', 'dp')
- prior_gain_grad: float32 [1024], P('rep')
- prior_out_grad: float32 [1024, 1024], P('rep', 'dp')
- enc_in_grad: float32 [1024, 512], P('rep', 'dp')
- enc_gain_grad: float32 [512], P('rep')
- enc_out_grad: float32 [512, 64], P('rep')
The draws below stay inside these ranges and needn't reach their ends.
Inputs may be any that keep to these rules, and one draw needn't show every extreme that they name: `lengths`: in the 2 sequences of every device one has exactly 64 frames. `regroup`: each row is a permutation of 0 to 127.
All inputs are finite; a program needn't handle non-finite values. Where the reference program divides by a largest or mean magnitude, that divisor is 1e-20 or more. No bound on the sum of `resets` or of `terminal` on one device may be relied on, other than what follows from the above.
Results may differ from the reference program's by a relative error of at most 0.01.
The reference program's roundings to bfloat16 on the way count: a program that leaves them out, or rounds other values in their place, can miss the bound.
Values may be sent and summed in bfloat16 or wider, within the bound.
A program may use at most 320 MiB of HBM per device.

```python
import math
import jax
import jax.numpy as jnp
from jax import lax

H = 1024
ZG = 32
ZK = 32
U = 512
GC = 8
GK = 8
NA = 17
E = 1536
LEN = 64
HOR = 16
SEQ_DEV = 2
Z = 1024
GCODE = 64
ROWS = 128
SEQS = 64
SLOTS = 4096
N_DP = 8
N_REP = 4
DEVICES = 32


def draw_lengths(key, part):
    key = jax.random.fold_in(key, 11)
    first_key, second_key = jax.random.split(key)
    drawn = jax.random.randint(first_key, (SEQS,), 8, LEN + 1)
    picked = jax.random.randint(second_key, (SEQS // SEQ_DEV, 1), 0, SEQ_DEV)
    placed = (jnp.arange(SEQ_DEV, dtype=jnp.int32)[None, :] == picked).reshape(SEQS)
    return jnp.where(placed, LEN, drawn).astype(jnp.int32)


def with_ends(entries, stream_key, low, high):
    spot = [jax.random.randint(jax.random.fold_in(stream_key, axis), (), 0, length) for axis, length in enumerate(entries.shape)]
    main_axis = entries.shape.index(max(entries.shape))
    neighbour = spot[:main_axis] + [(spot[main_axis] + 1) % entries.shape[main_axis]] + spot[main_axis + 1:]
    return entries.at[tuple(spot)].set(low).at[tuple(neighbour)].set(high)


def level_of(own_key, extent, pieces, smallest, largest):
    factor_of, own = 1.0, jax.random.fold_in(own_key, 6)
    for dim, shards_of in pieces:
        draws = jnp.exp(jax.random.uniform(jax.random.fold_in(own, dim), (shards_of,), jnp.float32, smallest / len(pieces), largest / len(pieces)))
        factor_of = factor_of * jnp.repeat(draws, extent[dim] // shards_of).reshape([-1 if axis == dim else 1 for axis in range(len(extent))])
    return factor_of


def noise(own_key, dims, spread, limit, cuts=(), kind=jnp.bfloat16):
    entries = spread * jax.random.normal(own_key, dims, jnp.float32)
    if cuts:
        entries = entries * level_of(own_key, dims, cuts, -0.22, 0.18)
    return jnp.clip(entries, -limit, limit).astype(kind)


def setup_inputs(seed: int = 0) -> dict:
    arg_keys = jax.random.split(jax.random.key(seed), 40)
    return {
        "deter_states": noise(arg_keys[0], (SEQS, LEN, H), 1.0, 6.0, ((0, 32),)),
        "embed": noise(arg_keys[1], (SEQS, LEN, E), 1.0, 6.0, ((0, 32),)),
        "lengths": draw_lengths(jax.random.fold_in(arg_keys[39], 71), 0),
        "resets": with_ends((jax.random.randint(arg_keys[3], (SEQS, LEN), 0, 16) < 1).astype(jnp.int32), jax.random.fold_in(arg_keys[3], 1), 0, 1),
        "terminal": with_ends((jax.random.randint(arg_keys[4], (SEQS, LEN), 0, 32) < 1).astype(jnp.int32), jax.random.fold_in(arg_keys[4], 1), 0, 1),
        "rewards": noise(arg_keys[5], (SEQS, LEN), 1.0, 6.0, ((0, 32),), jnp.float32),
        "prev_stoch": with_ends(jax.random.randint(arg_keys[6], (SEQS, LEN, ZG), 0, ZK), jax.random.fold_in(arg_keys[6], 1), 0, ZK - 1).astype(jnp.int32),
        "prev_action": with_ends(jax.random.randint(arg_keys[7], (SEQS, LEN), 0, NA), jax.random.fold_in(arg_keys[7], 1), 0, NA - 1).astype(jnp.int32),
        "regroup": jax.vmap(lambda own: jax.random.permutation(own, ROWS))(jax.random.split(arg_keys[8], DEVICES)).reshape((DEVICES, ROWS)).astype(jnp.int32),
        "goal_codes": with_ends(jax.random.randint(arg_keys[9], (SLOTS, GC), 0, GK), jax.random.fold_in(arg_keys[9], 1), 0, GK - 1).astype(jnp.int32),
        "samples": with_ends(jax.random.randint(arg_keys[10], (SLOTS, HOR, ZG), 0, ZK), jax.random.fold_in(arg_keys[10], 1), 0, ZK - 1).astype(jnp.int32),
        "actions": with_ends(jax.random.randint(arg_keys[11], (SLOTS, HOR), 0, NA), jax.random.fold_in(arg_keys[11], 1), 0, NA - 1).astype(jnp.int32),
        "obs_gain": jnp.clip(1.0 + 0.1 * jax.random.normal(arg_keys[12], (H,), jnp.float32), 0.5, 1.5).astype(jnp.bfloat16),
        "manager_in": noise(arg_keys[13], (H, U), H ** -0.5, 0.1875, ((0, 4),)),
        "manager_gain": jnp.clip(1.0 + 0.1 * jax.random.normal(arg_keys[14], (U,), jnp.float32), 0.5, 1.5).astype(jnp.bfloat16),
        "manager_out": noise(arg_keys[15], (U,), U ** -0.5, 0.25, ((0, 4),)),
        "goal_in": noise(arg_keys[16], (GCODE, U), GC ** -0.5, 2.0, ((0, 4),)),
        "goal_gain": jnp.clip(1.0 + 0.1 * jax.random.normal(arg_keys[17], (U,), jnp.float32), 0.5, 1.5).astype(jnp.bfloat16),
        "goal_out": noise(arg_keys[18], (U, H), U ** -0.5, 0.25, ((0, 4),)),
        "actor_in": noise(arg_keys[19], (2 * H + Z, U), (2 * H) ** -0.5, 0.125, ((0, 4),)),
        "actor_gain": jnp.clip(1.0 + 0.1 * jax.random.normal(arg_keys[20], (U,), jnp.float32), 0.5, 1.5).astype(jnp.bfloat16),
        "actor_out": noise(arg_keys[21], (U, NA), U ** -0.5, 0.25, ((0, 4),)),
        "critic_in": noise(arg_keys[22], (2 * H + Z, U), (2 * H) ** -0.5, 0.125, ((0, 4),)),
        "critic_gain": jnp.clip(1.0 + 0.1 * jax.random.normal(arg_keys[23], (U,), jnp.float32), 0.5, 1.5).astype(jnp.bfloat16),
        "critic_out": noise(arg_keys[24], (U,), U ** -0.5, 0.25, ((0, 4),)),
        "img_stoch": noise(arg_keys[25], (Z, H), ZG ** -0.5, 1.0, ((0, 4),)),
        "img_action": noise(arg_keys[26], (NA, H), 1 ** -0.5, 6.0, ((1, 4),)),
        "img_gain": jnp.clip(1.0 + 0.1 * jax.random.normal(arg_keys[27], (H,), jnp.float32), 0.5, 1.5).astype(jnp.bfloat16),
        "gru_weight": noise(arg_keys[28], (2 * H, 3 * H), (2 * H) ** -0.5, 0.125, ((0, 4),)),
        "gru_gain": jnp.clip(1.0 + 0.1 * jax.random.normal(arg_keys[29], (3 * H,), jnp.float32), 0.5, 1.5).astype(jnp.bfloat16),
        "post_in": noise(arg_keys[30], (H + E, H), (H + E) ** -0.5, 0.125, ((0, 4),)),
        "post_gain": jnp.clip(1.0 + 0.1 * jax.random.normal(arg_keys[31], (H,), jnp.float32), 0.5, 1.5).astype(jnp.bfloat16),
        "post_out": noise(arg_keys[32], (H, Z), H ** -0.5, 0.1875, ((0, 4),)),
        "prior_in": noise(arg_keys[33], (H, H), H ** -0.5, 0.1875, ((0, 4),)),
        "prior_gain": jnp.clip(1.0 + 0.1 * jax.random.normal(arg_keys[34], (H,), jnp.float32), 0.5, 1.5).astype(jnp.bfloat16),
        "prior_out": noise(arg_keys[35], (H, Z), H ** -0.5, 0.1875, ((0, 4),)),
        "enc_in": noise(arg_keys[36], (H, U), H ** -0.5, 0.1875, ((0, 4),)),
        "enc_gain": jnp.clip(1.0 + 0.1 * jax.random.normal(arg_keys[37], (U,), jnp.float32), 0.5, 1.5).astype(jnp.bfloat16),
        "enc_out": noise(arg_keys[38], (U, GCODE), U ** -0.5, 0.25, ((0, 4),)),
    }


discount = 0.99
return_mix = 0.95
epsilon = 1e-05
small_floor = 1e-06
highest = lax.Precision.HIGHEST

@jax.custom_vjp
def low(v):
    return lax.optimization_barrier(v.astype(jnp.bfloat16)).astype(jnp.float32)

@jax.custom_vjp
def low_back(v):
    return v

def low_keep(v):
    return (low(v), None)

def low_pass(kept, grad):
    return (grad,)

def back_keep(v):
    return (v, None)

def back_low(kept, grad):
    return (low(grad),)
low.defvjp(low_keep, low_pass)
low_back.defvjp(back_keep, back_low)

def matmul(left, right):
    return jnp.dot(left, right, precision=highest)

def layer_norm(values_in, scaling):
    row_mean = lax.optimization_barrier(jnp.mean(values_in, -1, keepdims=True))
    centred = values_in - row_mean
    inverse = lax.rsqrt(lax.optimization_barrier(jnp.mean(centred * centred, -1, keepdims=True)) + epsilon)
    return centred * inverse * scaling

def hidden_layer(pre_act, scaling):
    return low(jax.nn.elu(layer_norm(low_back(pre_act), scaling)))

def one_hot(index_values, classes):
    return (index_values[..., None] == jnp.arange(classes, dtype=jnp.int32)).astype(jnp.float32)

def group_log_softmax(flat_logits, groups):
    return jax.nn.log_softmax(flat_logits.reshape(flat_logits.shape[0], groups, -1), axis=-1)

def chain_returns(values_now, rewards_now, linked, carried):

    def back_step(carry_pair, inputs):
        later_return, later_value = carry_pair
        current, reward_now, link_now, carry_now = inputs
        blended = (1.0 - return_mix) * later_value + return_mix * later_return
        result = jnp.where(link_now, reward_now + discount * carry_now * blended, current)
        return ((result, current), result)
    zero_start = jnp.zeros(values_now.shape[:1], jnp.float32)
    _, stacked = lax.scan(back_step, (zero_start, zero_start), (values_now.T, rewards_now.T, linked.T, carried.T), reverse=True)
    return stacked.T

def frame_pass(weights, prev_rows, embed_rows, stoch_ids, action_ids):
    obs_gain, manager_in, manager_gain, manager_out, goal_in, goal_gain, goal_out, actor_in, actor_gain, actor_out, critic_in, critic_gain, critic_out, img_stoch, img_action, img_gain, gru_weight, gru_gain, post_in, post_gain, post_out, prior_in, prior_gain, prior_out, enc_in, enc_gain, enc_out = weights
    row_count = prev_rows.shape[0]
    img_pre = matmul(one_hot(stoch_ids, ZK).reshape(row_count, Z), img_stoch) + matmul(one_hot(action_ids, NA), img_action)
    img_hidden = hidden_layer(img_pre, img_gain)
    gru_parts = layer_norm(low_back(matmul(jnp.concatenate([img_hidden, low(prev_rows)], 1), gru_weight)), gru_gain)
    reset_gate = jax.nn.sigmoid(gru_parts[:, :H])
    candidate = jnp.tanh(reset_gate * gru_parts[:, H:2 * H])
    update_gate = jax.nn.sigmoid(gru_parts[:, 2 * H:] - 1.0)
    deter_state = update_gate * candidate + (1.0 - update_gate) * prev_rows
    deter_low = low(deter_state)
    feature = low(layer_norm(deter_state, obs_gain))
    manager_value = matmul(hidden_layer(matmul(feature, manager_in), manager_gain), manager_out)
    post_hidden = hidden_layer(matmul(jnp.concatenate([deter_low, embed_rows], 1), post_in), post_gain)
    post_log = group_log_softmax(low_back(matmul(post_hidden, post_out)), ZG)
    prior_hidden = hidden_layer(matmul(deter_low, prior_in), prior_gain)
    prior_log = group_log_softmax(low_back(matmul(prior_hidden, prior_out)), ZG)
    state_kl = lax.optimization_barrier(jnp.sum(jnp.exp(post_log) * (post_log - prior_log), (1, 2)))
    enc_hidden = hidden_layer(matmul(deter_low, enc_in), enc_gain)
    code_log = group_log_softmax(low_back(matmul(enc_hidden, enc_out)), GC)
    code_prob = jnp.exp(code_log)
    code_kl = lax.optimization_barrier(jnp.sum(code_prob * (code_log + math.log(GK)), (1, 2)))
    soft_code = low(code_prob.reshape(row_count, GCODE))
    recon = low_back(matmul(hidden_layer(matmul(soft_code, goal_in), goal_gain), goal_out))
    recon_err = recon - deter_state
    return (deter_low, manager_value, state_kl + code_kl + 0.5 * lax.optimization_barrier(jnp.mean(recon_err * recon_err, -1)))

def worker_hidden(start_state, goal_low, stoch_hot, first_layer, scaling):
    slot_part = low_back(matmul(start_state, first_layer[:H]) + matmul(goal_low, first_layer[H + Z:]))
    varying = jnp.einsum('rkz,zu->rku', stoch_hot, first_layer[H:H + Z], precision=highest)
    return hidden_layer(slot_part[:, None, :] + varying, scaling)

def worker_outputs(weights, start_state, code_ids, stoch_ids, action_ids):
    goal_in = weights[4]
    goal_gain = weights[5]
    goal_out = weights[6]
    actor_in = weights[7]
    actor_gain = weights[8]
    actor_out = weights[9]
    critic_in = weights[10]
    critic_gain = weights[11]
    critic_out = weights[12]
    slot_count = start_state.shape[0]
    code_hot = one_hot(code_ids, GK).reshape(slot_count, GCODE)
    goal_hidden = hidden_layer(matmul(code_hot, goal_in), goal_gain)
    goal_vector = low_back(matmul(goal_hidden, goal_out))
    goal_low = low(goal_vector)
    stoch_hot = one_hot(stoch_ids, ZK).reshape(slot_count, HOR, Z)
    action_hot = one_hot(action_ids, NA)
    actor_hidden = worker_hidden(start_state, goal_low, stoch_hot, actor_in, actor_gain)
    logits = low_back(jnp.einsum('rku,ua->rka', actor_hidden, actor_out, precision=highest))
    chosen = lax.optimization_barrier(jnp.sum(jax.nn.log_softmax(logits, axis=-1) * action_hot, -1))
    critic_hidden = worker_hidden(start_state, goal_low, stoch_hot, critic_in, critic_gain)
    worker_value = jnp.einsum('rku,u->rk', critic_hidden, critic_out, precision=highest)
    return (goal_vector, chosen, worker_value)

def reference(deter_states, embed, lengths, resets, terminal, rewards, prev_stoch, prev_action, regroup, goal_codes, samples, actions, obs_gain, manager_in, manager_gain, manager_out, goal_in, goal_gain, goal_out, actor_in, actor_gain, actor_out, critic_in, critic_gain, critic_out, img_stoch, img_action, img_gain, gru_weight, gru_gain, post_in, post_gain, post_out, prior_in, prior_gain, prior_out, enc_in, enc_gain, enc_out):
    params = tuple((weight.astype(jnp.float32) for weight in (obs_gain, manager_in, manager_gain, manager_out, goal_in, goal_gain, goal_out, actor_in, actor_gain, actor_out, critic_in, critic_gain, critic_out, img_stoch, img_action, img_gain, gru_weight, gru_gain, post_in, post_gain, post_out, prior_in, prior_gain, prior_out, enc_in, enc_gain, enc_out)))
    prev_blocks = deter_states.astype(jnp.float32).reshape(DEVICES, ROWS, H)
    embed_blocks = embed.astype(jnp.float32).reshape(DEVICES, ROWS, E)
    stoch_blocks = prev_stoch.reshape(DEVICES, ROWS, ZG)
    action_blocks = prev_action.reshape(DEVICES, ROWS)
    positions = jnp.arange(LEN, dtype=jnp.int32)[None, :]
    is_valid = positions < lengths[:, None]
    next_valid = jnp.concatenate([is_valid[:, 1:], jnp.zeros((SEQS, 1), jnp.bool_)], 1)
    next_reset = jnp.concatenate([resets[:, 1:], jnp.ones((SEQS, 1), jnp.int32)], 1)
    linked = next_valid & (next_reset == 0)
    carried = 1.0 - terminal.astype(jnp.float32)
    valid_float = is_valid.astype(jnp.float32)
    valid_blocks = valid_float.reshape(DEVICES, ROWS)
    reward_blocks = rewards.reshape(DEVICES, SEQ_DEV, LEN)
    link_blocks = linked.reshape(DEVICES, SEQ_DEV, LEN)
    carry_blocks = carried.reshape(DEVICES, SEQ_DEV, LEN)
    send_order = regroup.reshape(N_DP, N_REP, ROWS)

    def regroup_rows(table_rows):
        tail_shape = table_rows.shape[1:]
        grid_rows = table_rows.reshape((N_DP, N_REP, ROWS) + tail_shape)
        picked = jax.vmap(jax.vmap(lambda block_rows, order_row: block_rows[order_row]))(grid_rows, send_order)
        picked = picked.reshape((N_DP, N_REP, N_DP, ROWS // N_DP) + tail_shape)
        return jnp.swapaxes(picked, 0, 2).reshape((DEVICES, ROWS) + tail_shape)

    def frame_targets(inputs):
        prev_rows, embed_rows, stoch_ids, action_ids, reward_rows, link_rows, carry_rows = inputs
        deter_low, manager_value, _ = frame_pass(params, prev_rows, embed_rows, stoch_ids, action_ids)
        manager_return = chain_returns(manager_value.reshape(SEQ_DEV, LEN), reward_rows, link_rows, carry_rows)
        return (deter_low, manager_return.reshape(ROWS))
    deter_low_blocks, manager_return = lax.map(frame_targets, (prev_blocks, embed_blocks, stoch_blocks, action_blocks, reward_blocks, link_blocks, carry_blocks))
    slot_weight = regroup_rows(valid_float.reshape(SEQS * LEN))
    start_blocks = regroup_rows(deter_low_blocks.reshape(SEQS * LEN, H))
    step_link = jnp.broadcast_to(jnp.arange(HOR, dtype=jnp.int32)[None, :] < HOR - 1, (ROWS, HOR))
    step_carry = jnp.ones((ROWS, HOR), jnp.float32)
    blocked_codes = goal_codes.reshape(DEVICES, ROWS, GC)
    blocked_samples = samples.reshape(DEVICES, ROWS, HOR, ZG)
    blocked_actions = actions.reshape(DEVICES, ROWS, HOR)

    def block_targets(inputs):
        start_state, code_ids, stoch_ids, action_ids = inputs
        goal_vector, chosen, worker_value = worker_outputs(params, start_state, code_ids, stoch_ids, action_ids)
        alignment = lax.optimization_barrier(jnp.sum(goal_vector * start_state, -1))
        largest_square = jnp.maximum(lax.optimization_barrier(jnp.sum(goal_vector * goal_vector, -1)), lax.optimization_barrier(jnp.sum(start_state * start_state, -1))) + small_floor
        reward_slot = alignment / largest_square
        worker_return = chain_returns(worker_value, jnp.broadcast_to(reward_slot[:, None], (ROWS, HOR)), step_link, step_carry)
        return (worker_return, worker_value)
    worker_return, worker_value = lax.map(block_targets, (start_blocks, blocked_codes, blocked_samples, blocked_actions))
    advantage = worker_return - worker_value
    return_scale = jnp.max(slot_weight[..., None] * jnp.abs(advantage)) + small_floor

    def total_loss(prev_all, embed_all, weights):

        def frame_loss(running, inputs):
            prev_rows, embed_rows, stoch_ids, action_ids, valid_rows, return_rows = inputs
            deter_low, manager_value, frame_terms = frame_pass(weights, prev_rows, embed_rows, stoch_ids, action_ids)
            misfit = manager_value - return_rows
            frame_part = jnp.sum(valid_rows * (0.5 * misfit * misfit + frame_terms)) / (SEQ_DEV * LEN)
            return (running + frame_part, deter_low)
        frame_total, deter_low_all = lax.scan(jax.checkpoint(frame_loss), jnp.zeros((), jnp.float32), (prev_all, embed_all, stoch_blocks, action_blocks, valid_blocks, manager_return))
        starts = low_back(regroup_rows(deter_low_all.reshape(SEQS * LEN, H)))

        def block_loss(running, inputs):
            start_state, code_ids, stoch_ids, action_ids, weight_row, return_row, advantage_row = inputs
            goal_vector, chosen, values_now = worker_outputs(weights, start_state, code_ids, stoch_ids, action_ids)
            misfit = values_now - return_row
            critic_part = 0.5 * jnp.sum(weight_row[:, None] * misfit * misfit)
            actor_part = jnp.sum(weight_row[:, None] * chosen * advantage_row) / return_scale
            return (running + (critic_part - actor_part) / (ROWS * HOR), None)
        rollout_loss, _ = lax.scan(jax.checkpoint(block_loss), jnp.zeros((), jnp.float32), (starts, blocked_codes, blocked_samples, blocked_actions, slot_weight, worker_return, advantage))
        return frame_total + rollout_loss
    loss_value, pullback = jax.vjp(total_loss, prev_blocks, embed_blocks, params)
    grad_prev, grad_embed, grad_params = pullback(jnp.ones((), jnp.float32))
    return (loss_value, grad_prev.reshape(SEQS, LEN, H), grad_embed.reshape(SEQS, LEN, E), grad_params[0], grad_params[1], grad_params[2], grad_params[3], grad_params[4], grad_params[5], grad_params[6], grad_params[7], grad_params[8], grad_params[9], grad_params[10], grad_params[11], grad_params[12], grad_params[13], grad_params[14], grad_params[15], grad_params[16], grad_params[17], grad_params[18], grad_params[19], grad_params[20], grad_params[21], grad_params[22], grad_params[23], grad_params[24], grad_params[25], grad_params[26])
```

```python
import math
from typing import Any, NamedTuple

import jax
import jax.numpy as jnp
from jax import lax
from jax.experimental import pallas as pl
from jax.experimental.pallas import tpu as pltpu
from jax.sharding import PartitionSpec as P

H = 1024
ZG = 32
ZK = 32
U = 512
GC = 8
GK = 8
NA = 17
E = 1536
LEN = 64
HOR = 16
SEQ_DEV = 2
Z = 1024
GCODE = 64
ROWS = 128


discount = 0.99
return_mix = 0.95
epsilon = 1e-05
small_floor = 1e-06
highest = lax.Precision.HIGHEST


MESH = pl.DeviceIdType.MESH
BF = jnp.bfloat16
F32 = jnp.float32
LANES = 128
VMEM_BYTES = 62 * 2**20


class Arg(NamedTuple):
    kind: Any
    shape: Any
    dtype: Any
    here: bool = True


TAKEN, GIVEN, KEPT, SIGNAL = range(4)


def taken(*shape, dtype=BF, here=True):
    return Arg(TAKEN, shape, dtype, here)


def given(*shape, dtype=BF, here=True):
    return Arg(GIVEN, shape, dtype, here)


def kept(*shape, dtype=BF):
    return Arg(KEPT, shape, dtype)


def signal(*shape):
    return Arg(SIGNAL, shape, None)


def run_kernel(body, layout, inputs, name, collective=None):
    def kernel(*refs):
        body(type(layout)(*refs))

    def place(arg):
        return pl.BlockSpec(memory_space=pltpu.VMEM if arg.here else pl.ANY)

    outs = [a for a in layout if a.kind == GIVEN]
    more = {} if collective is None else dict(collective_id=collective, has_side_effects=True)
    results = pl.pallas_call(
        kernel,
        out_shape=[jax.ShapeDtypeStruct(a.shape, a.dtype) for a in outs],
        in_specs=[place(a) for a in layout if a.kind == TAKEN],
        out_specs=[place(a) for a in outs],
        scratch_shapes=[
            pltpu.VMEM(a.shape, a.dtype) if a.kind == KEPT else pltpu.SemaphoreType.DMA(a.shape)
            for a in layout
            if a.kind >= KEPT
        ],
        compiler_params=pltpu.CompilerParams(vmem_limit_bytes=VMEM_BYTES, **more),
        name=name,
    )(*inputs)
    results = iter(results)
    return type(layout)(*[next(results) if a.kind == GIVEN else None for a in layout])


def product(left, right):
    return jnp.dot(left, right, preferred_element_type=jnp.float32)


def normalize(values_in):
    row_mean = jnp.mean(values_in, -1, keepdims=True)
    centred = values_in - row_mean
    inverse = lax.rsqrt(jnp.mean(centred * centred, -1, keepdims=True) + epsilon)
    return (centred * inverse, inverse)


def normalize_back(grad_normed, normed, inverse):
    return inverse * (
        grad_normed
        - jnp.mean(grad_normed, -1, keepdims=True)
        - normed * jnp.mean(grad_normed * normed, -1, keepdims=True)
    )


def matmul_into(out_ref, left, weight_ref, turned=False, tile=256, low=0, extra=None):
    total = out_ref.shape[-1]

    def one(j, carry):
        start = pl.multiple_of(j * tile, tile)
        if turned:
            value = lax.dot_general(
                left,
                weight_ref[pl.ds(pl.multiple_of(low + j * tile, tile), tile), :],
                (((1,), (1,)), ((), ())),
                preferred_element_type=F32,
            )
        else:
            value = product(left, weight_ref[:, pl.ds(start, tile)])
        if extra is not None:
            value = value + extra(start, tile)
        out_ref[:, pl.ds(start, tile)] = value
        return carry

    lax.fori_loop(0, total // tile, one, 0)


def by_rows(count, size, body, carry=0):
    def one(i, carry):
        return body(pl.ds(pl.multiple_of(i * size, size), size), carry)

    return lax.fori_loop(0, count // size, one, carry)


def elu_of(value):
    return jnp.where(value > 0, value, jnp.exp(jnp.minimum(value, 0.0)) - 1.0)


def normalize_rows(ref, inverse_ref, size):
    def one(rows, carry):
        normed, inverse = normalize(ref[rows, :])
        ref[rows, :] = normed
        inverse_ref[rows, :] = inverse
        return carry

    by_rows(ref.shape[0], size, one)


def hidden_rows(ref, inverse_ref, gain, hidden_ref, size=32):
    def one(rows, carry):
        normed, inverse = normalize(ref[rows, :])
        ref[rows, :] = normed
        inverse_ref[rows, :] = inverse
        hidden_ref[rows, :] = elu_of(normed * gain).astype(BF)
        return carry

    by_rows(ref.shape[0], size, one)


def hidden_rows_back(grad_of, ref, inverse_ref, gain, pre_ref, size=32):
    def one(rows, total):
        normed = ref[rows, :]
        scaled = normed * gain
        grad_scaled = grad_of(rows) * jnp.where(
            scaled > 0, 1.0, jnp.exp(jnp.minimum(scaled, 0.0))
        )
        total = total + jnp.sum(grad_scaled * normed, 0, keepdims=True)
        back = normalize_back(grad_scaled * gain, normed, inverse_ref[rows, :])
        pre_ref[rows, :] = back.astype(pre_ref.dtype)
        return total

    return by_rows(ref.shape[0], size, one, jnp.zeros((1, ref.shape[1]), F32))


def turn_into(out_ref, value_ref, low=0):
    for j in range(value_ref.shape[1] // LANES):
        tile = value_ref[:, j * LANES : (j + 1) * LANES].astype(F32).T
        out_ref[low + j * LANES : low + (j + 1) * LANES, :] = tile.astype(out_ref.dtype)


def class_spread(groups, classes, rows, width):
    group = lax.broadcasted_iota(jnp.int32, (rows, width), 0)
    lane = lax.broadcasted_iota(jnp.int32, (rows, width), 1)
    inside = (lane >= group * classes) & (lane < group * classes + classes) & (group < groups)
    return jnp.where(inside, 1.0, 0.0).astype(BF)


def hot_rows(ids, classes, groups, width):
    here = product(ids.astype(BF), class_spread(groups, classes, ids.shape[1], width))
    lane = lax.broadcasted_iota(jnp.int32, (1, width), 1)
    same = here == jnp.bitwise_and(lane, classes - 1).astype(F32)
    return jnp.where(same & (lane < groups * classes), 1.0, 0.0)


def vector_of(packed, low, tiles):
    return jnp.concatenate(
        [packed[r, low + i : low + i + 1, :] for r in range(4) for i in range(tiles)], 1
    )


def put_vector(small_ref, low, value):
    tiles = value.shape[1] // (4 * LANES)
    for r in range(4):
        for i in range(tiles):
            start = (r * tiles + i) * LANES
            small_ref[r % 2, r // 2, low + i : low + i + 1, :] = value[:, start : start + LANES]


def put_table(small_ref, low, value, rows):
    for r in range(4):
        small_ref[r % 2, r // 2, low : low + rows, :] = value[
            0:rows, r * LANES : (r + 1) * LANES
        ]


OBS, MAN_G, MAN_O, GOAL_G, ACT_G, CRI_G, CRI_O, IMG_G, GRU_G, POST_G, PRIOR_G, ENC_G, LOSS = (
    0, 2, 3, 4, 5, 6, 7, 8, 10, 16, 18, 20, 21,
)
ACT_T, ENC_T, IMG_T, SMALL_TILES = (24, 48, 112, 160)
TAB_ACT, TAB_ENC, TAB_IMG, TAB_GOAL, TABLES = (0, 32, 96, 160, 224)
VECTOR_TILES = 24


def spread_lanes(low_ref, out_ref, first_row, which):
    lane = lax.broadcasted_iota(jnp.int32, (ROWS, LANES), 1)
    keep = (lane < 64) if which == 0 else (lane >= 64)
    for j in range(4):
        tile = low_ref[:, j * LANES : (j + 1) * LANES].astype(F32)
        turned = pltpu.roll(tile, 64, 1)
        for x in range(2):
            source = tile if x == which else turned
            lanes = slice((2 * j + x) * LANES, (2 * j + x + 1) * LANES)
            out_ref[first_row : first_row + ROWS, lanes] = jnp.where(keep, source, 0.0).astype(BF)


def column(meta, k):
    return meta[:, k : k + 1]


class Frames(NamedTuple):
    meta: Any = taken(ROWS, LANES, dtype=F32)
    prev: Any = taken(ROWS, H)
    embed: Any = taken(ROWS, E)
    vector_share: Any = taken(VECTOR_TILES, LANES, dtype=F32)
    table_share: Any = taken(TABLES, LANES)
    img_stoch_share: Any = taken(Z // 4, H, here=False)
    gru_weight_share: Any = taken(H // 2, 3 * H, here=False)
    manager_in_share: Any = taken(H // 4, U, here=False)
    enc_in_share: Any = taken(H // 4, U, here=False)
    goal_out_share: Any = taken(U // 4, H, here=False)
    prior_in_share: Any = taken(H // 4, H, here=False)
    post_in_share: Any = taken((H + E) // 4, H, here=False)
    prior_out_share: Any = taken(H // 4, Z, here=False)
    post_out_share: Any = taken(H // 4, Z, here=False)
    actor_in_share: Any = taken(768, U, here=False)
    critic_in_share: Any = taken(768, U, here=False)
    gru_weight_out: Any = given(2 * H, 3 * H, here=False)
    goal_out_out: Any = given(U, H, here=False)
    actor_in_out: Any = given(3 * H, U, here=False)
    critic_in_out: Any = given(3 * H, U, here=False)
    vectors: Any = given(4, VECTOR_TILES, LANES, dtype=F32)
    tables: Any = given(4, TABLES, LANES)
    start_state: Any = given(ROWS, H + LANES)
    gru_left: Any = given(2 * H, ROWS)
    post_left: Any = given(H + E, ROWS)
    post_out_left: Any = given(H, ROWS)
    prior_out_left: Any = given(H, ROWS)
    img_left: Any = given(Z, ROWS)
    me_left: Any = given(H, 2 * ROWS)
    dec_left: Any = given(U, ROWS)
    soft_turned: Any = given(GCODE, ROWS)
    post_right: Any = given(ROWS, H)
    prior_right: Any = given(ROWS, H)
    post_out_right: Any = given(ROWS, Z)
    prior_out_right: Any = given(ROWS, Z)
    me_right: Any = given(2 * ROWS, 2 * U)
    recon_low: Any = given(ROWS, H)
    dec_pair: Any = given(ROWS, 2 * U)
    gru_normed: Any = given(ROWS, 3 * H, dtype=F32)
    gru_inverse: Any = given(ROWS, 1, dtype=F32)
    img_normed: Any = given(ROWS, H, dtype=F32)
    img_inverse: Any = given(ROWS, 1, dtype=F32)
    grad_deter: Any = given(ROWS, H, dtype=F32)
    embed_grad: Any = given(ROWS, E, dtype=F32)
    small: Any = given(2, 2, SMALL_TILES, LANES, dtype=F32)
    img_stoch: Any = kept(Z, H)
    gru_weight: Any = kept(2 * H, 3 * H)
    manager_in: Any = kept(H, U)
    enc_in: Any = kept(H, U)
    goal_out: Any = kept(U, H)
    prior_in: Any = kept(H, H)
    post_in: Any = kept(H + E, H)
    prior_out: Any = kept(H, Z)
    post_out: Any = kept(H, Z)
    actor_in: Any = kept(3 * H, U)
    critic_in: Any = kept(3 * H, U)
    img_action: Any = kept(32, H)
    enc_out: Any = kept(GCODE, U)
    goal_in: Any = kept(GCODE, U)
    hot: Any = kept(ROWS, Z)
    meta_turned: Any = kept(LANES, ROWS, dtype=F32)
    img_hidden: Any = kept(ROWS, H)
    deter: Any = kept(ROWS, H, dtype=F32)
    deter_low: Any = kept(ROWS, H)
    feature: Any = kept(ROWS, H)
    obs_normed: Any = kept(ROWS, H, dtype=F32)
    obs_inverse: Any = kept(ROWS, 1, dtype=F32)
    outgoing: Any = kept(ROWS, H + LANES)
    incoming: Any = kept(ROWS, H + LANES)
    pre_512: Any = kept(ROWS, U, dtype=F32)
    hid_512: Any = kept(ROWS, U)
    back_512: Any = kept(ROWS, U)
    wide_512: Any = kept(ROWS, U, dtype=F32)
    inverse: Any = kept(ROWS, 1, dtype=F32)
    grad_value: Any = kept(ROWS, 1, dtype=F32)
    dec_normed: Any = kept(ROWS, U, dtype=F32)
    dec_inverse: Any = kept(ROWS, 1, dtype=F32)
    dec_hidden: Any = kept(ROWS, U)
    dec_pre: Any = kept(ROWS, U)
    wide: Any = kept(ROWS, H, dtype=F32)
    prior_normed: Any = kept(ROWS, H, dtype=F32)
    prior_inverse: Any = kept(ROWS, 1, dtype=F32)
    prior_hidden: Any = kept(ROWS, H)
    post_normed: Any = kept(ROWS, H, dtype=F32)
    post_inverse: Any = kept(ROWS, 1, dtype=F32)
    post_hidden: Any = kept(ROWS, H)
    post_turned: Any = kept(Z, ROWS, dtype=F32)
    prior_turned: Any = kept(Z, ROWS, dtype=F32)
    loss: Any = kept(1, 1, dtype=F32)
    piece_send: Any = signal(14, 8)
    piece_recv: Any = signal(14, 8)
    load_done: Any = signal(14)
    save_done: Any = signal(4)
    small_send: Any = signal(2, 3)
    small_recv: Any = signal(2, 3)
    state_send: Any = signal(8)
    state_recv: Any = signal(8)

    def start(self):
        meta = self.meta[...]
        hot = hot_rows(meta[:, 0:ZG], ZK, ZG, Z)
        self.hot[...] = hot.astype(BF)
        turn_into(self.img_left, self.hot)
        turn_into(self.gru_left, self.prev, H)
        turn_into(self.post_left, self.embed, H)
        self.meta_turned[...] = meta.T
        self.small[...] = jnp.zeros(self.small.shape, F32)

    def unpack(self):
        for r in range(4):
            for i in range(2):
                self.img_action[:, (2 * r + i) * LANES : (2 * r + i + 1) * LANES] = self.tables[
                    r, TAB_IMG + 32 * i : TAB_IMG + 32 * (i + 1), :
                ]
            self.enc_out[:, r * LANES : (r + 1) * LANES] = self.tables[
                r, TAB_ENC : TAB_ENC + 64, :
            ]
            for i in range(4):
                self.goal_in[16 * r : 16 * (r + 1), i * LANES : (i + 1) * LANES] = self.tables[
                    r, TAB_GOAL + 16 * i : TAB_GOAL + 16 * (i + 1), :
                ]

    def gain(self, low, size):
        return vector_of(self.vectors, low, size // (4 * LANES))

    def img(self):
        meta = self.meta[...]
        lane = lax.broadcasted_iota(jnp.int32, (ROWS, 32), 1).astype(F32)
        action = jnp.where(column(meta, 32) == lane, 1.0, 0.0).astype(BF)
        matmul_into(
            self.img_normed, self.hot[...], self.img_stoch,
            extra=lambda start, tile: product(action, self.img_action[:, pl.ds(start, tile)]),
        )
        hidden_rows(self.img_normed, self.img_inverse, self.gain(IMG_G, H), self.img_hidden)
        turn_into(self.gru_left, self.img_hidden)

    def gru(self, third):
        low = third * H
        out = self.gru_normed.at[:, low : low + H]

        def one(j, carry):
            start = pl.multiple_of(low + j * 256, 256)
            value = product(self.img_hidden[...], self.gru_weight[0:H, pl.ds(start, 256)])
            value = value + product(
                self.prev[...], self.gru_weight[H : 2 * H, pl.ds(start, 256)]
            )
            self.gru_normed[:, pl.ds(start, 256)] = value
            return carry

        lax.fori_loop(0, 4, one, 0)

    def state(self):
        gain = self.gain(GRU_G, 3 * H)
        obs_gain = self.gain(OBS, H)

        def one(rows, carry):
            normed, inverse = normalize(self.gru_normed[rows, :])
            self.gru_normed[rows, :] = normed
            self.gru_inverse[rows, :] = inverse
            parts = normed * gain
            reset = 1.0 / (1.0 + jnp.exp(-parts[:, :H]))
            candidate = jnp.tanh(reset * parts[:, H : 2 * H])
            update = 1.0 / (1.0 + jnp.exp(1.0 - parts[:, 2 * H :]))
            state = update * candidate + (1.0 - update) * self.prev[rows, :].astype(F32)
            self.deter[rows, :] = state
            self.deter_low[rows, :] = state.astype(BF)
            obs, obs_inverse = normalize(state)
            self.obs_normed[rows, :] = obs
            self.obs_inverse[rows, :] = obs_inverse
            self.feature[rows, :] = (obs * obs_gain).astype(BF)
            return carry

        by_rows(ROWS, 16, one)
        turn_into(self.post_left, self.deter_low)

    def picked(self):
        meta = self.meta[...]
        lane = lax.broadcasted_iota(jnp.int32, (ROWS, ROWS), 1).astype(F32)
        pick = jnp.where(column(meta, 37) == lane, 1.0, 0.0).astype(BF)

        def one(j, carry):
            lanes = pl.ds(pl.multiple_of(j * 256, 256), 256)
            self.outgoing[:, lanes] = product(pick, self.deter_low[:, lanes]).astype(BF)
            return carry

        lax.fori_loop(0, H // 256, one, 0)
        valid = jnp.broadcast_to(column(meta, 33), (ROWS, LANES)).astype(BF)
        self.outgoing[:, H:] = product(pick, valid).astype(BF)

    def manager(self):
        meta = self.meta[...]
        gain, head = (self.gain(MAN_G, U), self.gain(MAN_O, U))
        for j in range(H // LANES):
            lanes = slice(j * LANES, (j + 1) * LANES)
            self.me_left[lanes, 0:ROWS] = self.feature[:, lanes].astype(F32).T.astype(BF)
            self.me_left[lanes, ROWS:] = self.deter_low[:, lanes].astype(F32).T.astype(BF)
        matmul_into(self.pre_512, self.feature[...], self.manager_in)
        hidden_rows(self.pre_512, self.inverse, gain, self.hid_512)
        value = jnp.sum(self.hid_512[...].astype(F32) * head, -1, keepdims=True)
        valid, linked, carried, rewards = (column(meta, 33 + i) for i in range(4))
        later = pltpu.roll(jnp.broadcast_to(value, (ROWS, LANES)), ROWS - 1, 0)
        base = jnp.where(
            linked > 0, rewards + discount * carried * ((1.0 - return_mix) * later), value
        )
        slope = jnp.broadcast_to(linked * (discount * return_mix) * carried, (ROWS, LANES))
        step = 1
        while step < LEN:
            base = base + slope * pltpu.roll(base, ROWS - step, 0)
            slope = slope * pltpu.roll(slope, ROWS - step, 0)
            step *= 2
        misfit = value - base[:, 0:1]
        scale = valid * (1.0 / ROWS)
        self.loss[...] = 0.5 * jnp.sum(scale * misfit * misfit, 0, keepdims=True)
        grad_value = scale * misfit
        put_vector(
            self.small, MAN_O,
            jnp.sum(self.hid_512[...].astype(F32) * grad_value, 0, keepdims=True),
        )
        self.grad_value[...] = grad_value
        total = hidden_rows_back(
            lambda rows: self.grad_value[rows, :] * head,
            self.pre_512, self.inverse, gain, self.back_512,
        )
        put_vector(self.small, MAN_G, total)
        spread_lanes(self.back_512, self.me_right, 0, 0)
        self.feature_back()

    def feature_back(self):
        obs_gain = self.gain(OBS, H)
        matmul_into(self.wide, self.back_512[...], self.manager_in, turned=True)

        def one(rows, total):
            grad = self.wide[rows, :]
            normed = self.obs_normed[rows, :]
            total = total + jnp.sum(grad * normed, 0, keepdims=True)
            self.grad_deter[rows, :] = normalize_back(
                grad * obs_gain, normed, self.obs_inverse[rows, :]
            )
            return total

        put_vector(self.small, OBS, by_rows(ROWS, 32, one, jnp.zeros((1, H), F32)))

    def add_back(self, left_ref, weight_ref):
        def one(j, carry):
            lanes = pl.ds(pl.multiple_of(j * 256, 256), 256)
            self.grad_deter[:, lanes] += lax.dot_general(
                left_ref[...], weight_ref[lanes, :], (((1,), (1,)), ((), ())),
                preferred_element_type=F32,
            )
            return carry

        lax.fori_loop(0, H // 256, one, 0)

    def encoder(self):
        gain, goal_gain = (self.gain(ENC_G, U), self.gain(GOAL_G, U))
        valid_row = self.meta_turned[33:34, :]
        scale_row = valid_row * (1.0 / ROWS)
        scale = column(self.meta[...], 33) * (1.0 / ROWS)
        matmul_into(self.pre_512, self.deter_low[...], self.enc_in)
        hidden_rows(self.pre_512, self.inverse, gain, self.hid_512)
        logits = lax.dot_general(
            self.enc_out[...], self.hid_512[...], (((1,), (1,)), ((), ())),
            preferred_element_type=F32,
        ).reshape(GC, GK, ROWS)
        shifted = logits - jnp.max(logits, 1, keepdims=True)
        code_log = shifted - jnp.log(jnp.sum(jnp.exp(shifted), 1, keepdims=True))
        code = jnp.exp(code_log)
        spread = jnp.sum(code * code_log, 1, keepdims=True)
        code_kl = jnp.sum(jnp.sum(code * (code_log + math.log(GK)), 1), 0, keepdims=True)
        flat = jnp.concatenate(
            [code.reshape(GCODE, ROWS), jnp.zeros((ROWS - GCODE, ROWS), F32)], 0
        )
        self.soft_turned[...] = flat[0:GCODE].astype(BF)
        soft = flat.T[:, 0:GCODE].astype(BF)
        matmul_into(self.dec_normed, soft, self.goal_in)
        hidden_rows(self.dec_normed, self.dec_inverse, goal_gain, self.dec_hidden)
        turn_into(self.dec_left, self.dec_hidden)

        def one(j, total):
            lanes = pl.ds(pl.multiple_of(j * 256, 256), 256)
            err = product(self.dec_hidden[...], self.goal_out[:, lanes]) - self.deter[:, lanes]
            grad = scale * err * (1.0 / H)
            self.grad_deter[:, lanes] -= grad
            self.recon_low[:, lanes] = grad.astype(BF)
            return total + jnp.sum(err * err, -1, keepdims=True)

        squares = lax.fori_loop(0, H // 256, one, jnp.zeros((ROWS, 1), F32))
        self.loss[...] += jnp.sum(scale * (0.5 / H) * squares, 0, keepdims=True) + jnp.sum(
            scale_row * code_kl, 1, keepdims=True
        )
        matmul_into(self.wide_512, self.recon_low[...], self.goal_out, turned=True)
        total = hidden_rows_back(
            lambda rows: self.wide_512[rows, :],
            self.dec_normed, self.dec_inverse, goal_gain, self.dec_pre,
        )
        put_vector(self.small, GOAL_G, total)
        spread_lanes(self.dec_pre, self.dec_pair, 0, 0)
        grad_code = lax.dot_general(
            self.goal_in[...], self.dec_pre[...], (((1,), (1,)), ((), ())),
            preferred_element_type=F32,
        ).reshape(GC, GK, ROWS)
        grad_logits = code * (grad_code - jnp.sum(code * grad_code, 1, keepdims=True))
        grad_logits = grad_logits + scale_row[None] * code * (code_log - spread)
        grad_turned = grad_logits.reshape(GCODE, ROWS)
        grad_low = jnp.concatenate(
            [grad_turned, jnp.zeros((ROWS - GCODE, ROWS), F32)], 0
        ).T[:, 0:GCODE].astype(BF)
        put_table(
            self.small, ENC_T, product(grad_turned.astype(BF), self.hid_512[...]), GCODE
        )
        matmul_into(self.wide_512, grad_low, self.enc_out)
        total = hidden_rows_back(
            lambda rows: self.wide_512[rows, :],
            self.pre_512, self.inverse, gain, self.back_512,
        )
        put_vector(self.small, ENC_G, total)
        spread_lanes(self.back_512, self.me_right, ROWS, 1)
        self.add_back(self.back_512, self.enc_in)

    def prior(self):
        matmul_into(self.prior_normed, self.deter_low[...], self.prior_in)
        hidden_rows(
            self.prior_normed, self.prior_inverse, self.gain(PRIOR_G, H), self.prior_hidden
        )
        turn_into(self.prior_out_left, self.prior_hidden)

    def post(self):
        def one(j, carry):
            lanes = pl.ds(pl.multiple_of(j * 256, 256), 256)
            value = product(self.deter_low[...], self.post_in[0:H, lanes])
            self.post_normed[:, lanes] = value + product(
                self.embed[...], self.post_in[H : H + E, lanes]
            )
            return carry

        lax.fori_loop(0, H // 256, one, 0)
        hidden_rows(self.post_normed, self.post_inverse, self.gain(POST_G, H), self.post_hidden)
        turn_into(self.post_out_left, self.post_hidden)

    def logits(self, hidden_ref, weight_ref, turned_ref):
        matmul_into(self.wide, hidden_ref[...], weight_ref)
        turn_into(turned_ref, self.wide)

    def state_kl(self):
        scale_row = self.meta_turned[33:34, :] * (1.0 / ROWS)

        def log_part(value):
            shifted = value - jnp.max(value, 0, keepdims=True)
            return shifted - jnp.log(jnp.sum(jnp.exp(shifted), 0, keepdims=True))

        def one(rows, total):
            post_log = log_part(self.post_turned[rows, :])
            prior_log = log_part(self.prior_turned[rows, :])
            post = jnp.exp(post_log)
            gap = post_log - prior_log
            kl = jnp.sum(post * gap, 0, keepdims=True)
            self.post_turned[rows, :] = scale_row * post * (gap - kl)
            self.prior_turned[rows, :] = scale_row * (jnp.exp(prior_log) - post)
            return total + kl

        total = by_rows(Z, ZK, one, jnp.zeros((1, ROWS), F32))
        self.loss[...] += jnp.sum(scale_row * total, 1, keepdims=True)
        for turned, low in (
            (self.post_turned, self.post_out_right), (self.prior_turned, self.prior_out_right),
        ):
            for j in range(Z // LANES):
                lanes = slice(j * LANES, (j + 1) * LANES)
                low[:, lanes] = turned[lanes, :].T.astype(BF)

    def prior_back(self):
        matmul_into(self.wide, self.prior_out_right[...], self.prior_out, turned=True)
        total = hidden_rows_back(
            lambda rows: self.wide[rows, :],
            self.prior_normed, self.prior_inverse, self.gain(PRIOR_G, H), self.prior_right,
        )
        put_vector(self.small, PRIOR_G, total)
        self.add_back(self.prior_right, self.prior_in)

    def post_back(self):
        matmul_into(self.wide, self.post_out_right[...], self.post_out, turned=True)
        total = hidden_rows_back(
            lambda rows: self.wide[rows, :],
            self.post_normed, self.post_inverse, self.gain(POST_G, H), self.post_right,
        )
        put_vector(self.small, POST_G, total)
        self.add_back(self.post_right, self.post_in)
        matmul_into(self.embed_grad, self.post_right[...], self.post_in, turned=True, low=H)
        for y in range(2):
            for c in range(2):
                self.small[c, y, LOSS : LOSS + 1, :] = jnp.broadcast_to(
                    self.loss[...], (1, LANES)
                )


class Places:
    def __init__(self):
        dp, rep = (lax.axis_index("dp"), lax.axis_index("rep"))
        self.dp, self.rep = (dp, rep)
        self.x, self.z, self.w = (lax.rem(dp, 2), lax.rem(dp // 2, 2), dp // 4)
        self.y, self.c = (rep // 2, lax.rem(rep, 2))
        self.to_x = (dp + 1 - 2 * self.x, rep)
        self.to_z = (dp + 2 - 4 * self.z, rep)
        self.to_w = (dp + 4 - 8 * self.w, rep)
        self.to_y = (dp, rep + 2 - 4 * self.y)
        self.to_c = (dp, rep + 1 - 2 * self.c)
        self.to_d = (dp, 3 - rep)

    def around(self, offset):
        return lax.rem(self.dp + offset, 8)


def greet(devices):
    barrier = pltpu.get_barrier_semaphore()
    for device in devices:
        pl.semaphore_signal(barrier, inc=1, device_id=device, device_id_type=MESH)
    pl.semaphore_wait(barrier, len(devices))


def send_to(source, target, send_sem, recv_sem, device):
    return pltpu.make_async_remote_copy(
        src_ref=source,
        dst_ref=target,
        send_sem=send_sem,
        recv_sem=recv_sem,
        device_id=device,
        device_id_type=MESH,
    )


def regroup_start(places, outgoing, incoming, send_sem, recv_sem):
    count = ROWS // 8
    mine = pl.ds(pl.multiple_of(places.dp * count, 16), count)
    copies = []
    for offset in range(1, 8):
        there = places.around(offset)
        copy = send_to(
            outgoing.at[pl.ds(pl.multiple_of(there * count, 16), count)],
            incoming.at[mine],
            send_sem.at[offset],
            recv_sem.at[offset],
            (there, places.rep),
        )
        copy.start()
        copies.append(copy)
    incoming[mine, :] = outgoing[mine, :]
    return copies


def diagonal_split(quarter):
    over_y = quarter // 3 // 16 * 16
    over_x = (quarter - over_y) // 2 // 16 * 16
    over_z = quarter - over_y - over_x
    return (over_z, over_x, over_y) if over_y < over_z else (over_y, over_x, over_z)


OWN, Y_A, Y_B, X_A, Z_A, X_B, Z_B, RELAY = range(8)


class Gather:
    def __init__(self, places, units, send_sem, recv_sem, load_sem):
        self.places, self.units = (places, units)
        self.send_sem, self.recv_sem, self.load_sem = (send_sem, recv_sem, load_sem)
        self.far = places.rep + 2 - 4 * places.y
        self.mine = places.x * 2 + places.z
        self.across = 3 - self.mine
        self.from_x = (1 - places.x) * 2 + places.z
        self.from_z = places.x * 2 + 1 - places.z
        self.copies = {}
        self.loads = {}

    def remote(self, u, kind, source, target, device):
        copy = send_to(
            source, target, self.send_sem.at[u, kind], self.recv_sem.at[u, kind], device
        )
        copy.start()
        self.copies[u, kind] = copy

    def rows(self, u, share, piece, low, number):
        extent = self.units[u][0].shape[0]
        start = share * extent + piece * (extent // 4) + low
        return pl.ds(pl.multiple_of(start, 16), number)

    def part(self, u, rows, whole=True):
        share, all_rows, low, count = self.units[u]
        return (all_rows if whole else share).at[rows, pl.ds(low, count)]

    def extent(self, u):
        return self.units[u][0].shape[0]

    def load(self, u):
        everything = self.rows(u, 0, 0, 0, self.extent(u))
        copy = pltpu.make_async_copy(
            self.part(u, everything, False),
            self.part(u, self.rows(u, self.places.rep, 0, 0, self.extent(u))),
            self.load_sem.at[u],
        )
        copy.start()
        self.loads[u] = copy

    def over_y(self, u):
        if u >= len(self.units):
            return
        rep, quarter = (self.places.rep, self.extent(u) // 4)
        first = diagonal_split(quarter)[0]
        self.remote(
            u, Y_A,
            self.part(u, self.rows(u, 0, self.mine, 0, quarter), False),
            self.part(u, self.rows(u, rep, self.mine, 0, quarter)),
            self.places.to_y,
        )
        if first:
            self.remote(
                u, Y_B,
                self.part(u, self.rows(u, 0, self.across, 0, first), False),
                self.part(u, self.rows(u, rep, self.across, 0, first)),
                self.places.to_y,
            )
        everything = self.rows(u, 0, 0, 0, self.extent(u))
        self.remote(
            u, OWN,
            self.part(u, everything, False),
            self.part(u, self.rows(u, rep, 0, 0, self.extent(u))),
            self.places.to_c,
        )

    def stage_1(self, u):
        self.copies[u, Y_A].wait_recv()
        piece = self.part(u, self.rows(u, self.far, self.mine, 0, self.extent(u) // 4))
        self.remote(u, X_A, piece, piece, self.places.to_x)
        self.remote(u, Z_A, piece, piece, self.places.to_z)

    def stage_2(self, u):
        first, second, third = diagonal_split(self.extent(u) // 4)
        self.copies[u, Z_A].wait_recv()
        if second:
            piece = self.part(u, self.rows(u, self.far, self.from_z, first, second))
            self.remote(u, X_B, piece, piece, self.places.to_x)
        self.copies[u, X_A].wait_recv()
        if third:
            piece = self.part(u, self.rows(u, self.far, self.from_x, first + second, third))
            self.remote(u, Z_B, piece, piece, self.places.to_z)

    def stage_3(self, u):
        for kind in (Y_B, X_B, Z_B):
            if (u, kind) in self.copies:
                self.copies[u, kind].wait_recv()
        share = self.part(u, self.rows(u, self.far, 0, 0, self.extent(u)))
        self.remote(u, RELAY, share, share, self.places.to_c)

    def pump(self, t, ahead):
        count = len(self.units)
        if t < count:
            self.stage_1(t)
            self.over_y(t + ahead)
        if 0 <= t - 1 < count:
            self.stage_2(t - 1)
        if 0 <= t - 2 < count:
            self.stage_3(t - 2)

    def complete(self, u):
        self.loads[u].wait()
        self.copies[u, OWN].wait_recv()
        self.copies[u, RELAY].wait_recv()

    def drain(self):
        for copy in self.copies.values():
            copy.wait_send()


AHEAD = 3


def frames_kernel(f):
    places = Places()
    units = [(f.img_stoch_share, f.img_stoch, 0, H)]
    units += [(f.gru_weight_share, f.gru_weight, i * H, H) for i in range(3)]
    units += [
        (f.manager_in_share, f.manager_in, 0, U),
        (f.enc_in_share, f.enc_in, 0, U),
        (f.goal_out_share, f.goal_out, 0, H),
        (f.prior_in_share, f.prior_in, 0, H),
        (f.post_in_share, f.post_in, 0, U),
        (f.post_in_share, f.post_in, U, U),
        (f.prior_out_share, f.prior_out, 0, Z),
        (f.post_out_share, f.post_out, 0, Z),
        (f.actor_in_share, f.actor_in, 0, U),
        (f.critic_in_share, f.critic_in, 0, U),
    ]
    gather = Gather(places, units, f.piece_send, f.piece_recv, f.load_done)
    for u in range(len(units)):
        gather.load(u)
    greet(
        [(places.around(o), places.rep) for o in range(1, 8)]
        + [places.to_c, places.to_y, places.to_d]
    )
    packs = []
    for i, (share, whole) in enumerate(((f.vector_share, f.vectors), (f.table_share, f.tables))):
        for k, device in enumerate((places.to_c, places.to_y, places.to_d)):
            copy = send_to(
                share, whole.at[places.rep], f.small_send.at[i, k], f.small_recv.at[i, k], device
            )
            copy.start()
            packs.append(copy)
    for u in range(AHEAD):
        gather.over_y(u)
    f.vectors[places.rep] = f.vector_share[...]
    f.tables[places.rep] = f.table_share[...]
    f.start()
    saves = []

    def save(k, source, target):
        copy = pltpu.make_async_copy(source, target, f.save_done.at[k])
        copy.start()
        saves.append(copy)

    def pump(t):
        gather.pump(t, AHEAD)

    pump(0)
    pump(1)
    pump(2)
    for copy in packs:
        copy.wait()
    f.unpack()
    gather.complete(0)
    f.img()
    for third in range(3):
        pump(3 + third)
        gather.complete(1 + third)
        f.gru(third)
    save(0, f.gru_weight, f.gru_weight_out)
    f.state()
    f.picked()
    states = regroup_start(places, f.outgoing, f.incoming, f.state_send, f.state_recv)
    pump(6)
    gather.complete(4)
    f.manager()
    pump(7)
    gather.complete(5)
    pump(8)
    gather.complete(6)
    save(1, f.goal_out, f.goal_out_out)
    f.encoder()
    pump(9)
    gather.complete(7)
    f.prior()
    pump(10)
    pump(11)
    gather.complete(8)
    gather.complete(9)
    f.post()
    pump(12)
    gather.complete(10)
    f.logits(f.prior_hidden, f.prior_out, f.prior_turned)
    pump(13)
    gather.complete(11)
    f.logits(f.post_hidden, f.post_out, f.post_turned)
    pump(14)
    f.state_kl()
    pump(15)
    f.prior_back()
    for copy in states:
        copy.wait()
    f.start_state[...] = f.incoming[...]
    gather.complete(12)
    save(2, f.actor_in, f.actor_in_out)
    gather.complete(13)
    save(3, f.critic_in, f.critic_in_out)
    f.post_back()
    for copy in saves:
        copy.wait()
    gather.drain()


class Worker(NamedTuple):
    meta: Any = taken(ROWS, LANES, dtype=F32)
    samples: Any = taken(HOR, ROWS, ZG, dtype=F32)
    vectors: Any = taken(4, VECTOR_TILES, LANES, dtype=F32)
    tables: Any = taken(4, TABLES, LANES)
    start_state: Any = taken(ROWS, H + LANES)
    goal_out: Any = taken(U, H)
    actor_in: Any = taken(3 * H, U)
    critic_in: Any = taken(3 * H, U)
    worker_left: Any = given(3 * H, 2 * U)
    returned: Any = given(ROWS, H)
    goal_left: Any = given(U, ROWS)
    code_turned: Any = given(GCODE, ROWS)
    goal_right: Any = given(ROWS, H)
    goal_pair: Any = given(ROWS, 2 * U)
    small: Any = given(2, 2, SMALL_TILES, LANES, dtype=F32)
    act_out: Any = kept(32, U)
    goal_in: Any = kept(GCODE, U)
    goal_normed: Any = kept(ROWS, U, dtype=F32)
    goal_inverse: Any = kept(ROWS, 1, dtype=F32)
    goal_hidden: Any = kept(ROWS, U)
    goal_pre: Any = kept(ROWS, U)
    goal_low: Any = kept(ROWS, H)
    turned: Any = kept(2 * H, ROWS)
    slot_part: Any = kept(2, ROWS, U, dtype=F32)
    normed: Any = kept(2, HOR * ROWS, U, dtype=F32)
    inverse: Any = kept(2, HOR * ROWS, 1, dtype=F32)
    hidden: Any = kept(2, HOR * ROWS, U)
    hot_turned: Any = kept(Z, HOR * ROWS)
    log_chance: Any = kept(HOR * ROWS, 32, dtype=F32)
    chosen: Any = kept(HOR, ROWS, 1, dtype=F32)
    value: Any = kept(HOR, ROWS, 1, dtype=F32)
    returns: Any = kept(HOR, ROWS, 1, dtype=F32)
    pre: Any = kept(HOR * ROWS, U, dtype=F32)
    pre_pair: Any = kept(HOR * ROWS, 2 * U)
    summed: Any = kept(2, ROWS, U, dtype=F32)
    sum_low: Any = kept(2, ROWS, U)
    sum_pair: Any = kept(ROWS, 2 * U)
    to_state: Any = kept(ROWS, H)
    incoming: Any = kept(ROWS, H)
    wide: Any = kept(ROWS, H, dtype=F32)
    wide_512: Any = kept(ROWS, U, dtype=F32)
    top: Any = kept(8, LANES, dtype=F32)
    top_in: Any = kept(5, 8, LANES, dtype=F32)
    top_send: Any = signal(5)
    top_recv: Any = signal(5)
    state_send: Any = signal(8)
    state_recv: Any = signal(8)

    def gain(self, low, size):
        return vector_of(self.vectors, low, size // (4 * LANES))

    def goal(self):
        self.small[...] = jnp.zeros(self.small.shape, F32)
        for r in range(4):
            self.act_out[:, r * LANES : (r + 1) * LANES] = self.tables[
                r, TAB_ACT : TAB_ACT + 32, :
            ]
            for i in range(4):
                self.goal_in[16 * r : 16 * (r + 1), i * LANES : (i + 1) * LANES] = self.tables[
                    r, TAB_GOAL + 16 * i : TAB_GOAL + 16 * (i + 1), :
                ]
        hot = hot_rows(self.meta[:, 0:32], GK, GC, LANES)
        self.code_turned[...] = hot.T[0:GCODE].astype(BF)
        matmul_into(self.goal_normed, hot[:, 0:GCODE].astype(BF), self.goal_in)
        hidden_rows(
            self.goal_normed, self.goal_inverse, self.gain(GOAL_G, U), self.goal_hidden
        )
        turn_into(self.goal_left, self.goal_hidden)

        def one(j, totals):
            lanes = pl.ds(pl.multiple_of(j * 256, 256), 256)
            goal = product(self.goal_hidden[...], self.goal_out[:, lanes])
            state = self.start_state[:, lanes].astype(F32)
            self.goal_low[:, lanes] = goal.astype(BF)
            terms = (goal * state, goal * goal, state * state)
            return tuple(
                t + jnp.sum(term, -1, keepdims=True) for t, term in zip(totals, terms)
            )

        zero = jnp.zeros((ROWS, 1), F32)
        aligned, goal_square, state_square = lax.fori_loop(0, H // 256, one, (zero,) * 3)
        turn_into(self.turned, self.start_state.at[:, 0:H])
        turn_into(self.turned, self.goal_low, H)
        return aligned / (jnp.maximum(goal_square, state_square) + small_floor)

    def slots(self):
        for which, weight in enumerate((self.actor_in, self.critic_in)):
            def one(j, carry):
                lanes = pl.ds(pl.multiple_of(j * 256, 256), 256)
                self.slot_part[which, :, lanes] = product(
                    self.start_state[:, 0:H], weight[0:H, lanes]
                ) + product(self.goal_low[...], weight[2 * H : 3 * H, lanes])
                return carry

            lax.fori_loop(0, U // 256, one, 0)

    def forward(self):
        gains = (self.gain(ACT_G, U), self.gain(CRI_G, U))
        head = self.gain(CRI_O, U)
        spread = class_spread(ZG, ZK, ZG, Z)
        lane = lax.broadcasted_iota(jnp.int32, (1, Z), 1)
        lane_class = jnp.bitwise_and(lane, ZK - 1).astype(F32)
        group = lax.broadcasted_iota(jnp.int32, (Z, LANES), 1)
        place = lax.broadcasted_iota(jnp.int32, (Z, LANES), 0)
        inside = (place >= group * ZK) & (place < group * ZK + ZK) & (group < ZG)
        spread_turned = jnp.where(inside, 1.0, 0.0).astype(BF)
        place_class = jnp.bitwise_and(
            lax.broadcasted_iota(jnp.int32, (Z, 1), 0), ZK - 1
        ).astype(F32)
        act_lane = lax.broadcasted_iota(jnp.int32, (1, 32), 1)

        def step(k, carry):
            rows = pl.ds(pl.multiple_of(k * ROWS, ROWS), ROWS)
            ids = self.samples[k]
            hot = jnp.where(product(ids.astype(BF), spread) == lane_class, 1.0, 0.0).astype(BF)
            ids_turned = jnp.concatenate(
                [ids, jnp.zeros((ROWS, LANES - ZG), F32)], 1
            ).T.astype(BF)
            self.hot_turned[:, rows] = jnp.where(
                product(spread_turned, ids_turned) == place_class, 1.0, 0.0
            ).astype(BF)
            for which, weight in enumerate((self.actor_in, self.critic_in)):
                pre = product(hot, weight[H : 2 * H, :]) + self.slot_part[which]
                normed, inverse = normalize(pre)
                self.normed[which, rows, :] = normed
                self.inverse[which, rows, :] = inverse
                hidden = elu_of(normed * gains[which]).astype(BF)
                self.hidden[which, rows, :] = hidden
                if which == 0:
                    logits = lax.dot_general(
                        hidden, self.act_out[...], (((1,), (1,)), ((), ())),
                        preferred_element_type=F32,
                    )
                    logits = jnp.where(act_lane < NA, logits, -1e30)
                    shifted = logits - jnp.max(logits, -1, keepdims=True)
                    total = jnp.sum(jnp.exp(shifted), -1, keepdims=True)
                    log_chance = shifted - jnp.log(total)
                    self.log_chance[rows, :] = log_chance
                    self.chosen[k] = jnp.sum(
                        jnp.where(self.action_here(k), log_chance, 0.0), -1, keepdims=True
                    )
                else:
                    self.value[k] = jnp.sum(hidden.astype(F32) * head, -1, keepdims=True)
            return carry

        lax.fori_loop(0, HOR, step, 0)

    def action_here(self, k):
        meta = self.meta[...]
        lane = lax.broadcasted_iota(jnp.int32, (ROWS, LANES), 1)
        action = jnp.sum(jnp.where(lane == 32 + k, meta, 0.0), -1, keepdims=True)
        return action == lax.broadcasted_iota(jnp.int32, (1, 32), 1).astype(F32)

    def targets(self, reward):
        weight = self.start_state[:, H : H + 1].astype(F32)
        later = self.value[HOR - 1]
        self.returns[HOR - 1] = later
        result = later
        top = jnp.zeros((ROWS, 1), F32)
        for k in range(HOR - 2, -1, -1):
            blended = (1.0 - return_mix) * later + return_mix * result
            result = reward + discount * blended
            self.returns[k] = result
            later = self.value[k]
            top = jnp.maximum(top, weight * jnp.abs(result - later))
        self.top[...] = jnp.broadcast_to(jnp.max(top, 0, keepdims=True), (8, LANES))

    def critic_back(self, first, last, total):
        gain, head = (self.gain(CRI_G, U), self.gain(CRI_O, U))
        weight = self.start_state[:, H : H + 1].astype(F32)

        def step(k, totals):
            rows = pl.ds(pl.multiple_of(k * ROWS, ROWS), ROWS)
            grad = weight * (self.value[k] - self.returns[k]) * (1.0 / (ROWS * HOR))
            self.wide_512[...] = grad * head
            head_total = totals[1] + jnp.sum(
                self.hidden[1, rows, :].astype(F32) * grad, 0, keepdims=True
            )
            gain_total = totals[0] + hidden_rows_back(
                lambda r: self.wide_512[r, :],
                self.normed.at[1, rows], self.inverse.at[1, rows], gain, self.pre.at[rows],
                64,
            )
            low = self.pre[rows, :].astype(BF).astype(F32)
            self.pre[rows, :] = low
            self.summed[1] += low
            return (gain_total, head_total)

        return lax.fori_loop(first, last, step, total)

    def pair(self, first, second, out_ref, rows):
        lane = lax.broadcasted_iota(jnp.int32, (ROWS, LANES), 1)
        for j in range(4):
            lanes = slice(j * LANES, (j + 1) * LANES)
            a, b = (first[:, lanes], second[:, lanes])
            out_ref[rows, 2 * j * LANES : (2 * j + 1) * LANES] = jnp.where(
                lane < 64, a, pltpu.roll(b, 64, 1)
            ).astype(BF)
            out_ref[rows, (2 * j + 1) * LANES : (2 * j + 2) * LANES] = jnp.where(
                lane < 64, pltpu.roll(a, 64, 1), b
            ).astype(BF)

    def actor_back(self):
        gain = self.gain(ACT_G, U)
        weight = self.start_state[:, H : H + 1].astype(F32)
        scale = self.top[0:1, 0:1] + small_floor

        def step(k, totals):
            rows = pl.ds(pl.multiple_of(k * ROWS, ROWS), ROWS)
            advantage = self.returns[k] - self.value[k]
            chosen_grad = -weight * advantage / scale * (1.0 / (ROWS * HOR))
            hot = jnp.where(self.action_here(k), 1.0, 0.0)
            grad = chosen_grad * (hot - jnp.exp(self.log_chance[rows, :]))
            grad_low = grad.astype(BF)
            grad_turned = jnp.concatenate(
                [grad, jnp.zeros((ROWS, LANES - 32), F32)], 1
            ).T[0:32].astype(BF)
            out_total = totals[1] + product(grad_turned, self.hidden[0, rows, :])
            self.wide_512[...] = product(grad_low, self.act_out[...])
            gain_total = totals[0] + hidden_rows_back(
                lambda r: self.wide_512[r, :],
                self.normed.at[0, rows], self.inverse.at[0, rows], gain,
                self.normed.at[0, rows], 64,
            )
            low = self.normed[0, rows, :].astype(BF).astype(F32)
            self.summed[0] += low
            self.pair(low, self.pre[rows, :], self.pre_pair, rows)
            loss = totals[2] + jnp.sum(
                weight * self.chosen[k] * advantage / scale, 0, keepdims=True
            )
            return (gain_total, out_total, loss)

        start = (jnp.zeros((1, U), F32), jnp.zeros((32, U), F32), jnp.zeros((1, 1), F32))
        return lax.fori_loop(0, HOR, step, start)

    def inputs_back(self, low, out_ref):
        def one(j, carry):
            rows = pl.ds(pl.multiple_of(low + j * 256, 256), 256)
            total = 0.0
            for which, weight in enumerate((self.actor_in, self.critic_in)):
                total = total + lax.dot_general(
                    self.sum_low[which], weight[rows, :], (((1,), (1,)), ((), ())),
                    preferred_element_type=F32,
                )
            out_ref[:, pl.ds(pl.multiple_of(j * 256, 256), 256)] = total.astype(BF)
            return carry

        lax.fori_loop(0, H // 256, one, 0)

    def goal_back(self):
        matmul_into(self.wide_512, self.goal_right[...], self.goal_out, turned=True)
        total = hidden_rows_back(
            lambda rows: self.wide_512[rows, :],
            self.goal_normed, self.goal_inverse, self.gain(GOAL_G, U), self.goal_pre,
        )
        put_vector(self.small, GOAL_G, total)
        spread_lanes(self.goal_pre, self.goal_pair, 0, 0)

    def weights(self):
        def one(j, carry):
            lanes = pl.ds(pl.multiple_of(j * 256, 256), 256)
            self.worker_left[H : 2 * H, lanes] = product(
                self.hot_turned[...], self.pre_pair[:, lanes]
            ).astype(BF)
            pair = self.sum_pair[:, lanes]
            self.worker_left[0:H, lanes] = product(self.turned[0:H], pair).astype(BF)
            self.worker_left[2 * H : 3 * H, lanes] = product(
                self.turned[H : 2 * H], pair
            ).astype(BF)
            return carry

        lax.fori_loop(0, 2 * U // 256, one, 0)


def worker_kernel(f):
    places = Places()
    peers = (places.to_c, places.to_y, places.to_x, places.to_z, places.to_w)
    greet(
        [(places.around(o), places.rep) for o in range(1, 8)] + [places.to_c, places.to_y]
    )
    reward = f.goal()
    f.slots()
    f.forward()
    f.targets(reward)
    f.summed[...] = jnp.zeros(f.summed.shape, F32)
    totals = (jnp.zeros((1, U), F32), jnp.zeros((1, U), F32))
    steps = (0, 3, 6, 9, 12, HOR)
    for k in range(5):
        copy = send_to(f.top, f.top_in.at[k], f.top_send.at[k], f.top_recv.at[k], peers[k])
        copy.start()
        totals = f.critic_back(steps[k], steps[k + 1], totals)
        copy.wait()
        f.top[...] = jnp.maximum(f.top[...], f.top_in[k])
    put_vector(f.small, CRI_G, totals[0])
    put_vector(f.small, CRI_O, totals[1])
    actor_gain, actor_out, chosen = f.actor_back()
    put_vector(f.small, ACT_G, actor_gain)
    put_table(f.small, ACT_T, actor_out, 24)
    weight = f.start_state[:, H : H + 1].astype(F32)
    squares = jnp.zeros((ROWS, 1), F32)
    for k in range(HOR):
        misfit = f.value[k] - f.returns[k]
        squares = squares + misfit * misfit
    loss = (0.5 * jnp.sum(weight * squares, 0, keepdims=True) - chosen) * (1.0 / (ROWS * HOR))
    for y in range(2):
        for c in range(2):
            f.small[c, y, LOSS : LOSS + 1, :] = jnp.broadcast_to(loss, (1, LANES))
    for which in range(2):
        f.sum_low[which] = f.summed[which].astype(BF)
    everything = pl.ds(0, ROWS)
    f.pair(f.sum_low[0].astype(F32), f.sum_low[1].astype(F32), f.sum_pair, everything)
    f.inputs_back(0, f.to_state)
    states = regroup_start(places, f.to_state, f.incoming, f.state_send, f.state_recv)
    f.inputs_back(2 * H, f.goal_right)
    f.goal_back()
    f.weights()
    for copy in states:
        copy.wait()
    f.returned[...] = f.incoming[...]


class Back(NamedTuple):
    meta: Any = taken(ROWS, LANES, dtype=F32)
    prev: Any = taken(ROWS, H)
    vectors: Any = taken(4, VECTOR_TILES, LANES, dtype=F32)
    gru_weight: Any = taken(2 * H, 3 * H)
    returned: Any = taken(ROWS, H)
    grad_partial: Any = taken(ROWS, H, dtype=F32)
    gru_normed: Any = taken(ROWS, 3 * H, dtype=F32)
    gru_inverse: Any = taken(ROWS, 1, dtype=F32)
    img_normed: Any = taken(ROWS, H, dtype=F32)
    img_inverse: Any = taken(ROWS, 1, dtype=F32)
    small_1: Any = taken(2, 2, SMALL_TILES, LANES, dtype=F32)
    small_2: Any = taken(2, 2, SMALL_TILES, LANES, dtype=F32)
    deter_grad: Any = given(ROWS, H, dtype=F32)
    gru_right: Any = given(ROWS, 3 * H)
    img_right: Any = given(ROWS, H)
    small: Any = given(2, 2, SMALL_TILES, LANES, dtype=F32)
    grad: Any = kept(ROWS, H, dtype=F32)
    wide: Any = kept(ROWS, 2 * H, dtype=F32)


def back_kernel(f):
    f.small[...] = f.small_1[...] + f.small_2[...]
    gain = vector_of(f.vectors, GRU_G, 6)
    meta = f.meta[...]
    lane = lax.broadcasted_iota(jnp.int32, (ROWS, LANES), 1)
    order = jnp.where(lane == 37, meta, 0.0).T[37:38, :]
    frame = lax.broadcasted_iota(jnp.int32, (ROWS, ROWS), 0).astype(F32)
    place = jnp.where(order == frame, 1.0, 0.0).astype(BF)

    def add(j, carry):
        lanes = pl.ds(pl.multiple_of(j * 256, 256), 256)
        f.grad[:, lanes] = f.grad_partial[:, lanes] + product(place, f.returned[:, lanes])
        return carry

    lax.fori_loop(0, H // 256, add, 0)

    def one(rows, total):
        normed = f.gru_normed[rows, :]
        parts = normed * gain
        inner = parts[:, H : 2 * H]
        reset = 1.0 / (1.0 + jnp.exp(-parts[:, :H]))
        candidate = jnp.tanh(reset * inner)
        update = 1.0 / (1.0 + jnp.exp(1.0 - parts[:, 2 * H :]))
        grad = f.grad[rows, :]
        prev = f.prev[rows, :].astype(F32)
        grad_inner = grad * update * (1.0 - candidate * candidate)
        grad_parts = jnp.concatenate(
            [
                grad_inner * inner * reset * (1.0 - reset),
                grad_inner * reset,
                grad * (candidate - prev) * update * (1.0 - update),
            ],
            1,
        )
        f.deter_grad[rows, :] = grad * (1.0 - update)
        total = total + jnp.sum(grad_parts * normed, 0, keepdims=True)
        back = normalize_back(grad_parts * gain, normed, f.gru_inverse[rows, :])
        f.gru_right[rows, :] = back.astype(BF)
        return total

    put_vector(f.small, GRU_G, by_rows(ROWS, 16, one, jnp.zeros((1, 3 * H), F32)))
    matmul_into(f.wide, f.gru_right[...], f.gru_weight, turned=True)
    f.deter_grad[...] += f.wide[:, H : 2 * H]
    total = hidden_rows_back(
        lambda rows: f.wide[rows, 0:H],
        f.img_normed, f.img_inverse, vector_of(f.vectors, IMG_G, 2), f.img_right,
    )
    put_vector(f.small, IMG_G, total)
    lane = lax.broadcasted_iota(jnp.int32, (ROWS, LANES), 1)
    action = jnp.sum(jnp.where(lane == 32, meta, 0.0), -1, keepdims=True)
    hot = jnp.where(action == lane.astype(F32), 1.0, 0.0).T[0:24].astype(BF)
    for r in range(4):
        for i in range(2):
            start = (2 * r + i) * LANES
            f.small[r % 2, r // 2, IMG_T + 24 * i : IMG_T + 24 * (i + 1), :] = product(
                hot, f.img_right[:, start : start + LANES]
            )


class Source(NamedTuple):
    rows: int
    parts: Any
    columns: int

    @property
    def depth(self):
        return sum(self.parts)


GRU, POST, PRIOR, POST_OUT, PRIOR_OUT, IMG, MAN_ENC, GOAL_OUT, GOAL_IN, WORKER = range(10)
SOURCES = (
    Source(512, (ROWS,), 3072),
    Source(640, (ROWS,), 1024),
    Source(256, (ROWS,), 1024),
    Source(256, (ROWS,), 1024),
    Source(256, (ROWS,), 1024),
    Source(256, (ROWS,), 1024),
    Source(256, (2 * ROWS,), 1024),
    Source(128, (ROWS, ROWS), 1024),
    Source(16, (ROWS, ROWS), 1024),
)
WORKER_SHARE = (768, 1024)
ALONG_X, ALONG_Z, ALONG_W, ALONG_Y = range(4)
Y_FIRST = (ALONG_Y, ALONG_X, ALONG_Z, ALONG_W)
X_FIRST = (ALONG_X, ALONG_Z, ALONG_Y, ALONG_W)
Z_FIRST = (ALONG_Z, ALONG_Y, ALONG_X, ALONG_W)
UNITS = (
    (POST, 128, 0, Y_FIRST),
    (WORKER, 128, 0, X_FIRST),
    (POST_OUT, 128, 0, Z_FIRST),
    (GRU, 384, 0, Y_FIRST),
    (GRU, 384, 128, X_FIRST),
    (GRU, 384, 256, Z_FIRST),
    (PRIOR_OUT, 128, 0, Y_FIRST),
    (IMG, 128, 0, X_FIRST),
    (PRIOR, 128, 0, Z_FIRST),
    (MAN_ENC, 128, 0, Y_FIRST),
    (GOAL_OUT, 128, 0, X_FIRST),
    (GOAL_IN, 128, 0, Z_FIRST),
)


def unit_rows(unit):
    return WORKER_SHARE[0] if unit[0] == WORKER else SOURCES[unit[0]].rows


def reduce_kernel(*refs):
    count, units = (len(SOURCES), len(UNITS))
    parts = sum(len(source.parts) for source in SOURCES)
    refs = iter(refs)

    def take(number):
        return [next(refs) for _ in range(number)]

    left_parts, right_parts = (take(parts), take(parts))
    worker, small = take(2)
    outs, (small_out,) = (take(units), take(1))
    left_2, right_2 = (take(count), take(count))
    worker_own, worker_sib = take(2)
    outbox = [take(4) for _ in range(units)]
    inbox = [take(4) for _ in range(units)]
    small_in = take(5)
    ex_send, ex_recv, wk_send, wk_recv, wk_local, st_send, st_recv, sm_send, sm_recv = take(9)
    places = Places()
    core = places.c
    bits = (places.x, places.z, places.w, places.y)
    peers = (places.to_x, places.to_z, places.to_w, places.to_y)
    greet((places.to_c,) + peers)
    exchange, own = ([], [])
    part = 0
    for s, source in enumerate(SOURCES):
        group, low = ([], 0)
        for depth in source.parts:
            left, right = (left_parts[part], right_parts[part])
            high = source.depth + low
            group.append(
                send_to(
                    right, right_2[s].at[pl.ds(high, depth)],
                    ex_send.at[part, 0], ex_recv.at[part, 0], places.to_c,
                )
            )
            for y in range(2):
                start = (2 * y + 1 - core) * source.rows
                group.append(
                    send_to(
                        left.at[pl.ds(pl.multiple_of(start, 16), source.rows)],
                        left_2[s].at[y, :, pl.ds(high, depth)],
                        ex_send.at[part, 1 + y], ex_recv.at[part, 1 + y], places.to_c,
                    )
                )
            own.append((s, left, right, low, depth))
            low += depth
            part += 1
        exchange.append(group)
    group = []
    for y in range(2):
        theirs = pl.ds(pl.multiple_of((2 * y + 1 - core) * WORKER_SHARE[0], 16), WORKER_SHARE[0])
        ours = pl.ds(pl.multiple_of((2 * y + core) * WORKER_SHARE[0], 16), WORKER_SHARE[0])
        group.append(
            send_to(worker.at[theirs], worker_sib.at[y], wk_send.at[y], wk_recv.at[y], places.to_c)
        )
        group.append(pltpu.make_async_copy(worker.at[ours], worker_own.at[y], wk_local.at[y]))
    exchange.append(group)
    for unit in UNITS:
        for copy in exchange[unit[0]] if unit[2] == 0 else ():
            copy.start()
    for s, left, right, low, depth in own:
        right_2[s][low : low + depth] = right[...]
        for y in range(2):
            start = pl.multiple_of((2 * y + core) * SOURCES[s].rows, 16)
            left_2[s][y, :, low : low + depth] = left[pl.ds(start, SOURCES[s].rows)]
    arrived = set()

    def term(u, y, device):
        s, stride, offset, _ = UNITS[u]
        lanes = pl.ds(pl.multiple_of(device * stride + offset, LANES), LANES)
        if s == WORKER:
            return worker_own[y, :, lanes].astype(F32) + worker_sib[y, :, lanes].astype(F32)
        return product(left_2[s][y], right_2[s][:, lanes])

    def block(u, k, j):
        order = UNITS[u][3]
        place = {}
        for i, along in enumerate(order):
            if i < k:
                place[along] = bits[along]
            elif i == k:
                place[along] = 1 - bits[along]
            else:
                place[along] = lax.rem(j // (1 << (3 - i)), 2)
        device = place[ALONG_W] * 4 + place[ALONG_Z] * 2 + place[ALONG_X]
        total = term(u, place[ALONG_Y], device)
        for i in range(k):
            index = 0
            for p in range(i + 1, 4):
                index = index * 2 + place[order[p]]
            total = total + inbox[u][i][index].astype(F32)
        return total

    started = {}

    def step(u, k):
        s = UNITS[u][0]
        if s not in arrived:
            arrived.add(s)
            for copy in exchange[s]:
                copy.wait()
        if k > 0:
            started[u, k - 1].wait_recv()

        def one(j, carry):
            outbox[u][k][j] = block(u, k, j).astype(BF)
            return carry

        if k == 3:
            one(0, 0)
        else:
            lax.fori_loop(0, 1 << (3 - k), one, 0)
        copy = send_to(
            outbox[u][k], inbox[u][k], st_send.at[u, k], st_recv.at[u, k], peers[UNITS[u][3][k]]
        )
        copy.start()
        started[u, k] = copy

    small_copies = []

    def small_step(k):
        if k > 0:
            small_copies[k - 1].wait()
        if k == 0:
            source, target, device = (small.at[1 - core], small_in[0], places.to_c)
        elif k == 1:
            small_in[0][...] = small_in[0][...] + small[core]
            source, target, device = (small_in[0].at[1 - places.y], small_in[1], places.to_y)
        else:
            if k == 2:
                small_out[...] = small_in[0][places.y] + small_in[1][...]
            else:
                small_out[...] = small_out[...] + small_in[k - 1][...]
            if k == 5:
                return
            source, target, device = (small_out, small_in[k], peers[k - 2])
        copy = send_to(source, target, sm_send.at[k], sm_recv.at[k], device)
        copy.start()
        small_copies.append(copy)

    small_step(0)
    for k in range(4):
        for u in range(units):
            step(u, k)
        small_step(k + 1)
    for u in range(units):
        started[u, 3].wait_recv()
        outs[u][...] = block(u, 4, 0)
    small_step(5)
    for copy in started.values():
        copy.wait_send()


def reduce_call(left, right, worker, small):
    vmem, dma = (pltpu.VMEM, pltpu.SemaphoreType.DMA)
    parts, units = (len(left), len(UNITS))
    scratch = [vmem((2, s.rows, 2 * s.depth), BF) for s in SOURCES]
    scratch += [vmem((2 * s.depth, s.columns), BF) for s in SOURCES]
    scratch += [vmem((2,) + WORKER_SHARE, BF)] * 2
    for _ in range(2):
        for unit in UNITS:
            scratch += [vmem((1 << (3 - k), unit_rows(unit), LANES), BF) for k in range(4)]
    scratch += [vmem((2, SMALL_TILES, LANES), F32)] + [vmem((SMALL_TILES, LANES), F32)] * 4
    scratch += [dma((parts, 3))] * 2 + [dma((2,))] * 3 + [dma((units, 4))] * 2 + [dma((5,))] * 2
    whole = pl.BlockSpec(memory_space=vmem)
    anywhere = pl.BlockSpec(memory_space=pl.ANY)
    out = pl.pallas_call(
        reduce_kernel,
        out_shape=[jax.ShapeDtypeStruct((unit_rows(unit), LANES), F32) for unit in UNITS]
        + [jax.ShapeDtypeStruct((SMALL_TILES, LANES), F32)],
        in_specs=[whole] * (2 * parts) + [anywhere, whole],
        out_specs=[whole] * (units + 1),
        scratch_shapes=scratch,
        compiler_params=pltpu.CompilerParams(
            collective_id=2, has_side_effects=True, vmem_limit_bytes=VMEM_BYTES
        ),
        name="reduce",
    )(*left, *right, worker, small)
    large = {}
    for (source, _, _, _), value in zip(UNITS, out):
        large.setdefault(source, []).append(value)
    return (large, out[units])


class Weights(NamedTuple):
    obs_gain: Any = None
    manager_in: Any = None
    manager_gain: Any = None
    manager_out: Any = None
    goal_in: Any = None
    goal_gain: Any = None
    goal_out: Any = None
    actor_in: Any = None
    actor_gain: Any = None
    actor_out: Any = None
    critic_in: Any = None
    critic_gain: Any = None
    critic_out: Any = None
    img_stoch: Any = None
    img_action: Any = None
    img_gain: Any = None
    gru_weight: Any = None
    gru_gain: Any = None
    post_in: Any = None
    post_gain: Any = None
    post_out: Any = None
    prior_in: Any = None
    prior_gain: Any = None
    prior_out: Any = None
    enc_in: Any = None
    enc_gain: Any = None
    enc_out: Any = None


class Data(NamedTuple):
    deter_states: Any
    embed: Any
    lengths: Any
    resets: Any
    terminal: Any
    rewards: Any
    prev_stoch: Any
    prev_action: Any
    regroup: Any
    goal_codes: Any
    samples: Any
    actions: Any


def vectors_in_order(w):
    return (
        w.obs_gain, w.manager_gain, w.manager_out, w.goal_gain, w.actor_gain, w.critic_gain,
        w.critic_out, w.img_gain, w.gru_gain, w.post_gain, w.prior_gain, w.enc_gain,
    )


def step_in_kernels(data, w):
    positions = lax.broadcasted_iota(jnp.int32, (SEQ_DEV, LEN), 1)
    is_valid = positions < data.lengths[:, None]
    next_valid = jnp.concatenate([is_valid[:, 1:], jnp.zeros((SEQ_DEV, 1), jnp.bool_)], 1)
    next_reset = jnp.concatenate([data.resets[:, 1:], jnp.ones((SEQ_DEV, 1), jnp.int32)], 1)
    columns = (
        data.prev_action, is_valid, next_valid & (next_reset == 0), 1 - data.terminal,
        data.rewards, data.regroup,
    )
    meta = jnp.concatenate(
        [data.prev_stoch.reshape(ROWS, ZG).astype(F32)]
        + [value.reshape(ROWS, 1).astype(F32) for value in columns]
        + [jnp.zeros((ROWS, LANES - ZG - 6), F32)],
        1,
    )
    slot_meta = jnp.concatenate(
        [
            data.goal_codes.astype(F32), jnp.zeros((ROWS, 32 - GC), F32),
            data.actions.astype(F32), jnp.zeros((ROWS, LANES - 32 - HOR), F32),
        ],
        1,
    )
    samples = data.samples.transpose(1, 0, 2).astype(F32)
    vectors = jnp.concatenate([v.astype(F32).reshape(-1, LANES) for v in vectors_in_order(w)], 0)
    vectors = jnp.pad(vectors, ((0, VECTOR_TILES - vectors.shape[0]), (0, 0)))
    tables = jnp.concatenate(
        [
            jnp.pad(w.actor_out.T, ((0, 32 - NA), (0, 0))),
            w.enc_out.T,
            jnp.pad(w.img_action[:, :LANES], ((0, 32 - NA), (0, 0))),
            jnp.pad(w.img_action[:, LANES:], ((0, 32 - NA), (0, 0))),
        ]
        + [w.goal_in[:, i * LANES : (i + 1) * LANES] for i in range(4)],
        0,
    )
    prev = data.deter_states.reshape(ROWS, H)
    f = run_kernel(
        frames_kernel, Frames(),
        (
            meta, prev, data.embed.reshape(ROWS, E), vectors, tables, w.img_stoch, w.gru_weight,
            w.manager_in, w.enc_in, w.goal_out, w.prior_in, w.post_in, w.prior_out, w.post_out,
            w.actor_in, w.critic_in,
        ),
        "frames", 0,
    )
    s = run_kernel(
        worker_kernel, Worker(),
        (
            slot_meta, samples, f.vectors, f.tables, f.start_state, f.goal_out_out,
            f.actor_in_out, f.critic_in_out,
        ),
        "worker", 1,
    )
    b = run_kernel(
        back_kernel, Back(),
        (
            meta, prev, f.vectors, f.gru_weight_out, s.returned, f.grad_deter, f.gru_normed,
            f.gru_inverse, f.img_normed, f.img_inverse, f.small, s.small,
        ),
        "back",
    )
    large, small = reduce_call(
        (
            f.gru_left, f.post_left, f.post_left, f.post_out_left, f.prior_out_left, f.img_left,
            f.me_left, s.goal_left, f.dec_left, s.code_turned, f.soft_turned,
        ),
        (
            b.gru_right, f.post_right, f.prior_right, f.post_out_right, f.prior_out_right,
            b.img_right, f.me_right, s.goal_right, f.recon_low, s.goal_pair, f.dec_pair,
        ),
        s.worker_left, b.small,
    )

    def vector(low, tiles):
        return small[low : low + tiles].reshape(-1)

    man_enc, worker = (large[MAN_ENC][0], large[WORKER][0])
    out = Weights(
        obs_gain=vector(OBS, 2), manager_gain=vector(MAN_G, 1), manager_out=vector(MAN_O, 1),
        goal_gain=vector(GOAL_G, 1), actor_gain=vector(ACT_G, 1), critic_gain=vector(CRI_G, 1),
        critic_out=vector(CRI_O, 1), img_gain=vector(IMG_G, 2), gru_gain=vector(GRU_G, 6),
        post_gain=vector(POST_G, 2), prior_gain=vector(PRIOR_G, 2), enc_gain=vector(ENC_G, 1),
        actor_out=small[ACT_T : ACT_T + NA].T, enc_out=small[ENC_T : ENC_T + GCODE].T,
        img_action=jnp.concatenate(
            [small[IMG_T : IMG_T + NA], small[IMG_T + 24 : IMG_T + 24 + NA]], 1
        ),
        manager_in=man_enc[:, :64], enc_in=man_enc[:, 64:],
        actor_in=worker[:, :64], critic_in=worker[:, 64:],
        goal_in=large[GOAL_IN][0][:, :64], goal_out=large[GOAL_OUT][0],
        img_stoch=large[IMG][0], gru_weight=jnp.concatenate(large[GRU], 1),
        post_in=large[POST][0], post_out=large[POST_OUT][0],
        prior_in=large[PRIOR][0], prior_out=large[PRIOR_OUT][0],
    )
    deter_grad = b.deter_grad.reshape(SEQ_DEV, LEN, H)
    return (small[LOSS, 0], deter_grad, f.embed_grad.reshape(SEQ_DEV, LEN, E)) + tuple(out)


DP, REP = ("dp", "rep")
IMG_ACTION = 14
LARGE = Weights(**dict.fromkeys(Weights._fields, False))._replace(
    manager_in=True,
    goal_in=True,
    goal_out=True,
    actor_in=True,
    critic_in=True,
    img_stoch=True,
    gru_weight=True,
    post_in=True,
    post_out=True,
    prior_in=True,
    prior_out=True,
    enc_in=True,
)


def hidden_forward(pre_act, scaling):
    normed, inverse = normalize(pre_act)
    scaled = normed * scaling
    return ((normed, inverse, scaled), jax.nn.elu(scaled).astype(jnp.bfloat16))


def hidden_backward(grad_hidden, cache, scaling):
    normed, inverse, scaled = cache
    grad_scaled = grad_hidden * jnp.where(scaled > 0, 1.0, jnp.exp(jnp.minimum(scaled, 0.0)))
    grad_gain = jnp.sum(grad_scaled * normed, tuple(range(scaled.ndim - 1)))
    return (normalize_back(grad_scaled * scaling, normed, inverse).astype(jnp.bfloat16), grad_gain)


def input_backward(grad_pre, input_low, weight):
    grad_weight = jnp.einsum("nk,nu->ku", input_low, grad_pre, preferred_element_type=jnp.float32)
    to_input = jnp.einsum("nu,ku->nk", grad_pre, weight, preferred_element_type=jnp.float32)
    return (grad_weight, to_input)


def head_backward(grad_head, hidden_low, head, cache, scaling):
    grad_weight = jnp.einsum("nu,nk->uk", hidden_low, grad_head, preferred_element_type=jnp.float32)
    grad_hidden = jnp.einsum("nk,uk->nu", grad_head, head, preferred_element_type=jnp.float32)
    grad_pre, grad_gain = hidden_backward(grad_hidden, cache, scaling)
    return (grad_weight, grad_pre, grad_gain)


def group_softmax(flat_logits, groups):
    log_part = jax.nn.log_softmax(flat_logits.reshape(flat_logits.shape[0], groups, -1), axis=-1)
    return (log_part, jnp.exp(log_part))


def chain_returns(values_now, rewards_now, linked, carried):

    def back_step(carry_pair, inputs):
        later_return, later_value = carry_pair
        current, reward_now, link_now, carry_now = inputs
        blended = (1.0 - return_mix) * later_value + return_mix * later_return
        result = jnp.where(link_now, reward_now + discount * carry_now * blended, current)
        return ((result, current), result)

    zero_start = jnp.zeros(values_now.shape[:1], jnp.float32)
    _, stacked = lax.scan(
        back_step,
        (zero_start, zero_start),
        (values_now.T, rewards_now.T, linked.T, carried.T),
        reverse=True,
    )
    return stacked.T


def worker_forward(start_state, goal_low, stoch_hot, first_layer, scaling):
    slot_part = product(start_state, first_layer[:H]) + product(goal_low, first_layer[H + Z :])
    varying = product(stoch_hot, first_layer[H : H + Z]).reshape(start_state.shape[0], HOR, U)
    return hidden_forward(slot_part[:, None, :] + varying, scaling)


def worker_backward(grad_pre, start_state, goal_low, stoch_hot, first_layer):
    slot_count = grad_pre.shape[0]
    grad_stoch = jnp.einsum(
        "nz,nu->zu",
        stoch_hot,
        grad_pre.reshape(slot_count * HOR, U),
        preferred_element_type=jnp.float32,
    )
    summed = jnp.sum(grad_pre, 1, dtype=jnp.float32).astype(jnp.bfloat16)
    grad_state_rows, to_state = input_backward(summed, start_state, first_layer[:H])
    grad_goal_rows, to_goal = input_backward(summed, goal_low, first_layer[H + Z :])
    return (jnp.concatenate([grad_state_rows, grad_stoch, grad_goal_rows], 0), to_state, to_goal)


def step_plain(data, shares):
    (deter_states, embed, lengths, resets, terminal, rewards, prev_stoch, prev_action, regroup, goal_codes, samples, actions) = data
    full = [
        lax.all_gather(share, REP, axis=1 if i == IMG_ACTION else 0, tiled=True)
        for i, share in enumerate(shares)
    ]
    (obs_gain, manager_in, manager_gain, manager_out, goal_in, goal_gain, goal_out, actor_in, actor_gain, actor_out, critic_in, critic_gain, critic_out, img_stoch, img_action, img_gain, gru_weight, gru_gain, post_in, post_gain, post_out, prior_in, prior_gain, prior_out, enc_in, enc_gain, enc_out) = full
    prev_low = deter_states.reshape(ROWS, H)
    prev_float = prev_low.astype(jnp.float32)
    embed_low = embed.reshape(ROWS, E)
    positions = lax.broadcasted_iota(jnp.int32, (SEQ_DEV, LEN), 1)
    is_valid = positions < lengths[:, None]
    next_valid = jnp.concatenate([is_valid[:, 1:], jnp.zeros((SEQ_DEV, 1), jnp.bool_)], 1)
    next_reset = jnp.concatenate([resets[:, 1:], jnp.ones((SEQ_DEV, 1), jnp.int32)], 1)
    linked = next_valid & (next_reset == 0)
    carried = 1.0 - terminal.astype(jnp.float32)
    valid_rows = is_valid.astype(jnp.float32).reshape(ROWS)
    frame_scale = valid_rows / ROWS
    stoch_prev_hot = (
        (prev_stoch[..., None] == lax.broadcasted_iota(jnp.int32, (1, 1, 1, ZK), 3))
        .astype(jnp.bfloat16)
        .reshape(ROWS, Z)
    )
    action_prev_hot = (
        prev_action.reshape(ROWS)[:, None] == lax.broadcasted_iota(jnp.int32, (1, NA), 1)
    ).astype(jnp.bfloat16)
    img_cache, img_hidden = hidden_forward(
        product(stoch_prev_hot, img_stoch) + product(action_prev_hot, img_action), img_gain
    )
    gru_input = jnp.concatenate([img_hidden, prev_low], 1)
    gru_normed, gru_inverse = normalize(product(gru_input, gru_weight))
    gru_parts = gru_normed * gru_gain
    reset_gate = jax.nn.sigmoid(gru_parts[:, :H])
    candidate_in = gru_parts[:, H : 2 * H]
    candidate = jnp.tanh(reset_gate * candidate_in)
    update_gate = jax.nn.sigmoid(gru_parts[:, 2 * H :] - 1.0)
    deter_state = update_gate * candidate + (1.0 - update_gate) * prev_float
    deter_low = deter_state.astype(jnp.bfloat16)
    obs_normed, obs_inverse = normalize(deter_state)
    feature = (obs_normed * obs_gain).astype(jnp.bfloat16)
    man_cache, man_hidden = hidden_forward(product(feature, manager_in), manager_gain)
    manager_value = product(man_hidden, manager_out).reshape(SEQ_DEV, LEN)
    manager_return = chain_returns(manager_value, rewards, linked, carried)
    manager_misfit = (manager_value - manager_return).reshape(ROWS)
    post_input = jnp.concatenate([deter_low, embed_low], 1)
    post_cache, post_hidden = hidden_forward(product(post_input, post_in), post_gain)
    post_log, post_prob = group_softmax(product(post_hidden, post_out), ZG)
    prior_cache, prior_hidden = hidden_forward(product(deter_low, prior_in), prior_gain)
    prior_log, prior_prob = group_softmax(product(prior_hidden, prior_out), ZG)
    log_gap = post_log - prior_log
    group_kl = jnp.sum(post_prob * log_gap, -1, keepdims=True)
    enc_cache, enc_hidden = hidden_forward(product(deter_low, enc_in), enc_gain)
    code_log, code_prob = group_softmax(product(enc_hidden, enc_out), GC)
    code_kl = jnp.sum(code_prob * (code_log + math.log(GK)), (1, 2))
    code_spread = jnp.sum(code_prob * code_log, -1, keepdims=True)
    soft_code = code_prob.reshape(ROWS, GCODE).astype(jnp.bfloat16)
    dec_cache, dec_hidden = hidden_forward(product(soft_code, goal_in), goal_gain)
    recon_err = product(dec_hidden, goal_out) - deter_state
    frame_terms = (
        jnp.sum(post_prob * log_gap, (1, 2)) + code_kl + 0.5 * jnp.mean(recon_err * recon_err, -1)
    )
    frame_loss = jnp.sum(valid_rows * (0.5 * manager_misfit * manager_misfit + frame_terms)) / ROWS
    send_order = regroup[0]
    start_state, slot_flag = (
        lax.all_to_all(deter_low[send_order], DP, split_axis=0, concat_axis=0, tiled=True),
        lax.all_to_all(
            valid_rows[send_order].astype(jnp.bfloat16),
            DP,
            split_axis=0,
            concat_axis=0,
            tiled=True,
        ),
    )
    slot_weight = slot_flag.astype(jnp.float32)
    code_hot = (
        (goal_codes[:, :, None] == lax.broadcasted_iota(jnp.int32, (1, 1, GK), 2))
        .astype(jnp.bfloat16)
        .reshape(ROWS, GCODE)
    )
    goal_cache, goal_hidden = hidden_forward(product(code_hot, goal_in), goal_gain)
    goal_vector = product(goal_hidden, goal_out)
    goal_low = goal_vector.astype(jnp.bfloat16)
    state_float = start_state.astype(jnp.float32)
    alignment = jnp.sum(goal_vector * state_float, -1)
    largest_square = (
        jnp.maximum(jnp.sum(goal_vector * goal_vector, -1), jnp.sum(state_float * state_float, -1))
        + small_floor
    )
    reward_slot = alignment / largest_square
    stoch_hot = (
        (samples[..., None] == lax.broadcasted_iota(jnp.int32, (1, 1, 1, ZK), 3))
        .astype(jnp.bfloat16)
        .reshape(ROWS * HOR, Z)
    )
    action_hot = (actions[..., None] == lax.broadcasted_iota(jnp.int32, (1, 1, NA), 2)).astype(
        jnp.float32
    )
    actor_cache, actor_hidden = worker_forward(
        start_state, goal_low, stoch_hot, actor_in, actor_gain
    )
    logits = jnp.einsum("rku,ua->rka", actor_hidden, actor_out, preferred_element_type=jnp.float32)
    log_chance = jax.nn.log_softmax(logits, axis=-1)
    chosen = jnp.sum(log_chance * action_hot, -1)
    critic_cache, critic_hidden = worker_forward(
        start_state, goal_low, stoch_hot, critic_in, critic_gain
    )
    worker_value = jnp.einsum(
        "rku,u->rk", critic_hidden, critic_out, preferred_element_type=jnp.float32
    )
    step_link = lax.broadcasted_iota(jnp.int32, (ROWS, HOR), 1) < HOR - 1
    worker_return = chain_returns(
        worker_value,
        jnp.broadcast_to(reward_slot[:, None], (ROWS, HOR)),
        step_link,
        jnp.ones((ROWS, HOR), jnp.float32),
    )
    advantage = worker_return - worker_value
    local_top = jnp.max(slot_weight[:, None] * jnp.abs(advantage))
    return_scale = lax.pmax(local_top, (DP, REP)) + small_floor
    step_total = ROWS * HOR
    value_misfit = worker_value - worker_return
    critic_part = 0.5 * jnp.sum(slot_weight[:, None] * value_misfit * value_misfit)
    actor_part = jnp.sum(slot_weight[:, None] * chosen * advantage) / return_scale
    local_loss = frame_loss + (critic_part - actor_part) / step_total
    grad_value = slot_weight[:, None] * value_misfit / step_total
    grad_chosen = -slot_weight[:, None] * advantage / return_scale / step_total
    grad_logits = (grad_chosen[..., None] * (action_hot - jnp.exp(log_chance))).astype(jnp.bfloat16)
    grad_actor_out = jnp.einsum(
        "rku,rka->ua", actor_hidden, grad_logits, preferred_element_type=jnp.float32
    )
    grad_actor_hidden = jnp.einsum(
        "rka,ua->rku", grad_logits, actor_out, preferred_element_type=jnp.float32
    )
    actor_pre, grad_actor_gain = hidden_backward(grad_actor_hidden, actor_cache, actor_gain)
    grad_critic_out = jnp.einsum("rku,rk->u", critic_hidden, grad_value, precision=highest)
    critic_pre, grad_critic_gain = hidden_backward(
        grad_value[..., None] * critic_out, critic_cache, critic_gain
    )
    grad_actor_in, actor_to_state, actor_to_goal = worker_backward(
        actor_pre, start_state, goal_low, stoch_hot, actor_in
    )
    grad_critic_in, critic_to_state, critic_to_goal = worker_backward(
        critic_pre, start_state, goal_low, stoch_hot, critic_in
    )
    grad_goal_low = (actor_to_goal + critic_to_goal).astype(jnp.bfloat16)
    worker_goal_out, goal_pre, worker_goal_gain = head_backward(
        grad_goal_low, goal_hidden, goal_out, goal_cache, goal_gain
    )
    worker_goal_in = jnp.einsum("ng,nu->gu", code_hot, goal_pre, preferred_element_type=jnp.float32)
    returned = lax.all_to_all(
        (actor_to_state + critic_to_state).astype(jnp.bfloat16),
        DP,
        split_axis=0,
        concat_axis=0,
        tiled=True,
    )
    grad_manager_value = frame_scale * manager_misfit
    grad_manager_out = jnp.dot(grad_manager_value, man_hidden, precision=highest)
    manager_pre, grad_manager_gain = hidden_backward(
        grad_manager_value[:, None] * manager_out, man_cache, manager_gain
    )
    grad_manager_in, grad_feature = input_backward(manager_pre, feature, manager_in)
    grad_obs_gain = jnp.sum(grad_feature * obs_normed, 0)
    obs_back = normalize_back(grad_feature * obs_gain, obs_normed, obs_inverse)
    weight_cube = frame_scale[:, None, None]
    post_grad_logits = (
        (weight_cube * post_prob * (log_gap - group_kl)).reshape(ROWS, Z).astype(jnp.bfloat16)
    )
    prior_grad_logits = (
        (weight_cube * (prior_prob - post_prob)).reshape(ROWS, Z).astype(jnp.bfloat16)
    )
    grad_post_out, post_pre, grad_post_gain = head_backward(
        post_grad_logits, post_hidden, post_out, post_cache, post_gain
    )
    grad_post_in, post_back = input_backward(post_pre, post_input, post_in)
    grad_prior_out, prior_pre, grad_prior_gain = head_backward(
        prior_grad_logits, prior_hidden, prior_out, prior_cache, prior_gain
    )
    grad_prior_in, prior_back = input_backward(prior_pre, deter_low, prior_in)
    recon_grad = frame_scale[:, None] * recon_err / H
    dec_goal_out, dec_pre, dec_goal_gain = head_backward(
        recon_grad.astype(jnp.bfloat16), dec_hidden, goal_out, dec_cache, goal_gain
    )
    dec_goal_in, grad_code = input_backward(dec_pre, soft_code, goal_in)
    grad_code = grad_code.reshape(ROWS, GC, GK)
    code_grad_logits = code_prob * (
        grad_code - jnp.sum(code_prob * grad_code, -1, keepdims=True)
    ) + weight_cube * code_prob * (code_log - code_spread)
    grad_enc_out, enc_pre, grad_enc_gain = head_backward(
        code_grad_logits.reshape(ROWS, GCODE).astype(jnp.bfloat16),
        enc_hidden,
        enc_out,
        enc_cache,
        enc_gain,
    )
    grad_enc_in, enc_back = input_backward(enc_pre, deter_low, enc_in)
    grad_goal_out = worker_goal_out + dec_goal_out
    grad_goal_in = worker_goal_in + dec_goal_in
    grad_goal_gain = worker_goal_gain + dec_goal_gain
    scattered = jnp.zeros((ROWS, H), jnp.float32).at[send_order].add(returned.astype(jnp.float32))
    grad_deter = obs_back + post_back[:, :H] + prior_back + enc_back + scattered - recon_grad
    grad_inner = grad_deter * update_gate * (1.0 - candidate * candidate)
    grad_parts = jnp.concatenate(
        [
            grad_inner * candidate_in * reset_gate * (1.0 - reset_gate),
            grad_inner * reset_gate,
            grad_deter * (candidate - prev_float) * update_gate * (1.0 - update_gate),
        ],
        1,
    )
    grad_gru_gain = jnp.sum(grad_parts * gru_normed, 0)
    gru_pre = normalize_back(grad_parts * gru_gain, gru_normed, gru_inverse).astype(jnp.bfloat16)
    grad_gru_weight, gru_back = input_backward(gru_pre, gru_input, gru_weight)
    img_pre, grad_img_gain = hidden_backward(gru_back[:, :H], img_cache, img_gain)
    grad_img_stoch = jnp.einsum(
        "nz,nh->zh", stoch_prev_hot, img_pre, preferred_element_type=jnp.float32
    )
    grad_img_action = jnp.einsum(
        "na,nh->ah", action_prev_hot, img_pre, preferred_element_type=jnp.float32
    )
    grad_prev = grad_deter * (1.0 - update_gate) + gru_back[:, H:]
    embed_grad = post_back[:, H:]
    count = lax.axis_size(REP)
    loss_share = lax.psum_scatter(
        jnp.full((count,), local_loss), REP, scatter_dimension=0, tiled=True
    )
    grads = Weights(
        obs_gain=grad_obs_gain,
        manager_in=grad_manager_in,
        manager_gain=grad_manager_gain,
        manager_out=grad_manager_out,
        goal_in=grad_goal_in,
        goal_gain=grad_goal_gain,
        goal_out=grad_goal_out,
        actor_in=grad_actor_in,
        actor_gain=grad_actor_gain,
        actor_out=grad_actor_out,
        critic_in=grad_critic_in,
        critic_gain=grad_critic_gain,
        critic_out=grad_critic_out,
        img_stoch=grad_img_stoch,
        img_action=grad_img_action,
        img_gain=grad_img_gain,
        gru_weight=grad_gru_weight,
        gru_gain=grad_gru_gain,
        post_in=grad_post_in,
        post_gain=grad_post_gain,
        post_out=grad_post_out,
        prior_in=grad_prior_in,
        prior_gain=grad_prior_gain,
        prior_out=grad_prior_out,
        enc_in=grad_enc_in,
        enc_gain=grad_enc_gain,
        enc_out=grad_enc_out,
    )
    shares = []
    for i, (grad, by_column) in enumerate(zip(grads, LARGE)):
        grad = lax.psum_scatter(
            grad, REP, scatter_dimension=1 if i == IMG_ACTION else 0, tiled=True
        )
        if by_column:
            shares.append(lax.psum_scatter(grad, DP, scatter_dimension=1, tiled=True))
        else:
            shares.append(lax.psum(grad, DP))
    return (
        lax.psum(loss_share, DP)[0],
        grad_prev.reshape(SEQ_DEV, LEN, H),
        embed_grad.reshape(SEQ_DEV, LEN, E),
    ) + tuple(shares)


def solution(mesh):
    split, over_rep = (P((DP, REP)), P(REP))
    in_kernels = mesh.shape[DP] == 8 and mesh.shape[REP] == 4

    def per_device(*arguments):
        data, shares = (Data(*arguments[:12]), Weights(*arguments[12:]))
        return (step_in_kernels if in_kernels else step_plain)(data, shares)

    in_specs, out_specs = ((split,) * 12, (P(), split, split))
    for i, by_column in enumerate(LARGE):
        spec = P(None, REP) if i == IMG_ACTION else over_rep
        in_specs += (spec,)
        out_specs += (P(REP, DP) if by_column else spec,)
    return jax.shard_map(
        per_device, mesh=mesh, in_specs=in_specs, out_specs=out_specs, check_vma=False
    )
```

```python
import math
from typing import Any, NamedTuple

import jax
import jax.numpy as jnp
from jax import lax
from jax.experimental import pallas as pl
from jax.experimental.pallas import tpu as pltpu
from jax.sharding import PartitionSpec as P

H = 1024
ZG = 32
ZK = 32
U = 512
GC = 8
GK = 8
NA = 17
E = 1536
LEN = 64
HOR = 16
SEQ_DEV = 2
Z = 1024
GCODE = 64
ROWS = 128


discount = 0.99
return_mix = 0.95
epsilon = 1e-05
small_floor = 1e-06
highest = lax.Precision.HIGHEST


MESH = pl.DeviceIdType.MESH
BF = jnp.bfloat16
F32 = jnp.float32
LANES = 128
VMEM_BYTES = 62 * 2**20


class Arg(NamedTuple):
    kind: Any
    shape: Any
    dtype: Any
    here: bool = True


TAKEN, GIVEN, KEPT, SIGNAL = range(4)


def taken(*shape, dtype=BF, here=True):
    return Arg(TAKEN, shape, dtype, here)


def given(*shape, dtype=BF, here=True):
    return Arg(GIVEN, shape, dtype, here)


def kept(*shape, dtype=BF):
    return Arg(KEPT, shape, dtype)


def signal(*shape):
    return Arg(SIGNAL, shape, None)


def run_kernel(body, layout, inputs, name, collective=None):
    leaves, tree = jax.tree.flatten(layout, is_leaf=lambda a: isinstance(a, Arg))

    def kernel(*refs):
        body(jax.tree.unflatten(tree, refs))

    def place(arg):
        return pl.BlockSpec(memory_space=pltpu.VMEM if arg.here else pl.ANY)

    outs = [a for a in leaves if a.kind == GIVEN]
    more = {} if collective is None else dict(collective_id=collective, has_side_effects=True)
    results = pl.pallas_call(
        kernel,
        out_shape=[jax.ShapeDtypeStruct(a.shape, a.dtype) for a in outs],
        in_specs=[place(a) for a in leaves if a.kind == TAKEN],
        out_specs=[place(a) for a in outs],
        scratch_shapes=[
            pltpu.VMEM(a.shape, a.dtype) if a.kind == KEPT else pltpu.SemaphoreType.DMA(a.shape)
            for a in leaves
            if a.kind >= KEPT
        ],
        compiler_params=pltpu.CompilerParams(vmem_limit_bytes=VMEM_BYTES, **more),
        name=name,
    )(*inputs)
    results = iter(results)
    return jax.tree.unflatten(
        tree, [next(results) if a.kind == GIVEN else None for a in leaves]
    )


def product(left, right):
    return jnp.dot(left, right, preferred_element_type=jnp.float32)


def normalize(values_in):
    row_mean = jnp.mean(values_in, -1, keepdims=True)
    centred = values_in - row_mean
    inverse = lax.rsqrt(jnp.mean(centred * centred, -1, keepdims=True) + epsilon)
    return (centred * inverse, inverse)


def normalize_back(grad_normed, normed, inverse):
    return inverse * (
        grad_normed
        - jnp.mean(grad_normed, -1, keepdims=True)
        - normed * jnp.mean(grad_normed * normed, -1, keepdims=True)
    )


def matmul_into(out_ref, left, weight_ref, turned=False, tile=256, low=0, extra=None):
    total = out_ref.shape[-1]

    def one(j, carry):
        start = pl.multiple_of(j * tile, tile)
        if turned:
            value = lax.dot_general(
                left,
                weight_ref[pl.ds(pl.multiple_of(low + j * tile, tile), tile), :],
                (((1,), (1,)), ((), ())),
                preferred_element_type=F32,
            )
        else:
            value = product(left, weight_ref[:, pl.ds(start, tile)])
        if extra is not None:
            value = value + extra(start, tile)
        out_ref[:, pl.ds(start, tile)] = value
        return carry

    lax.fori_loop(0, total // tile, one, 0)


def by_rows(count, size, body, carry=0):
    def one(i, carry):
        return body(pl.ds(pl.multiple_of(i * size, size), size), carry)

    return lax.fori_loop(0, count // size, one, carry)


def elu_of(value):
    return jnp.where(value > 0, value, jnp.exp(jnp.minimum(value, 0.0)) - 1.0)


def normalize_rows(ref, inverse_ref, size):
    def one(rows, carry):
        normed, inverse = normalize(ref[rows, :])
        ref[rows, :] = normed
        inverse_ref[rows, :] = inverse
        return carry

    by_rows(ref.shape[0], size, one)


def hidden_rows(ref, inverse_ref, gain, hidden_ref, size=128):
    def one(rows, carry):
        normed, inverse = normalize(ref[rows, :])
        ref[rows, :] = normed
        inverse_ref[rows, :] = inverse
        hidden_ref[rows, :] = elu_of(normed * gain).astype(BF)
        return carry

    by_rows(ref.shape[0], size, one)


def hidden_rows_back(grad_of, ref, inverse_ref, gain, pre_ref, size=128, hidden_ref=None):
    def one(rows, total):
        normed = ref[rows, :]
        scaled = normed * gain
        power = jnp.exp(jnp.minimum(scaled, 0.0))
        if hidden_ref is not None:
            hidden_ref[rows, :] = jnp.where(scaled > 0, scaled, power - 1.0).astype(BF)
        grad_scaled = grad_of(rows) * jnp.where(scaled > 0, 1.0, power)
        total = total + jnp.sum(grad_scaled * normed, 0, keepdims=True)
        back = normalize_back(grad_scaled * gain, normed, inverse_ref[rows, :])
        pre_ref[rows, :] = back.astype(pre_ref.dtype)
        return total

    return by_rows(ref.shape[0], size, one, jnp.zeros((1, ref.shape[1]), F32))


def turn_into(out_ref, value_ref, low=0):
    for j in range(value_ref.shape[1] // LANES):
        tile = value_ref[:, j * LANES : (j + 1) * LANES].astype(F32).T
        out_ref[low + j * LANES : low + (j + 1) * LANES, :] = tile.astype(out_ref.dtype)


def class_spread(groups, classes, rows, width):
    group = lax.broadcasted_iota(jnp.int32, (rows, width), 0)
    lane = lax.broadcasted_iota(jnp.int32, (rows, width), 1)
    inside = (lane >= group * classes) & (lane < group * classes + classes) & (group < groups)
    return jnp.where(inside, 1.0, 0.0).astype(BF)


def hot_rows(ids, classes, groups, width):
    here = product(ids.astype(BF), class_spread(groups, classes, ids.shape[1], width))
    lane = lax.broadcasted_iota(jnp.int32, (1, width), 1)
    same = here == jnp.bitwise_and(lane, classes - 1).astype(F32)
    return jnp.where(same & (lane < groups * classes), 1.0, 0.0)


def columns_of(rows):
    count = rows.shape[0]
    return jnp.concatenate([rows, jnp.zeros((LANES - count, rows.shape[1]), F32)], 0).T


def vector_of(packed, low, tiles):
    return jnp.concatenate(
        [packed[r, low + i : low + i + 1, :] for r in range(4) for i in range(tiles)], 1
    )


def put_vector(small_ref, low, value):
    tiles = value.shape[1] // (4 * LANES)
    for r in range(4):
        for i in range(tiles):
            start = (r * tiles + i) * LANES
            small_ref[r % 2, r // 2, low + i : low + i + 1, :] = value[:, start : start + LANES]


def put_table(small_ref, low, value, rows):
    for r in range(4):
        small_ref[r % 2, r // 2, low : low + rows, :] = value[
            0:rows, r * LANES : (r + 1) * LANES
        ]


OBS, MAN_G, MAN_O, GOAL_G, ACT_G, CRI_G, CRI_O, IMG_G, GRU_G, POST_G, PRIOR_G, ENC_G, LOSS = (
    0, 2, 3, 4, 5, 6, 7, 8, 10, 16, 18, 20, 21,
)
ACT_T, ENC_T, IMG_T, SMALL_TILES = (24, 48, 112, 160)
TAB_ACT, TAB_ENC, TAB_IMG, TAB_GOAL, TABLES = (0, 32, 96, 160, 224)
VECTOR_TILES = 24


def spread_lanes(low_ref, out_ref, first_row, which):
    lane = lax.broadcasted_iota(jnp.int32, (ROWS, LANES), 1)
    keep = (lane < 64) if which == 0 else (lane >= 64)
    for j in range(4):
        tile = low_ref[:, j * LANES : (j + 1) * LANES].astype(F32)
        turned = pltpu.roll(tile, 64, 1)
        for x in range(2):
            source = tile if x == which else turned
            lanes = slice((2 * j + x) * LANES, (2 * j + x + 1) * LANES)
            out_ref[first_row : first_row + ROWS, lanes] = jnp.where(keep, source, 0.0).astype(BF)


def column(meta, k):
    return meta[:, k : k + 1]


class Frames(NamedTuple):
    lengths: Any = taken(SEQ_DEV, dtype=jnp.int32)
    resets: Any = taken(SEQ_DEV, LEN, dtype=jnp.int32)
    terminal: Any = taken(SEQ_DEV, LEN, dtype=jnp.int32)
    rewards: Any = taken(SEQ_DEV, LEN, dtype=F32)
    prev_stoch: Any = taken(SEQ_DEV, ZG, LEN, dtype=jnp.int32)
    prev_action: Any = taken(SEQ_DEV, LEN, dtype=jnp.int32)
    regroup: Any = taken(1, ROWS, dtype=jnp.int32)
    prev: Any = taken(ROWS, H)
    embed: Any = taken(ROWS, E)
    obs_gain: Any = taken(H // 4)
    manager_gain: Any = taken(U // 4)
    manager_head: Any = taken(U // 4)
    goal_gain: Any = taken(U // 4)
    actor_gain: Any = taken(U // 4)
    critic_gain: Any = taken(U // 4)
    critic_head: Any = taken(U // 4)
    img_gain: Any = taken(H // 4)
    gru_gain: Any = taken(3 * H // 4)
    post_gain: Any = taken(H // 4)
    prior_gain: Any = taken(H // 4)
    enc_gain: Any = taken(U // 4)
    actor_head: Any = taken(NA, U // 4)
    enc_head: Any = taken(GCODE, U // 4)
    img_action_share: Any = taken(NA, H // 4)
    goal_in_share: Any = taken(GCODE // 4, U)
    img_stoch_share: Any = taken(Z // 4, H, here=False)
    gru_weight_share: Any = taken(H // 2, 3 * H, here=False)
    manager_in_share: Any = taken(H // 4, U, here=False)
    enc_in_share: Any = taken(H // 4, U, here=False)
    goal_out_share: Any = taken(U // 4, H, here=False)
    prior_in_share: Any = taken(H // 4, H, here=False)
    post_in_share: Any = taken((H + E) // 4, H, here=False)
    prior_out_share: Any = taken(H // 4, Z, here=False)
    post_out_share: Any = taken(H // 4, Z, here=False)
    actor_in_share: Any = taken(768, U, here=False)
    critic_in_share: Any = taken(768, U, here=False)
    gru_weight_out: Any = given(2 * H, 3 * H, here=False)
    goal_out_out: Any = given(U, H, here=False)
    actor_in_out: Any = given(3 * H, U, here=False)
    critic_in_out: Any = given(3 * H, U, here=False)
    vectors: Any = given(4, VECTOR_TILES, LANES, dtype=F32)
    tables: Any = given(4, TABLES, LANES)
    meta_turned: Any = given(LANES, ROWS, dtype=F32)
    start_state: Any = given(ROWS, H + LANES)
    gru_left: Any = given(2 * H, ROWS)
    post_left: Any = given(H + E, ROWS)
    post_out_left: Any = given(H, ROWS)
    prior_out_left: Any = given(H, ROWS)
    img_left: Any = given(Z, ROWS)
    me_left: Any = given(H, 2 * ROWS)
    dec_left: Any = given(U, ROWS)
    soft_turned: Any = given(GCODE, ROWS)
    post_right: Any = given(ROWS, H)
    prior_right: Any = given(ROWS, H)
    post_out_right: Any = given(ROWS, Z)
    prior_out_right: Any = given(ROWS, Z)
    me_right: Any = given(2 * ROWS, 2 * U)
    recon_low: Any = given(ROWS, H)
    dec_pair: Any = given(ROWS, 2 * U)
    gru_normed: Any = given(ROWS, 3 * H, dtype=F32)
    gru_inverse: Any = given(ROWS, 1, dtype=F32)
    img_normed: Any = given(ROWS, H, dtype=F32)
    img_inverse: Any = given(ROWS, 1, dtype=F32)
    grad_deter: Any = given(ROWS, H, dtype=F32)
    embed_grad: Any = given(ROWS, E, dtype=F32)
    small: Any = given(2, 2, SMALL_TILES, LANES, dtype=F32)
    img_stoch: Any = kept(Z, H)
    gru_weight: Any = kept(2 * H, 3 * H)
    manager_in: Any = kept(H, U)
    enc_in: Any = kept(H, U)
    goal_out: Any = kept(U, H)
    prior_in: Any = kept(H, H)
    post_in: Any = kept(H + E, H)
    prior_out: Any = kept(H, Z)
    post_out: Any = kept(H, Z)
    actor_in: Any = kept(3 * H, U)
    critic_in: Any = kept(3 * H, U)
    img_action: Any = kept(32, H)
    enc_out: Any = kept(GCODE, U)
    goal_in: Any = kept(GCODE, U)
    vector_share: Any = kept(VECTOR_TILES, LANES, dtype=F32)
    table_share: Any = kept(TABLES, LANES)
    meta: Any = kept(ROWS, LANES, dtype=F32)
    hot: Any = kept(ROWS, Z)
    img_hidden: Any = kept(ROWS, H)
    deter: Any = kept(ROWS, H, dtype=F32)
    deter_low: Any = kept(ROWS, H)
    feature: Any = kept(ROWS, H)
    obs_normed: Any = kept(ROWS, H, dtype=F32)
    obs_inverse: Any = kept(ROWS, 1, dtype=F32)
    outgoing: Any = kept(ROWS, H + LANES)
    incoming: Any = kept(ROWS, H + LANES)
    pre_512: Any = kept(ROWS, U, dtype=F32)
    hid_512: Any = kept(ROWS, U)
    back_512: Any = kept(ROWS, U)
    wide_512: Any = kept(ROWS, U, dtype=F32)
    inverse: Any = kept(ROWS, 1, dtype=F32)
    grad_value: Any = kept(ROWS, 1, dtype=F32)
    dec_normed: Any = kept(ROWS, U, dtype=F32)
    dec_inverse: Any = kept(ROWS, 1, dtype=F32)
    dec_hidden: Any = kept(ROWS, U)
    dec_pre: Any = kept(ROWS, U)
    wide: Any = kept(ROWS, H, dtype=F32)
    prior_normed: Any = kept(ROWS, H, dtype=F32)
    prior_inverse: Any = kept(ROWS, 1, dtype=F32)
    prior_hidden: Any = kept(ROWS, H)
    post_normed: Any = kept(ROWS, H, dtype=F32)
    post_inverse: Any = kept(ROWS, 1, dtype=F32)
    post_hidden: Any = kept(ROWS, H)
    post_turned: Any = kept(Z, ROWS, dtype=F32)
    prior_turned: Any = kept(Z, ROWS, dtype=F32)
    loss: Any = kept(1, 1, dtype=F32)
    piece_send: Any = signal(14, 8)
    piece_recv: Any = signal(14, 8)
    load_done: Any = signal(14)
    save_done: Any = signal(4)
    small_send: Any = signal(2, 3)
    small_recv: Any = signal(2, 3)
    state_send: Any = signal(8)
    state_recv: Any = signal(8)

    def pack(self):
        vectors = (
            self.obs_gain, self.manager_gain, self.manager_head, self.goal_gain, self.actor_gain,
            self.critic_gain, self.critic_head, self.img_gain, self.gru_gain, self.post_gain,
            self.prior_gain, self.enc_gain,
        )
        low = 0
        for vector in vectors:
            for i in range(vector.shape[0] // LANES):
                self.vector_share[low, :] = vector[pl.ds(i * LANES, LANES)].astype(F32)
                low += 1
        self.vector_share[low:, :] = jnp.zeros((VECTOR_TILES - low, LANES), F32)
        self.table_share[...] = jnp.zeros(self.table_share.shape, BF)
        self.table_share[TAB_ACT : TAB_ACT + NA, :] = self.actor_head[...]
        self.table_share[TAB_ENC : TAB_ENC + GCODE, :] = self.enc_head[...]
        for i in range(2):
            low = TAB_IMG + 32 * i
            lanes = slice(i * LANES, (i + 1) * LANES)
            self.table_share[low : low + NA, :] = self.img_action_share[:, lanes]
        for i in range(4):
            low = TAB_GOAL + 16 * i
            lanes = slice(i * LANES, (i + 1) * LANES)
            self.table_share[low : low + 16, :] = self.goal_in_share[:, lanes]

    def start(self):
        def row(ref):
            value = ref[...].astype(F32)
            return jnp.concatenate([value[0:1], value[1:2]], 1)

        position = lax.broadcasted_iota(jnp.int32, (SEQ_DEV, LEN), 1)
        length = self.lengths[...].reshape(SEQ_DEV, 1)
        later = jnp.where((position + 1 < length) & (position + 1 < LEN), 1.0, 0.0)
        kinds = (
            row(self.prev_action),
            row(jnp.where(position < length, 1.0, 0.0)),
            row(later) * (1.0 - jnp.minimum(pltpu.roll(row(self.resets), ROWS - 1, 1), 1.0)),
            1.0 - row(self.terminal),
            row(self.rewards),
            self.regroup[...].astype(F32),
        )
        self.meta_turned[...] = jnp.zeros(self.meta_turned.shape, F32)
        for i, kind in enumerate(kinds):
            self.meta_turned[32 + i : 33 + i, :] = kind
        self.meta[...] = self.meta_turned[...].T
        ids = jnp.concatenate([self.prev_stoch[0], self.prev_stoch[1]], 1).astype(F32)
        self.hot[...] = hot_rows(columns_of(ids)[:, 0:ZG], ZK, ZG, Z).astype(BF)

    def turns(self):
        turn_into(self.img_left, self.hot)
        turn_into(self.gru_left, self.prev, H)
        turn_into(self.post_left, self.embed, H)
        self.small[...] = jnp.zeros(self.small.shape, F32)

    def unpack(self):
        for r in range(4):
            for i in range(2):
                self.img_action[:, (2 * r + i) * LANES : (2 * r + i + 1) * LANES] = self.tables[
                    r, TAB_IMG + 32 * i : TAB_IMG + 32 * (i + 1), :
                ]
            self.enc_out[:, r * LANES : (r + 1) * LANES] = self.tables[
                r, TAB_ENC : TAB_ENC + 64, :
            ]
            for i in range(4):
                self.goal_in[16 * r : 16 * (r + 1), i * LANES : (i + 1) * LANES] = self.tables[
                    r, TAB_GOAL + 16 * i : TAB_GOAL + 16 * (i + 1), :
                ]

    def gain(self, low, size):
        return vector_of(self.vectors, low, size // (4 * LANES))

    def img(self):
        meta = self.meta[...]
        lane = lax.broadcasted_iota(jnp.int32, (ROWS, 32), 1).astype(F32)
        action = jnp.where(column(meta, 32) == lane, 1.0, 0.0).astype(BF)
        matmul_into(
            self.img_normed, self.hot[...], self.img_stoch,
            extra=lambda start, tile: product(action, self.img_action[:, pl.ds(start, tile)]),
        )
        hidden_rows(self.img_normed, self.img_inverse, self.gain(IMG_G, H), self.img_hidden)
        turn_into(self.gru_left, self.img_hidden)

    def gru(self, third):
        low = third * H
        out = self.gru_normed.at[:, low : low + H]

        def one(j, carry):
            start = pl.multiple_of(low + j * 256, 256)
            value = product(self.img_hidden[...], self.gru_weight[0:H, pl.ds(start, 256)])
            value = value + product(
                self.prev[...], self.gru_weight[H : 2 * H, pl.ds(start, 256)]
            )
            self.gru_normed[:, pl.ds(start, 256)] = value
            return carry

        lax.fori_loop(0, 4, one, 0)

    def state(self):
        gain = self.gain(GRU_G, 3 * H)
        obs_gain = self.gain(OBS, H)

        def one(rows, carry):
            normed, inverse = normalize(self.gru_normed[rows, :])
            self.gru_normed[rows, :] = normed
            self.gru_inverse[rows, :] = inverse
            parts = normed * gain
            reset = 1.0 / (1.0 + jnp.exp(-parts[:, :H]))
            candidate = jnp.tanh(reset * parts[:, H : 2 * H])
            update = 1.0 / (1.0 + jnp.exp(1.0 - parts[:, 2 * H :]))
            state = update * candidate + (1.0 - update) * self.prev[rows, :].astype(F32)
            self.deter[rows, :] = state
            self.deter_low[rows, :] = state.astype(BF)
            obs, obs_inverse = normalize(state)
            self.obs_normed[rows, :] = obs
            self.obs_inverse[rows, :] = obs_inverse
            self.feature[rows, :] = (obs * obs_gain).astype(BF)
            return carry

        by_rows(ROWS, 16, one)
        turn_into(self.post_left, self.deter_low)

    def picked(self):
        meta = self.meta[...]
        lane = lax.broadcasted_iota(jnp.int32, (ROWS, ROWS), 1).astype(F32)
        pick = jnp.where(column(meta, 37) == lane, 1.0, 0.0).astype(BF)

        def one(j, carry):
            lanes = pl.ds(pl.multiple_of(j * 256, 256), 256)
            self.outgoing[:, lanes] = product(pick, self.deter_low[:, lanes]).astype(BF)
            return carry

        lax.fori_loop(0, H // 256, one, 0)
        valid = jnp.broadcast_to(column(meta, 33), (ROWS, LANES)).astype(BF)
        self.outgoing[:, H:] = product(pick, valid).astype(BF)

    def manager(self):
        meta = self.meta[...]
        gain, head = (self.gain(MAN_G, U), self.gain(MAN_O, U))
        for j in range(H // LANES):
            lanes = slice(j * LANES, (j + 1) * LANES)
            self.me_left[lanes, 0:ROWS] = self.feature[:, lanes].astype(F32).T.astype(BF)
            self.me_left[lanes, ROWS:] = self.deter_low[:, lanes].astype(F32).T.astype(BF)
        matmul_into(self.pre_512, self.feature[...], self.manager_in)
        hidden_rows(self.pre_512, self.inverse, gain, self.hid_512)
        value = jnp.sum(self.hid_512[...].astype(F32) * head, -1, keepdims=True)
        valid, linked, carried, rewards = (column(meta, 33 + i) for i in range(4))
        later = pltpu.roll(jnp.broadcast_to(value, (ROWS, LANES)), ROWS - 1, 0)
        base = jnp.where(
            linked > 0, rewards + discount * carried * ((1.0 - return_mix) * later), value
        )
        slope = jnp.broadcast_to(linked * (discount * return_mix) * carried, (ROWS, LANES))
        step = 1
        while step < LEN:
            base = base + slope * pltpu.roll(base, ROWS - step, 0)
            slope = slope * pltpu.roll(slope, ROWS - step, 0)
            step *= 2
        misfit = value - base[:, 0:1]
        scale = valid * (1.0 / ROWS)
        self.loss[...] = 0.5 * jnp.sum(scale * misfit * misfit, 0, keepdims=True)
        grad_value = scale * misfit
        put_vector(
            self.small, MAN_O,
            jnp.sum(self.hid_512[...].astype(F32) * grad_value, 0, keepdims=True),
        )
        self.grad_value[...] = grad_value
        total = hidden_rows_back(
            lambda rows: self.grad_value[rows, :] * head,
            self.pre_512, self.inverse, gain, self.back_512,
        )
        put_vector(self.small, MAN_G, total)
        spread_lanes(self.back_512, self.me_right, 0, 0)
        self.feature_back()

    def feature_back(self):
        obs_gain = self.gain(OBS, H)
        matmul_into(self.wide, self.back_512[...], self.manager_in, turned=True)

        def one(rows, total):
            grad = self.wide[rows, :]
            normed = self.obs_normed[rows, :]
            total = total + jnp.sum(grad * normed, 0, keepdims=True)
            self.grad_deter[rows, :] = normalize_back(
                grad * obs_gain, normed, self.obs_inverse[rows, :]
            )
            return total

        put_vector(self.small, OBS, by_rows(ROWS, 32, one, jnp.zeros((1, H), F32)))

    def add_back(self, left_ref, weight_ref):
        def one(j, carry):
            lanes = pl.ds(pl.multiple_of(j * 256, 256), 256)
            self.grad_deter[:, lanes] += lax.dot_general(
                left_ref[...], weight_ref[lanes, :], (((1,), (1,)), ((), ())),
                preferred_element_type=F32,
            )
            return carry

        lax.fori_loop(0, H // 256, one, 0)

    def encoder(self):
        gain, goal_gain = (self.gain(ENC_G, U), self.gain(GOAL_G, U))
        valid_row = self.meta_turned[33:34, :]
        scale_row = valid_row * (1.0 / ROWS)
        scale = column(self.meta[...], 33) * (1.0 / ROWS)
        matmul_into(self.pre_512, self.deter_low[...], self.enc_in)
        hidden_rows(self.pre_512, self.inverse, gain, self.hid_512)
        logits = lax.dot_general(
            self.enc_out[...], self.hid_512[...], (((1,), (1,)), ((), ())),
            preferred_element_type=F32,
        ).reshape(GC, GK, ROWS)
        shifted = logits - jnp.max(logits, 1, keepdims=True)
        code_log = shifted - jnp.log(jnp.sum(jnp.exp(shifted), 1, keepdims=True))
        code = jnp.exp(code_log)
        spread = jnp.sum(code * code_log, 1, keepdims=True)
        code_kl = jnp.sum(jnp.sum(code * (code_log + math.log(GK)), 1), 0, keepdims=True)
        flat = jnp.concatenate(
            [code.reshape(GCODE, ROWS), jnp.zeros((ROWS - GCODE, ROWS), F32)], 0
        )
        self.soft_turned[...] = flat[0:GCODE].astype(BF)
        soft = flat.T[:, 0:GCODE].astype(BF)
        matmul_into(self.dec_normed, soft, self.goal_in)
        hidden_rows(self.dec_normed, self.dec_inverse, goal_gain, self.dec_hidden)
        turn_into(self.dec_left, self.dec_hidden)

        def one(j, total):
            lanes = pl.ds(pl.multiple_of(j * 256, 256), 256)
            err = product(self.dec_hidden[...], self.goal_out[:, lanes]) - self.deter[:, lanes]
            grad = scale * err * (1.0 / H)
            self.grad_deter[:, lanes] -= grad
            self.recon_low[:, lanes] = grad.astype(BF)
            return total + jnp.sum(err * err, -1, keepdims=True)

        squares = lax.fori_loop(0, H // 256, one, jnp.zeros((ROWS, 1), F32))
        self.loss[...] += jnp.sum(scale * (0.5 / H) * squares, 0, keepdims=True) + jnp.sum(
            scale_row * code_kl, 1, keepdims=True
        )
        matmul_into(self.wide_512, self.recon_low[...], self.goal_out, turned=True)
        total = hidden_rows_back(
            lambda rows: self.wide_512[rows, :],
            self.dec_normed, self.dec_inverse, goal_gain, self.dec_pre,
        )
        put_vector(self.small, GOAL_G, total)
        spread_lanes(self.dec_pre, self.dec_pair, 0, 0)
        grad_code = lax.dot_general(
            self.goal_in[...], self.dec_pre[...], (((1,), (1,)), ((), ())),
            preferred_element_type=F32,
        ).reshape(GC, GK, ROWS)
        grad_logits = code * (grad_code - jnp.sum(code * grad_code, 1, keepdims=True))
        grad_logits = grad_logits + scale_row[None] * code * (code_log - spread)
        grad_turned = grad_logits.reshape(GCODE, ROWS)
        grad_low = jnp.concatenate(
            [grad_turned, jnp.zeros((ROWS - GCODE, ROWS), F32)], 0
        ).T[:, 0:GCODE].astype(BF)
        put_table(
            self.small, ENC_T, product(grad_turned.astype(BF), self.hid_512[...]), GCODE
        )
        matmul_into(self.wide_512, grad_low, self.enc_out)
        total = hidden_rows_back(
            lambda rows: self.wide_512[rows, :],
            self.pre_512, self.inverse, gain, self.back_512,
        )
        put_vector(self.small, ENC_G, total)
        spread_lanes(self.back_512, self.me_right, ROWS, 1)
        self.add_back(self.back_512, self.enc_in)

    def prior(self):
        matmul_into(self.prior_normed, self.deter_low[...], self.prior_in)
        hidden_rows(
            self.prior_normed, self.prior_inverse, self.gain(PRIOR_G, H), self.prior_hidden
        )
        turn_into(self.prior_out_left, self.prior_hidden)

    def post(self):
        def one(j, carry):
            lanes = pl.ds(pl.multiple_of(j * 256, 256), 256)
            value = product(self.deter_low[...], self.post_in[0:H, lanes])
            self.post_normed[:, lanes] = value + product(
                self.embed[...], self.post_in[H : H + E, lanes]
            )
            return carry

        lax.fori_loop(0, H // 256, one, 0)
        hidden_rows(self.post_normed, self.post_inverse, self.gain(POST_G, H), self.post_hidden)
        turn_into(self.post_out_left, self.post_hidden)

    def logits(self, hidden_ref, weight_ref, turned_ref):
        matmul_into(self.wide, hidden_ref[...], weight_ref)
        turn_into(turned_ref, self.wide)

    def state_kl(self):
        scale_row = self.meta_turned[33:34, :] * (1.0 / ROWS)

        def log_part(value):
            shifted = value - jnp.max(value, 0, keepdims=True)
            return shifted - jnp.log(jnp.sum(jnp.exp(shifted), 0, keepdims=True))

        def one(rows, total):
            post_log = log_part(self.post_turned[rows, :])
            prior_log = log_part(self.prior_turned[rows, :])
            post = jnp.exp(post_log)
            gap = post_log - prior_log
            kl = jnp.sum(post * gap, 0, keepdims=True)
            self.post_turned[rows, :] = scale_row * post * (gap - kl)
            self.prior_turned[rows, :] = scale_row * (jnp.exp(prior_log) - post)
            return total + kl

        total = by_rows(Z, ZK, one, jnp.zeros((1, ROWS), F32))
        self.loss[...] += jnp.sum(scale_row * total, 1, keepdims=True)
        for turned, low in (
            (self.post_turned, self.post_out_right), (self.prior_turned, self.prior_out_right),
        ):
            for j in range(Z // LANES):
                lanes = slice(j * LANES, (j + 1) * LANES)
                low[:, lanes] = turned[lanes, :].T.astype(BF)

    def prior_back(self):
        matmul_into(self.wide, self.prior_out_right[...], self.prior_out, turned=True)
        total = hidden_rows_back(
            lambda rows: self.wide[rows, :],
            self.prior_normed, self.prior_inverse, self.gain(PRIOR_G, H), self.prior_right,
        )
        put_vector(self.small, PRIOR_G, total)
        self.add_back(self.prior_right, self.prior_in)

    def post_back(self):
        matmul_into(self.wide, self.post_out_right[...], self.post_out, turned=True)
        total = hidden_rows_back(
            lambda rows: self.wide[rows, :],
            self.post_normed, self.post_inverse, self.gain(POST_G, H), self.post_right,
        )
        put_vector(self.small, POST_G, total)
        self.add_back(self.post_right, self.post_in)
        matmul_into(self.embed_grad, self.post_right[...], self.post_in, turned=True, low=H)
        for y in range(2):
            for c in range(2):
                self.small[c, y, LOSS : LOSS + 1, :] = jnp.broadcast_to(
                    self.loss[...], (1, LANES)
                )


class Places:
    def __init__(self):
        dp, rep = (lax.axis_index("dp"), lax.axis_index("rep"))
        self.dp, self.rep = (dp, rep)
        self.x, self.z, self.w = (lax.rem(dp, 2), lax.rem(dp // 2, 2), dp // 4)
        self.y, self.c = (rep // 2, lax.rem(rep, 2))
        self.to_x = (dp + 1 - 2 * self.x, rep)
        self.to_z = (dp + 2 - 4 * self.z, rep)
        self.to_w = (dp + 4 - 8 * self.w, rep)
        self.to_y = (dp, rep + 2 - 4 * self.y)
        self.to_c = (dp, rep + 1 - 2 * self.c)
        self.to_d = (dp, 3 - rep)

    def around(self, offset):
        return lax.rem(self.dp + offset, 8)


def greet(devices):
    barrier = pltpu.get_barrier_semaphore()
    for device in devices:
        pl.semaphore_signal(barrier, inc=1, device_id=device, device_id_type=MESH)
    pl.semaphore_wait(barrier, len(devices))


def send_to(source, target, send_sem, recv_sem, device):
    return pltpu.make_async_remote_copy(
        src_ref=source,
        dst_ref=target,
        send_sem=send_sem,
        recv_sem=recv_sem,
        device_id=device,
        device_id_type=MESH,
    )


def regroup_start(places, outgoing, incoming, send_sem, recv_sem):
    count = ROWS // 8
    mine = pl.ds(pl.multiple_of(places.dp * count, 16), count)
    copies = []
    for offset in range(1, 8):
        there = places.around(offset)
        copy = send_to(
            outgoing.at[pl.ds(pl.multiple_of(there * count, 16), count)],
            incoming.at[mine],
            send_sem.at[offset],
            recv_sem.at[offset],
            (there, places.rep),
        )
        copy.start()
        copies.append(copy)
    incoming[mine, :] = outgoing[mine, :]
    return copies


def diagonal_split(quarter):
    over_y = quarter // 3 // 16 * 16
    over_x = (quarter - over_y) // 2 // 16 * 16
    over_z = quarter - over_y - over_x
    return (over_z, over_x, over_y) if over_y < over_z else (over_y, over_x, over_z)


OWN, Y_A, Y_B, X_A, Z_A, X_B, Z_B, RELAY = range(8)


class Gather:
    def __init__(self, places, units, send_sem, recv_sem, load_sem):
        self.places, self.units = (places, units)
        self.send_sem, self.recv_sem, self.load_sem = (send_sem, recv_sem, load_sem)
        self.far = places.rep + 2 - 4 * places.y
        self.mine = places.x * 2 + places.z
        self.across = 3 - self.mine
        self.from_x = (1 - places.x) * 2 + places.z
        self.from_z = places.x * 2 + 1 - places.z
        self.copies = {}
        self.loads = {}

    def remote(self, u, kind, source, target, device):
        copy = send_to(
            source, target, self.send_sem.at[u, kind], self.recv_sem.at[u, kind], device
        )
        copy.start()
        self.copies[u, kind] = copy

    def rows(self, u, share, piece, low, number):
        extent = self.units[u][0].shape[0]
        start = share * extent + piece * (extent // 4) + low
        return pl.ds(pl.multiple_of(start, 16), number)

    def part(self, u, rows, whole=True):
        share, all_rows, low, count = self.units[u]
        return (all_rows if whole else share).at[rows, pl.ds(low, count)]

    def extent(self, u):
        return self.units[u][0].shape[0]

    def load(self, u):
        everything = self.rows(u, 0, 0, 0, self.extent(u))
        copy = pltpu.make_async_copy(
            self.part(u, everything, False),
            self.part(u, self.rows(u, self.places.rep, 0, 0, self.extent(u))),
            self.load_sem.at[u],
        )
        copy.start()
        self.loads[u] = copy

    def over_y(self, u):
        if u >= len(self.units):
            return
        rep, quarter = (self.places.rep, self.extent(u) // 4)
        first = diagonal_split(quarter)[0]
        self.remote(
            u, Y_A,
            self.part(u, self.rows(u, 0, self.mine, 0, quarter), False),
            self.part(u, self.rows(u, rep, self.mine, 0, quarter)),
            self.places.to_y,
        )
        if first:
            self.remote(
                u, Y_B,
                self.part(u, self.rows(u, 0, self.across, 0, first), False),
                self.part(u, self.rows(u, rep, self.across, 0, first)),
                self.places.to_y,
            )
        everything = self.rows(u, 0, 0, 0, self.extent(u))
        self.remote(
            u, OWN,
            self.part(u, everything, False),
            self.part(u, self.rows(u, rep, 0, 0, self.extent(u))),
            self.places.to_c,
        )

    def stage_1(self, u):
        self.copies[u, Y_A].wait_recv()
        piece = self.part(u, self.rows(u, self.far, self.mine, 0, self.extent(u) // 4))
        self.remote(u, X_A, piece, piece, self.places.to_x)
        self.remote(u, Z_A, piece, piece, self.places.to_z)

    def stage_2(self, u):
        first, second, third = diagonal_split(self.extent(u) // 4)
        self.copies[u, Z_A].wait_recv()
        if second:
            piece = self.part(u, self.rows(u, self.far, self.from_z, first, second))
            self.remote(u, X_B, piece, piece, self.places.to_x)
        self.copies[u, X_A].wait_recv()
        if third:
            piece = self.part(u, self.rows(u, self.far, self.from_x, first + second, third))
            self.remote(u, Z_B, piece, piece, self.places.to_z)

    def stage_3(self, u):
        for kind in (Y_B, X_B, Z_B):
            if (u, kind) in self.copies:
                self.copies[u, kind].wait_recv()
        share = self.part(u, self.rows(u, self.far, 0, 0, self.extent(u)))
        self.remote(u, RELAY, share, share, self.places.to_c)

    def pump(self, t, ahead):
        count = len(self.units)
        if t < count:
            self.stage_1(t)
            self.over_y(t + ahead)
        if 0 <= t - 1 < count:
            self.stage_2(t - 1)
        if 0 <= t - 2 < count:
            self.stage_3(t - 2)

    def complete(self, u):
        self.loads[u].wait()
        self.copies[u, OWN].wait_recv()
        self.copies[u, RELAY].wait_recv()

    def drain(self):
        for copy in self.copies.values():
            copy.wait_send()


AHEAD = 3


def frames_kernel(f):
    places = Places()
    units = [(f.img_stoch_share, f.img_stoch, 0, H)]
    units += [(f.gru_weight_share, f.gru_weight, i * H, H) for i in range(3)]
    units += [
        (f.manager_in_share, f.manager_in, 0, U),
        (f.enc_in_share, f.enc_in, 0, U),
        (f.goal_out_share, f.goal_out, 0, H),
        (f.prior_in_share, f.prior_in, 0, H),
        (f.post_in_share, f.post_in, 0, U),
        (f.post_in_share, f.post_in, U, U),
        (f.prior_out_share, f.prior_out, 0, Z),
        (f.post_out_share, f.post_out, 0, Z),
        (f.actor_in_share, f.actor_in, 0, U),
        (f.critic_in_share, f.critic_in, 0, U),
    ]
    gather = Gather(places, units, f.piece_send, f.piece_recv, f.load_done)
    for u in range(len(units)):
        gather.load(u)
    f.pack()
    greet(
        [(places.around(o), places.rep) for o in range(1, 8)]
        + [places.to_c, places.to_y, places.to_d]
    )
    packs = []
    for i, (share, whole) in enumerate(((f.vector_share, f.vectors), (f.table_share, f.tables))):
        for k, device in enumerate((places.to_c, places.to_y, places.to_d)):
            copy = send_to(
                share, whole.at[places.rep], f.small_send.at[i, k], f.small_recv.at[i, k], device
            )
            copy.start()
            packs.append(copy)
    for u in range(AHEAD):
        gather.over_y(u)
    f.vectors[places.rep] = f.vector_share[...]
    f.tables[places.rep] = f.table_share[...]
    saves = []

    def save(k, source, target):
        copy = pltpu.make_async_copy(source, target, f.save_done.at[k])
        copy.start()
        saves.append(copy)

    def pump(t):
        gather.pump(t, AHEAD)

    f.start()
    pump(0)
    f.turns()
    pump(1)
    pump(2)
    for copy in packs:
        copy.wait()
    f.unpack()
    gather.complete(0)
    f.img()
    for third in range(3):
        pump(3 + third)
        gather.complete(1 + third)
        f.gru(third)
    save(0, f.gru_weight, f.gru_weight_out)
    f.state()
    f.picked()
    states = regroup_start(places, f.outgoing, f.incoming, f.state_send, f.state_recv)
    pump(6)
    gather.complete(4)
    f.manager()
    pump(7)
    gather.complete(5)
    pump(8)
    gather.complete(6)
    save(1, f.goal_out, f.goal_out_out)
    f.encoder()
    pump(9)
    gather.complete(7)
    f.prior()
    pump(10)
    pump(11)
    gather.complete(8)
    gather.complete(9)
    f.post()
    pump(12)
    gather.complete(10)
    f.logits(f.prior_hidden, f.prior_out, f.prior_turned)
    pump(13)
    gather.complete(11)
    f.logits(f.post_hidden, f.post_out, f.post_turned)
    pump(14)
    f.state_kl()
    pump(15)
    f.prior_back()
    for copy in states:
        copy.wait()
    f.start_state[...] = f.incoming[...]
    gather.complete(12)
    save(2, f.actor_in, f.actor_in_out)
    gather.complete(13)
    save(3, f.critic_in, f.critic_in_out)
    f.post_back()
    for copy in saves:
        copy.wait()
    gather.drain()


class Source(NamedTuple):
    rows: int
    parts: Any
    columns: int

    @property
    def depth(self):
        return sum(self.parts)


SOURCE_POST = Source((H + E) // 4, (ROWS,), H)
SOURCE_1024 = Source(H // 4, (ROWS,), H)
SOURCE_MAN_ENC = Source(H // 4, (2 * ROWS,), 2 * U)
SOURCE_GRU = Source(H // 2, (ROWS,), 3 * H)
SOURCE_GOAL_OUT = Source(U // 4, (ROWS, ROWS), H)
SOURCE_GOAL_IN = Source(GCODE // 4, (ROWS, ROWS), 2 * U)
WORKER_SHARE = (768, 1024)
ALONG_X, ALONG_Z, ALONG_W, ALONG_Y = range(4)
Y_FIRST = (ALONG_Y, ALONG_X, ALONG_Z, ALONG_W)
X_FIRST = (ALONG_X, ALONG_Y, ALONG_Z, ALONG_W)
Z_FIRST = (ALONG_Z, ALONG_Y, ALONG_X, ALONG_W)


class Exchange:
    def __init__(self, places, source, left_2, right_2, send_sem, recv_sem, local_sem, first):
        self.places, self.source = (places, source)
        self.left_2, self.right_2 = (left_2, right_2)
        self.sems, self.first = ((send_sem, recv_sem, local_sem), first)
        self.copies = []

    def move(self, part, j, mine, target, theirs, place):
        send_sem, recv_sem, local_sem = (sem.at[self.first + part, j] for sem in self.sems)
        remote = send_to(theirs, place, send_sem, recv_sem, self.places.to_c)
        local = pltpu.make_async_copy(mine, target, local_sem)
        remote.start()
        local.start()
        self.copies += [remote, local]

    def lows(self, part):
        low = sum(self.source.parts[:part])
        depth = self.source.parts[part]
        return (pl.ds(low, depth), pl.ds(self.source.depth + low, depth))

    def start_left(self, part, left):
        low, high = self.lows(part)
        for y in range(2):
            ours, theirs = (
                pl.ds(pl.multiple_of((2 * y + core) * self.source.rows, 16), self.source.rows)
                for core in (self.places.c, 1 - self.places.c)
            )
            self.move(
                part, y, left.at[ours], self.left_2.at[y, :, low],
                left.at[theirs], self.left_2.at[y, :, high],
            )

    def start_right(self, part, right):
        low, high = self.lows(part)
        self.move(part, 2, right, self.right_2.at[low], right, self.right_2.at[high])

    def start(self, part, left, right):
        self.start_right(part, right)
        self.start_left(part, left)

    def ready(self):
        while self.copies:
            self.copies.pop(0).wait()

    def term(self, y, rows, lanes):
        return product(self.left_2[y, rows, :], self.right_2[:, lanes])


class Addition:
    def __init__(self, places, own, sibling, send_sem, recv_sem, local_sem):
        self.places, self.own, self.sibling = (places, own, sibling)
        self.sems = (send_sem, recv_sem, local_sem)
        self.copies = []

    def start(self, whole):
        rows = self.own.shape[1]
        for y in range(2):
            ours, theirs = (
                pl.ds(pl.multiple_of((2 * y + core) * rows, 16), rows)
                for core in (self.places.c, 1 - self.places.c)
            )
            send_sem, recv_sem, local_sem = (sem.at[y] for sem in self.sems)
            remote = send_to(
                whole.at[theirs], self.sibling.at[y], send_sem, recv_sem, self.places.to_c
            )
            local = pltpu.make_async_copy(whole.at[ours], self.own.at[y], local_sem)
            remote.start()
            local.start()
            self.copies += [remote, local]

    def ready(self):
        while self.copies:
            self.copies.pop(0).wait()

    def term(self, y, rows, lanes):
        return self.own[y, rows, lanes].astype(F32) + self.sibling[y, rows, lanes].astype(F32)


class Halving:
    def __init__(self, places, units, outbox, inbox, send_sem, recv_sem, outs, groups):
        self.units, self.groups = (units, groups)
        self.outbox, self.inbox, self.outs = (outbox, inbox, outs)
        self.send_sem, self.recv_sem = (send_sem, recv_sem)
        self.bits = (places.x, places.z, places.w, places.y)
        self.peers = (places.to_x, places.to_z, places.to_w, places.to_y)
        self.copies = {}

    def block(self, u, k, j):
        source, stride, offset, order, first, count = self.units[u]
        place = {}
        for i, along in enumerate(order):
            if i < k:
                place[along] = self.bits[along]
            elif i == k:
                place[along] = 1 - self.bits[along]
            else:
                place[along] = lax.rem(j // (1 << (3 - i)), 2)
        device = place[ALONG_W] * 4 + place[ALONG_Z] * 2 + place[ALONG_X]
        lanes = pl.ds(pl.multiple_of(device * stride + offset, LANES), LANES)
        total = source.term(place[ALONG_Y], pl.ds(first, count), lanes)
        for i in range(k):
            index = 0
            for p in range(i + 1, 4):
                index = index * 2 + place[order[p]]
            total = total + self.inbox[u][i][index].astype(F32)
        return total

    def step(self, u, k):
        if k == 0:
            self.units[u][0].ready()
        else:
            self.copies[u, k - 1].wait_recv()
        if k == 4:
            self.outs[u][...] = self.block(u, 4, 0)
            return

        def one(j, carry):
            self.outbox[u][k][j] = self.block(u, k, j).astype(BF)
            return carry

        if k == 3:
            one(0, 0)
        else:
            lax.fori_loop(0, 1 << (3 - k), one, 0)
        copy = send_to(
            self.outbox[u][k], self.inbox[u][k], self.send_sem.at[u, k], self.recv_sem.at[u, k],
            self.peers[self.units[u][3][k]],
        )
        copy.start()
        self.copies[u, k] = copy

    def slot(self, t):
        for k in range(5):
            if 0 <= t - k < len(self.groups):
                for u in self.groups[t - k]:
                    self.step(u, k)

    def drain(self):
        for copy in self.copies.values():
            copy.wait_send()


def boxes(units):
    return tuple(
        tuple(kept(1 << (3 - k), unit[-1], LANES) for k in range(4)) for unit in units
    )


HEAD_POST, HEAD_PRIOR, HEAD_POST_OUT, HEAD_PRIOR_OUT, HEAD_MAN_ENC = range(5)
HEAD_SOURCES = (SOURCE_POST, SOURCE_1024, SOURCE_1024, SOURCE_1024, SOURCE_MAN_ENC)
HEAD_UNITS = (
    (HEAD_POST, 128, 0, Y_FIRST, 0, 128),
    (HEAD_PRIOR, 128, 0, X_FIRST, 0, 256),
    (HEAD_POST_OUT, 128, 0, Z_FIRST, 0, 128),
    (HEAD_POST, 128, 0, Y_FIRST, 128, 128),
    (HEAD_POST, 128, 0, X_FIRST, 384, 256),
    (HEAD_POST_OUT, 128, 0, Z_FIRST, 128, 128),
    (HEAD_POST, 128, 0, Y_FIRST, 256, 128),
    (HEAD_MAN_ENC, 128, 0, X_FIRST, 0, 256),
    (HEAD_PRIOR_OUT, 128, 0, Z_FIRST, 0, 256),
)
HEAD_GROUPS = ((0, 1, 2), (3, 4, 5), (6, 7, 8))
LAST_WORKER, LAST_GOAL_OUT, LAST_GOAL_IN, LAST_GRU, LAST_IMG = range(5)
LAST_SOURCES = (None, SOURCE_GOAL_OUT, SOURCE_GOAL_IN, SOURCE_GRU, SOURCE_1024)
LAST_UNITS = (
    (LAST_WORKER, 128, 0, Y_FIRST, 0, 256),
    (LAST_WORKER, 128, 0, X_FIRST, 256, 256),
    (LAST_WORKER, 128, 0, Z_FIRST, 512, 256),
    (LAST_GOAL_OUT, 128, 0, Z_FIRST, 0, 128),
    (LAST_GOAL_IN, 128, 0, Z_FIRST, 0, 16),
    (LAST_GRU, 384, 0, Y_FIRST, 0, 128),
    (LAST_GRU, 384, 0, X_FIRST, 128, 256),
    (LAST_GRU, 384, 0, Z_FIRST, 384, 128),
    (LAST_GRU, 384, 128, Y_FIRST, 0, 128),
    (LAST_IMG, 128, 0, X_FIRST, 0, 256),
    (LAST_GRU, 384, 128, Z_FIRST, 384, 128),
    (LAST_GRU, 384, 256, Y_FIRST, 0, 128),
    (LAST_GRU, 384, 128, X_FIRST, 128, 256),
    (LAST_GRU, 384, 256, Z_FIRST, 256, 256),
    (LAST_GRU, 384, 256, X_FIRST, 128, 128),
)
LAST_EARLY = ((0, 1, 2), (3, 4))
LAST_LATE = ((5, 6, 7), (8, 9, 10), (11, 12, 13), (14,))


FORWARD_ROWS, BACK_ROWS = (128, 128)


class Worker(NamedTuple):
    goal_codes: Any = taken(GC, ROWS, dtype=jnp.int32)
    actions: Any = taken(HOR, ROWS, dtype=jnp.int32)
    samples: Any = taken(HOR, ZG, ROWS, dtype=jnp.int32)
    vectors: Any = taken(4, VECTOR_TILES, LANES, dtype=F32)
    tables: Any = taken(4, TABLES, LANES)
    start_state: Any = taken(ROWS, H + LANES)
    goal_out: Any = taken(U, H)
    actor_in: Any = taken(3 * H, U)
    critic_in: Any = taken(3 * H, U)
    post_left: Any = taken(H + E, ROWS, here=False)
    post_out_left: Any = taken(H, ROWS, here=False)
    prior_out_left: Any = taken(H, ROWS, here=False)
    me_left: Any = taken(H, 2 * ROWS, here=False)
    post_right: Any = taken(ROWS, H, here=False)
    prior_right: Any = taken(ROWS, H, here=False)
    post_out_right: Any = taken(ROWS, Z, here=False)
    prior_out_right: Any = taken(ROWS, Z, here=False)
    me_right: Any = taken(2 * ROWS, 2 * U, here=False)
    worker_left: Any = given(3 * H, 2 * U)
    returned: Any = given(ROWS, H)
    goal_left: Any = given(U, ROWS)
    code_turned: Any = given(GCODE, ROWS)
    goal_right: Any = given(ROWS, H)
    goal_pair: Any = given(ROWS, 2 * U)
    small: Any = given(2, 2, SMALL_TILES, LANES, dtype=F32)
    sums: Any = tuple(given(unit[-1], LANES, dtype=F32) for unit in HEAD_UNITS)
    act_out: Any = kept(32, U)
    goal_in: Any = kept(GCODE, U)
    action_columns: Any = kept(ROWS, LANES, dtype=F32)
    goal_normed: Any = kept(ROWS, U, dtype=F32)
    goal_inverse: Any = kept(ROWS, 1, dtype=F32)
    goal_hidden: Any = kept(ROWS, U)
    goal_pre: Any = kept(ROWS, U)
    goal_low: Any = kept(ROWS, H)
    turned: Any = kept(2 * H, ROWS)
    slot_part: Any = kept(2, ROWS, U, dtype=F32)
    hot: Any = kept(2 * ROWS, Z)
    pre: Any = kept(2 * ROWS, U, dtype=F32)
    hidden: Any = kept(2 * ROWS, U)
    normed: Any = kept(2, HOR * ROWS, U, dtype=F32)
    inverse: Any = kept(2, HOR * ROWS, 1, dtype=F32)
    hot_turned: Any = kept(Z, HOR * ROWS)
    log_chance: Any = kept(HOR * ROWS, 32, dtype=F32)
    chosen: Any = kept(ROWS, LANES, dtype=F32)
    value: Any = kept(ROWS, LANES, dtype=F32)
    returns: Any = kept(ROWS, LANES, dtype=F32)
    pre_pair: Any = kept(HOR * ROWS, 2 * U)
    summed: Any = kept(2, ROWS, U, dtype=F32)
    sum_low: Any = kept(2, ROWS, U)
    sum_pair: Any = kept(ROWS, 2 * U)
    low_512: Any = kept(ROWS, U)
    grad_column: Any = kept(ROWS, 1, dtype=F32)
    to_state: Any = kept(ROWS, H)
    incoming: Any = kept(ROWS, H)
    wide_512: Any = kept(ROWS, U, dtype=F32)
    top: Any = kept(8, LANES, dtype=F32)
    top_in: Any = kept(5, 8, LANES, dtype=F32)
    left_2: Any = tuple(kept(2, s.rows, 2 * s.depth) for s in HEAD_SOURCES)
    right_2: Any = tuple(kept(2 * s.depth, s.columns) for s in HEAD_SOURCES)
    outbox: Any = boxes(HEAD_UNITS)
    inbox: Any = boxes(HEAD_UNITS)
    top_send: Any = signal(5)
    top_recv: Any = signal(5)
    state_send: Any = signal(8)
    state_recv: Any = signal(8)
    pair_send: Any = signal(len(HEAD_SOURCES), 3)
    pair_recv: Any = signal(len(HEAD_SOURCES), 3)
    pair_local: Any = signal(len(HEAD_SOURCES), 3)
    half_send: Any = signal(len(HEAD_UNITS), 4)
    half_recv: Any = signal(len(HEAD_UNITS), 4)

    def gain(self, low, size):
        return vector_of(self.vectors, low, size // (4 * LANES))

    def goal(self):
        self.small[...] = jnp.zeros(self.small.shape, F32)
        for r in range(4):
            self.act_out[:, r * LANES : (r + 1) * LANES] = self.tables[
                r, TAB_ACT : TAB_ACT + 32, :
            ]
            for i in range(4):
                self.goal_in[16 * r : 16 * (r + 1), i * LANES : (i + 1) * LANES] = self.tables[
                    r, TAB_GOAL + 16 * i : TAB_GOAL + 16 * (i + 1), :
                ]
        self.action_columns[...] = columns_of(self.actions[...].astype(F32))
        hot = hot_rows(columns_of(self.goal_codes[...].astype(F32)), GK, GC, LANES)
        self.code_turned[...] = hot.T[0:GCODE].astype(BF)
        matmul_into(self.goal_normed, hot[:, 0:GCODE].astype(BF), self.goal_in)
        hidden_rows(
            self.goal_normed, self.goal_inverse, self.gain(GOAL_G, U), self.goal_hidden
        )
        turn_into(self.goal_left, self.goal_hidden)

        def one(j, totals):
            lanes = pl.ds(pl.multiple_of(j * 256, 256), 256)
            goal = product(self.goal_hidden[...], self.goal_out[:, lanes])
            state = self.start_state[:, lanes].astype(F32)
            self.goal_low[:, lanes] = goal.astype(BF)
            terms = (goal * state, goal * goal, state * state)
            return tuple(
                t + jnp.sum(term, -1, keepdims=True) for t, term in zip(totals, terms)
            )

        zero = jnp.zeros((ROWS, 1), F32)
        aligned, goal_square, state_square = lax.fori_loop(0, H // 256, one, (zero,) * 3)
        turn_into(self.turned, self.start_state.at[:, 0:H])
        turn_into(self.turned, self.goal_low, H)
        return aligned / (jnp.maximum(goal_square, state_square) + small_floor)

    def slots(self):
        for which, weight in enumerate((self.actor_in, self.critic_in)):
            def one(j, carry):
                lanes = pl.ds(pl.multiple_of(j * 256, 256), 256)
                self.slot_part[which, :, lanes] = product(
                    self.start_state[:, 0:H], weight[0:H, lanes]
                ) + product(self.goal_low[...], weight[2 * H : 3 * H, lanes])
                return carry

            lax.fori_loop(0, U // 256, one, 0)

    def forward(self, first, last):
        gains = (self.gain(ACT_G, U), self.gain(CRI_G, U))
        head = self.gain(CRI_O, U)
        spread = class_spread(ZG, ZK, ZG, Z)
        lane = lax.broadcasted_iota(jnp.int32, (1, Z), 1)
        lane_class = jnp.bitwise_and(lane, ZK - 1).astype(F32)
        group = lax.broadcasted_iota(jnp.int32, (Z, ZG), 1)
        place = lax.broadcasted_iota(jnp.int32, (Z, ZG), 0)
        inside = (place >= group * ZK) & (place < group * ZK + ZK)
        spread_turned = jnp.where(inside, 1.0, 0.0).astype(BF)
        place_class = jnp.bitwise_and(
            lax.broadcasted_iota(jnp.int32, (Z, 1), 0), ZK - 1
        ).astype(F32)
        act_lane = lax.broadcasted_iota(jnp.int32, (1, 32), 1)
        step_lane = lax.broadcasted_iota(jnp.int32, (1, LANES), 1)

        def pair(i, carry):
            start = pl.multiple_of(i * 2 * ROWS, 2 * ROWS)
            for half in range(2):
                k = 2 * i + half
                rows = pl.ds(pl.multiple_of(start + half * ROWS, ROWS), ROWS)
                ids = self.samples[k].astype(F32)
                self.hot[half * ROWS : (half + 1) * ROWS, :] = jnp.where(
                    product(columns_of(ids)[:, 0:ZG].astype(BF), spread) == lane_class, 1.0, 0.0
                ).astype(BF)
                self.hot_turned[:, rows] = jnp.where(
                    product(spread_turned, ids.astype(BF)) == place_class, 1.0, 0.0
                ).astype(BF)
            for which, weight in enumerate((self.actor_in, self.critic_in)):
                self.pre[...] = product(self.hot[...], weight[H : 2 * H, :])
                for low in range(0, 2 * ROWS, FORWARD_ROWS):
                    rows = pl.ds(pl.multiple_of(start + low, FORWARD_ROWS), FORWARD_ROWS)
                    slot = pl.ds(low % ROWS, FORWARD_ROWS)
                    pre = self.pre[low : low + FORWARD_ROWS, :] + self.slot_part[which, slot, :]
                    normed, inverse = normalize(pre)
                    self.normed[which, rows, :] = normed
                    self.inverse[which, rows, :] = inverse
                    hidden = elu_of(normed * gains[which]).astype(BF)
                    if which == 0:
                        self.hidden[low : low + FORWARD_ROWS, :] = hidden
                    else:
                        value = jnp.sum(hidden.astype(F32) * head, -1, keepdims=True)
                        here = step_lane == 2 * i + low // ROWS
                        self.value[slot, :] = jnp.where(here, value, self.value[slot, :])
            logits = lax.dot_general(
                self.hidden[...], self.act_out[...], (((1,), (1,)), ((), ())),
                preferred_element_type=F32,
            )
            logits = jnp.where(act_lane < NA, logits, -1e30)
            shifted = logits - jnp.max(logits, -1, keepdims=True)
            total = jnp.sum(jnp.exp(shifted), -1, keepdims=True)
            self.log_chance[pl.ds(start, 2 * ROWS), :] = shifted - jnp.log(total)
            return carry

        lax.fori_loop(first, last, pair, 0)

    def action_here(self, k):
        action = self.at_step(self.action_columns, k)
        return action == lax.broadcasted_iota(jnp.int32, (1, 32), 1).astype(F32)

    def at_step(self, ref, k):
        lane = lax.broadcasted_iota(jnp.int32, (ROWS, LANES), 1)
        return jnp.sum(jnp.where(lane == k, ref[...], 0.0), -1, keepdims=True)

    def targets(self, reward):
        weight = self.start_state[:, H : H + 1].astype(F32)
        lane = lax.broadcasted_iota(jnp.int32, (ROWS, LANES), 1)
        later = self.value[:, HOR - 1 : HOR]
        result = later
        returns = jnp.where(lane == HOR - 1, result, 0.0)
        for k in range(HOR - 2, -1, -1):
            blended = (1.0 - return_mix) * later + return_mix * result
            result = reward + discount * blended
            returns = jnp.where(lane == k, result, returns)
            later = self.value[:, k : k + 1]
        self.returns[...] = returns
        gaps = jnp.where(lane < HOR, jnp.abs(returns - self.value[...]), 0.0)
        top = jnp.max(weight * gaps, 0, keepdims=True)
        self.top[...] = jnp.broadcast_to(jnp.max(top, 1, keepdims=True), (8, LANES))

    def critic_back(self, first, last, total):
        gain, head = (self.gain(CRI_G, U), self.gain(CRI_O, U))
        weight = self.start_state[:, H : H + 1].astype(F32)

        def step(k, totals):
            rows = pl.ds(pl.multiple_of(k * ROWS, ROWS), ROWS)
            misfit = self.at_step(self.value, k) - self.at_step(self.returns, k)
            grad = weight * misfit * (1.0 / (ROWS * HOR))
            self.grad_column[...] = grad
            gain_total = totals[0] + hidden_rows_back(
                lambda r: self.grad_column[r, :] * head,
                self.normed.at[1, rows], self.inverse.at[1, rows], gain, self.low_512, BACK_ROWS,
                self.hidden,
            )
            head_total = totals[1] + jnp.sum(
                self.hidden[0:ROWS, :].astype(F32) * grad, 0, keepdims=True
            )
            for j in range(4):
                tile = self.low_512[:, j * LANES : (j + 1) * LANES].astype(F32)
                self.summed[1, :, j * LANES : (j + 1) * LANES] += tile
                turned = pltpu.roll(tile, 64, 1)
                self.pre_pair[rows, 2 * j * LANES : (2 * j + 1) * LANES] = turned.astype(BF)
                self.pre_pair[rows, (2 * j + 1) * LANES : (2 * j + 2) * LANES] = tile.astype(BF)
            return (gain_total, head_total)

        return lax.fori_loop(first, last, step, total)

    def pair(self, first, second, out_ref, rows):
        lane = lax.broadcasted_iota(jnp.int32, (ROWS, LANES), 1)
        for j in range(4):
            lanes = slice(j * LANES, (j + 1) * LANES)
            even = slice(2 * j * LANES, (2 * j + 1) * LANES)
            odd = slice((2 * j + 1) * LANES, (2 * j + 2) * LANES)
            a = first[:, lanes].astype(F32)
            if second is None:
                b_even, b_odd = (out_ref[rows, even].astype(F32), out_ref[rows, odd].astype(F32))
            else:
                b_odd = second[:, lanes].astype(F32)
                b_even = pltpu.roll(b_odd, 64, 1)
            out_ref[rows, even] = jnp.where(lane < 64, a, b_even).astype(BF)
            out_ref[rows, odd] = jnp.where(lane < 64, pltpu.roll(a, 64, 1), b_odd).astype(BF)

    def actor_back(self, first, last, totals):
        gain = self.gain(ACT_G, U)
        weight = self.start_state[:, H : H + 1].astype(F32)
        scale = self.top[0:1, 0:1] + small_floor

        def step(k, totals):
            rows = pl.ds(pl.multiple_of(k * ROWS, ROWS), ROWS)
            advantage = self.at_step(self.returns, k) - self.at_step(self.value, k)
            gained = weight * advantage / scale
            here = self.action_here(k)
            log_chance = self.log_chance[rows, :]
            chance = jnp.exp(log_chance)
            grad = (gained * (-1.0 / (ROWS * HOR))) * (jnp.where(here, 1.0, 0.0) - chance)
            grad_turned = jnp.concatenate(
                [grad, jnp.zeros((ROWS, LANES - 32), F32)], 1
            ).T[0:32].astype(BF)
            self.wide_512[...] = product(grad.astype(BF), self.act_out[...])
            gain_total = totals[0] + hidden_rows_back(
                lambda r: self.wide_512[r, :],
                self.normed.at[0, rows], self.inverse.at[0, rows], gain, self.low_512, BACK_ROWS,
                self.hidden,
            )
            out_total = totals[1] + product(grad_turned, self.hidden[0:ROWS, :])
            self.summed[0] += self.low_512[...].astype(F32)
            self.pair(self.low_512, None, self.pre_pair, rows)
            chosen = jnp.sum(jnp.where(here, log_chance, 0.0), -1, keepdims=True)
            loss = totals[2] + jnp.sum(chosen * gained, 0, keepdims=True)
            return (gain_total, out_total, loss)

        return lax.fori_loop(first, last, step, totals)

    def inputs_back(self, low, out_ref):
        def one(j, carry):
            rows = pl.ds(pl.multiple_of(low + j * 256, 256), 256)
            total = 0.0
            for which, weight in enumerate((self.actor_in, self.critic_in)):
                total = total + lax.dot_general(
                    self.sum_low[which], weight[rows, :], (((1,), (1,)), ((), ())),
                    preferred_element_type=F32,
                )
            out_ref[:, pl.ds(pl.multiple_of(j * 256, 256), 256)] = total.astype(BF)
            return carry

        lax.fori_loop(0, H // 256, one, 0)

    def goal_back(self):
        matmul_into(self.wide_512, self.goal_right[...], self.goal_out, turned=True)
        total = hidden_rows_back(
            lambda rows: self.wide_512[rows, :],
            self.goal_normed, self.goal_inverse, self.gain(GOAL_G, U), self.goal_pre,
        )
        put_vector(self.small, GOAL_G, total)
        spread_lanes(self.goal_pre, self.goal_pair, 0, 0)

    def weights(self):
        def one(j, carry):
            lanes = pl.ds(pl.multiple_of(j * 256, 256), 256)
            self.worker_left[H : 2 * H, lanes] = product(
                self.hot_turned[...], self.pre_pair[:, lanes]
            ).astype(BF)
            pair = self.sum_pair[:, lanes]
            self.worker_left[0:H, lanes] = product(self.turned[0:H], pair).astype(BF)
            self.worker_left[2 * H : 3 * H, lanes] = product(
                self.turned[H : 2 * H], pair
            ).astype(BF)
            return carry

        lax.fori_loop(0, 2 * U // 256, one, 0)


def worker_kernel(f):
    places = Places()
    peers = (places.to_c, places.to_y, places.to_x, places.to_z, places.to_w)
    greet(
        [(places.around(o), places.rep) for o in range(1, 8)] + [places.to_c, places.to_y]
    )
    heads = []
    lefts = (f.post_left, f.post_left, f.post_out_left, f.prior_out_left, f.me_left)
    rights = (f.post_right, f.prior_right, f.post_out_right, f.prior_out_right, f.me_right)
    for i, source in enumerate(HEAD_SOURCES):
        heads.append(
            Exchange(
                places, source, f.left_2[i], f.right_2[i], f.pair_send, f.pair_recv,
                f.pair_local, i,
            )
        )
    for i in (HEAD_POST, HEAD_PRIOR, HEAD_POST_OUT):
        heads[i].start(0, lefts[i], rights[i])
    halving = Halving(
        places, [(heads[unit[0]],) + unit[1:] for unit in HEAD_UNITS], f.outbox, f.inbox,
        f.half_send, f.half_recv, f.sums, HEAD_GROUPS,
    )
    reward = f.goal()
    halving.slot(0)
    for i in (HEAD_MAN_ENC, HEAD_PRIOR_OUT):
        heads[i].start(0, lefts[i], rights[i])
    f.slots()
    f.value[...] = jnp.zeros(f.value.shape, F32)
    f.summed[...] = jnp.zeros(f.summed.shape, F32)
    f.forward(0, 3)
    halving.slot(1)
    f.forward(3, 6)
    halving.slot(2)
    f.forward(6, HOR // 2)
    f.targets(reward)
    totals = (jnp.zeros((1, U), F32), jnp.zeros((1, U), F32))
    steps = (0, 3, 6, 9, 12, HOR)
    for k in range(5):
        copy = send_to(f.top, f.top_in.at[k], f.top_send.at[k], f.top_recv.at[k], peers[k])
        copy.start()
        totals = f.critic_back(steps[k], steps[k + 1], totals)
        copy.wait()
        f.top[...] = jnp.maximum(f.top[...], f.top_in[k])
        if k == 1:
            halving.slot(3)
    put_vector(f.small, CRI_G, totals[0])
    put_vector(f.small, CRI_O, totals[1])
    halving.slot(4)
    totals = (jnp.zeros((1, U), F32), jnp.zeros((32, U), F32), jnp.zeros((1, 1), F32))
    totals = f.actor_back(0, HOR // 2, totals)
    halving.slot(5)
    actor_gain, actor_out, chosen = f.actor_back(HOR // 2, HOR, totals)
    put_vector(f.small, ACT_G, actor_gain)
    put_table(f.small, ACT_T, actor_out, 24)
    for which in range(2):
        f.sum_low[which] = f.summed[which].astype(BF)
    f.inputs_back(0, f.to_state)
    states = regroup_start(places, f.to_state, f.incoming, f.state_send, f.state_recv)
    f.pair(f.sum_low.at[0], f.sum_low.at[1], f.sum_pair, slice(0, ROWS))
    f.inputs_back(2 * H, f.goal_right)
    f.goal_back()
    halving.slot(6)
    weight = f.start_state[:, H : H + 1].astype(F32)
    misfit = f.value[...] - f.returns[...]
    squares = jnp.sum(jnp.sum(weight * misfit * misfit, -1, keepdims=True), 0, keepdims=True)
    loss = (0.5 * squares - chosen) * (1.0 / (ROWS * HOR))
    for y in range(2):
        for c in range(2):
            f.small[c, y, LOSS : LOSS + 1, :] = jnp.broadcast_to(loss, (1, LANES))
    f.weights()
    for copy in states:
        copy.wait()
    f.returned[...] = f.incoming[...]
    halving.drain()


class Last(NamedTuple):
    meta_turned: Any = taken(LANES, ROWS, dtype=F32)
    prev: Any = taken(ROWS, H)
    vectors: Any = taken(4, VECTOR_TILES, LANES, dtype=F32)
    returned: Any = taken(ROWS, H)
    grad_partial: Any = taken(ROWS, H, dtype=F32)
    gru_normed: Any = taken(ROWS, 3 * H, dtype=F32)
    gru_inverse: Any = taken(ROWS, 1, dtype=F32)
    img_normed: Any = taken(ROWS, H, dtype=F32)
    img_inverse: Any = taken(ROWS, 1, dtype=F32)
    small_1: Any = taken(2, 2, SMALL_TILES, LANES, dtype=F32)
    small_2: Any = taken(2, 2, SMALL_TILES, LANES, dtype=F32)
    gru_share: Any = taken(2 * H, 3 * H, here=False)
    worker_left: Any = taken(3 * H, 2 * U, here=False)
    goal_left: Any = taken(U, ROWS, here=False)
    dec_left: Any = taken(U, ROWS, here=False)
    code_turned: Any = taken(GCODE, ROWS, here=False)
    soft_turned: Any = taken(GCODE, ROWS, here=False)
    gru_left: Any = taken(2 * H, ROWS, here=False)
    img_left: Any = taken(Z, ROWS, here=False)
    goal_right: Any = taken(ROWS, H, here=False)
    recon_low: Any = taken(ROWS, H, here=False)
    goal_pair: Any = taken(ROWS, 2 * U, here=False)
    dec_pair: Any = taken(ROWS, 2 * U, here=False)
    deter_grad: Any = given(ROWS, H, dtype=F32)
    small_sum: Any = given(SMALL_TILES, LANES, dtype=F32)
    sums: Any = tuple(given(unit[-1], LANES, dtype=F32) for unit in LAST_UNITS)
    gru_weight: Any = kept(2 * H, 3 * H)
    gru_right: Any = kept(ROWS, 3 * H)
    img_right: Any = kept(ROWS, H)
    grad: Any = kept(ROWS, H, dtype=F32)
    wide: Any = kept(ROWS, 2 * H, dtype=F32)
    small: Any = kept(2, 2, SMALL_TILES, LANES, dtype=F32)
    small_pair: Any = kept(2, SMALL_TILES, LANES, dtype=F32)
    small_in: Any = kept(4, SMALL_TILES, LANES, dtype=F32)
    worker_own: Any = kept(2, *WORKER_SHARE)
    worker_sibling: Any = kept(2, *WORKER_SHARE)
    left_2: Any = tuple(kept(2, s.rows, 2 * s.depth) for s in LAST_SOURCES[1:])
    right_2: Any = tuple(kept(2 * s.depth, s.columns) for s in LAST_SOURCES[1:])
    outbox: Any = boxes(LAST_UNITS)
    inbox: Any = boxes(LAST_UNITS)
    load_done: Any = signal(1)
    add_send: Any = signal(2)
    add_recv: Any = signal(2)
    add_local: Any = signal(2)
    pair_send: Any = signal(6, 3)
    pair_recv: Any = signal(6, 3)
    pair_local: Any = signal(6, 3)
    half_send: Any = signal(len(LAST_UNITS), 4)
    half_recv: Any = signal(len(LAST_UNITS), 4)
    small_send: Any = signal(5)
    small_recv: Any = signal(5)

    def state_back(self):
        gain = vector_of(self.vectors, GRU_G, 6)
        frame = lax.broadcasted_iota(jnp.int32, (ROWS, ROWS), 0).astype(F32)
        place = jnp.where(self.meta_turned[37:38, :] == frame, 1.0, 0.0).astype(BF)

        def add(j, carry):
            lanes = pl.ds(pl.multiple_of(j * 256, 256), 256)
            self.grad[:, lanes] = self.grad_partial[:, lanes] + product(
                place, self.returned[:, lanes]
            )
            return carry

        lax.fori_loop(0, H // 256, add, 0)

        def one(rows, total):
            normed = self.gru_normed[rows, :]
            parts = normed * gain
            inner = parts[:, H : 2 * H]
            reset = 1.0 / (1.0 + jnp.exp(-parts[:, :H]))
            candidate = jnp.tanh(reset * inner)
            update = 1.0 / (1.0 + jnp.exp(1.0 - parts[:, 2 * H :]))
            grad = self.grad[rows, :]
            prev = self.prev[rows, :].astype(F32)
            grad_inner = grad * update * (1.0 - candidate * candidate)
            grad_parts = jnp.concatenate(
                [
                    grad_inner * inner * reset * (1.0 - reset),
                    grad_inner * reset,
                    grad * (candidate - prev) * update * (1.0 - update),
                ],
                1,
            )
            self.deter_grad[rows, :] = grad * (1.0 - update)
            total = total + jnp.sum(grad_parts * normed, 0, keepdims=True)
            back = normalize_back(grad_parts * gain, normed, self.gru_inverse[rows, :])
            self.gru_right[rows, :] = back.astype(BF)
            return total

        put_vector(self.small, GRU_G, by_rows(ROWS, 16, one, jnp.zeros((1, 3 * H), F32)))

    def input_back(self):
        matmul_into(self.wide, self.gru_right[...], self.gru_weight, turned=True)
        self.deter_grad[...] += self.wide[:, H : 2 * H]
        total = hidden_rows_back(
            lambda rows: self.wide[rows, 0:H],
            self.img_normed, self.img_inverse, vector_of(self.vectors, IMG_G, 2), self.img_right,
        )
        put_vector(self.small, IMG_G, total)

    def action_back(self):
        place = lax.broadcasted_iota(jnp.int32, (24, ROWS), 0).astype(F32)
        hot = jnp.where(self.meta_turned[32:33, :] == place, 1.0, 0.0).astype(BF)
        for r in range(4):
            for i in range(2):
                start = (2 * r + i) * LANES
                low = IMG_T + 24 * i
                self.small[r % 2, r // 2, low : low + 24, :] = product(
                    hot, self.img_right[:, start : start + LANES]
                )


class SmallSum:
    def __init__(self, places, f):
        self.places, self.f = (places, f)
        self.copies = []

    def step(self, k):
        f, places = (self.f, self.places)
        if k > 0:
            self.copies[k - 1].wait()
        if k == 0:
            source, target, device = (f.small.at[1 - places.c], f.small_pair, places.to_c)
        elif k == 1:
            f.small_pair[...] = f.small_pair[...] + f.small[places.c]
            source, target, device = (
                f.small_pair.at[1 - places.y], f.small_in.at[0], places.to_y,
            )
        else:
            if k == 2:
                f.small_sum[...] = f.small_pair[places.y] + f.small_in[0]
            else:
                f.small_sum[...] = f.small_sum[...] + f.small_in[k - 2]
            if k == 5:
                return
            device = (places.to_x, places.to_z, places.to_w)[k - 2]
            source, target = (f.small_sum, f.small_in.at[k - 1])
        copy = send_to(source, target, f.small_send.at[k], f.small_recv.at[k], device)
        copy.start()
        self.copies.append(copy)


def last_kernel(f):
    places = Places()
    load = pltpu.make_async_copy(f.gru_share, f.gru_weight, f.load_done.at[0])
    load.start()
    greet((places.to_c, places.to_y, places.to_x, places.to_z, places.to_w))
    worker = Addition(
        places, f.worker_own, f.worker_sibling, f.add_send, f.add_recv, f.add_local
    )
    worker.start(f.worker_left)
    sources, part = ([worker], 0)
    for i, source in enumerate(LAST_SOURCES[1:]):
        sources.append(
            Exchange(
                places, source, f.left_2[i], f.right_2[i], f.pair_send, f.pair_recv,
                f.pair_local, part,
            )
        )
        part += len(source.parts)
    sources[LAST_GOAL_OUT].start(0, f.goal_left, f.goal_right)
    sources[LAST_GOAL_OUT].start(1, f.dec_left, f.recon_low)
    sources[LAST_GOAL_IN].start(0, f.code_turned, f.goal_pair)
    sources[LAST_GOAL_IN].start(1, f.soft_turned, f.dec_pair)
    sources[LAST_GRU].start_left(0, f.gru_left)
    sources[LAST_IMG].start_left(0, f.img_left)
    halving = Halving(
        places, [(sources[unit[0]],) + unit[1:] for unit in LAST_UNITS], f.outbox, f.inbox,
        f.half_send, f.half_recv, f.sums, LAST_EARLY + LAST_LATE,
    )
    f.small[...] = f.small_1[...] + f.small_2[...]
    f.state_back()
    sources[LAST_GRU].start_right(0, f.gru_right)
    halving.slot(0)
    load.wait()
    f.input_back()
    sources[LAST_IMG].start_right(0, f.img_right)
    halving.slot(1)
    f.action_back()
    small = SmallSum(places, f)
    small.step(0)
    groups = len(halving.groups)
    for t in range(2, groups + 4):
        halving.slot(t)
        if t < 7:
            small.step(t - 1)
    halving.drain()


class Unpack(NamedTuple):
    heads: Any = tuple(taken(unit[-1], LANES, dtype=F32) for unit in HEAD_UNITS)
    last: Any = tuple(taken(unit[-1], LANES, dtype=F32) for unit in LAST_UNITS)
    small: Any = taken(SMALL_TILES, LANES, dtype=F32)
    deter: Any = taken(ROWS, H, dtype=F32)
    embed: Any = taken(ROWS, E, dtype=F32)
    loss: Any = given(1, LANES, dtype=F32)
    deter_grad: Any = given(ROWS, H, dtype=F32)
    embed_grad: Any = given(ROWS, E, dtype=F32)
    obs_gain: Any = given(H // 4, dtype=F32)
    manager_in: Any = given(U // 8, H // 4, dtype=F32)
    manager_gain: Any = given(U // 4, dtype=F32)
    manager_out: Any = given(U // 4, dtype=F32)
    goal_in: Any = given(GCODE // 4, U // 8, dtype=F32)
    goal_gain: Any = given(U // 4, dtype=F32)
    goal_out: Any = given(U // 4, H // 8, dtype=F32)
    actor_in: Any = given(U // 8, 3 * H // 4, dtype=F32)
    actor_gain: Any = given(U // 4, dtype=F32)
    actor_out: Any = given(NA, U // 4, dtype=F32)
    critic_in: Any = given(U // 8, 3 * H // 4, dtype=F32)
    critic_gain: Any = given(U // 4, dtype=F32)
    critic_out: Any = given(U // 4, dtype=F32)
    img_stoch: Any = given(Z // 4, H // 8, dtype=F32)
    img_action: Any = given(NA, H // 4, dtype=F32)
    img_gain: Any = given(H // 4, dtype=F32)
    gru_weight: Any = given(H // 2, 3 * H // 8, dtype=F32)
    gru_gain: Any = given(3 * H // 4, dtype=F32)
    post_in: Any = given((H + E) // 4, H // 8, dtype=F32)
    post_gain: Any = given(H // 4, dtype=F32)
    post_out: Any = given(H // 4, Z // 8, dtype=F32)
    prior_in: Any = given(H // 4, H // 8, dtype=F32)
    prior_gain: Any = given(H // 4, dtype=F32)
    prior_out: Any = given(H // 4, Z // 8, dtype=F32)
    enc_in: Any = given(U // 8, H // 4, dtype=F32)
    enc_gain: Any = given(U // 4, dtype=F32)
    enc_out: Any = given(GCODE, U // 4, dtype=F32)


def unpack_kernel(f):
    f.loss[...] = f.small[LOSS : LOSS + 1, :]
    f.deter_grad[...] = f.deter[...]
    f.embed_grad[...] = f.embed[...]
    for low, vector in (
        (OBS, f.obs_gain), (MAN_G, f.manager_gain), (MAN_O, f.manager_out),
        (GOAL_G, f.goal_gain), (ACT_G, f.actor_gain), (CRI_G, f.critic_gain),
        (CRI_O, f.critic_out), (IMG_G, f.img_gain), (GRU_G, f.gru_gain), (POST_G, f.post_gain),
        (PRIOR_G, f.prior_gain), (ENC_G, f.enc_gain),
    ):
        for i in range(vector.shape[0] // LANES):
            vector[pl.ds(i * LANES, LANES)] = f.small[low + i, :]
    f.actor_out[...] = f.small[ACT_T : ACT_T + NA, :]
    f.enc_out[...] = f.small[ENC_T : ENC_T + GCODE, :]
    for i in range(2):
        f.img_action[:, i * LANES : (i + 1) * LANES] = f.small[
            IMG_T + 24 * i : IMG_T + 24 * i + NA, :
        ]

    def halves(value, rows, first, second):
        for low in range(0, value.shape[0], LANES):
            turned = value[low : low + LANES, :].T
            places = slice(rows.start + low, rows.start + low + LANES)
            first[:, places] = turned[0:64]
            second[:, places] = turned[64:LANES]

    whole = {
        HEAD_POST: f.post_in, HEAD_PRIOR: f.prior_in, HEAD_POST_OUT: f.post_out,
        HEAD_PRIOR_OUT: f.prior_out,
    }
    for unit, value in zip(HEAD_UNITS, f.heads):
        rows = slice(unit[4], unit[4] + unit[5])
        if unit[0] == HEAD_MAN_ENC:
            halves(value, rows, f.manager_in, f.enc_in)
        else:
            whole[unit[0]][rows, :] = value[...]
    whole = {LAST_GOAL_OUT: f.goal_out, LAST_IMG: f.img_stoch}
    for unit, value in zip(LAST_UNITS, f.last):
        rows = slice(unit[4], unit[4] + unit[5])
        if unit[0] == LAST_WORKER:
            halves(value, rows, f.actor_in, f.critic_in)
        elif unit[0] == LAST_GOAL_IN:
            f.goal_in[...] = value[:, 0:64]
        elif unit[0] == LAST_GRU:
            f.gru_weight[rows, unit[2] : unit[2] + LANES] = value[...]
        else:
            whole[unit[0]][rows, :] = value[...]


class Weights(NamedTuple):
    obs_gain: Any = None
    manager_in: Any = None
    manager_gain: Any = None
    manager_out: Any = None
    goal_in: Any = None
    goal_gain: Any = None
    goal_out: Any = None
    actor_in: Any = None
    actor_gain: Any = None
    actor_out: Any = None
    critic_in: Any = None
    critic_gain: Any = None
    critic_out: Any = None
    img_stoch: Any = None
    img_action: Any = None
    img_gain: Any = None
    gru_weight: Any = None
    gru_gain: Any = None
    post_in: Any = None
    post_gain: Any = None
    post_out: Any = None
    prior_in: Any = None
    prior_gain: Any = None
    prior_out: Any = None
    enc_in: Any = None
    enc_gain: Any = None
    enc_out: Any = None


class Data(NamedTuple):
    deter_states: Any
    embed: Any
    lengths: Any
    resets: Any
    terminal: Any
    rewards: Any
    prev_stoch: Any
    prev_action: Any
    regroup: Any
    goal_codes: Any
    samples: Any
    actions: Any


def step_in_kernels(data, w):
    prev = data.deter_states.reshape(ROWS, H)
    f = run_kernel(
        frames_kernel, Frames(),
        (
            data.lengths, data.resets, data.terminal, data.rewards,
            data.prev_stoch.transpose(0, 2, 1), data.prev_action, data.regroup, prev,
            data.embed.reshape(ROWS, E), w.obs_gain, w.manager_gain, w.manager_out, w.goal_gain,
            w.actor_gain, w.critic_gain, w.critic_out, w.img_gain, w.gru_gain, w.post_gain,
            w.prior_gain, w.enc_gain, w.actor_out.T, w.enc_out.T, w.img_action, w.goal_in,
            w.img_stoch, w.gru_weight, w.manager_in, w.enc_in, w.goal_out, w.prior_in, w.post_in,
            w.prior_out, w.post_out, w.actor_in, w.critic_in,
        ),
        "frames", 0,
    )
    s = run_kernel(
        worker_kernel, Worker(),
        (
            data.goal_codes.T, data.actions.T, data.samples.transpose(1, 2, 0), f.vectors,
            f.tables, f.start_state, f.goal_out_out, f.actor_in_out, f.critic_in_out, f.post_left,
            f.post_out_left, f.prior_out_left, f.me_left, f.post_right, f.prior_right,
            f.post_out_right, f.prior_out_right, f.me_right,
        ),
        "worker", 1,
    )
    b = run_kernel(
        last_kernel, Last(),
        (
            f.meta_turned, prev, f.vectors, s.returned, f.grad_deter, f.gru_normed, f.gru_inverse,
            f.img_normed, f.img_inverse, f.small, s.small, f.gru_weight_out, s.worker_left,
            s.goal_left, f.dec_left, s.code_turned, f.soft_turned, f.gru_left, f.img_left,
            s.goal_right, f.recon_low, s.goal_pair, f.dec_pair,
        ),
        "last", 2,
    )
    u = run_kernel(
        unpack_kernel, Unpack(),
        tuple(s.sums) + tuple(b.sums) + (b.small_sum, b.deter_grad, f.embed_grad),
        "unpack",
    )
    first = len(Unpack._fields) - len(Weights._fields)
    grads = Weights(*tuple(u)[first:])
    grads = grads._replace(
        manager_in=grads.manager_in.T, actor_in=grads.actor_in.T, critic_in=grads.critic_in.T,
        enc_in=grads.enc_in.T, actor_out=grads.actor_out.T, enc_out=grads.enc_out.T,
    )
    return (
        u.loss[0, 0],
        u.deter_grad.reshape(SEQ_DEV, LEN, H),
        u.embed_grad.reshape(SEQ_DEV, LEN, E),
    ) + tuple(grads)


DP, REP = ("dp", "rep")
IMG_ACTION = 14
LARGE = Weights(**dict.fromkeys(Weights._fields, False))._replace(
    manager_in=True,
    goal_in=True,
    goal_out=True,
    actor_in=True,
    critic_in=True,
    img_stoch=True,
    gru_weight=True,
    post_in=True,
    post_out=True,
    prior_in=True,
    prior_out=True,
    enc_in=True,
)


def hidden_forward(pre_act, scaling):
    normed, inverse = normalize(pre_act)
    scaled = normed * scaling
    return ((normed, inverse, scaled), jax.nn.elu(scaled).astype(jnp.bfloat16))


def hidden_backward(grad_hidden, cache, scaling):
    normed, inverse, scaled = cache
    grad_scaled = grad_hidden * jnp.where(scaled > 0, 1.0, jnp.exp(jnp.minimum(scaled, 0.0)))
    grad_gain = jnp.sum(grad_scaled * normed, tuple(range(scaled.ndim - 1)))
    return (normalize_back(grad_scaled * scaling, normed, inverse).astype(jnp.bfloat16), grad_gain)


def input_backward(grad_pre, input_low, weight):
    grad_weight = jnp.einsum("nk,nu->ku", input_low, grad_pre, preferred_element_type=jnp.float32)
    to_input = jnp.einsum("nu,ku->nk", grad_pre, weight, preferred_element_type=jnp.float32)
    return (grad_weight, to_input)


def head_backward(grad_head, hidden_low, head, cache, scaling):
    grad_weight = jnp.einsum("nu,nk->uk", hidden_low, grad_head, preferred_element_type=jnp.float32)
    grad_hidden = jnp.einsum("nk,uk->nu", grad_head, head, preferred_element_type=jnp.float32)
    grad_pre, grad_gain = hidden_backward(grad_hidden, cache, scaling)
    return (grad_weight, grad_pre, grad_gain)


def group_softmax(flat_logits, groups):
    log_part = jax.nn.log_softmax(flat_logits.reshape(flat_logits.shape[0], groups, -1), axis=-1)
    return (log_part, jnp.exp(log_part))


def chain_returns(values_now, rewards_now, linked, carried):

    def back_step(carry_pair, inputs):
        later_return, later_value = carry_pair
        current, reward_now, link_now, carry_now = inputs
        blended = (1.0 - return_mix) * later_value + return_mix * later_return
        result = jnp.where(link_now, reward_now + discount * carry_now * blended, current)
        return ((result, current), result)

    zero_start = jnp.zeros(values_now.shape[:1], jnp.float32)
    _, stacked = lax.scan(
        back_step,
        (zero_start, zero_start),
        (values_now.T, rewards_now.T, linked.T, carried.T),
        reverse=True,
    )
    return stacked.T


def worker_forward(start_state, goal_low, stoch_hot, first_layer, scaling):
    slot_part = product(start_state, first_layer[:H]) + product(goal_low, first_layer[H + Z :])
    varying = product(stoch_hot, first_layer[H : H + Z]).reshape(start_state.shape[0], HOR, U)
    return hidden_forward(slot_part[:, None, :] + varying, scaling)


def worker_backward(grad_pre, start_state, goal_low, stoch_hot, first_layer):
    slot_count = grad_pre.shape[0]
    grad_stoch = jnp.einsum(
        "nz,nu->zu",
        stoch_hot,
        grad_pre.reshape(slot_count * HOR, U),
        preferred_element_type=jnp.float32,
    )
    summed = jnp.sum(grad_pre, 1, dtype=jnp.float32).astype(jnp.bfloat16)
    grad_state_rows, to_state = input_backward(summed, start_state, first_layer[:H])
    grad_goal_rows, to_goal = input_backward(summed, goal_low, first_layer[H + Z :])
    return (jnp.concatenate([grad_state_rows, grad_stoch, grad_goal_rows], 0), to_state, to_goal)


def step_plain(data, shares):
    (deter_states, embed, lengths, resets, terminal, rewards, prev_stoch, prev_action, regroup, goal_codes, samples, actions) = data
    full = [
        lax.all_gather(share, REP, axis=1 if i == IMG_ACTION else 0, tiled=True)
        for i, share in enumerate(shares)
    ]
    (obs_gain, manager_in, manager_gain, manager_out, goal_in, goal_gain, goal_out, actor_in, actor_gain, actor_out, critic_in, critic_gain, critic_out, img_stoch, img_action, img_gain, gru_weight, gru_gain, post_in, post_gain, post_out, prior_in, prior_gain, prior_out, enc_in, enc_gain, enc_out) = full
    prev_low = deter_states.reshape(ROWS, H)
    prev_float = prev_low.astype(jnp.float32)
    embed_low = embed.reshape(ROWS, E)
    positions = lax.broadcasted_iota(jnp.int32, (SEQ_DEV, LEN), 1)
    is_valid = positions < lengths[:, None]
    next_valid = jnp.concatenate([is_valid[:, 1:], jnp.zeros((SEQ_DEV, 1), jnp.bool_)], 1)
    next_reset = jnp.concatenate([resets[:, 1:], jnp.ones((SEQ_DEV, 1), jnp.int32)], 1)
    linked = next_valid & (next_reset == 0)
    carried = 1.0 - terminal.astype(jnp.float32)
    valid_rows = is_valid.astype(jnp.float32).reshape(ROWS)
    frame_scale = valid_rows / ROWS
    stoch_prev_hot = (
        (prev_stoch[..., None] == lax.broadcasted_iota(jnp.int32, (1, 1, 1, ZK), 3))
        .astype(jnp.bfloat16)
        .reshape(ROWS, Z)
    )
    action_prev_hot = (
        prev_action.reshape(ROWS)[:, None] == lax.broadcasted_iota(jnp.int32, (1, NA), 1)
    ).astype(jnp.bfloat16)
    img_cache, img_hidden = hidden_forward(
        product(stoch_prev_hot, img_stoch) + product(action_prev_hot, img_action), img_gain
    )
    gru_input = jnp.concatenate([img_hidden, prev_low], 1)
    gru_normed, gru_inverse = normalize(product(gru_input, gru_weight))
    gru_parts = gru_normed * gru_gain
    reset_gate = jax.nn.sigmoid(gru_parts[:, :H])
    candidate_in = gru_parts[:, H : 2 * H]
    candidate = jnp.tanh(reset_gate * candidate_in)
    update_gate = jax.nn.sigmoid(gru_parts[:, 2 * H :] - 1.0)
    deter_state = update_gate * candidate + (1.0 - update_gate) * prev_float
    deter_low = deter_state.astype(jnp.bfloat16)
    obs_normed, obs_inverse = normalize(deter_state)
    feature = (obs_normed * obs_gain).astype(jnp.bfloat16)
    man_cache, man_hidden = hidden_forward(product(feature, manager_in), manager_gain)
    manager_value = product(man_hidden, manager_out).reshape(SEQ_DEV, LEN)
    manager_return = chain_returns(manager_value, rewards, linked, carried)
    manager_misfit = (manager_value - manager_return).reshape(ROWS)
    post_input = jnp.concatenate([deter_low, embed_low], 1)
    post_cache, post_hidden = hidden_forward(product(post_input, post_in), post_gain)
    post_log, post_prob = group_softmax(product(post_hidden, post_out), ZG)
    prior_cache, prior_hidden = hidden_forward(product(deter_low, prior_in), prior_gain)
    prior_log, prior_prob = group_softmax(product(prior_hidden, prior_out), ZG)
    log_gap = post_log - prior_log
    group_kl = jnp.sum(post_prob * log_gap, -1, keepdims=True)
    enc_cache, enc_hidden = hidden_forward(product(deter_low, enc_in), enc_gain)
    code_log, code_prob = group_softmax(product(enc_hidden, enc_out), GC)
    code_kl = jnp.sum(code_prob * (code_log + math.log(GK)), (1, 2))
    code_spread = jnp.sum(code_prob * code_log, -1, keepdims=True)
    soft_code = code_prob.reshape(ROWS, GCODE).astype(jnp.bfloat16)
    dec_cache, dec_hidden = hidden_forward(product(soft_code, goal_in), goal_gain)
    recon_err = product(dec_hidden, goal_out) - deter_state
    frame_terms = (
        jnp.sum(post_prob * log_gap, (1, 2)) + code_kl + 0.5 * jnp.mean(recon_err * recon_err, -1)
    )
    frame_loss = jnp.sum(valid_rows * (0.5 * manager_misfit * manager_misfit + frame_terms)) / ROWS
    send_order = regroup[0]
    start_state, slot_flag = (
        lax.all_to_all(deter_low[send_order], DP, split_axis=0, concat_axis=0, tiled=True),
        lax.all_to_all(
            valid_rows[send_order].astype(jnp.bfloat16),
            DP,
            split_axis=0,
            concat_axis=0,
            tiled=True,
        ),
    )
    slot_weight = slot_flag.astype(jnp.float32)
    code_hot = (
        (goal_codes[:, :, None] == lax.broadcasted_iota(jnp.int32, (1, 1, GK), 2))
        .astype(jnp.bfloat16)
        .reshape(ROWS, GCODE)
    )
    goal_cache, goal_hidden = hidden_forward(product(code_hot, goal_in), goal_gain)
    goal_vector = product(goal_hidden, goal_out)
    goal_low = goal_vector.astype(jnp.bfloat16)
    state_float = start_state.astype(jnp.float32)
    alignment = jnp.sum(goal_vector * state_float, -1)
    largest_square = (
        jnp.maximum(jnp.sum(goal_vector * goal_vector, -1), jnp.sum(state_float * state_float, -1))
        + small_floor
    )
    reward_slot = alignment / largest_square
    stoch_hot = (
        (samples[..., None] == lax.broadcasted_iota(jnp.int32, (1, 1, 1, ZK), 3))
        .astype(jnp.bfloat16)
        .reshape(ROWS * HOR, Z)
    )
    action_hot = (actions[..., None] == lax.broadcasted_iota(jnp.int32, (1, 1, NA), 2)).astype(
        jnp.float32
    )
    actor_cache, actor_hidden = worker_forward(
        start_state, goal_low, stoch_hot, actor_in, actor_gain
    )
    logits = jnp.einsum("rku,ua->rka", actor_hidden, actor_out, preferred_element_type=jnp.float32)
    log_chance = jax.nn.log_softmax(logits, axis=-1)
    chosen = jnp.sum(log_chance * action_hot, -1)
    critic_cache, critic_hidden = worker_forward(
        start_state, goal_low, stoch_hot, critic_in, critic_gain
    )
    worker_value = jnp.einsum(
        "rku,u->rk", critic_hidden, critic_out, preferred_element_type=jnp.float32
    )
    step_link = lax.broadcasted_iota(jnp.int32, (ROWS, HOR), 1) < HOR - 1
    worker_return = chain_returns(
        worker_value,
        jnp.broadcast_to(reward_slot[:, None], (ROWS, HOR)),
        step_link,
        jnp.ones((ROWS, HOR), jnp.float32),
    )
    advantage = worker_return - worker_value
    local_top = jnp.max(slot_weight[:, None] * jnp.abs(advantage))
    return_scale = lax.pmax(local_top, (DP, REP)) + small_floor
    step_total = ROWS * HOR
    value_misfit = worker_value - worker_return
    critic_part = 0.5 * jnp.sum(slot_weight[:, None] * value_misfit * value_misfit)
    actor_part = jnp.sum(slot_weight[:, None] * chosen * advantage) / return_scale
    local_loss = frame_loss + (critic_part - actor_part) / step_total
    grad_value = slot_weight[:, None] * value_misfit / step_total
    grad_chosen = -slot_weight[:, None] * advantage / return_scale / step_total
    grad_logits = (grad_chosen[..., None] * (action_hot - jnp.exp(log_chance))).astype(jnp.bfloat16)
    grad_actor_out = jnp.einsum(
        "rku,rka->ua", actor_hidden, grad_logits, preferred_element_type=jnp.float32
    )
    grad_actor_hidden = jnp.einsum(
        "rka,ua->rku", grad_logits, actor_out, preferred_element_type=jnp.float32
    )
    actor_pre, grad_actor_gain = hidden_backward(grad_actor_hidden, actor_cache, actor_gain)
    grad_critic_out = jnp.einsum("rku,rk->u", critic_hidden, grad_value, precision=highest)
    critic_pre, grad_critic_gain = hidden_backward(
        grad_value[..., None] * critic_out, critic_cache, critic_gain
    )
    grad_actor_in, actor_to_state, actor_to_goal = worker_backward(
        actor_pre, start_state, goal_low, stoch_hot, actor_in
    )
    grad_critic_in, critic_to_state, critic_to_goal = worker_backward(
        critic_pre, start_state, goal_low, stoch_hot, critic_in
    )
    grad_goal_low = (actor_to_goal + critic_to_goal).astype(jnp.bfloat16)
    worker_goal_out, goal_pre, worker_goal_gain = head_backward(
        grad_goal_low, goal_hidden, goal_out, goal_cache, goal_gain
    )
    worker_goal_in = jnp.einsum("ng,nu->gu", code_hot, goal_pre, preferred_element_type=jnp.float32)
    returned = lax.all_to_all(
        (actor_to_state + critic_to_state).astype(jnp.bfloat16),
        DP,
        split_axis=0,
        concat_axis=0,
        tiled=True,
    )
    grad_manager_value = frame_scale * manager_misfit
    grad_manager_out = jnp.dot(grad_manager_value, man_hidden, precision=highest)
    manager_pre, grad_manager_gain = hidden_backward(
        grad_manager_value[:, None] * manager_out, man_cache, manager_gain
    )
    grad_manager_in, grad_feature = input_backward(manager_pre, feature, manager_in)
    grad_obs_gain = jnp.sum(grad_feature * obs_normed, 0)
    obs_back = normalize_back(grad_feature * obs_gain, obs_normed, obs_inverse)
    weight_cube = frame_scale[:, None, None]
    post_grad_logits = (
        (weight_cube * post_prob * (log_gap - group_kl)).reshape(ROWS, Z).astype(jnp.bfloat16)
    )
    prior_grad_logits = (
        (weight_cube * (prior_prob - post_prob)).reshape(ROWS, Z).astype(jnp.bfloat16)
    )
    grad_post_out, post_pre, grad_post_gain = head_backward(
        post_grad_logits, post_hidden, post_out, post_cache, post_gain
    )
    grad_post_in, post_back = input_backward(post_pre, post_input, post_in)
    grad_prior_out, prior_pre, grad_prior_gain = head_backward(
        prior_grad_logits, prior_hidden, prior_out, prior_cache, prior_gain
    )
    grad_prior_in, prior_back = input_backward(prior_pre, deter_low, prior_in)
    recon_grad = frame_scale[:, None] * recon_err / H
    dec_goal_out, dec_pre, dec_goal_gain = head_backward(
        recon_grad.astype(jnp.bfloat16), dec_hidden, goal_out, dec_cache, goal_gain
    )
    dec_goal_in, grad_code = input_backward(dec_pre, soft_code, goal_in)
    grad_code = grad_code.reshape(ROWS, GC, GK)
    code_grad_logits = code_prob * (
        grad_code - jnp.sum(code_prob * grad_code, -1, keepdims=True)
    ) + weight_cube * code_prob * (code_log - code_spread)
    grad_enc_out, enc_pre, grad_enc_gain = head_backward(
        code_grad_logits.reshape(ROWS, GCODE).astype(jnp.bfloat16),
        enc_hidden,
        enc_out,
        enc_cache,
        enc_gain,
    )
    grad_enc_in, enc_back = input_backward(enc_pre, deter_low, enc_in)
    grad_goal_out = worker_goal_out + dec_goal_out
    grad_goal_in = worker_goal_in + dec_goal_in
    grad_goal_gain = worker_goal_gain + dec_goal_gain
    scattered = jnp.zeros((ROWS, H), jnp.float32).at[send_order].add(returned.astype(jnp.float32))
    grad_deter = obs_back + post_back[:, :H] + prior_back + enc_back + scattered - recon_grad
    grad_inner = grad_deter * update_gate * (1.0 - candidate * candidate)
    grad_parts = jnp.concatenate(
        [
            grad_inner * candidate_in * reset_gate * (1.0 - reset_gate),
            grad_inner * reset_gate,
            grad_deter * (candidate - prev_float) * update_gate * (1.0 - update_gate),
        ],
        1,
    )
    grad_gru_gain = jnp.sum(grad_parts * gru_normed, 0)
    gru_pre = normalize_back(grad_parts * gru_gain, gru_normed, gru_inverse).astype(jnp.bfloat16)
    grad_gru_weight, gru_back = input_backward(gru_pre, gru_input, gru_weight)
    img_pre, grad_img_gain = hidden_backward(gru_back[:, :H], img_cache, img_gain)
    grad_img_stoch = jnp.einsum(
        "nz,nh->zh", stoch_prev_hot, img_pre, preferred_element_type=jnp.float32
    )
    grad_img_action = jnp.einsum(
        "na,nh->ah", action_prev_hot, img_pre, preferred_element_type=jnp.float32
    )
    grad_prev = grad_deter * (1.0 - update_gate) + gru_back[:, H:]
    embed_grad = post_back[:, H:]
    count = lax.axis_size(REP)
    loss_share = lax.psum_scatter(
        jnp.full((count,), local_loss), REP, scatter_dimension=0, tiled=True
    )
    grads = Weights(
        obs_gain=grad_obs_gain,
        manager_in=grad_manager_in,
        manager_gain=grad_manager_gain,
        manager_out=grad_manager_out,
        goal_in=grad_goal_in,
        goal_gain=grad_goal_gain,
        goal_out=grad_goal_out,
        actor_in=grad_actor_in,
        actor_gain=grad_actor_gain,
        actor_out=grad_actor_out,
        critic_in=grad_critic_in,
        critic_gain=grad_critic_gain,
        critic_out=grad_critic_out,
        img_stoch=grad_img_stoch,
        img_action=grad_img_action,
        img_gain=grad_img_gain,
        gru_weight=grad_gru_weight,
        gru_gain=grad_gru_gain,
        post_in=grad_post_in,
        post_gain=grad_post_gain,
        post_out=grad_post_out,
        prior_in=grad_prior_in,
        prior_gain=grad_prior_gain,
        prior_out=grad_prior_out,
        enc_in=grad_enc_in,
        enc_gain=grad_enc_gain,
        enc_out=grad_enc_out,
    )
    shares = []
    for i, (grad, by_column) in enumerate(zip(grads, LARGE)):
        grad = lax.psum_scatter(
            grad, REP, scatter_dimension=1 if i == IMG_ACTION else 0, tiled=True
        )
        if by_column:
            shares.append(lax.psum_scatter(grad, DP, scatter_dimension=1, tiled=True))
        else:
            shares.append(lax.psum(grad, DP))
    return (
        lax.psum(loss_share, DP)[0],
        grad_prev.reshape(SEQ_DEV, LEN, H),
        embed_grad.reshape(SEQ_DEV, LEN, E),
    ) + tuple(shares)


def solution(mesh):
    split, over_rep = (P((DP, REP)), P(REP))
    in_kernels = mesh.shape[DP] == 8 and mesh.shape[REP] == 4

    def per_device(*arguments):
        data, shares = (Data(*arguments[:12]), Weights(*arguments[12:]))
        return (step_in_kernels if in_kernels else step_plain)(data, shares)

    in_specs, out_specs = ((split,) * 12, (P(), split, split))
    for i, by_column in enumerate(LARGE):
        spec = P(None, REP) if i == IMG_ACTION else over_rep
        in_specs += (spec,)
        out_specs += (P(REP, DP) if by_column else spec,)
    return jax.shard_map(
        per_device, mesh=mesh, in_specs=in_specs, out_specs=out_specs, check_vma=False
    )
```

```python
import math
from typing import Any, NamedTuple

import jax
import jax.numpy as jnp
from jax import lax
from jax.experimental import pallas as pl
from jax.experimental.pallas import tpu as pltpu
from jax.sharding import PartitionSpec as P

H = 1024
ZG = 32
ZK = 32
U = 512
GC = 8
GK = 8
NA = 17
E = 1536
LEN = 64
HOR = 16
SEQ_DEV = 2
Z = 1024
GCODE = 64
ROWS = 128


discount = 0.99
return_mix = 0.95
epsilon = 1e-05
small_floor = 1e-06
highest = lax.Precision.HIGHEST


MESH = pl.DeviceIdType.MESH
BF = jnp.bfloat16
F32 = jnp.float32
LANES = 128
VMEM_BYTES = 62 * 2**20


class Arg(NamedTuple):
    kind: Any
    shape: Any
    dtype: Any
    here: bool = True


TAKEN, GIVEN, KEPT, SIGNAL = range(4)


def taken(*shape, dtype=BF, here=True):
    return Arg(TAKEN, shape, dtype, here)


def given(*shape, dtype=BF, here=True):
    return Arg(GIVEN, shape, dtype, here)


def kept(*shape, dtype=BF):
    return Arg(KEPT, shape, dtype)


def signal(*shape):
    return Arg(SIGNAL, shape, None)


def run_kernel(body, layout, inputs, name, collective=None):
    leaves, tree = jax.tree.flatten(layout, is_leaf=lambda a: isinstance(a, Arg))

    def kernel(*refs):
        body(jax.tree.unflatten(tree, refs))

    def place(arg):
        return pl.BlockSpec(memory_space=pltpu.VMEM if arg.here else pl.ANY)

    outs = [a for a in leaves if a.kind == GIVEN]
    more = {} if collective is None else dict(collective_id=collective, has_side_effects=True)
    results = pl.pallas_call(
        kernel,
        out_shape=[jax.ShapeDtypeStruct(a.shape, a.dtype) for a in outs],
        in_specs=[place(a) for a in leaves if a.kind == TAKEN],
        out_specs=[place(a) for a in outs],
        scratch_shapes=[
            pltpu.VMEM(a.shape, a.dtype) if a.kind == KEPT else pltpu.SemaphoreType.DMA(a.shape)
            for a in leaves
            if a.kind >= KEPT
        ],
        compiler_params=pltpu.CompilerParams(vmem_limit_bytes=VMEM_BYTES, **more),
        name=name,
    )(*inputs)
    results = iter(results)
    return jax.tree.unflatten(
        tree, [next(results) if a.kind == GIVEN else None for a in leaves]
    )


def product(left, right):
    return jnp.dot(left, right, preferred_element_type=jnp.float32)


def normalize(values_in):
    row_mean = jnp.mean(values_in, -1, keepdims=True)
    centred = values_in - row_mean
    inverse = lax.rsqrt(jnp.mean(centred * centred, -1, keepdims=True) + epsilon)
    return (centred * inverse, inverse)


def normalize_back(grad_normed, normed, inverse):
    return inverse * (
        grad_normed
        - jnp.mean(grad_normed, -1, keepdims=True)
        - normed * jnp.mean(grad_normed * normed, -1, keepdims=True)
    )


def matmul_into(out_ref, left, weight_ref, turned=False, tile=256, low=0, extra=None):
    total = out_ref.shape[-1]

    def one(j, carry):
        start = pl.multiple_of(j * tile, tile)
        if turned:
            value = lax.dot_general(
                left,
                weight_ref[pl.ds(pl.multiple_of(low + j * tile, tile), tile), :],
                (((1,), (1,)), ((), ())),
                preferred_element_type=F32,
            )
        else:
            value = product(left, weight_ref[:, pl.ds(start, tile)])
        if extra is not None:
            value = value + extra(start, tile)
        out_ref[:, pl.ds(start, tile)] = value
        return carry

    lax.fori_loop(0, total // tile, one, 0)


def by_rows(count, size, body, carry=0):
    def one(i, carry):
        return body(pl.ds(pl.multiple_of(i * size, size), size), carry)

    return lax.fori_loop(0, count // size, one, carry)


def elu_of(value):
    return jnp.where(value > 0, value, jnp.exp(jnp.minimum(value, 0.0)) - 1.0)


def normalize_rows(ref, inverse_ref, size):
    def one(rows, carry):
        normed, inverse = normalize(ref[rows, :])
        ref[rows, :] = normed
        inverse_ref[rows, :] = inverse
        return carry

    by_rows(ref.shape[0], size, one)


def hidden_rows(ref, inverse_ref, gain, hidden_ref, size=128):
    def one(rows, carry):
        normed, inverse = normalize(ref[rows, :])
        ref[rows, :] = normed
        inverse_ref[rows, :] = inverse
        hidden_ref[rows, :] = elu_of(normed * gain).astype(BF)
        return carry

    by_rows(ref.shape[0], size, one)


def hidden_rows_back(grad_of, ref, inverse_ref, gain, pre_ref, size=128, hidden_ref=None):
    def one(rows, total):
        normed = ref[rows, :]
        scaled = normed * gain
        power = jnp.exp(jnp.minimum(scaled, 0.0))
        if hidden_ref is not None:
            hidden_ref[rows, :] = jnp.where(scaled > 0, scaled, power - 1.0).astype(BF)
        grad_scaled = grad_of(rows) * jnp.where(scaled > 0, 1.0, power)
        total = total + jnp.sum(grad_scaled * normed, 0, keepdims=True)
        back = normalize_back(grad_scaled * gain, normed, inverse_ref[rows, :])
        pre_ref[rows, :] = back.astype(pre_ref.dtype)
        return total

    return by_rows(ref.shape[0], size, one, jnp.zeros((1, ref.shape[1]), F32))


def turn_into(out_ref, value_ref, low=0):
    for j in range(value_ref.shape[1] // LANES):
        tile = value_ref[:, j * LANES : (j + 1) * LANES].astype(F32).T
        out_ref[low + j * LANES : low + (j + 1) * LANES, :] = tile.astype(out_ref.dtype)


def class_spread(groups, classes, rows, width):
    group = lax.broadcasted_iota(jnp.int32, (rows, width), 0)
    lane = lax.broadcasted_iota(jnp.int32, (rows, width), 1)
    inside = (lane >= group * classes) & (lane < group * classes + classes) & (group < groups)
    return jnp.where(inside, 1.0, 0.0).astype(BF)


def hot_rows(ids, classes, groups, width):
    here = product(ids.astype(BF), class_spread(groups, classes, ids.shape[1], width))
    lane = lax.broadcasted_iota(jnp.int32, (1, width), 1)
    same = here == jnp.bitwise_and(lane, classes - 1).astype(F32)
    return jnp.where(same & (lane < groups * classes), 1.0, 0.0)


def columns_of(rows):
    count = rows.shape[0]
    return jnp.concatenate([rows, jnp.zeros((LANES - count, rows.shape[1]), F32)], 0).T


def vector_of(packed, low, tiles):
    return jnp.concatenate(
        [packed[r, low + i : low + i + 1, :] for r in range(4) for i in range(tiles)], 1
    )


def put_vector(small_ref, low, value):
    tiles = value.shape[1] // (4 * LANES)
    for r in range(4):
        for i in range(tiles):
            start = (r * tiles + i) * LANES
            small_ref[r % 2, r // 2, low + i : low + i + 1, :] = value[:, start : start + LANES]


def put_table(small_ref, low, value, rows):
    for r in range(4):
        small_ref[r % 2, r // 2, low : low + rows, :] = value[
            0:rows, r * LANES : (r + 1) * LANES
        ]


OBS, MAN_G, MAN_O, GOAL_G, ACT_G, CRI_G, CRI_O, IMG_G, GRU_G, POST_G, PRIOR_G, ENC_G, LOSS = (
    0, 2, 3, 4, 5, 6, 7, 8, 10, 16, 18, 20, 21,
)
ACT_T, ENC_T, IMG_T, SMALL_TILES = (24, 48, 112, 160)
TAB_ACT, TAB_ENC, TAB_IMG, TAB_GOAL, TABLES = (0, 32, 96, 160, 224)
VECTOR_TILES = 24


def spread_lanes(low_ref, out_ref, first_row, which):
    lane = lax.broadcasted_iota(jnp.int32, (ROWS, LANES), 1)
    keep = (lane < 64) if which == 0 else (lane >= 64)
    for j in range(4):
        tile = low_ref[:, j * LANES : (j + 1) * LANES].astype(F32)
        turned = pltpu.roll(tile, 64, 1)
        for x in range(2):
            source = tile if x == which else turned
            lanes = slice((2 * j + x) * LANES, (2 * j + x + 1) * LANES)
            out_ref[first_row : first_row + ROWS, lanes] = jnp.where(keep, source, 0.0).astype(BF)


def column(meta, k):
    return meta[:, k : k + 1]


class Frames(NamedTuple):
    lengths: Any = taken(SEQ_DEV, dtype=jnp.int32)
    resets: Any = taken(SEQ_DEV, LEN, dtype=jnp.int32)
    terminal: Any = taken(SEQ_DEV, LEN, dtype=jnp.int32)
    rewards: Any = taken(SEQ_DEV, LEN, dtype=F32)
    prev_stoch: Any = taken(SEQ_DEV, ZG, LEN, dtype=jnp.int32)
    prev_action: Any = taken(SEQ_DEV, LEN, dtype=jnp.int32)
    regroup: Any = taken(1, ROWS, dtype=jnp.int32)
    prev: Any = taken(ROWS, H)
    embed: Any = taken(ROWS, E)
    obs_gain: Any = taken(H // 4)
    manager_gain: Any = taken(U // 4)
    manager_head: Any = taken(U // 4)
    goal_gain: Any = taken(U // 4)
    actor_gain: Any = taken(U // 4)
    critic_gain: Any = taken(U // 4)
    critic_head: Any = taken(U // 4)
    img_gain: Any = taken(H // 4)
    gru_gain: Any = taken(3 * H // 4)
    post_gain: Any = taken(H // 4)
    prior_gain: Any = taken(H // 4)
    enc_gain: Any = taken(U // 4)
    actor_head: Any = taken(NA, U // 4)
    enc_head: Any = taken(GCODE, U // 4)
    img_action_share: Any = taken(NA, H // 4)
    goal_in_share: Any = taken(GCODE // 4, U)
    img_stoch_share: Any = taken(Z // 4, H, here=False)
    gru_weight_share: Any = taken(H // 2, 3 * H, here=False)
    manager_in_share: Any = taken(H // 4, U, here=False)
    enc_in_share: Any = taken(H // 4, U, here=False)
    goal_out_share: Any = taken(U // 4, H, here=False)
    prior_in_share: Any = taken(H // 4, H, here=False)
    post_in_share: Any = taken((H + E) // 4, H, here=False)
    prior_out_share: Any = taken(H // 4, Z, here=False)
    post_out_share: Any = taken(H // 4, Z, here=False)
    actor_in_share: Any = taken(768, U, here=False)
    critic_in_share: Any = taken(768, U, here=False)
    gru_weight_out: Any = given(2 * H, 3 * H, here=False)
    goal_out_out: Any = given(U, H, here=False)
    actor_in_out: Any = given(3 * H, U, here=False)
    critic_in_out: Any = given(3 * H, U, here=False)
    vectors: Any = given(4, VECTOR_TILES, LANES, dtype=F32)
    tables: Any = given(4, TABLES, LANES)
    meta_turned: Any = given(LANES, ROWS, dtype=F32)
    start_state: Any = given(ROWS, H + LANES)
    gru_left: Any = given(2 * H, ROWS)
    post_left: Any = given(H + E, ROWS)
    post_out_left: Any = given(H, ROWS)
    prior_out_left: Any = given(H, ROWS)
    img_left: Any = given(Z, ROWS)
    me_left: Any = given(H, 2 * ROWS)
    dec_left: Any = given(U, ROWS)
    soft_turned: Any = given(GCODE, ROWS)
    post_right: Any = given(ROWS, H)
    prior_right: Any = given(ROWS, H)
    post_out_right: Any = given(ROWS, Z)
    prior_out_right: Any = given(ROWS, Z)
    me_right: Any = given(2 * ROWS, 2 * U)
    recon_low: Any = given(ROWS, H)
    dec_pair: Any = given(ROWS, 2 * U)
    gru_normed: Any = given(ROWS, 3 * H, dtype=F32)
    gru_inverse: Any = given(ROWS, 1, dtype=F32)
    img_normed: Any = given(ROWS, H, dtype=F32)
    img_inverse: Any = given(ROWS, 1, dtype=F32)
    grad_deter: Any = given(ROWS, H, dtype=F32)
    embed_grad: Any = given(ROWS, E, dtype=F32)
    small: Any = given(2, 2, SMALL_TILES, LANES, dtype=F32)
    img_stoch: Any = kept(Z, H)
    gru_weight: Any = kept(2 * H, 3 * H)
    manager_in: Any = kept(H, U)
    enc_in: Any = kept(H, U)
    goal_out: Any = kept(U, H)
    prior_in: Any = kept(H, H)
    post_in: Any = kept(H + E, H)
    prior_out: Any = kept(H, Z)
    post_out: Any = kept(H, Z)
    actor_in: Any = kept(3 * H, U)
    critic_in: Any = kept(3 * H, U)
    img_action: Any = kept(32, H)
    enc_out: Any = kept(GCODE, U)
    goal_in: Any = kept(GCODE, U)
    vector_share: Any = kept(VECTOR_TILES, LANES, dtype=F32)
    table_share: Any = kept(TABLES, LANES)
    meta: Any = kept(ROWS, LANES, dtype=F32)
    hot: Any = kept(ROWS, Z)
    img_hidden: Any = kept(ROWS, H)
    deter: Any = kept(ROWS, H, dtype=F32)
    deter_low: Any = kept(ROWS, H)
    feature: Any = kept(ROWS, H)
    obs_normed: Any = kept(ROWS, H, dtype=F32)
    obs_inverse: Any = kept(ROWS, 1, dtype=F32)
    outgoing: Any = kept(ROWS, H + LANES)
    incoming: Any = kept(ROWS, H + LANES)
    pre_512: Any = kept(ROWS, U, dtype=F32)
    hid_512: Any = kept(ROWS, U)
    back_512: Any = kept(ROWS, U)
    wide_512: Any = kept(ROWS, U, dtype=F32)
    inverse: Any = kept(ROWS, 1, dtype=F32)
    grad_value: Any = kept(ROWS, 1, dtype=F32)
    dec_normed: Any = kept(ROWS, U, dtype=F32)
    dec_inverse: Any = kept(ROWS, 1, dtype=F32)
    dec_hidden: Any = kept(ROWS, U)
    dec_pre: Any = kept(ROWS, U)
    wide: Any = kept(ROWS, H, dtype=F32)
    prior_normed: Any = kept(ROWS, H, dtype=F32)
    prior_inverse: Any = kept(ROWS, 1, dtype=F32)
    prior_hidden: Any = kept(ROWS, H)
    post_normed: Any = kept(ROWS, H, dtype=F32)
    post_inverse: Any = kept(ROWS, 1, dtype=F32)
    post_hidden: Any = kept(ROWS, H)
    post_turned: Any = kept(Z, ROWS, dtype=F32)
    prior_turned: Any = kept(Z, ROWS, dtype=F32)
    loss: Any = kept(1, 1, dtype=F32)
    piece_send: Any = signal(17, 8)
    piece_recv: Any = signal(17, 8)
    load_done: Any = signal(17)
    save_done: Any = signal(4)
    small_send: Any = signal(2, 3)
    small_recv: Any = signal(2, 3)
    state_send: Any = signal(8)
    state_recv: Any = signal(8)

    def pack(self):
        vectors = (
            self.obs_gain, self.manager_gain, self.manager_head, self.goal_gain, self.actor_gain,
            self.critic_gain, self.critic_head, self.img_gain, self.gru_gain, self.post_gain,
            self.prior_gain, self.enc_gain,
        )
        low = 0
        for vector in vectors:
            for i in range(vector.shape[0] // LANES):
                self.vector_share[low, :] = vector[pl.ds(i * LANES, LANES)].astype(F32)
                low += 1
        self.vector_share[low:, :] = jnp.zeros((VECTOR_TILES - low, LANES), F32)
        self.table_share[...] = jnp.zeros(self.table_share.shape, BF)
        self.table_share[TAB_ACT : TAB_ACT + NA, :] = self.actor_head[...]
        self.table_share[TAB_ENC : TAB_ENC + GCODE, :] = self.enc_head[...]
        for i in range(2):
            low = TAB_IMG + 32 * i
            lanes = slice(i * LANES, (i + 1) * LANES)
            self.table_share[low : low + NA, :] = self.img_action_share[:, lanes]
        for i in range(4):
            low = TAB_GOAL + 16 * i
            lanes = slice(i * LANES, (i + 1) * LANES)
            self.table_share[low : low + 16, :] = self.goal_in_share[:, lanes]

    def start(self):
        def row(ref):
            value = ref[...].astype(F32)
            return jnp.concatenate([value[0:1], value[1:2]], 1)

        position = lax.broadcasted_iota(jnp.int32, (SEQ_DEV, LEN), 1)
        length = self.lengths[...].reshape(SEQ_DEV, 1)
        later = jnp.where((position + 1 < length) & (position + 1 < LEN), 1.0, 0.0)
        kinds = (
            row(self.prev_action),
            row(jnp.where(position < length, 1.0, 0.0)),
            row(later) * (1.0 - jnp.minimum(pltpu.roll(row(self.resets), ROWS - 1, 1), 1.0)),
            1.0 - row(self.terminal),
            row(self.rewards),
            self.regroup[...].astype(F32),
        )
        self.meta_turned[...] = jnp.zeros(self.meta_turned.shape, F32)
        for i, kind in enumerate(kinds):
            self.meta_turned[32 + i : 33 + i, :] = kind
        self.meta[...] = self.meta_turned[...].T
        ids = jnp.concatenate([self.prev_stoch[0], self.prev_stoch[1]], 1).astype(F32)
        self.hot[...] = hot_rows(columns_of(ids)[:, 0:ZG], ZK, ZG, Z).astype(BF)

    def turns(self):
        turn_into(self.img_left, self.hot)
        turn_into(self.gru_left, self.prev, H)
        turn_into(self.post_left, self.embed, H)
        self.small[...] = jnp.zeros(self.small.shape, F32)

    def unpack(self):
        for r in range(4):
            for i in range(2):
                self.img_action[:, (2 * r + i) * LANES : (2 * r + i + 1) * LANES] = self.tables[
                    r, TAB_IMG + 32 * i : TAB_IMG + 32 * (i + 1), :
                ]
            self.enc_out[:, r * LANES : (r + 1) * LANES] = self.tables[
                r, TAB_ENC : TAB_ENC + 64, :
            ]
            for i in range(4):
                self.goal_in[16 * r : 16 * (r + 1), i * LANES : (i + 1) * LANES] = self.tables[
                    r, TAB_GOAL + 16 * i : TAB_GOAL + 16 * (i + 1), :
                ]

    def gain(self, low, size):
        return vector_of(self.vectors, low, size // (4 * LANES))

    def img(self):
        meta = self.meta[...]
        lane = lax.broadcasted_iota(jnp.int32, (ROWS, 32), 1).astype(F32)
        action = jnp.where(column(meta, 32) == lane, 1.0, 0.0).astype(BF)
        matmul_into(
            self.img_normed, self.hot[...], self.img_stoch,
            extra=lambda start, tile: product(action, self.img_action[:, pl.ds(start, tile)]),
        )
        hidden_rows(self.img_normed, self.img_inverse, self.gain(IMG_G, H), self.img_hidden)
        turn_into(self.gru_left, self.img_hidden)

    def gru(self, third):
        low = third * H
        out = self.gru_normed.at[:, low : low + H]

        def one(j, carry):
            start = pl.multiple_of(low + j * 256, 256)
            value = product(self.img_hidden[...], self.gru_weight[0:H, pl.ds(start, 256)])
            value = value + product(
                self.prev[...], self.gru_weight[H : 2 * H, pl.ds(start, 256)]
            )
            self.gru_normed[:, pl.ds(start, 256)] = value
            return carry

        lax.fori_loop(0, 4, one, 0)

    def state(self):
        gain = self.gain(GRU_G, 3 * H)
        obs_gain = self.gain(OBS, H)

        def one(rows, carry):
            normed, inverse = normalize(self.gru_normed[rows, :])
            self.gru_normed[rows, :] = normed
            self.gru_inverse[rows, :] = inverse
            parts = normed * gain
            reset = 1.0 / (1.0 + jnp.exp(-parts[:, :H]))
            candidate = jnp.tanh(reset * parts[:, H : 2 * H])
            update = 1.0 / (1.0 + jnp.exp(1.0 - parts[:, 2 * H :]))
            state = update * candidate + (1.0 - update) * self.prev[rows, :].astype(F32)
            self.deter[rows, :] = state
            self.deter_low[rows, :] = state.astype(BF)
            obs, obs_inverse = normalize(state)
            self.obs_normed[rows, :] = obs
            self.obs_inverse[rows, :] = obs_inverse
            self.feature[rows, :] = (obs * obs_gain).astype(BF)
            return carry

        by_rows(ROWS, 16, one)
        turn_into(self.post_left, self.deter_low)

    def picked(self):
        meta = self.meta[...]
        lane = lax.broadcasted_iota(jnp.int32, (ROWS, ROWS), 1).astype(F32)
        pick = jnp.where(column(meta, 37) == lane, 1.0, 0.0).astype(BF)

        def one(j, carry):
            lanes = pl.ds(pl.multiple_of(j * 256, 256), 256)
            self.outgoing[:, lanes] = product(pick, self.deter_low[:, lanes]).astype(BF)
            return carry

        lax.fori_loop(0, H // 256, one, 0)
        valid = jnp.broadcast_to(column(meta, 33), (ROWS, LANES)).astype(BF)
        self.outgoing[:, H:] = product(pick, valid).astype(BF)

    def manager(self):
        meta = self.meta[...]
        gain, head = (self.gain(MAN_G, U), self.gain(MAN_O, U))
        for j in range(H // LANES):
            lanes = slice(j * LANES, (j + 1) * LANES)
            self.me_left[lanes, 0:ROWS] = self.feature[:, lanes].astype(F32).T.astype(BF)
            self.me_left[lanes, ROWS:] = self.deter_low[:, lanes].astype(F32).T.astype(BF)
        matmul_into(self.pre_512, self.feature[...], self.manager_in)
        hidden_rows(self.pre_512, self.inverse, gain, self.hid_512)
        value = jnp.sum(self.hid_512[...].astype(F32) * head, -1, keepdims=True)
        valid, linked, carried, rewards = (column(meta, 33 + i) for i in range(4))
        later = pltpu.roll(jnp.broadcast_to(value, (ROWS, LANES)), ROWS - 1, 0)
        base = jnp.where(
            linked > 0, rewards + discount * carried * ((1.0 - return_mix) * later), value
        )
        slope = jnp.broadcast_to(linked * (discount * return_mix) * carried, (ROWS, LANES))
        step = 1
        while step < LEN:
            base = base + slope * pltpu.roll(base, ROWS - step, 0)
            slope = slope * pltpu.roll(slope, ROWS - step, 0)
            step *= 2
        misfit = value - base[:, 0:1]
        scale = valid * (1.0 / ROWS)
        self.loss[...] = 0.5 * jnp.sum(scale * misfit * misfit, 0, keepdims=True)
        grad_value = scale * misfit
        put_vector(
            self.small, MAN_O,
            jnp.sum(self.hid_512[...].astype(F32) * grad_value, 0, keepdims=True),
        )
        self.grad_value[...] = grad_value
        total = hidden_rows_back(
            lambda rows: self.grad_value[rows, :] * head,
            self.pre_512, self.inverse, gain, self.back_512,
        )
        put_vector(self.small, MAN_G, total)
        spread_lanes(self.back_512, self.me_right, 0, 0)
        self.feature_back()

    def feature_back(self):
        obs_gain = self.gain(OBS, H)
        matmul_into(self.wide, self.back_512[...], self.manager_in, turned=True)

        def one(rows, total):
            grad = self.wide[rows, :]
            normed = self.obs_normed[rows, :]
            total = total + jnp.sum(grad * normed, 0, keepdims=True)
            self.grad_deter[rows, :] = normalize_back(
                grad * obs_gain, normed, self.obs_inverse[rows, :]
            )
            return total

        put_vector(self.small, OBS, by_rows(ROWS, 32, one, jnp.zeros((1, H), F32)))

    def add_back(self, left_ref, weight_ref):
        def one(j, carry):
            lanes = pl.ds(pl.multiple_of(j * 256, 256), 256)
            self.grad_deter[:, lanes] += lax.dot_general(
                left_ref[...], weight_ref[lanes, :], (((1,), (1,)), ((), ())),
                preferred_element_type=F32,
            )
            return carry

        lax.fori_loop(0, H // 256, one, 0)

    def encoder(self):
        gain, goal_gain = (self.gain(ENC_G, U), self.gain(GOAL_G, U))
        valid_row = self.meta_turned[33:34, :]
        scale_row = valid_row * (1.0 / ROWS)
        scale = column(self.meta[...], 33) * (1.0 / ROWS)
        matmul_into(self.pre_512, self.deter_low[...], self.enc_in)
        hidden_rows(self.pre_512, self.inverse, gain, self.hid_512)
        logits = lax.dot_general(
            self.enc_out[...], self.hid_512[...], (((1,), (1,)), ((), ())),
            preferred_element_type=F32,
        ).reshape(GC, GK, ROWS)
        shifted = logits - jnp.max(logits, 1, keepdims=True)
        code_log = shifted - jnp.log(jnp.sum(jnp.exp(shifted), 1, keepdims=True))
        code = jnp.exp(code_log)
        spread = jnp.sum(code * code_log, 1, keepdims=True)
        code_kl = jnp.sum(jnp.sum(code * (code_log + math.log(GK)), 1), 0, keepdims=True)
        flat = jnp.concatenate(
            [code.reshape(GCODE, ROWS), jnp.zeros((ROWS - GCODE, ROWS), F32)], 0
        )
        self.soft_turned[...] = flat[0:GCODE].astype(BF)
        soft = flat.T[:, 0:GCODE].astype(BF)
        matmul_into(self.dec_normed, soft, self.goal_in)
        hidden_rows(self.dec_normed, self.dec_inverse, goal_gain, self.dec_hidden)
        turn_into(self.dec_left, self.dec_hidden)

        def one(j, total):
            lanes = pl.ds(pl.multiple_of(j * 256, 256), 256)
            err = product(self.dec_hidden[...], self.goal_out[:, lanes]) - self.deter[:, lanes]
            grad = scale * err * (1.0 / H)
            self.grad_deter[:, lanes] -= grad
            self.recon_low[:, lanes] = grad.astype(BF)
            return total + jnp.sum(err * err, -1, keepdims=True)

        squares = lax.fori_loop(0, H // 256, one, jnp.zeros((ROWS, 1), F32))
        self.loss[...] += jnp.sum(scale * (0.5 / H) * squares, 0, keepdims=True) + jnp.sum(
            scale_row * code_kl, 1, keepdims=True
        )
        matmul_into(self.wide_512, self.recon_low[...], self.goal_out, turned=True)
        total = hidden_rows_back(
            lambda rows: self.wide_512[rows, :],
            self.dec_normed, self.dec_inverse, goal_gain, self.dec_pre,
        )
        put_vector(self.small, GOAL_G, total)
        spread_lanes(self.dec_pre, self.dec_pair, 0, 0)
        grad_code = lax.dot_general(
            self.goal_in[...], self.dec_pre[...], (((1,), (1,)), ((), ())),
            preferred_element_type=F32,
        ).reshape(GC, GK, ROWS)
        grad_logits = code * (grad_code - jnp.sum(code * grad_code, 1, keepdims=True))
        grad_logits = grad_logits + scale_row[None] * code * (code_log - spread)
        grad_turned = grad_logits.reshape(GCODE, ROWS)
        grad_low = jnp.concatenate(
            [grad_turned, jnp.zeros((ROWS - GCODE, ROWS), F32)], 0
        ).T[:, 0:GCODE].astype(BF)
        put_table(
            self.small, ENC_T, product(grad_turned.astype(BF), self.hid_512[...]), GCODE
        )
        matmul_into(self.wide_512, grad_low, self.enc_out)
        total = hidden_rows_back(
            lambda rows: self.wide_512[rows, :],
            self.pre_512, self.inverse, gain, self.back_512,
        )
        put_vector(self.small, ENC_G, total)
        spread_lanes(self.back_512, self.me_right, ROWS, 1)
        self.add_back(self.back_512, self.enc_in)

    def prior(self):
        matmul_into(self.prior_normed, self.deter_low[...], self.prior_in)
        hidden_rows(
            self.prior_normed, self.prior_inverse, self.gain(PRIOR_G, H), self.prior_hidden
        )
        turn_into(self.prior_out_left, self.prior_hidden)

    def post(self):
        def one(j, carry):
            lanes = pl.ds(pl.multiple_of(j * 256, 256), 256)
            value = product(self.deter_low[...], self.post_in[0:H, lanes])
            self.post_normed[:, lanes] = value + product(
                self.embed[...], self.post_in[H : H + E, lanes]
            )
            return carry

        lax.fori_loop(0, H // 256, one, 0)
        hidden_rows(self.post_normed, self.post_inverse, self.gain(POST_G, H), self.post_hidden)
        turn_into(self.post_out_left, self.post_hidden)

    def logits(self, hidden_ref, weight_ref, turned_ref):
        matmul_into(self.wide, hidden_ref[...], weight_ref)
        turn_into(turned_ref, self.wide)

    def state_kl(self):
        scale_row = self.meta_turned[33:34, :] * (1.0 / ROWS)

        def log_part(value):
            shifted = value - jnp.max(value, 0, keepdims=True)
            return shifted - jnp.log(jnp.sum(jnp.exp(shifted), 0, keepdims=True))

        def one(rows, total):
            post_log = log_part(self.post_turned[rows, :])
            prior_log = log_part(self.prior_turned[rows, :])
            post = jnp.exp(post_log)
            gap = post_log - prior_log
            kl = jnp.sum(post * gap, 0, keepdims=True)
            self.post_turned[rows, :] = scale_row * post * (gap - kl)
            self.prior_turned[rows, :] = scale_row * (jnp.exp(prior_log) - post)
            return total + kl

        total = by_rows(Z, ZK, one, jnp.zeros((1, ROWS), F32))
        self.loss[...] += jnp.sum(scale_row * total, 1, keepdims=True)
        for turned, low in (
            (self.post_turned, self.post_out_right), (self.prior_turned, self.prior_out_right),
        ):
            for j in range(Z // LANES):
                lanes = slice(j * LANES, (j + 1) * LANES)
                low[:, lanes] = turned[lanes, :].T.astype(BF)

    def prior_back(self):
        matmul_into(self.wide, self.prior_out_right[...], self.prior_out, turned=True)
        total = hidden_rows_back(
            lambda rows: self.wide[rows, :],
            self.prior_normed, self.prior_inverse, self.gain(PRIOR_G, H), self.prior_right,
        )
        put_vector(self.small, PRIOR_G, total)
        self.add_back(self.prior_right, self.prior_in)

    def post_back(self):
        matmul_into(self.wide, self.post_out_right[...], self.post_out, turned=True)
        total = hidden_rows_back(
            lambda rows: self.wide[rows, :],
            self.post_normed, self.post_inverse, self.gain(POST_G, H), self.post_right,
        )
        put_vector(self.small, POST_G, total)
        self.add_back(self.post_right, self.post_in)
        matmul_into(self.embed_grad, self.post_right[...], self.post_in, turned=True, low=H)
        for y in range(2):
            for c in range(2):
                self.small[c, y, LOSS : LOSS + 1, :] = jnp.broadcast_to(
                    self.loss[...], (1, LANES)
                )


class Places:
    def __init__(self):
        dp, rep = (lax.axis_index("dp"), lax.axis_index("rep"))
        self.dp, self.rep = (dp, rep)
        self.x, self.z, self.w = (lax.rem(dp, 2), lax.rem(dp // 2, 2), dp // 4)
        self.y, self.c = (rep // 2, lax.rem(rep, 2))
        self.to_x = (dp + 1 - 2 * self.x, rep)
        self.to_z = (dp + 2 - 4 * self.z, rep)
        self.to_w = (dp + 4 - 8 * self.w, rep)
        self.to_y = (dp, rep + 2 - 4 * self.y)
        self.to_c = (dp, rep + 1 - 2 * self.c)
        self.to_d = (dp, 3 - rep)

    def around(self, offset):
        return lax.rem(self.dp + offset, 8)


def greet(devices):
    barrier = pltpu.get_barrier_semaphore()
    for device in devices:
        pl.semaphore_signal(barrier, inc=1, device_id=device, device_id_type=MESH)
    pl.semaphore_wait(barrier, len(devices))


def send_to(source, target, send_sem, recv_sem, device):
    return pltpu.make_async_remote_copy(
        src_ref=source,
        dst_ref=target,
        send_sem=send_sem,
        recv_sem=recv_sem,
        device_id=device,
        device_id_type=MESH,
    )


def regroup_start(places, outgoing, incoming, send_sem, recv_sem):
    count = ROWS // 8
    mine = pl.ds(pl.multiple_of(places.dp * count, 16), count)
    copies = []
    for offset in range(1, 8):
        there = places.around(offset)
        copy = send_to(
            outgoing.at[pl.ds(pl.multiple_of(there * count, 16), count)],
            incoming.at[mine],
            send_sem.at[offset],
            recv_sem.at[offset],
            (there, places.rep),
        )
        copy.start()
        copies.append(copy)
    incoming[mine, :] = outgoing[mine, :]
    return copies


def diagonal_split(u, columns):
    tiles = columns // LANES
    shares = [tiles // 3 + (1 if (i - u) % 3 < tiles % 3 else 0) for i in range(3)]
    return tuple(share * LANES for share in shares)


OWN, Y_A, Y_B, X_A, Z_A, X_B, Z_B, RELAY = range(8)


class Gather:
    def __init__(self, places, units, send_sem, recv_sem, load_sem):
        self.places, self.units = (places, units)
        self.send_sem, self.recv_sem, self.load_sem = (send_sem, recv_sem, load_sem)
        self.far = places.rep + 2 - 4 * places.y
        self.mine = places.x * 2 + places.z
        self.across = 3 - self.mine
        self.from_x = (1 - places.x) * 2 + places.z
        self.from_z = places.x * 2 + 1 - places.z
        self.copies = {}
        self.loads = {}

    def remote(self, u, kind, source, target, device):
        copy = send_to(
            source, target, self.send_sem.at[u, kind], self.recv_sem.at[u, kind], device
        )
        copy.start()
        self.copies[u, kind] = copy

    def rows(self, u, share, piece, low, number):
        extent = self.units[u][0].shape[0]
        start = share * extent + piece * (extent // 4) + low
        return pl.ds(pl.multiple_of(start, 16), number)

    def part(self, u, rows, whole=True, first=0, columns=None):
        share, all_rows, low, count = self.units[u]
        lanes = pl.ds(low + first, count if columns is None else columns)
        return (all_rows if whole else share).at[rows, lanes]

    def diagonal(self, u, share, piece, over, whole=True):
        split = diagonal_split(u, self.units[u][3])
        return self.part(
            u, self.rows(u, share, piece, 0, self.extent(u) // 4), whole, sum(split[:over]),
            split[over],
        )

    def extent(self, u):
        return self.units[u][0].shape[0]

    def load(self, u):
        everything = self.rows(u, 0, 0, 0, self.extent(u))
        copy = pltpu.make_async_copy(
            self.part(u, everything, False),
            self.part(u, self.rows(u, self.places.rep, 0, 0, self.extent(u))),
            self.load_sem.at[u],
        )
        copy.start()
        self.loads[u] = copy

    def over_y(self, u):
        if u >= len(self.units):
            return
        rep, quarter = (self.places.rep, self.extent(u) // 4)
        self.remote(
            u, Y_A,
            self.part(u, self.rows(u, 0, self.mine, 0, quarter), False),
            self.part(u, self.rows(u, rep, self.mine, 0, quarter)),
            self.places.to_y,
        )

    def over_y_more(self, u):
        if u >= len(self.units):
            return
        rep = self.places.rep
        if diagonal_split(u, self.units[u][3])[0]:
            self.remote(
                u, Y_B, self.diagonal(u, 0, self.across, 0, False),
                self.diagonal(u, rep, self.across, 0), self.places.to_y,
            )
        everything = self.rows(u, 0, 0, 0, self.extent(u))
        self.remote(
            u, OWN,
            self.part(u, everything, False),
            self.part(u, self.rows(u, rep, 0, 0, self.extent(u))),
            self.places.to_c,
        )

    def stage_1(self, u):
        self.copies[u, Y_A].wait_recv()
        piece = self.part(u, self.rows(u, self.far, self.mine, 0, self.extent(u) // 4))
        self.remote(u, X_A, piece, piece, self.places.to_x)
        self.remote(u, Z_A, piece, piece, self.places.to_z)

    def stage_2(self, u):
        _, second, third = diagonal_split(u, self.units[u][3])
        self.copies[u, Z_A].wait_recv()
        if second:
            piece = self.diagonal(u, self.far, self.from_z, 1)
            self.remote(u, X_B, piece, piece, self.places.to_x)
        self.copies[u, X_A].wait_recv()
        if third:
            piece = self.diagonal(u, self.far, self.from_x, 2)
            self.remote(u, Z_B, piece, piece, self.places.to_z)

    def stage_3(self, u):
        for kind in (Y_B, X_B, Z_B):
            if (u, kind) in self.copies:
                self.copies[u, kind].wait_recv()
        share = self.part(u, self.rows(u, self.far, 0, 0, self.extent(u)))
        self.remote(u, RELAY, share, share, self.places.to_c)

    def open(self):
        for u in range(AHEAD):
            self.over_y(u)
            if u < MORE:
                self.over_y_more(u)

    def pump(self, t):
        count = len(self.units)
        if t < count:
            self.stage_1(t)
            self.over_y(t + AHEAD)
        if 0 <= t < count:
            self.over_y_more(t + MORE)
        if 0 <= t - LAG_2 < count:
            self.stage_2(t - LAG_2)
        if 0 <= t - LAG_3 < count:
            self.stage_3(t - LAG_3)

    def complete(self, u):
        self.loads[u].wait()
        self.copies[u, OWN].wait_recv()
        self.copies[u, RELAY].wait_recv()

    def drain(self):
        for copy in self.copies.values():
            copy.wait_send()


AHEAD, MORE, LAG_2, LAG_3, DONE = (8, 4, 2, 4, 5)


def frames_kernel(f):
    places = Places()
    units = [(f.img_stoch_share, f.img_stoch, 0, H)]
    units += [(f.gru_weight_share, f.gru_weight, i * H, H) for i in range(3)]
    units += [
        (f.manager_in_share, f.manager_in, 0, U),
        (f.enc_in_share, f.enc_in, 0, U),
        (f.goal_out_share, f.goal_out, 0, H),
        (f.prior_in_share, f.prior_in, 0, H),
        (f.post_in_share, f.post_in, 0, U),
        (f.post_in_share, f.post_in, U, U),
        (f.prior_out_share, f.prior_out, 0, Z),
        (f.post_out_share, f.post_out, 0, Z),
        (f.actor_in_share, f.actor_in, 0, 256),
        (f.actor_in_share, f.actor_in, 256, 256),
        (f.critic_in_share, f.critic_in, 0, 256),
        (f.critic_in_share, f.critic_in, 256, 128),
        (f.critic_in_share, f.critic_in, 384, 128),
    ]
    gather = Gather(places, units, f.piece_send, f.piece_recv, f.load_done)
    for u in range(len(units)):
        gather.load(u)
    f.pack()
    greet(
        [(places.around(o), places.rep) for o in range(1, 8)]
        + [places.to_c, places.to_y, places.to_d]
    )
    packs = []
    for i, (share, whole) in enumerate(((f.vector_share, f.vectors), (f.table_share, f.tables))):
        for k, device in enumerate((places.to_c, places.to_y, places.to_d)):
            copy = send_to(
                share, whole.at[places.rep], f.small_send.at[i, k], f.small_recv.at[i, k], device
            )
            copy.start()
            packs.append(copy)
    gather.open()
    f.vectors[places.rep] = f.vector_share[...]
    f.tables[places.rep] = f.table_share[...]
    saves = []

    def save(k, source, target):
        copy = pltpu.make_async_copy(source, target, f.save_done.at[k])
        copy.start()
        saves.append(copy)

    def pump(t):
        gather.pump(t)

    f.start()
    pump(0)
    f.turns()
    states = []

    def first():
        for copy in packs:
            copy.wait()
        f.unpack()
        f.img()

    def state():
        f.gru(2)
        save(0, f.gru_weight, f.gru_weight_out)
        f.state()
        f.picked()
        states.extend(
            regroup_start(places, f.outgoing, f.incoming, f.state_send, f.state_recv)
        )

    def encoder():
        save(1, f.goal_out, f.goal_out_out)
        f.encoder()

    def posterior():
        f.logits(f.post_hidden, f.post_out, f.post_turned)
        f.state_kl()

    def arrived():
        for copy in states:
            copy.wait()
        f.start_state[...] = f.incoming[...]

    work = {
        0: first, 1: lambda: f.gru(0), 2: lambda: f.gru(1), 3: state, 4: f.manager, 6: encoder,
        7: f.prior, 9: f.post,
        10: lambda: f.logits(f.prior_hidden, f.prior_out, f.prior_turned),
        11: posterior, 12: f.prior_back, 13: f.post_back, 14: arrived,
    }
    count = len(units)
    for t in range(1, count + DONE):
        pump(t)
        if 0 <= t - DONE:
            gather.complete(t - DONE)
            work.get(t - DONE, lambda: None)()
    save(2, f.actor_in, f.actor_in_out)
    save(3, f.critic_in, f.critic_in_out)
    for copy in saves:
        copy.wait()
    gather.drain()


class Source(NamedTuple):
    rows: int
    parts: Any
    columns: int

    @property
    def depth(self):
        return sum(self.parts)


SOURCE_POST = Source((H + E) // 4, (ROWS,), H)
SOURCE_1024 = Source(H // 4, (ROWS,), H)
SOURCE_MAN_ENC = Source(H // 4, (2 * ROWS,), 2 * U)
SOURCE_GRU = Source(H // 2, (ROWS,), 3 * H)
SOURCE_GOAL_OUT = Source(U // 4, (ROWS, ROWS), H)
SOURCE_GOAL_IN = Source(GCODE // 4, (ROWS, ROWS), 2 * U)
WORKER_SHARE = (768, 1024)
ALONG_X, ALONG_Z, ALONG_W, ALONG_Y = range(4)
Y_FIRST = (ALONG_Y, ALONG_X, ALONG_Z, ALONG_W)
X_FIRST = (ALONG_X, ALONG_Y, ALONG_Z, ALONG_W)
Z_FIRST = (ALONG_Z, ALONG_Y, ALONG_X, ALONG_W)
X_ONLY = (ALONG_X, ALONG_Z, ALONG_W)
Z_ONLY = (ALONG_Z, ALONG_X, ALONG_W)


def side_by_side(left, right_ref, lanes):
    right = jnp.concatenate([right_ref[:, lane] for lane in lanes], 1)
    wide = product(left, right)
    return [wide[:, i * LANES : (i + 1) * LANES] for i in range(len(lanes))]


class Exchange:
    def __init__(self, places, source, left_2, right_2, send_sem, recv_sem, local_sem, first):
        self.places, self.source = (places, source)
        self.left_2, self.right_2 = (left_2, right_2)
        self.sems, self.first = ((send_sem, recv_sem, local_sem), first)
        self.copies = []

    def move(self, part, j, mine, target, theirs, place):
        send_sem, recv_sem, local_sem = (sem.at[self.first + part, j] for sem in self.sems)
        remote = send_to(theirs, place, send_sem, recv_sem, self.places.to_c)
        local = pltpu.make_async_copy(mine, target, local_sem)
        remote.start()
        local.start()
        self.copies += [remote, local]

    def lows(self, part):
        low = sum(self.source.parts[:part])
        depth = self.source.parts[part]
        return (pl.ds(low, depth), pl.ds(self.source.depth + low, depth))

    def start_left(self, part, left):
        low, high = self.lows(part)
        for y in range(2):
            ours, theirs = (
                pl.ds(pl.multiple_of((2 * y + core) * self.source.rows, 16), self.source.rows)
                for core in (self.places.c, 1 - self.places.c)
            )
            self.move(
                part, y, left.at[ours], self.left_2.at[y, :, low],
                left.at[theirs], self.left_2.at[y, :, high],
            )

    def start_right(self, part, right):
        low, high = self.lows(part)
        self.move(part, 2, right, self.right_2.at[low], right, self.right_2.at[high])

    def start(self, part, left, right):
        self.start_right(part, right)
        self.start_left(part, left)

    def ready(self, first=0):
        while self.copies:
            self.copies.pop(0).wait()

    def terms(self, y, rows, lanes):
        return side_by_side(self.left_2[y, rows, :], self.right_2, lanes)


class Wide:
    def __init__(self, places, rows, depth, left_4, right_4, send_sem, recv_sem, local_sem):
        self.places, self.rows, self.depth = (places, rows, depth)
        self.left_4, self.right_4 = (left_4, right_4)
        self.send_sem, self.recv_sem, self.local_sem = (send_sem, recv_sem, local_sem)
        self.copies = []
        self.from_y = None

    def part(self, i):
        return pl.ds(i * self.depth, self.depth)

    def remote(self, k, source, target, device):
        copy = send_to(source, target, self.send_sem.at[k], self.recv_sem.at[k], device)
        copy.start()
        return copy

    def local(self, k, source, target):
        copy = pltpu.make_async_copy(source, target, self.local_sem.at[k])
        copy.start()
        self.copies.append(copy)

    def start_left(self, left):
        rep, places = (self.places.rep, self.places)
        across = (places.to_c, places.to_y, places.to_d)
        for i, device in enumerate(across):
            rows = pl.ds(pl.multiple_of(device[1] * self.rows, 16), self.rows)
            self.copies.append(
                self.remote(i, left.at[rows], self.left_4.at[:, self.part(1 + i)], device)
            )
        rows = pl.ds(pl.multiple_of(rep * self.rows, 16), self.rows)
        self.local(0, left.at[rows], self.left_4.at[:, self.part(0)])

    def start_right(self, right):
        self.from_y = self.remote(3, right, self.right_4.at[self.part(2)], self.places.to_y)
        self.copies.append(
            self.remote(4, right, self.right_4.at[self.part(1)], self.places.to_c)
        )
        self.local(1, right, self.right_4.at[self.part(0)])

    def relay(self):
        self.from_y.wait()
        piece = self.right_4.at[self.part(2)]
        self.copies.append(
            self.remote(5, piece, self.right_4.at[self.part(3)], self.places.to_c)
        )

    def ready(self, first=0):
        while self.copies:
            self.copies.pop(0).wait()

    def terms(self, y, rows, lanes):
        return side_by_side(self.left_4[rows, :], self.right_4, lanes)


class Addition:
    def __init__(self, places, own, sibling, send_sem, recv_sem, local_sem):
        self.places, self.own, self.sibling = (places, own, sibling)
        self.sems = (send_sem, recv_sem, local_sem)
        self.copies = {}

    def start(self, whole, part):
        rows, half = (self.own.shape[1], self.own.shape[1] // 2)
        here = pl.ds(part * half, half)
        copies = []
        for y in range(2):
            ours, theirs = (
                pl.ds(pl.multiple_of((2 * y + core) * rows + part * half, 16), half)
                for core in (self.places.c, 1 - self.places.c)
            )
            send_sem, recv_sem, local_sem = (sem.at[part, y] for sem in self.sems)
            copies.append(
                send_to(
                    whole.at[theirs], self.sibling.at[y, here], send_sem, recv_sem,
                    self.places.to_c,
                )
            )
            copies.append(pltpu.make_async_copy(whole.at[ours], self.own.at[y, here], local_sem))
        for copy in copies:
            copy.start()
        self.copies[part] = copies

    def ready(self, first=0):
        for copy in self.copies.pop(first // (self.own.shape[1] // 2), ()):
            copy.wait()

    def terms(self, y, rows, lanes):
        return [
            self.own[y, rows, lane].astype(F32) + self.sibling[y, rows, lane].astype(F32)
            for lane in lanes
        ]


class Halving:
    def __init__(self, places, units, outbox, inbox, send_sem, recv_sem, outs, groups):
        self.units, self.groups = (units, groups)
        self.outbox, self.inbox, self.outs = (outbox, inbox, outs)
        self.send_sem, self.recv_sem = (send_sem, recv_sem)
        self.bits = (places.x, places.z, places.w, places.y)
        self.peers = (places.to_x, places.to_z, places.to_w, places.to_y)
        self.copies = {}

    def blocks(self, u, k):
        source, stride, offset, order, first, count = self.units[u]
        free = order[k + 1 :]
        place = {ALONG_Y: self.bits[ALONG_Y]}
        for i, along in enumerate(order[: k + 1]):
            place[along] = self.bits[along] if i < k else 1 - self.bits[along]
        choices = [
            {along: (j >> (len(free) - 1 - i)) & 1 for i, along in enumerate(free)}
            for j in range(1 << len(free))
        ]
        results = [None] * len(choices)
        for y in (0, 1) if ALONG_Y in free else (None,):
            chosen = [j for j, choice in enumerate(choices) if choice.get(ALONG_Y) == y]
            lanes = []
            for j in chosen:
                bits = place | choices[j]
                device = bits[ALONG_W] * 4 + bits[ALONG_Z] * 2 + bits[ALONG_X]
                start = device * stride + offset
                if not isinstance(start, int):
                    start = pl.multiple_of(start, LANES)
                lanes.append(pl.ds(start, LANES))
            terms = source.terms(place[ALONG_Y] if y is None else y, pl.ds(first, count), lanes)
            for j, total in zip(chosen, terms):
                bits = place | choices[j]
                for i in range(k):
                    index = 0
                    for along in order[i + 1 :]:
                        index = index * 2 + bits[along]
                    total = total + self.inbox[u][i][index].astype(F32)
                results[j] = total
        return results

    def step(self, u, k):
        if k == 0:
            self.units[u][0].ready(self.units[u][4])
        else:
            self.copies[u, k - 1].wait_recv()
        if k == len(self.units[u][3]):
            self.outs[u][...] = self.blocks(u, k)[0]
            return
        for j, block in enumerate(self.blocks(u, k)):
            self.outbox[u][k][j] = block.astype(BF)
        copy = send_to(
            self.outbox[u][k], self.inbox[u][k], self.send_sem.at[u, k], self.recv_sem.at[u, k],
            self.peers[self.units[u][3][k]],
        )
        copy.start()
        self.copies[u, k] = copy

    def slot(self, t, lag=1):
        for k in range(5):
            if 0 <= t - lag * k < len(self.groups):
                for u in self.groups[t - lag * k]:
                    if k <= len(self.units[u][3]):
                        self.step(u, k)

    def drain(self):
        for copy in self.copies.values():
            copy.wait_send()


def boxes(units):
    return tuple(
        tuple(kept(1 << k, unit[-1], LANES) for k in reversed(range(len(unit[3]))))
        for unit in units
    )


HEAD_POST, HEAD_PRIOR, HEAD_POST_OUT, HEAD_PRIOR_OUT, HEAD_MAN_ENC = range(5)
HEAD_SOURCES = (SOURCE_POST, SOURCE_1024, SOURCE_1024, SOURCE_1024, SOURCE_MAN_ENC)
HEAD_UNITS = (
    (HEAD_POST, 128, 0, Y_FIRST, 0, 128),
    (HEAD_PRIOR, 128, 0, X_FIRST, 0, 128),
    (HEAD_POST_OUT, 128, 0, Z_FIRST, 0, 128),
    (HEAD_POST, 128, 0, Y_FIRST, 128, 128),
    (HEAD_PRIOR, 128, 0, X_FIRST, 128, 128),
    (HEAD_POST_OUT, 128, 0, Z_FIRST, 128, 128),
    (HEAD_POST, 128, 0, Y_FIRST, 256, 128),
    (HEAD_MAN_ENC, 128, 0, X_FIRST, 0, 128),
    (HEAD_PRIOR_OUT, 128, 0, Z_FIRST, 0, 128),
    (HEAD_POST, 128, 0, Y_FIRST, 384, 128),
    (HEAD_MAN_ENC, 128, 0, X_FIRST, 128, 128),
    (HEAD_PRIOR_OUT, 128, 0, Z_FIRST, 128, 128),
    (HEAD_POST, 128, 0, X_FIRST, 512, 128),
)
HEAD_GROUPS = ((0, 1, 2), (3, 4, 5), (6, 7, 8), (9, 10, 11), (12,))
HEAD_TIMES = (0, 2, 4, 6, 8, 10, 12, 14, 16)
HEAD_LAG = 1
FORWARD_ROWS, BACK_ROWS = (128, 128)
LAST_WORKER, LAST_GOAL_OUT, LAST_GOAL_IN, LAST_IMG, LAST_GRU = range(5)
LAST_SOURCES = (None, SOURCE_GOAL_OUT, SOURCE_GOAL_IN, SOURCE_1024)
LAST_UNITS = (
    (LAST_WORKER, 128, 0, X_FIRST, 384, 256),
    (LAST_WORKER, 128, 0, Z_FIRST, 640, 128),
    (LAST_GOAL_OUT, 128, 0, Z_FIRST, 0, 128),
    (LAST_GOAL_IN, 128, 0, Z_FIRST, 0, 16),
    (LAST_IMG, 128, 0, X_FIRST, 0, 128),
    (LAST_GRU, 384, 0, X_ONLY, 0, 256),
    (LAST_GRU, 384, 256, Z_ONLY, 0, 256),
    (LAST_WORKER, 128, 0, Y_FIRST, 0, 128),
    (LAST_GRU, 384, 0, X_ONLY, 256, 256),
    (LAST_GRU, 384, 256, Z_ONLY, 256, 256),
    (LAST_WORKER, 128, 0, Y_FIRST, 128, 256),
    (LAST_GRU, 384, 128, X_ONLY, 0, 256),
    (LAST_GRU, 384, 128, Z_ONLY, 256, 128),
    (LAST_IMG, 128, 0, Y_FIRST, 128, 128),
    (LAST_GRU, 384, 128, X_ONLY, 384, 128),
)
LAST_GROUPS = ((0, 1), (2, 3, 4), (5, 6, 7), (8, 9, 10), (11, 12, 13), (14,))


class Worker(NamedTuple):
    goal_codes: Any = taken(GC, ROWS, dtype=jnp.int32)
    actions: Any = taken(HOR, ROWS, dtype=jnp.int32)
    samples: Any = taken(HOR, ZG, ROWS, dtype=jnp.int32)
    vectors: Any = taken(4, VECTOR_TILES, LANES, dtype=F32)
    tables: Any = taken(4, TABLES, LANES)
    start_state: Any = taken(ROWS, H + LANES)
    goal_out: Any = taken(U, H)
    actor_in: Any = taken(3 * H, U)
    critic_in: Any = taken(3 * H, U)
    post_left: Any = taken(H + E, ROWS, here=False)
    post_out_left: Any = taken(H, ROWS, here=False)
    prior_out_left: Any = taken(H, ROWS, here=False)
    me_left: Any = taken(H, 2 * ROWS, here=False)
    post_right: Any = taken(ROWS, H, here=False)
    prior_right: Any = taken(ROWS, H, here=False)
    post_out_right: Any = taken(ROWS, Z, here=False)
    prior_out_right: Any = taken(ROWS, Z, here=False)
    me_right: Any = taken(2 * ROWS, 2 * U, here=False)
    worker_left: Any = given(3 * H, 2 * U)
    returned: Any = given(ROWS, H)
    goal_left: Any = given(U, ROWS)
    code_turned: Any = given(GCODE, ROWS)
    goal_right: Any = given(ROWS, H)
    goal_pair: Any = given(ROWS, 2 * U)
    small: Any = given(2, 2, SMALL_TILES, LANES, dtype=F32)
    sums: Any = tuple(given(unit[-1], LANES, dtype=F32) for unit in HEAD_UNITS)
    act_out: Any = kept(32, U)
    goal_in: Any = kept(GCODE, U)
    action_columns: Any = kept(ROWS, LANES, dtype=F32)
    goal_normed: Any = kept(ROWS, U, dtype=F32)
    goal_inverse: Any = kept(ROWS, 1, dtype=F32)
    goal_hidden: Any = kept(ROWS, U)
    goal_pre: Any = kept(ROWS, U)
    goal_low: Any = kept(ROWS, H)
    turned: Any = kept(2 * H, ROWS)
    slot_part: Any = kept(2, ROWS, U, dtype=F32)
    hot: Any = kept(2 * ROWS, Z)
    pre: Any = kept(2 * ROWS, U, dtype=F32)
    hidden: Any = kept(2 * ROWS, U)
    normed: Any = kept(2, HOR * ROWS, U, dtype=F32)
    inverse: Any = kept(2, HOR * ROWS, 1, dtype=F32)
    hot_turned: Any = kept(Z, HOR * ROWS)
    log_chance: Any = kept(HOR * ROWS, 32, dtype=F32)
    chosen: Any = kept(ROWS, LANES, dtype=F32)
    value: Any = kept(ROWS, LANES, dtype=F32)
    returns: Any = kept(ROWS, LANES, dtype=F32)
    pre_pair: Any = kept(HOR * ROWS, 2 * U)
    summed: Any = kept(2, ROWS, U, dtype=F32)
    sum_low: Any = kept(2, ROWS, U)
    sum_pair: Any = kept(ROWS, 2 * U)
    low_512: Any = kept(ROWS, U)
    grad_column: Any = kept(ROWS, 1, dtype=F32)
    to_state: Any = kept(ROWS, H)
    incoming: Any = kept(ROWS, H)
    wide_512: Any = kept(ROWS, U, dtype=F32)
    top: Any = kept(2, 8, LANES, dtype=F32)
    top_in: Any = kept(10, 8, LANES, dtype=F32)
    left_2: Any = tuple(kept(2, s.rows, 2 * s.depth) for s in HEAD_SOURCES)
    right_2: Any = tuple(kept(2 * s.depth, s.columns) for s in HEAD_SOURCES)
    outbox: Any = boxes(HEAD_UNITS)
    inbox: Any = boxes(HEAD_UNITS)
    top_send: Any = signal(10)
    top_recv: Any = signal(10)
    state_send: Any = signal(8)
    state_recv: Any = signal(8)
    pair_send: Any = signal(len(HEAD_SOURCES), 3)
    pair_recv: Any = signal(len(HEAD_SOURCES), 3)
    pair_local: Any = signal(len(HEAD_SOURCES), 3)
    half_send: Any = signal(len(HEAD_UNITS), 4)
    half_recv: Any = signal(len(HEAD_UNITS), 4)

    def gain(self, low, size):
        return vector_of(self.vectors, low, size // (4 * LANES))

    def goal(self):
        self.small[...] = jnp.zeros(self.small.shape, F32)
        for r in range(4):
            self.act_out[:, r * LANES : (r + 1) * LANES] = self.tables[
                r, TAB_ACT : TAB_ACT + 32, :
            ]
            for i in range(4):
                self.goal_in[16 * r : 16 * (r + 1), i * LANES : (i + 1) * LANES] = self.tables[
                    r, TAB_GOAL + 16 * i : TAB_GOAL + 16 * (i + 1), :
                ]
        self.action_columns[...] = columns_of(self.actions[...].astype(F32))
        hot = hot_rows(columns_of(self.goal_codes[...].astype(F32)), GK, GC, LANES)
        self.code_turned[...] = hot.T[0:GCODE].astype(BF)
        matmul_into(self.goal_normed, hot[:, 0:GCODE].astype(BF), self.goal_in)
        hidden_rows(
            self.goal_normed, self.goal_inverse, self.gain(GOAL_G, U), self.goal_hidden
        )
        turn_into(self.goal_left, self.goal_hidden)

        def one(j, totals):
            lanes = pl.ds(pl.multiple_of(j * 256, 256), 256)
            goal = product(self.goal_hidden[...], self.goal_out[:, lanes])
            state = self.start_state[:, lanes].astype(F32)
            self.goal_low[:, lanes] = goal.astype(BF)
            terms = (goal * state, goal * goal, state * state)
            return tuple(
                t + jnp.sum(term, -1, keepdims=True) for t, term in zip(totals, terms)
            )

        zero = jnp.zeros((ROWS, 1), F32)
        aligned, goal_square, state_square = lax.fori_loop(0, H // 256, one, (zero,) * 3)
        turn_into(self.turned, self.start_state.at[:, 0:H])
        turn_into(self.turned, self.goal_low, H)
        return aligned / (jnp.maximum(goal_square, state_square) + small_floor)

    def slots(self):
        for which, weight in enumerate((self.actor_in, self.critic_in)):
            def one(j, carry):
                lanes = pl.ds(pl.multiple_of(j * 256, 256), 256)
                self.slot_part[which, :, lanes] = product(
                    self.start_state[:, 0:H], weight[0:H, lanes]
                ) + product(self.goal_low[...], weight[2 * H : 3 * H, lanes])
                return carry

            lax.fori_loop(0, U // 256, one, 0)

    def forward(self, first, last):
        gains = (self.gain(ACT_G, U), self.gain(CRI_G, U))
        head = self.gain(CRI_O, U)
        spread = class_spread(ZG, ZK, ZG, Z)
        lane = lax.broadcasted_iota(jnp.int32, (1, Z), 1)
        lane_class = jnp.bitwise_and(lane, ZK - 1).astype(F32)
        group = lax.broadcasted_iota(jnp.int32, (Z, ZG), 1)
        place = lax.broadcasted_iota(jnp.int32, (Z, ZG), 0)
        inside = (place >= group * ZK) & (place < group * ZK + ZK)
        spread_turned = jnp.where(inside, 1.0, 0.0).astype(BF)
        place_class = jnp.bitwise_and(
            lax.broadcasted_iota(jnp.int32, (Z, 1), 0), ZK - 1
        ).astype(F32)
        act_lane = lax.broadcasted_iota(jnp.int32, (1, 32), 1)
        step_lane = lax.broadcasted_iota(jnp.int32, (1, LANES), 1)

        def pair(i, carry):
            start = pl.multiple_of(i * 2 * ROWS, 2 * ROWS)
            for half in range(2):
                k = 2 * i + half
                rows = pl.ds(pl.multiple_of(start + half * ROWS, ROWS), ROWS)
                ids = self.samples[k].astype(F32)
                self.hot[half * ROWS : (half + 1) * ROWS, :] = jnp.where(
                    product(columns_of(ids)[:, 0:ZG].astype(BF), spread) == lane_class, 1.0, 0.0
                ).astype(BF)
                self.hot_turned[:, rows] = jnp.where(
                    product(spread_turned, ids.astype(BF)) == place_class, 1.0, 0.0
                ).astype(BF)
            for which, weight in enumerate((self.actor_in, self.critic_in)):
                self.pre[...] = product(self.hot[...], weight[H : 2 * H, :])
                for low in range(0, 2 * ROWS, FORWARD_ROWS):
                    rows = pl.ds(pl.multiple_of(start + low, FORWARD_ROWS), FORWARD_ROWS)
                    slot = pl.ds(low % ROWS, FORWARD_ROWS)
                    pre = self.pre[low : low + FORWARD_ROWS, :] + self.slot_part[which, slot, :]
                    normed, inverse = normalize(pre)
                    self.normed[which, rows, :] = normed
                    self.inverse[which, rows, :] = inverse
                    hidden = elu_of(normed * gains[which]).astype(BF)
                    if which == 0:
                        self.hidden[low : low + FORWARD_ROWS, :] = hidden
                    else:
                        value = jnp.sum(hidden.astype(F32) * head, -1, keepdims=True)
                        here = step_lane == 2 * i + low // ROWS
                        self.value[slot, :] = jnp.where(here, value, self.value[slot, :])
            logits = lax.dot_general(
                self.hidden[...], self.act_out[...], (((1,), (1,)), ((), ())),
                preferred_element_type=F32,
            )
            logits = jnp.where(act_lane < NA, logits, -1e30)
            shifted = logits - jnp.max(logits, -1, keepdims=True)
            total = jnp.sum(jnp.exp(shifted), -1, keepdims=True)
            self.log_chance[pl.ds(start, 2 * ROWS), :] = shifted - jnp.log(total)
            return carry

        lax.fori_loop(first, last, pair, 0)

    def action_here(self, k):
        action = self.at_step(self.action_columns, k)
        return action == lax.broadcasted_iota(jnp.int32, (1, 32), 1).astype(F32)

    def at_step(self, ref, k):
        lane = lax.broadcasted_iota(jnp.int32, (ROWS, LANES), 1)
        return jnp.sum(jnp.where(lane == k, ref[...], 0.0), -1, keepdims=True)

    def targets(self, reward):
        weight = self.start_state[:, H : H + 1].astype(F32)
        lane = lax.broadcasted_iota(jnp.int32, (ROWS, LANES), 1)
        later = self.value[:, HOR - 1 : HOR]
        result = later
        returns = jnp.where(lane == HOR - 1, result, 0.0)
        for k in range(HOR - 2, -1, -1):
            blended = (1.0 - return_mix) * later + return_mix * result
            result = reward + discount * blended
            returns = jnp.where(lane == k, result, returns)
            later = self.value[:, k : k + 1]
        self.returns[...] = returns
        gaps = jnp.where(lane < HOR, jnp.abs(returns - self.value[...]), 0.0)
        top = jnp.max(weight * gaps, 0, keepdims=True)
        self.top[0] = jnp.broadcast_to(jnp.max(top, 1, keepdims=True), (8, LANES))

    def critic_back(self, first, last, total):
        gain, head = (self.gain(CRI_G, U), self.gain(CRI_O, U))
        weight = self.start_state[:, H : H + 1].astype(F32)

        def step(k, totals):
            rows = pl.ds(pl.multiple_of(k * ROWS, ROWS), ROWS)
            misfit = self.at_step(self.value, k) - self.at_step(self.returns, k)
            grad = weight * misfit * (1.0 / (ROWS * HOR))
            self.grad_column[...] = grad
            gain_total = totals[0] + hidden_rows_back(
                lambda r: self.grad_column[r, :] * head,
                self.normed.at[1, rows], self.inverse.at[1, rows], gain, self.low_512, BACK_ROWS,
                self.hidden,
            )
            head_total = totals[1] + jnp.sum(
                self.hidden[0:ROWS, :].astype(F32) * grad, 0, keepdims=True
            )
            for j in range(4):
                tile = self.low_512[:, j * LANES : (j + 1) * LANES].astype(F32)
                self.summed[1, :, j * LANES : (j + 1) * LANES] += tile
                turned = pltpu.roll(tile, 64, 1)
                self.pre_pair[rows, 2 * j * LANES : (2 * j + 1) * LANES] = turned.astype(BF)
                self.pre_pair[rows, (2 * j + 1) * LANES : (2 * j + 2) * LANES] = tile.astype(BF)
            return (gain_total, head_total)

        return lax.fori_loop(first, last, step, total)

    def pair(self, first, second, out_ref, rows):
        lane = lax.broadcasted_iota(jnp.int32, (ROWS, LANES), 1)
        for j in range(4):
            lanes = slice(j * LANES, (j + 1) * LANES)
            even = slice(2 * j * LANES, (2 * j + 1) * LANES)
            odd = slice((2 * j + 1) * LANES, (2 * j + 2) * LANES)
            a = first[:, lanes].astype(F32)
            if second is None:
                b_even, b_odd = (out_ref[rows, even].astype(F32), out_ref[rows, odd].astype(F32))
            else:
                b_odd = second[:, lanes].astype(F32)
                b_even = pltpu.roll(b_odd, 64, 1)
            out_ref[rows, even] = jnp.where(lane < 64, a, b_even).astype(BF)
            out_ref[rows, odd] = jnp.where(lane < 64, pltpu.roll(a, 64, 1), b_odd).astype(BF)

    def actor_back(self, first, last, totals):
        gain = self.gain(ACT_G, U)
        weight = self.start_state[:, H : H + 1].astype(F32)
        scale = self.top[1, 0:1, 0:1] + small_floor

        def step(k, totals):
            rows = pl.ds(pl.multiple_of(k * ROWS, ROWS), ROWS)
            advantage = self.at_step(self.returns, k) - self.at_step(self.value, k)
            gained = weight * advantage / scale
            here = self.action_here(k)
            log_chance = self.log_chance[rows, :]
            chance = jnp.exp(log_chance)
            grad = (gained * (-1.0 / (ROWS * HOR))) * (jnp.where(here, 1.0, 0.0) - chance)
            grad_turned = jnp.concatenate(
                [grad, jnp.zeros((ROWS, LANES - 32), F32)], 1
            ).T[0:32].astype(BF)
            self.wide_512[...] = product(grad.astype(BF), self.act_out[...])
            gain_total = totals[0] + hidden_rows_back(
                lambda r: self.wide_512[r, :],
                self.normed.at[0, rows], self.inverse.at[0, rows], gain, self.low_512, BACK_ROWS,
                self.hidden,
            )
            out_total = totals[1] + product(grad_turned, self.hidden[0:ROWS, :])
            self.summed[0] += self.low_512[...].astype(F32)
            self.pair(self.low_512, None, self.pre_pair, rows)
            chosen = jnp.sum(jnp.where(here, log_chance, 0.0), -1, keepdims=True)
            loss = totals[2] + jnp.sum(chosen * gained, 0, keepdims=True)
            return (gain_total, out_total, loss)

        return lax.fori_loop(first, last, step, totals)

    def inputs_back(self, low, out_ref):
        def one(j, carry):
            rows = pl.ds(pl.multiple_of(low + j * 256, 256), 256)
            total = 0.0
            for which, weight in enumerate((self.actor_in, self.critic_in)):
                total = total + lax.dot_general(
                    self.sum_low[which], weight[rows, :], (((1,), (1,)), ((), ())),
                    preferred_element_type=F32,
                )
            out_ref[:, pl.ds(pl.multiple_of(j * 256, 256), 256)] = total.astype(BF)
            return carry

        lax.fori_loop(0, H // 256, one, 0)

    def goal_back(self):
        matmul_into(self.wide_512, self.goal_right[...], self.goal_out, turned=True)
        total = hidden_rows_back(
            lambda rows: self.wide_512[rows, :],
            self.goal_normed, self.goal_inverse, self.gain(GOAL_G, U), self.goal_pre,
        )
        put_vector(self.small, GOAL_G, total)
        spread_lanes(self.goal_pre, self.goal_pair, 0, 0)

    def weights(self):
        def one(j, carry):
            lanes = pl.ds(pl.multiple_of(j * 256, 256), 256)
            self.worker_left[H : 2 * H, lanes] = product(
                self.hot_turned[...], self.pre_pair[:, lanes]
            ).astype(BF)
            pair = self.sum_pair[:, lanes]
            self.worker_left[0:H, lanes] = product(self.turned[0:H], pair).astype(BF)
            self.worker_left[2 * H : 3 * H, lanes] = product(
                self.turned[H : 2 * H], pair
            ).astype(BF)
            return carry

        lax.fori_loop(0, 2 * U // 256, one, 0)


def worker_kernel(f):
    places = Places()
    greet(
        [(places.around(o), places.rep) for o in range(1, 8)]
        + [places.to_c, places.to_y, places.to_d]
    )
    heads = []
    lefts = (f.post_left, f.post_left, f.post_out_left, f.prior_out_left, f.me_left)
    rights = (f.post_right, f.prior_right, f.post_out_right, f.prior_out_right, f.me_right)
    for i, source in enumerate(HEAD_SOURCES):
        heads.append(
            Exchange(
                places, source, f.left_2[i], f.right_2[i], f.pair_send, f.pair_recv,
                f.pair_local, i,
            )
        )
    for i in (HEAD_POST, HEAD_PRIOR, HEAD_POST_OUT):
        heads[i].start(0, lefts[i], rights[i])
    halving = Halving(
        places, [(heads[unit[0]],) + unit[1:] for unit in HEAD_UNITS], f.outbox, f.inbox,
        f.half_send, f.half_recv, f.sums, HEAD_GROUPS,
    )
    events = iter(range(24))

    def beside():
        event = next(events)
        for t, place in enumerate(HEAD_TIMES):
            if place == event:
                halving.slot(t, HEAD_LAG)

    reward = f.goal()
    beside()
    for i in (HEAD_MAN_ENC, HEAD_PRIOR_OUT):
        heads[i].start(0, lefts[i], rights[i])
    f.slots()
    f.value[...] = jnp.zeros(f.value.shape, F32)
    f.summed[...] = jnp.zeros(f.summed.shape, F32)
    beside()
    for i in range(4):
        f.forward(2 * i, 2 * i + 2)
        beside()
    f.targets(reward)
    totals = (jnp.zeros((1, U), F32), jnp.zeros((1, U), F32))
    steps = (0, 3, 6, 9, 12, HOR)

    def send_top(which, first, devices):
        copies = []
        for i, device in enumerate(devices):
            k = first + i
            copies.append(
                send_to(f.top.at[which], f.top_in.at[k], f.top_send.at[k], f.top_recv.at[k], device)
            )
            copies[i].start()
        return copies

    def largest(which, first, copies):
        top = f.top[which]
        for i, copy in enumerate(copies):
            copy.wait()
            top = jnp.maximum(top, f.top_in[first + i])
        f.top[1] = top

    tops = send_top(0, 0, [(places.around(o), places.rep) for o in range(1, 8)])
    for k in range(5):
        if k == 3:
            largest(0, 0, tops)
            tops = send_top(1, 7, [places.to_c, places.to_y, places.to_d])
        totals = f.critic_back(steps[k], steps[k + 1], totals)
        beside()
    largest(1, 7, tops)
    put_vector(f.small, CRI_G, totals[0])
    put_vector(f.small, CRI_O, totals[1])
    totals = (jnp.zeros((1, U), F32), jnp.zeros((32, U), F32), jnp.zeros((1, 1), F32))
    for i in range(4):
        totals = f.actor_back(4 * i, 4 * i + 4, totals)
        beside()
    actor_gain, actor_out, chosen = totals
    put_vector(f.small, ACT_G, actor_gain)
    put_table(f.small, ACT_T, actor_out, 24)
    for which in range(2):
        f.sum_low[which] = f.summed[which].astype(BF)
    f.inputs_back(0, f.to_state)
    states = regroup_start(places, f.to_state, f.incoming, f.state_send, f.state_recv)
    f.pair(f.sum_low.at[0], f.sum_low.at[1], f.sum_pair, slice(0, ROWS))
    beside()
    f.weights()
    beside()
    f.inputs_back(2 * H, f.goal_right)
    f.goal_back()
    beside()
    weight = f.start_state[:, H : H + 1].astype(F32)
    misfit = f.value[...] - f.returns[...]
    squares = jnp.sum(jnp.sum(weight * misfit * misfit, -1, keepdims=True), 0, keepdims=True)
    loss = (0.5 * squares - chosen) * (1.0 / (ROWS * HOR))
    for y in range(2):
        for c in range(2):
            f.small[c, y, LOSS : LOSS + 1, :] = jnp.broadcast_to(loss, (1, LANES))
    for copy in states:
        copy.wait()
    f.returned[...] = f.incoming[...]
    halving.drain()


class Last(NamedTuple):
    meta_turned: Any = taken(LANES, ROWS, dtype=F32)
    prev: Any = taken(ROWS, H)
    vectors: Any = taken(4, VECTOR_TILES, LANES, dtype=F32)
    returned: Any = taken(ROWS, H)
    grad_partial: Any = taken(ROWS, H, dtype=F32)
    gru_normed: Any = taken(ROWS, 3 * H, dtype=F32)
    gru_inverse: Any = taken(ROWS, 1, dtype=F32)
    img_normed: Any = taken(ROWS, H, dtype=F32)
    img_inverse: Any = taken(ROWS, 1, dtype=F32)
    small_1: Any = taken(2, 2, SMALL_TILES, LANES, dtype=F32)
    small_2: Any = taken(2, 2, SMALL_TILES, LANES, dtype=F32)
    gru_share: Any = taken(2 * H, 3 * H, here=False)
    worker_left: Any = taken(3 * H, 2 * U, here=False)
    goal_left: Any = taken(U, ROWS, here=False)
    dec_left: Any = taken(U, ROWS, here=False)
    code_turned: Any = taken(GCODE, ROWS, here=False)
    soft_turned: Any = taken(GCODE, ROWS, here=False)
    gru_left: Any = taken(2 * H, ROWS, here=False)
    img_left: Any = taken(Z, ROWS, here=False)
    goal_right: Any = taken(ROWS, H, here=False)
    recon_low: Any = taken(ROWS, H, here=False)
    goal_pair: Any = taken(ROWS, 2 * U, here=False)
    dec_pair: Any = taken(ROWS, 2 * U, here=False)
    deter_grad: Any = given(ROWS, H, dtype=F32)
    small_sum: Any = given(SMALL_TILES, LANES, dtype=F32)
    sums: Any = tuple(given(unit[-1], LANES, dtype=F32) for unit in LAST_UNITS)
    gru_weight: Any = kept(2 * H, 3 * H)
    gru_right: Any = kept(ROWS, 3 * H)
    img_right: Any = kept(ROWS, H)
    grad: Any = kept(ROWS, H, dtype=F32)
    wide: Any = kept(ROWS, 2 * H, dtype=F32)
    small: Any = kept(2, 2, SMALL_TILES, LANES, dtype=F32)
    small_pair: Any = kept(2, SMALL_TILES, LANES, dtype=F32)
    small_in: Any = kept(4, SMALL_TILES, LANES, dtype=F32)
    worker_own: Any = kept(2, *WORKER_SHARE)
    worker_sibling: Any = kept(2, *WORKER_SHARE)
    gru_left_4: Any = kept(H // 2, 4 * ROWS)
    gru_right_4: Any = kept(4 * ROWS, 3 * H)
    left_2: Any = tuple(kept(2, s.rows, 2 * s.depth) for s in LAST_SOURCES[1:])
    right_2: Any = tuple(kept(2 * s.depth, s.columns) for s in LAST_SOURCES[1:])
    outbox: Any = boxes(LAST_UNITS)
    inbox: Any = boxes(LAST_UNITS)
    load_done: Any = signal(1)
    add_send: Any = signal(2, 2)
    add_recv: Any = signal(2, 2)
    add_local: Any = signal(2, 2)
    wide_send: Any = signal(6)
    wide_recv: Any = signal(6)
    wide_local: Any = signal(2)
    pair_send: Any = signal(5, 3)
    pair_recv: Any = signal(5, 3)
    pair_local: Any = signal(5, 3)
    half_send: Any = signal(len(LAST_UNITS), 4)
    half_recv: Any = signal(len(LAST_UNITS), 4)
    small_send: Any = signal(5)
    small_recv: Any = signal(5)

    def state_back(self):
        gain = vector_of(self.vectors, GRU_G, 6)
        frame = lax.broadcasted_iota(jnp.int32, (ROWS, ROWS), 0).astype(F32)
        place = jnp.where(self.meta_turned[37:38, :] == frame, 1.0, 0.0).astype(BF)

        def add(j, carry):
            lanes = pl.ds(pl.multiple_of(j * 256, 256), 256)
            self.grad[:, lanes] = self.grad_partial[:, lanes] + product(
                place, self.returned[:, lanes]
            )
            return carry

        lax.fori_loop(0, H // 256, add, 0)

        def one(rows, total):
            normed = self.gru_normed[rows, :]
            parts = normed * gain
            inner = parts[:, H : 2 * H]
            reset = 1.0 / (1.0 + jnp.exp(-parts[:, :H]))
            candidate = jnp.tanh(reset * inner)
            update = 1.0 / (1.0 + jnp.exp(1.0 - parts[:, 2 * H :]))
            grad = self.grad[rows, :]
            prev = self.prev[rows, :].astype(F32)
            grad_inner = grad * update * (1.0 - candidate * candidate)
            grad_parts = jnp.concatenate(
                [
                    grad_inner * inner * reset * (1.0 - reset),
                    grad_inner * reset,
                    grad * (candidate - prev) * update * (1.0 - update),
                ],
                1,
            )
            self.deter_grad[rows, :] = grad * (1.0 - update)
            total = total + jnp.sum(grad_parts * normed, 0, keepdims=True)
            back = normalize_back(grad_parts * gain, normed, self.gru_inverse[rows, :])
            self.gru_right[rows, :] = back.astype(BF)
            return total

        put_vector(self.small, GRU_G, by_rows(ROWS, 16, one, jnp.zeros((1, 3 * H), F32)))

    def input_back(self):
        matmul_into(self.wide, self.gru_right[...], self.gru_weight, turned=True)
        self.deter_grad[...] += self.wide[:, H : 2 * H]
        total = hidden_rows_back(
            lambda rows: self.wide[rows, 0:H],
            self.img_normed, self.img_inverse, vector_of(self.vectors, IMG_G, 2), self.img_right,
        )
        put_vector(self.small, IMG_G, total)

    def action_back(self):
        place = lax.broadcasted_iota(jnp.int32, (24, ROWS), 0).astype(F32)
        hot = jnp.where(self.meta_turned[32:33, :] == place, 1.0, 0.0).astype(BF)
        for r in range(4):
            for i in range(2):
                start = (2 * r + i) * LANES
                low = IMG_T + 24 * i
                self.small[r % 2, r // 2, low : low + 24, :] = product(
                    hot, self.img_right[:, start : start + LANES]
                )


class SmallSum:
    def __init__(self, places, f):
        self.places, self.f = (places, f)
        self.copies = []

    def step(self, k):
        f, places = (self.f, self.places)
        if k > 0:
            self.copies[k - 1].wait()
        if k == 0:
            source, target, device = (f.small.at[1 - places.c], f.small_pair, places.to_c)
        elif k == 1:
            f.small_pair[...] = f.small_pair[...] + f.small[places.c]
            source, target, device = (
                f.small_pair.at[1 - places.y], f.small_in.at[0], places.to_y,
            )
        else:
            if k == 2:
                f.small_sum[...] = f.small_pair[places.y] + f.small_in[0]
            else:
                f.small_sum[...] = f.small_sum[...] + f.small_in[k - 2]
            if k == 5:
                return
            device = (places.to_x, places.to_z, places.to_w)[k - 2]
            source, target = (f.small_sum, f.small_in.at[k - 1])
        copy = send_to(source, target, f.small_send.at[k], f.small_recv.at[k], device)
        copy.start()
        self.copies.append(copy)


def last_kernel(f):
    places = Places()
    load = pltpu.make_async_copy(f.gru_share, f.gru_weight, f.load_done.at[0])
    load.start()
    greet(
        (places.to_c, places.to_y, places.to_d, places.to_x, places.to_z, places.to_w)
    )
    worker = Addition(
        places, f.worker_own, f.worker_sibling, f.add_send, f.add_recv, f.add_local
    )
    worker.start(f.worker_left, 1)
    worker.start(f.worker_left, 0)
    sources, part = ([worker], 0)
    for i, source in enumerate(LAST_SOURCES[1:]):
        sources.append(
            Exchange(
                places, source, f.left_2[i], f.right_2[i], f.pair_send, f.pair_recv,
                f.pair_local, part,
            )
        )
        part += len(source.parts)
    gru = Wide(
        places, H // 2, ROWS, f.gru_left_4, f.gru_right_4, f.wide_send, f.wide_recv, f.wide_local
    )
    sources.append(gru)
    gru.start_left(f.gru_left)
    sources[LAST_GOAL_OUT].start(0, f.goal_left, f.goal_right)
    sources[LAST_GOAL_OUT].start(1, f.dec_left, f.recon_low)
    sources[LAST_GOAL_IN].start(0, f.code_turned, f.goal_pair)
    sources[LAST_GOAL_IN].start(1, f.soft_turned, f.dec_pair)
    sources[LAST_IMG].start_left(0, f.img_left)
    halving = Halving(
        places, [(sources[unit[0]],) + unit[1:] for unit in LAST_UNITS], f.outbox, f.inbox,
        f.half_send, f.half_recv, f.sums, LAST_GROUPS,
    )
    f.small[...] = f.small_1[...] + f.small_2[...]
    f.state_back()
    gru.start_right(f.gru_right)
    halving.slot(0)
    load.wait()
    f.input_back()
    sources[LAST_IMG].start_right(0, f.img_right)
    halving.slot(1)
    f.action_back()
    small = SmallSum(places, f)
    small.step(0)
    gru.relay()
    for t in range(2, len(LAST_GROUPS) + 4):
        halving.slot(t)
        if t < 7:
            small.step(t - 1)
    halving.drain()


class Unpack(NamedTuple):
    heads: Any = tuple(taken(unit[-1], LANES, dtype=F32) for unit in HEAD_UNITS)
    last: Any = tuple(taken(unit[-1], LANES, dtype=F32) for unit in LAST_UNITS)
    small: Any = taken(SMALL_TILES, LANES, dtype=F32)
    deter: Any = taken(ROWS, H, dtype=F32)
    embed: Any = taken(ROWS, E, dtype=F32)
    loss: Any = given(1, LANES, dtype=F32)
    deter_grad: Any = given(ROWS, H, dtype=F32)
    embed_grad: Any = given(ROWS, E, dtype=F32)
    obs_gain: Any = given(H // 4, dtype=F32)
    manager_in: Any = given(U // 8, H // 4, dtype=F32)
    manager_gain: Any = given(U // 4, dtype=F32)
    manager_out: Any = given(U // 4, dtype=F32)
    goal_in: Any = given(GCODE // 4, U // 8, dtype=F32)
    goal_gain: Any = given(U // 4, dtype=F32)
    goal_out: Any = given(U // 4, H // 8, dtype=F32)
    actor_in: Any = given(U // 8, 3 * H // 4, dtype=F32)
    actor_gain: Any = given(U // 4, dtype=F32)
    actor_out: Any = given(NA, U // 4, dtype=F32)
    critic_in: Any = given(U // 8, 3 * H // 4, dtype=F32)
    critic_gain: Any = given(U // 4, dtype=F32)
    critic_out: Any = given(U // 4, dtype=F32)
    img_stoch: Any = given(Z // 4, H // 8, dtype=F32)
    img_action: Any = given(NA, H // 4, dtype=F32)
    img_gain: Any = given(H // 4, dtype=F32)
    gru_weight: Any = given(H // 2, 3 * H // 8, dtype=F32)
    gru_gain: Any = given(3 * H // 4, dtype=F32)
    post_in: Any = given((H + E) // 4, H // 8, dtype=F32)
    post_gain: Any = given(H // 4, dtype=F32)
    post_out: Any = given(H // 4, Z // 8, dtype=F32)
    prior_in: Any = given(H // 4, H // 8, dtype=F32)
    prior_gain: Any = given(H // 4, dtype=F32)
    prior_out: Any = given(H // 4, Z // 8, dtype=F32)
    enc_in: Any = given(U // 8, H // 4, dtype=F32)
    enc_gain: Any = given(U // 4, dtype=F32)
    enc_out: Any = given(GCODE, U // 4, dtype=F32)


def unpack_kernel(f):
    f.loss[...] = f.small[LOSS : LOSS + 1, :]
    f.deter_grad[...] = f.deter[...]
    f.embed_grad[...] = f.embed[...]
    for low, vector in (
        (OBS, f.obs_gain), (MAN_G, f.manager_gain), (MAN_O, f.manager_out),
        (GOAL_G, f.goal_gain), (ACT_G, f.actor_gain), (CRI_G, f.critic_gain),
        (CRI_O, f.critic_out), (IMG_G, f.img_gain), (GRU_G, f.gru_gain), (POST_G, f.post_gain),
        (PRIOR_G, f.prior_gain), (ENC_G, f.enc_gain),
    ):
        for i in range(vector.shape[0] // LANES):
            vector[pl.ds(i * LANES, LANES)] = f.small[low + i, :]
    f.actor_out[...] = f.small[ACT_T : ACT_T + NA, :]
    f.enc_out[...] = f.small[ENC_T : ENC_T + GCODE, :]
    for i in range(2):
        f.img_action[:, i * LANES : (i + 1) * LANES] = f.small[
            IMG_T + 24 * i : IMG_T + 24 * i + NA, :
        ]

    def halves(value, rows, first, second):
        for low in range(0, value.shape[0], LANES):
            turned = value[low : low + LANES, :].T
            places = slice(rows.start + low, rows.start + low + LANES)
            first[:, places] = turned[0:64]
            second[:, places] = turned[64:LANES]

    whole = {
        HEAD_POST: f.post_in, HEAD_PRIOR: f.prior_in, HEAD_POST_OUT: f.post_out,
        HEAD_PRIOR_OUT: f.prior_out,
    }
    for unit, value in zip(HEAD_UNITS, f.heads):
        rows = slice(unit[4], unit[4] + unit[5])
        if unit[0] == HEAD_MAN_ENC:
            halves(value, rows, f.manager_in, f.enc_in)
        else:
            whole[unit[0]][rows, :] = value[...]
    whole = {LAST_GOAL_OUT: f.goal_out, LAST_IMG: f.img_stoch}
    for unit, value in zip(LAST_UNITS, f.last):
        rows = slice(unit[4], unit[4] + unit[5])
        if unit[0] == LAST_WORKER:
            halves(value, rows, f.actor_in, f.critic_in)
        elif unit[0] == LAST_GOAL_IN:
            f.goal_in[...] = value[:, 0:64]
        elif unit[0] == LAST_GRU:
            f.gru_weight[rows, unit[2] : unit[2] + LANES] = value[...]
        else:
            whole[unit[0]][rows, :] = value[...]


class Weights(NamedTuple):
    obs_gain: Any = None
    manager_in: Any = None
    manager_gain: Any = None
    manager_out: Any = None
    goal_in: Any = None
    goal_gain: Any = None
    goal_out: Any = None
    actor_in: Any = None
    actor_gain: Any = None
    actor_out: Any = None
    critic_in: Any = None
    critic_gain: Any = None
    critic_out: Any = None
    img_stoch: Any = None
    img_action: Any = None
    img_gain: Any = None
    gru_weight: Any = None
    gru_gain: Any = None
    post_in: Any = None
    post_gain: Any = None
    post_out: Any = None
    prior_in: Any = None
    prior_gain: Any = None
    prior_out: Any = None
    enc_in: Any = None
    enc_gain: Any = None
    enc_out: Any = None


class Data(NamedTuple):
    deter_states: Any
    embed: Any
    lengths: Any
    resets: Any
    terminal: Any
    rewards: Any
    prev_stoch: Any
    prev_action: Any
    regroup: Any
    goal_codes: Any
    samples: Any
    actions: Any


def step_in_kernels(data, w):
    prev = data.deter_states.reshape(ROWS, H)
    f = run_kernel(
        frames_kernel, Frames(),
        (
            data.lengths, data.resets, data.terminal, data.rewards,
            data.prev_stoch.transpose(0, 2, 1), data.prev_action, data.regroup, prev,
            data.embed.reshape(ROWS, E), w.obs_gain, w.manager_gain, w.manager_out, w.goal_gain,
            w.actor_gain, w.critic_gain, w.critic_out, w.img_gain, w.gru_gain, w.post_gain,
            w.prior_gain, w.enc_gain, w.actor_out.T, w.enc_out.T, w.img_action, w.goal_in,
            w.img_stoch, w.gru_weight, w.manager_in, w.enc_in, w.goal_out, w.prior_in, w.post_in,
            w.prior_out, w.post_out, w.actor_in, w.critic_in,
        ),
        "frames", 0,
    )
    s = run_kernel(
        worker_kernel, Worker(),
        (
            data.goal_codes.T, data.actions.T, data.samples.transpose(1, 2, 0), f.vectors,
            f.tables, f.start_state, f.goal_out_out, f.actor_in_out, f.critic_in_out, f.post_left,
            f.post_out_left, f.prior_out_left, f.me_left, f.post_right, f.prior_right,
            f.post_out_right, f.prior_out_right, f.me_right,
        ),
        "worker", 1,
    )
    b = run_kernel(
        last_kernel, Last(),
        (
            f.meta_turned, prev, f.vectors, s.returned, f.grad_deter, f.gru_normed, f.gru_inverse,
            f.img_normed, f.img_inverse, f.small, s.small, f.gru_weight_out, s.worker_left,
            s.goal_left, f.dec_left, s.code_turned, f.soft_turned, f.gru_left, f.img_left,
            s.goal_right, f.recon_low, s.goal_pair, f.dec_pair,
        ),
        "last", 2,
    )
    u = run_kernel(
        unpack_kernel, Unpack(),
        tuple(s.sums) + tuple(b.sums) + (b.small_sum, b.deter_grad, f.embed_grad),
        "unpack",
    )
    first = len(Unpack._fields) - len(Weights._fields)
    grads = Weights(*tuple(u)[first:])
    grads = grads._replace(
        manager_in=grads.manager_in.T, actor_in=grads.actor_in.T, critic_in=grads.critic_in.T,
        enc_in=grads.enc_in.T, actor_out=grads.actor_out.T, enc_out=grads.enc_out.T,
    )
    return (
        u.loss[0, 0],
        u.deter_grad.reshape(SEQ_DEV, LEN, H),
        u.embed_grad.reshape(SEQ_DEV, LEN, E),
    ) + tuple(grads)


DP, REP = ("dp", "rep")
IMG_ACTION = 14
LARGE = Weights(**dict.fromkeys(Weights._fields, False))._replace(
    manager_in=True,
    goal_in=True,
    goal_out=True,
    actor_in=True,
    critic_in=True,
    img_stoch=True,
    gru_weight=True,
    post_in=True,
    post_out=True,
    prior_in=True,
    prior_out=True,
    enc_in=True,
)


def hidden_forward(pre_act, scaling):
    normed, inverse = normalize(pre_act)
    scaled = normed * scaling
    return ((normed, inverse, scaled), jax.nn.elu(scaled).astype(jnp.bfloat16))


def hidden_backward(grad_hidden, cache, scaling):
    normed, inverse, scaled = cache
    grad_scaled = grad_hidden * jnp.where(scaled > 0, 1.0, jnp.exp(jnp.minimum(scaled, 0.0)))
    grad_gain = jnp.sum(grad_scaled * normed, tuple(range(scaled.ndim - 1)))
    return (normalize_back(grad_scaled * scaling, normed, inverse).astype(jnp.bfloat16), grad_gain)


def input_backward(grad_pre, input_low, weight):
    grad_weight = jnp.einsum("nk,nu->ku", input_low, grad_pre, preferred_element_type=jnp.float32)
    to_input = jnp.einsum("nu,ku->nk", grad_pre, weight, preferred_element_type=jnp.float32)
    return (grad_weight, to_input)


def head_backward(grad_head, hidden_low, head, cache, scaling):
    grad_weight = jnp.einsum("nu,nk->uk", hidden_low, grad_head, preferred_element_type=jnp.float32)
    grad_hidden = jnp.einsum("nk,uk->nu", grad_head, head, preferred_element_type=jnp.float32)
    grad_pre, grad_gain = hidden_backward(grad_hidden, cache, scaling)
    return (grad_weight, grad_pre, grad_gain)


def group_softmax(flat_logits, groups):
    log_part = jax.nn.log_softmax(flat_logits.reshape(flat_logits.shape[0], groups, -1), axis=-1)
    return (log_part, jnp.exp(log_part))


def chain_returns(values_now, rewards_now, linked, carried):

    def back_step(carry_pair, inputs):
        later_return, later_value = carry_pair
        current, reward_now, link_now, carry_now = inputs
        blended = (1.0 - return_mix) * later_value + return_mix * later_return
        result = jnp.where(link_now, reward_now + discount * carry_now * blended, current)
        return ((result, current), result)

    zero_start = jnp.zeros(values_now.shape[:1], jnp.float32)
    _, stacked = lax.scan(
        back_step,
        (zero_start, zero_start),
        (values_now.T, rewards_now.T, linked.T, carried.T),
        reverse=True,
    )
    return stacked.T


def worker_forward(start_state, goal_low, stoch_hot, first_layer, scaling):
    slot_part = product(start_state, first_layer[:H]) + product(goal_low, first_layer[H + Z :])
    varying = product(stoch_hot, first_layer[H : H + Z]).reshape(start_state.shape[0], HOR, U)
    return hidden_forward(slot_part[:, None, :] + varying, scaling)


def worker_backward(grad_pre, start_state, goal_low, stoch_hot, first_layer):
    slot_count = grad_pre.shape[0]
    grad_stoch = jnp.einsum(
        "nz,nu->zu",
        stoch_hot,
        grad_pre.reshape(slot_count * HOR, U),
        preferred_element_type=jnp.float32,
    )
    summed = jnp.sum(grad_pre, 1, dtype=jnp.float32).astype(jnp.bfloat16)
    grad_state_rows, to_state = input_backward(summed, start_state, first_layer[:H])
    grad_goal_rows, to_goal = input_backward(summed, goal_low, first_layer[H + Z :])
    return (jnp.concatenate([grad_state_rows, grad_stoch, grad_goal_rows], 0), to_state, to_goal)


def step_plain(data, shares):
    (deter_states, embed, lengths, resets, terminal, rewards, prev_stoch, prev_action, regroup, goal_codes, samples, actions) = data
    full = [
        lax.all_gather(share, REP, axis=1 if i == IMG_ACTION else 0, tiled=True)
        for i, share in enumerate(shares)
    ]
    (obs_gain, manager_in, manager_gain, manager_out, goal_in, goal_gain, goal_out, actor_in, actor_gain, actor_out, critic_in, critic_gain, critic_out, img_stoch, img_action, img_gain, gru_weight, gru_gain, post_in, post_gain, post_out, prior_in, prior_gain, prior_out, enc_in, enc_gain, enc_out) = full
    prev_low = deter_states.reshape(ROWS, H)
    prev_float = prev_low.astype(jnp.float32)
    embed_low = embed.reshape(ROWS, E)
    positions = lax.broadcasted_iota(jnp.int32, (SEQ_DEV, LEN), 1)
    is_valid = positions < lengths[:, None]
    next_valid = jnp.concatenate([is_valid[:, 1:], jnp.zeros((SEQ_DEV, 1), jnp.bool_)], 1)
    next_reset = jnp.concatenate([resets[:, 1:], jnp.ones((SEQ_DEV, 1), jnp.int32)], 1)
    linked = next_valid & (next_reset == 0)
    carried = 1.0 - terminal.astype(jnp.float32)
    valid_rows = is_valid.astype(jnp.float32).reshape(ROWS)
    frame_scale = valid_rows / ROWS
    stoch_prev_hot = (
        (prev_stoch[..., None] == lax.broadcasted_iota(jnp.int32, (1, 1, 1, ZK), 3))
        .astype(jnp.bfloat16)
        .reshape(ROWS, Z)
    )
    action_prev_hot = (
        prev_action.reshape(ROWS)[:, None] == lax.broadcasted_iota(jnp.int32, (1, NA), 1)
    ).astype(jnp.bfloat16)
    img_cache, img_hidden = hidden_forward(
        product(stoch_prev_hot, img_stoch) + product(action_prev_hot, img_action), img_gain
    )
    gru_input = jnp.concatenate([img_hidden, prev_low], 1)
    gru_normed, gru_inverse = normalize(product(gru_input, gru_weight))
    gru_parts = gru_normed * gru_gain
    reset_gate = jax.nn.sigmoid(gru_parts[:, :H])
    candidate_in = gru_parts[:, H : 2 * H]
    candidate = jnp.tanh(reset_gate * candidate_in)
    update_gate = jax.nn.sigmoid(gru_parts[:, 2 * H :] - 1.0)
    deter_state = update_gate * candidate + (1.0 - update_gate) * prev_float
    deter_low = deter_state.astype(jnp.bfloat16)
    obs_normed, obs_inverse = normalize(deter_state)
    feature = (obs_normed * obs_gain).astype(jnp.bfloat16)
    man_cache, man_hidden = hidden_forward(product(feature, manager_in), manager_gain)
    manager_value = product(man_hidden, manager_out).reshape(SEQ_DEV, LEN)
    manager_return = chain_returns(manager_value, rewards, linked, carried)
    manager_misfit = (manager_value - manager_return).reshape(ROWS)
    post_input = jnp.concatenate([deter_low, embed_low], 1)
    post_cache, post_hidden = hidden_forward(product(post_input, post_in), post_gain)
    post_log, post_prob = group_softmax(product(post_hidden, post_out), ZG)
    prior_cache, prior_hidden = hidden_forward(product(deter_low, prior_in), prior_gain)
    prior_log, prior_prob = group_softmax(product(prior_hidden, prior_out), ZG)
    log_gap = post_log - prior_log
    group_kl = jnp.sum(post_prob * log_gap, -1, keepdims=True)
    enc_cache, enc_hidden = hidden_forward(product(deter_low, enc_in), enc_gain)
    code_log, code_prob = group_softmax(product(enc_hidden, enc_out), GC)
    code_kl = jnp.sum(code_prob * (code_log + math.log(GK)), (1, 2))
    code_spread = jnp.sum(code_prob * code_log, -1, keepdims=True)
    soft_code = code_prob.reshape(ROWS, GCODE).astype(jnp.bfloat16)
    dec_cache, dec_hidden = hidden_forward(product(soft_code, goal_in), goal_gain)
    recon_err = product(dec_hidden, goal_out) - deter_state
    frame_terms = (
        jnp.sum(post_prob * log_gap, (1, 2)) + code_kl + 0.5 * jnp.mean(recon_err * recon_err, -1)
    )
    frame_loss = jnp.sum(valid_rows * (0.5 * manager_misfit * manager_misfit + frame_terms)) / ROWS
    send_order = regroup[0]
    start_state, slot_flag = (
        lax.all_to_all(deter_low[send_order], DP, split_axis=0, concat_axis=0, tiled=True),
        lax.all_to_all(
            valid_rows[send_order].astype(jnp.bfloat16),
            DP,
            split_axis=0,
            concat_axis=0,
            tiled=True,
        ),
    )
    slot_weight = slot_flag.astype(jnp.float32)
    code_hot = (
        (goal_codes[:, :, None] == lax.broadcasted_iota(jnp.int32, (1, 1, GK), 2))
        .astype(jnp.bfloat16)
        .reshape(ROWS, GCODE)
    )
    goal_cache, goal_hidden = hidden_forward(product(code_hot, goal_in), goal_gain)
    goal_vector = product(goal_hidden, goal_out)
    goal_low = goal_vector.astype(jnp.bfloat16)
    state_float = start_state.astype(jnp.float32)
    alignment = jnp.sum(goal_vector * state_float, -1)
    largest_square = (
        jnp.maximum(jnp.sum(goal_vector * goal_vector, -1), jnp.sum(state_float * state_float, -1))
        + small_floor
    )
    reward_slot = alignment / largest_square
    stoch_hot = (
        (samples[..., None] == lax.broadcasted_iota(jnp.int32, (1, 1, 1, ZK), 3))
        .astype(jnp.bfloat16)
        .reshape(ROWS * HOR, Z)
    )
    action_hot = (actions[..., None] == lax.broadcasted_iota(jnp.int32, (1, 1, NA), 2)).astype(
        jnp.float32
    )
    actor_cache, actor_hidden = worker_forward(
        start_state, goal_low, stoch_hot, actor_in, actor_gain
    )
    logits = jnp.einsum("rku,ua->rka", actor_hidden, actor_out, preferred_element_type=jnp.float32)
    log_chance = jax.nn.log_softmax(logits, axis=-1)
    chosen = jnp.sum(log_chance * action_hot, -1)
    critic_cache, critic_hidden = worker_forward(
        start_state, goal_low, stoch_hot, critic_in, critic_gain
    )
    worker_value = jnp.einsum(
        "rku,u->rk", critic_hidden, critic_out, preferred_element_type=jnp.float32
    )
    step_link = lax.broadcasted_iota(jnp.int32, (ROWS, HOR), 1) < HOR - 1
    worker_return = chain_returns(
        worker_value,
        jnp.broadcast_to(reward_slot[:, None], (ROWS, HOR)),
        step_link,
        jnp.ones((ROWS, HOR), jnp.float32),
    )
    advantage = worker_return - worker_value
    local_top = jnp.max(slot_weight[:, None] * jnp.abs(advantage))
    return_scale = lax.pmax(local_top, (DP, REP)) + small_floor
    step_total = ROWS * HOR
    value_misfit = worker_value - worker_return
    critic_part = 0.5 * jnp.sum(slot_weight[:, None] * value_misfit * value_misfit)
    actor_part = jnp.sum(slot_weight[:, None] * chosen * advantage) / return_scale
    local_loss = frame_loss + (critic_part - actor_part) / step_total
    grad_value = slot_weight[:, None] * value_misfit / step_total
    grad_chosen = -slot_weight[:, None] * advantage / return_scale / step_total
    grad_logits = (grad_chosen[..., None] * (action_hot - jnp.exp(log_chance))).astype(jnp.bfloat16)
    grad_actor_out = jnp.einsum(
        "rku,rka->ua", actor_hidden, grad_logits, preferred_element_type=jnp.float32
    )
    grad_actor_hidden = jnp.einsum(
        "rka,ua->rku", grad_logits, actor_out, preferred_element_type=jnp.float32
    )
    actor_pre, grad_actor_gain = hidden_backward(grad_actor_hidden, actor_cache, actor_gain)
    grad_critic_out = jnp.einsum("rku,rk->u", critic_hidden, grad_value, precision=highest)
    critic_pre, grad_critic_gain = hidden_backward(
        grad_value[..., None] * critic_out, critic_cache, critic_gain
    )
    grad_actor_in, actor_to_state, actor_to_goal = worker_backward(
        actor_pre, start_state, goal_low, stoch_hot, actor_in
    )
    grad_critic_in, critic_to_state, critic_to_goal = worker_backward(
        critic_pre, start_state, goal_low, stoch_hot, critic_in
    )
    grad_goal_low = (actor_to_goal + critic_to_goal).astype(jnp.bfloat16)
    worker_goal_out, goal_pre, worker_goal_gain = head_backward(
        grad_goal_low, goal_hidden, goal_out, goal_cache, goal_gain
    )
    worker_goal_in = jnp.einsum("ng,nu->gu", code_hot, goal_pre, preferred_element_type=jnp.float32)
    returned = lax.all_to_all(
        (actor_to_state + critic_to_state).astype(jnp.bfloat16),
        DP,
        split_axis=0,
        concat_axis=0,
        tiled=True,
    )
    grad_manager_value = frame_scale * manager_misfit
    grad_manager_out = jnp.dot(grad_manager_value, man_hidden, precision=highest)
    manager_pre, grad_manager_gain = hidden_backward(
        grad_manager_value[:, None] * manager_out, man_cache, manager_gain
    )
    grad_manager_in, grad_feature = input_backward(manager_pre, feature, manager_in)
    grad_obs_gain = jnp.sum(grad_feature * obs_normed, 0)
    obs_back = normalize_back(grad_feature * obs_gain, obs_normed, obs_inverse)
    weight_cube = frame_scale[:, None, None]
    post_grad_logits = (
        (weight_cube * post_prob * (log_gap - group_kl)).reshape(ROWS, Z).astype(jnp.bfloat16)
    )
    prior_grad_logits = (
        (weight_cube * (prior_prob - post_prob)).reshape(ROWS, Z).astype(jnp.bfloat16)
    )
    grad_post_out, post_pre, grad_post_gain = head_backward(
        post_grad_logits, post_hidden, post_out, post_cache, post_gain
    )
    grad_post_in, post_back = input_backward(post_pre, post_input, post_in)
    grad_prior_out, prior_pre, grad_prior_gain = head_backward(
        prior_grad_logits, prior_hidden, prior_out, prior_cache, prior_gain
    )
    grad_prior_in, prior_back = input_backward(prior_pre, deter_low, prior_in)
    recon_grad = frame_scale[:, None] * recon_err / H
    dec_goal_out, dec_pre, dec_goal_gain = head_backward(
        recon_grad.astype(jnp.bfloat16), dec_hidden, goal_out, dec_cache, goal_gain
    )
    dec_goal_in, grad_code = input_backward(dec_pre, soft_code, goal_in)
    grad_code = grad_code.reshape(ROWS, GC, GK)
    code_grad_logits = code_prob * (
        grad_code - jnp.sum(code_prob * grad_code, -1, keepdims=True)
    ) + weight_cube * code_prob * (code_log - code_spread)
    grad_enc_out, enc_pre, grad_enc_gain = head_backward(
        code_grad_logits.reshape(ROWS, GCODE).astype(jnp.bfloat16),
        enc_hidden,
        enc_out,
        enc_cache,
        enc_gain,
    )
    grad_enc_in, enc_back = input_backward(enc_pre, deter_low, enc_in)
    grad_goal_out = worker_goal_out + dec_goal_out
    grad_goal_in = worker_goal_in + dec_goal_in
    grad_goal_gain = worker_goal_gain + dec_goal_gain
    scattered = jnp.zeros((ROWS, H), jnp.float32).at[send_order].add(returned.astype(jnp.float32))
    grad_deter = obs_back + post_back[:, :H] + prior_back + enc_back + scattered - recon_grad
    grad_inner = grad_deter * update_gate * (1.0 - candidate * candidate)
    grad_parts = jnp.concatenate(
        [
            grad_inner * candidate_in * reset_gate * (1.0 - reset_gate),
            grad_inner * reset_gate,
            grad_deter * (candidate - prev_float) * update_gate * (1.0 - update_gate),
        ],
        1,
    )
    grad_gru_gain = jnp.sum(grad_parts * gru_normed, 0)
    gru_pre = normalize_back(grad_parts * gru_gain, gru_normed, gru_inverse).astype(jnp.bfloat16)
    grad_gru_weight, gru_back = input_backward(gru_pre, gru_input, gru_weight)
    img_pre, grad_img_gain = hidden_backward(gru_back[:, :H], img_cache, img_gain)
    grad_img_stoch = jnp.einsum(
        "nz,nh->zh", stoch_prev_hot, img_pre, preferred_element_type=jnp.float32
    )
    grad_img_action = jnp.einsum(
        "na,nh->ah", action_prev_hot, img_pre, preferred_element_type=jnp.float32
    )
    grad_prev = grad_deter * (1.0 - update_gate) + gru_back[:, H:]
    embed_grad = post_back[:, H:]
    count = lax.axis_size(REP)
    loss_share = lax.psum_scatter(
        jnp.full((count,), local_loss), REP, scatter_dimension=0, tiled=True
    )
    grads = Weights(
        obs_gain=grad_obs_gain,
        manager_in=grad_manager_in,
        manager_gain=grad_manager_gain,
        manager_out=grad_manager_out,
        goal_in=grad_goal_in,
        goal_gain=grad_goal_gain,
        goal_out=grad_goal_out,
        actor_in=grad_actor_in,
        actor_gain=grad_actor_gain,
        actor_out=grad_actor_out,
        critic_in=grad_critic_in,
        critic_gain=grad_critic_gain,
        critic_out=grad_critic_out,
        img_stoch=grad_img_stoch,
        img_action=grad_img_action,
        img_gain=grad_img_gain,
        gru_weight=grad_gru_weight,
        gru_gain=grad_gru_gain,
        post_in=grad_post_in,
        post_gain=grad_post_gain,
        post_out=grad_post_out,
        prior_in=grad_prior_in,
        prior_gain=grad_prior_gain,
        prior_out=grad_prior_out,
        enc_in=grad_enc_in,
        enc_gain=grad_enc_gain,
        enc_out=grad_enc_out,
    )
    shares = []
    for i, (grad, by_column) in enumerate(zip(grads, LARGE)):
        grad = lax.psum_scatter(
            grad, REP, scatter_dimension=1 if i == IMG_ACTION else 0, tiled=True
        )
        if by_column:
            shares.append(lax.psum_scatter(grad, DP, scatter_dimension=1, tiled=True))
        else:
            shares.append(lax.psum(grad, DP))
    return (
        lax.psum(loss_share, DP)[0],
        grad_prev.reshape(SEQ_DEV, LEN, H),
        embed_grad.reshape(SEQ_DEV, LEN, E),
    ) + tuple(shares)


def solution(mesh):
    split, over_rep = (P((DP, REP)), P(REP))
    in_kernels = mesh.shape[DP] == 8 and mesh.shape[REP] == 4

    def per_device(*arguments):
        data, shares = (Data(*arguments[:12]), Weights(*arguments[12:]))
        return (step_in_kernels if in_kernels else step_plain)(data, shares)

    in_specs, out_specs = ((split,) * 12, (P(), split, split))
    for i, by_column in enumerate(LARGE):
        spec = P(None, REP) if i == IMG_ACTION else over_rep
        in_specs += (spec,)
        out_specs += (P(REP, DP) if by_column else spec,)
    return jax.shard_map(
        per_device, mesh=mesh, in_specs=in_specs, out_specs=out_specs, check_vma=False
    )
```

```python
import math
from typing import Any, NamedTuple

import jax
import jax.numpy as jnp
from jax import lax
from jax.experimental import pallas as pl
from jax.experimental.pallas import tpu as pltpu
from jax.sharding import PartitionSpec as P

H = 1024
ZG = 32
ZK = 32
U = 512
GC = 8
GK = 8
NA = 17
E = 1536
LEN = 64
HOR = 16
SEQ_DEV = 2
Z = 1024
GCODE = 64
ROWS = 128


discount = 0.99
return_mix = 0.95
epsilon = 1e-05
small_floor = 1e-06
highest = lax.Precision.HIGHEST


MESH = pl.DeviceIdType.MESH
BF = jnp.bfloat16
F32 = jnp.float32
LANES = 128
VMEM_BYTES = 62 * 2**20
TILE = 512


class Arg(NamedTuple):
    kind: Any
    shape: Any
    dtype: Any
    here: bool = True


TAKEN, GIVEN, KEPT, SIGNAL = range(4)


def taken(*shape, dtype=BF, here=True):
    return Arg(TAKEN, shape, dtype, here)


def given(*shape, dtype=BF, here=True):
    return Arg(GIVEN, shape, dtype, here)


def kept(*shape, dtype=BF):
    return Arg(KEPT, shape, dtype)


def signal(*shape):
    return Arg(SIGNAL, shape, None)


def run_kernel(body, layout, inputs, name, collective=None):
    leaves, tree = jax.tree.flatten(layout, is_leaf=lambda a: isinstance(a, Arg))

    def kernel(*refs):
        body(jax.tree.unflatten(tree, refs))

    def place(arg):
        return pl.BlockSpec(memory_space=pltpu.VMEM if arg.here else pl.ANY)

    outs = [a for a in leaves if a.kind == GIVEN]
    more = {} if collective is None else dict(collective_id=collective, has_side_effects=True)
    results = pl.pallas_call(
        kernel,
        out_shape=[jax.ShapeDtypeStruct(a.shape, a.dtype) for a in outs],
        in_specs=[place(a) for a in leaves if a.kind == TAKEN],
        out_specs=[place(a) for a in outs],
        scratch_shapes=[
            pltpu.VMEM(a.shape, a.dtype) if a.kind == KEPT else pltpu.SemaphoreType.DMA(a.shape)
            for a in leaves
            if a.kind >= KEPT
        ],
        compiler_params=pltpu.CompilerParams(vmem_limit_bytes=VMEM_BYTES, **more),
        name=name,
    )(*inputs)
    results = iter(results)
    return jax.tree.unflatten(
        tree, [next(results) if a.kind == GIVEN else None for a in leaves]
    )


def product(left, right):
    return jnp.dot(left, right, preferred_element_type=jnp.float32)


def normalize(values_in):
    row_mean = jnp.mean(values_in, -1, keepdims=True)
    centred = values_in - row_mean
    inverse = lax.rsqrt(jnp.mean(centred * centred, -1, keepdims=True) + epsilon)
    return (centred * inverse, inverse)


def normalize_back(grad_normed, normed, inverse):
    return inverse * (
        grad_normed
        - jnp.mean(grad_normed, -1, keepdims=True)
        - normed * jnp.mean(grad_normed * normed, -1, keepdims=True)
    )


def matmul_into(out_ref, left, weight_ref, turned=False, tile=TILE, low=0, extra=None):
    total = out_ref.shape[-1]

    def one(j, carry):
        start = pl.multiple_of(j * tile, tile)
        if turned:
            value = lax.dot_general(
                left,
                weight_ref[pl.ds(pl.multiple_of(low + j * tile, tile), tile), :],
                (((1,), (1,)), ((), ())),
                preferred_element_type=F32,
            )
        else:
            value = product(left, weight_ref[:, pl.ds(start, tile)])
        if extra is not None:
            value = value + extra(start, tile)
        out_ref[:, pl.ds(start, tile)] = value
        return carry

    lax.fori_loop(0, total // tile, one, 0)


def by_rows(count, size, body, carry=0):
    def one(i, carry):
        return body(pl.ds(pl.multiple_of(i * size, size), size), carry)

    return lax.fori_loop(0, count // size, one, carry)


def elu_of(value):
    return jnp.where(value > 0, value, jnp.exp(jnp.minimum(value, 0.0)) - 1.0)


def normalize_rows(ref, inverse_ref, size):
    def one(rows, carry):
        normed, inverse = normalize(ref[rows, :])
        ref[rows, :] = normed
        inverse_ref[rows, :] = inverse
        return carry

    by_rows(ref.shape[0], size, one)


def hidden_rows(ref, inverse_ref, gain, hidden_ref, size=128):
    def one(rows, carry):
        normed, inverse = normalize(ref[rows, :])
        ref[rows, :] = normed
        inverse_ref[rows, :] = inverse
        hidden_ref[rows, :] = elu_of(normed * gain).astype(BF)
        return carry

    by_rows(ref.shape[0], size, one)


def hidden_rows_back(grad_of, ref, inverse_ref, gain, pre_ref, size=128, hidden_ref=None):
    def one(rows, total):
        normed = ref[rows, :]
        scaled = normed * gain
        power = jnp.exp(jnp.minimum(scaled, 0.0))
        if hidden_ref is not None:
            hidden_ref[rows, :] = jnp.where(scaled > 0, scaled, power - 1.0).astype(BF)
        grad_scaled = grad_of(rows) * jnp.where(scaled > 0, 1.0, power)
        total = total + jnp.sum(grad_scaled * normed, 0, keepdims=True)
        back = normalize_back(grad_scaled * gain, normed, inverse_ref[rows, :])
        pre_ref[rows, :] = back.astype(pre_ref.dtype)
        return total

    return by_rows(ref.shape[0], size, one, jnp.zeros((1, ref.shape[1]), F32))


def turn_into(out_ref, value_ref, low=0):
    for j in range(value_ref.shape[1] // LANES):
        tile = value_ref[:, j * LANES : (j + 1) * LANES].astype(F32).T
        out_ref[low + j * LANES : low + (j + 1) * LANES, :] = tile.astype(out_ref.dtype)


def class_spread(groups, classes, rows, width):
    group = lax.broadcasted_iota(jnp.int32, (rows, width), 0)
    lane = lax.broadcasted_iota(jnp.int32, (rows, width), 1)
    inside = (lane >= group * classes) & (lane < group * classes + classes) & (group < groups)
    return jnp.where(inside, 1.0, 0.0).astype(BF)


def hot_rows(ids, classes, groups, width):
    here = product(ids.astype(BF), class_spread(groups, classes, ids.shape[1], width))
    lane = lax.broadcasted_iota(jnp.int32, (1, width), 1)
    same = here == jnp.bitwise_and(lane, classes - 1).astype(F32)
    return jnp.where(same & (lane < groups * classes), 1.0, 0.0)


def columns_of(rows):
    count = rows.shape[0]
    return jnp.concatenate([rows, jnp.zeros((LANES - count, rows.shape[1]), F32)], 0).T


def vector_of(packed, low, tiles):
    return jnp.concatenate(
        [packed[r, low + i : low + i + 1, :] for r in range(4) for i in range(tiles)], 1
    )


def put_vector(small_ref, low, value):
    tiles = value.shape[1] // (4 * LANES)
    for r in range(4):
        for i in range(tiles):
            start = (r * tiles + i) * LANES
            small_ref[r % 2, r // 2, low + i : low + i + 1, :] = value[:, start : start + LANES]


def put_table(small_ref, low, value, rows):
    for r in range(4):
        small_ref[r % 2, r // 2, low : low + rows, :] = value[
            0:rows, r * LANES : (r + 1) * LANES
        ]


OBS, MAN_G, MAN_O, GOAL_G, ACT_G, CRI_G, CRI_O, IMG_G, GRU_G, POST_G, PRIOR_G, ENC_G, LOSS = (
    0, 2, 3, 4, 5, 6, 7, 8, 10, 16, 18, 20, 21,
)
ACT_T, ENC_T, IMG_T, SMALL_TILES = (24, 48, 112, 160)
TAB_ACT, TAB_ENC, TAB_IMG, TAB_GOAL, TABLES = (0, 32, 96, 160, 224)
VECTOR_TILES = 24


def spread_lanes(low_ref, out_ref, first_row, which):
    lane = lax.broadcasted_iota(jnp.int32, (ROWS, LANES), 1)
    keep = (lane < 64) if which == 0 else (lane >= 64)
    for j in range(4):
        tile = low_ref[:, j * LANES : (j + 1) * LANES].astype(F32)
        turned = pltpu.roll(tile, 64, 1)
        for x in range(2):
            source = tile if x == which else turned
            lanes = slice((2 * j + x) * LANES, (2 * j + x + 1) * LANES)
            out_ref[first_row : first_row + ROWS, lanes] = jnp.where(keep, source, 0.0).astype(BF)


def column(meta, k):
    return meta[:, k : k + 1]


class Frames(NamedTuple):
    lengths: Any = taken(SEQ_DEV, dtype=jnp.int32)
    resets: Any = taken(SEQ_DEV, LEN, dtype=jnp.int32)
    terminal: Any = taken(SEQ_DEV, LEN, dtype=jnp.int32)
    rewards: Any = taken(SEQ_DEV, LEN, dtype=F32)
    prev_stoch: Any = taken(SEQ_DEV, ZG, LEN, dtype=jnp.int32)
    prev_action: Any = taken(SEQ_DEV, LEN, dtype=jnp.int32)
    regroup: Any = taken(1, ROWS, dtype=jnp.int32)
    prev: Any = taken(ROWS, H)
    embed: Any = taken(ROWS, E)
    obs_gain: Any = taken(H // 4)
    manager_gain: Any = taken(U // 4)
    manager_head: Any = taken(U // 4)
    goal_gain: Any = taken(U // 4)
    actor_gain: Any = taken(U // 4)
    critic_gain: Any = taken(U // 4)
    critic_head: Any = taken(U // 4)
    img_gain: Any = taken(H // 4)
    gru_gain: Any = taken(3 * H // 4)
    post_gain: Any = taken(H // 4)
    prior_gain: Any = taken(H // 4)
    enc_gain: Any = taken(U // 4)
    actor_head: Any = taken(NA, U // 4)
    enc_head: Any = taken(GCODE, U // 4)
    img_action_share: Any = taken(NA, H // 4)
    goal_in_share: Any = taken(GCODE // 4, U)
    img_stoch_share: Any = taken(Z // 4, H, here=False)
    gru_weight_share: Any = taken(H // 2, 3 * H, here=False)
    manager_in_share: Any = taken(H // 4, U, here=False)
    enc_in_share: Any = taken(H // 4, U, here=False)
    goal_out_share: Any = taken(U // 4, H, here=False)
    prior_in_share: Any = taken(H // 4, H, here=False)
    post_in_share: Any = taken((H + E) // 4, H, here=False)
    prior_out_share: Any = taken(H // 4, Z, here=False)
    post_out_share: Any = taken(H // 4, Z, here=False)
    actor_in_share: Any = taken(768, U, here=False)
    critic_in_share: Any = taken(768, U, here=False)
    gru_weight_out: Any = given(2 * H, 3 * H, here=False)
    goal_out_out: Any = given(U, H, here=False)
    actor_in_out: Any = given(3 * H, U, here=False)
    critic_in_out: Any = given(3 * H, U, here=False)
    vectors: Any = given(4, VECTOR_TILES, LANES, dtype=F32)
    tables: Any = given(4, TABLES, LANES)
    meta_turned: Any = given(LANES, ROWS, dtype=F32)
    start_state: Any = given(ROWS, H + LANES)
    gru_left: Any = given(2 * H, ROWS)
    post_left: Any = given(H + E, ROWS)
    post_out_left: Any = given(H, ROWS)
    prior_out_left: Any = given(H, ROWS)
    img_left: Any = given(Z, ROWS)
    me_left: Any = given(H, 2 * ROWS)
    dec_left: Any = given(U, ROWS)
    soft_turned: Any = given(GCODE, ROWS)
    post_right: Any = given(ROWS, H)
    prior_right: Any = given(ROWS, H)
    post_out_right: Any = given(ROWS, Z)
    prior_out_right: Any = given(ROWS, Z)
    me_right: Any = given(2 * ROWS, 2 * U)
    recon_low: Any = given(ROWS, H)
    dec_pair: Any = given(ROWS, 2 * U)
    gru_normed: Any = given(ROWS, 3 * H, dtype=F32)
    gru_inverse: Any = given(ROWS, 1, dtype=F32)
    img_normed: Any = given(ROWS, H, dtype=F32)
    img_inverse: Any = given(ROWS, 1, dtype=F32)
    grad_deter: Any = given(ROWS, H, dtype=F32)
    embed_grad: Any = given(ROWS, E, dtype=F32)
    small: Any = given(2, 2, SMALL_TILES, LANES, dtype=F32)
    img_stoch: Any = kept(Z, H)
    gru_weight: Any = kept(2 * H, 3 * H)
    manager_in: Any = kept(H, U)
    enc_in: Any = kept(H, U)
    goal_out: Any = kept(U, H)
    prior_in: Any = kept(H, H)
    post_in: Any = kept(H + E, H)
    prior_out: Any = kept(H, Z)
    post_out: Any = kept(H, Z)
    actor_in: Any = kept(3 * H, U)
    critic_in: Any = kept(3 * H, U)
    img_action: Any = kept(32, H)
    enc_out: Any = kept(GCODE, U)
    goal_in: Any = kept(GCODE, U)
    vector_share: Any = kept(VECTOR_TILES, LANES, dtype=F32)
    table_share: Any = kept(TABLES, LANES)
    meta: Any = kept(ROWS, LANES, dtype=F32)
    hot: Any = kept(ROWS, Z)
    img_hidden: Any = kept(ROWS, H)
    deter: Any = kept(ROWS, H, dtype=F32)
    deter_low: Any = kept(ROWS, H)
    feature: Any = kept(ROWS, H)
    obs_normed: Any = kept(ROWS, H, dtype=F32)
    obs_inverse: Any = kept(ROWS, 1, dtype=F32)
    outgoing: Any = kept(ROWS, H + LANES)
    incoming: Any = kept(ROWS, H + LANES)
    pre_512: Any = kept(ROWS, U, dtype=F32)
    hid_512: Any = kept(ROWS, U)
    back_512: Any = kept(ROWS, U)
    wide_512: Any = kept(ROWS, U, dtype=F32)
    inverse: Any = kept(ROWS, 1, dtype=F32)
    grad_value: Any = kept(ROWS, 1, dtype=F32)
    dec_normed: Any = kept(ROWS, U, dtype=F32)
    dec_inverse: Any = kept(ROWS, 1, dtype=F32)
    dec_hidden: Any = kept(ROWS, U)
    dec_pre: Any = kept(ROWS, U)
    wide: Any = kept(ROWS, H, dtype=F32)
    prior_normed: Any = kept(ROWS, H, dtype=F32)
    prior_inverse: Any = kept(ROWS, 1, dtype=F32)
    prior_hidden: Any = kept(ROWS, H)
    post_normed: Any = kept(ROWS, H, dtype=F32)
    post_inverse: Any = kept(ROWS, 1, dtype=F32)
    post_hidden: Any = kept(ROWS, H)
    post_turned: Any = kept(Z, ROWS, dtype=F32)
    prior_turned: Any = kept(Z, ROWS, dtype=F32)
    loss: Any = kept(1, 1, dtype=F32)
    piece_send: Any = signal(17, 8)
    piece_recv: Any = signal(17, 8)
    load_done: Any = signal(17)
    save_done: Any = signal(4)
    small_send: Any = signal(2, 3)
    small_recv: Any = signal(2, 3)
    state_send: Any = signal(8)
    state_recv: Any = signal(8)

    def pack(self):
        vectors = (
            self.obs_gain, self.manager_gain, self.manager_head, self.goal_gain, self.actor_gain,
            self.critic_gain, self.critic_head, self.img_gain, self.gru_gain, self.post_gain,
            self.prior_gain, self.enc_gain,
        )
        low = 0
        for vector in vectors:
            for i in range(vector.shape[0] // LANES):
                self.vector_share[low, :] = vector[pl.ds(i * LANES, LANES)].astype(F32)
                low += 1
        self.vector_share[low:, :] = jnp.zeros((VECTOR_TILES - low, LANES), F32)
        self.table_share[...] = jnp.zeros(self.table_share.shape, BF)
        self.table_share[TAB_ACT : TAB_ACT + NA, :] = self.actor_head[...]
        self.table_share[TAB_ENC : TAB_ENC + GCODE, :] = self.enc_head[...]
        for i in range(2):
            low = TAB_IMG + 32 * i
            lanes = slice(i * LANES, (i + 1) * LANES)
            self.table_share[low : low + NA, :] = self.img_action_share[:, lanes]
        for i in range(4):
            low = TAB_GOAL + 16 * i
            lanes = slice(i * LANES, (i + 1) * LANES)
            self.table_share[low : low + 16, :] = self.goal_in_share[:, lanes]

    def start(self):
        def row(ref):
            value = ref[...].astype(F32)
            return jnp.concatenate([value[0:1], value[1:2]], 1)

        position = lax.broadcasted_iota(jnp.int32, (SEQ_DEV, LEN), 1)
        length = self.lengths[...].reshape(SEQ_DEV, 1)
        later = jnp.where((position + 1 < length) & (position + 1 < LEN), 1.0, 0.0)
        kinds = (
            row(self.prev_action),
            row(jnp.where(position < length, 1.0, 0.0)),
            row(later) * (1.0 - jnp.minimum(pltpu.roll(row(self.resets), ROWS - 1, 1), 1.0)),
            1.0 - row(self.terminal),
            row(self.rewards),
            self.regroup[...].astype(F32),
        )
        self.meta_turned[...] = jnp.zeros(self.meta_turned.shape, F32)
        for i, kind in enumerate(kinds):
            self.meta_turned[32 + i : 33 + i, :] = kind
        self.meta[...] = self.meta_turned[...].T
        ids = jnp.concatenate([self.prev_stoch[0], self.prev_stoch[1]], 1).astype(F32)
        self.hot[...] = hot_rows(columns_of(ids)[:, 0:ZG], ZK, ZG, Z).astype(BF)

    def turns(self):
        turn_into(self.img_left, self.hot)
        turn_into(self.gru_left, self.prev, H)
        turn_into(self.post_left, self.embed, H)
        self.small[...] = jnp.zeros(self.small.shape, F32)

    def unpack(self):
        for r in range(4):
            for i in range(2):
                self.img_action[:, (2 * r + i) * LANES : (2 * r + i + 1) * LANES] = self.tables[
                    r, TAB_IMG + 32 * i : TAB_IMG + 32 * (i + 1), :
                ]
            self.enc_out[:, r * LANES : (r + 1) * LANES] = self.tables[
                r, TAB_ENC : TAB_ENC + 64, :
            ]
            for i in range(4):
                self.goal_in[16 * r : 16 * (r + 1), i * LANES : (i + 1) * LANES] = self.tables[
                    r, TAB_GOAL + 16 * i : TAB_GOAL + 16 * (i + 1), :
                ]

    def gain(self, low, size):
        return vector_of(self.vectors, low, size // (4 * LANES))

    def img(self):
        meta = self.meta[...]
        lane = lax.broadcasted_iota(jnp.int32, (ROWS, 32), 1).astype(F32)
        action = jnp.where(column(meta, 32) == lane, 1.0, 0.0).astype(BF)
        matmul_into(
            self.img_normed, self.hot[...], self.img_stoch,
            extra=lambda start, tile: product(action, self.img_action[:, pl.ds(start, tile)]),
        )
        hidden_rows(self.img_normed, self.img_inverse, self.gain(IMG_G, H), self.img_hidden)
        turn_into(self.gru_left, self.img_hidden)

    def gru(self, third):
        low = third * H
        out = self.gru_normed.at[:, low : low + H]

        def one(j, carry):
            start = pl.multiple_of(low + j * TILE, TILE)
            value = product(self.img_hidden[...], self.gru_weight[0:H, pl.ds(start, TILE)])
            value = value + product(
                self.prev[...], self.gru_weight[H : 2 * H, pl.ds(start, TILE)]
            )
            self.gru_normed[:, pl.ds(start, TILE)] = value
            return carry

        lax.fori_loop(0, H // TILE, one, 0)

    def state(self):
        gain = self.gain(GRU_G, 3 * H)
        obs_gain = self.gain(OBS, H)

        def one(rows, carry):
            normed, inverse = normalize(self.gru_normed[rows, :])
            self.gru_normed[rows, :] = normed
            self.gru_inverse[rows, :] = inverse
            parts = normed * gain
            reset = 1.0 / (1.0 + jnp.exp(-parts[:, :H]))
            candidate = jnp.tanh(reset * parts[:, H : 2 * H])
            update = 1.0 / (1.0 + jnp.exp(1.0 - parts[:, 2 * H :]))
            state = update * candidate + (1.0 - update) * self.prev[rows, :].astype(F32)
            self.deter[rows, :] = state
            self.deter_low[rows, :] = state.astype(BF)
            obs, obs_inverse = normalize(state)
            self.obs_normed[rows, :] = obs
            self.obs_inverse[rows, :] = obs_inverse
            self.feature[rows, :] = (obs * obs_gain).astype(BF)
            return carry

        by_rows(ROWS, 16, one)
        turn_into(self.post_left, self.deter_low)

    def picked(self):
        meta = self.meta[...]
        lane = lax.broadcasted_iota(jnp.int32, (ROWS, ROWS), 1).astype(F32)
        pick = jnp.where(column(meta, 37) == lane, 1.0, 0.0).astype(BF)

        def one(j, carry):
            lanes = pl.ds(pl.multiple_of(j * TILE, TILE), TILE)
            self.outgoing[:, lanes] = product(pick, self.deter_low[:, lanes]).astype(BF)
            return carry

        lax.fori_loop(0, H // TILE, one, 0)
        valid = jnp.broadcast_to(column(meta, 33), (ROWS, LANES)).astype(BF)
        self.outgoing[:, H:] = product(pick, valid).astype(BF)

    def manager(self):
        meta = self.meta[...]
        gain, head = (self.gain(MAN_G, U), self.gain(MAN_O, U))
        for j in range(H // LANES):
            lanes = slice(j * LANES, (j + 1) * LANES)
            self.me_left[lanes, 0:ROWS] = self.feature[:, lanes].astype(F32).T.astype(BF)
            self.me_left[lanes, ROWS:] = self.deter_low[:, lanes].astype(F32).T.astype(BF)
        matmul_into(self.pre_512, self.feature[...], self.manager_in)
        hidden_rows(self.pre_512, self.inverse, gain, self.hid_512)
        value = jnp.sum(self.hid_512[...].astype(F32) * head, -1, keepdims=True)
        valid, linked, carried, rewards = (column(meta, 33 + i) for i in range(4))
        later = pltpu.roll(jnp.broadcast_to(value, (ROWS, LANES)), ROWS - 1, 0)
        base = jnp.where(
            linked > 0, rewards + discount * carried * ((1.0 - return_mix) * later), value
        )
        slope = jnp.broadcast_to(linked * (discount * return_mix) * carried, (ROWS, LANES))
        step = 1
        while step < LEN:
            base = base + slope * pltpu.roll(base, ROWS - step, 0)
            slope = slope * pltpu.roll(slope, ROWS - step, 0)
            step *= 2
        misfit = value - base[:, 0:1]
        scale = valid * (1.0 / ROWS)
        self.loss[...] = 0.5 * jnp.sum(scale * misfit * misfit, 0, keepdims=True)
        grad_value = scale * misfit
        put_vector(
            self.small, MAN_O,
            jnp.sum(self.hid_512[...].astype(F32) * grad_value, 0, keepdims=True),
        )
        self.grad_value[...] = grad_value
        total = hidden_rows_back(
            lambda rows: self.grad_value[rows, :] * head,
            self.pre_512, self.inverse, gain, self.back_512,
        )
        put_vector(self.small, MAN_G, total)
        spread_lanes(self.back_512, self.me_right, 0, 0)
        self.feature_back()

    def feature_back(self):
        obs_gain = self.gain(OBS, H)
        matmul_into(self.wide, self.back_512[...], self.manager_in, turned=True)

        def one(rows, total):
            grad = self.wide[rows, :]
            normed = self.obs_normed[rows, :]
            total = total + jnp.sum(grad * normed, 0, keepdims=True)
            self.grad_deter[rows, :] = normalize_back(
                grad * obs_gain, normed, self.obs_inverse[rows, :]
            )
            return total

        put_vector(self.small, OBS, by_rows(ROWS, 32, one, jnp.zeros((1, H), F32)))

    def add_back(self, left_ref, weight_ref):
        def one(j, carry):
            lanes = pl.ds(pl.multiple_of(j * TILE, TILE), TILE)
            self.grad_deter[:, lanes] += lax.dot_general(
                left_ref[...], weight_ref[lanes, :], (((1,), (1,)), ((), ())),
                preferred_element_type=F32,
            )
            return carry

        lax.fori_loop(0, H // TILE, one, 0)

    def encoder(self):
        gain, goal_gain = (self.gain(ENC_G, U), self.gain(GOAL_G, U))
        valid_row = self.meta_turned[33:34, :]
        scale_row = valid_row * (1.0 / ROWS)
        scale = column(self.meta[...], 33) * (1.0 / ROWS)
        matmul_into(self.pre_512, self.deter_low[...], self.enc_in)
        hidden_rows(self.pre_512, self.inverse, gain, self.hid_512)
        logits = lax.dot_general(
            self.enc_out[...], self.hid_512[...], (((1,), (1,)), ((), ())),
            preferred_element_type=F32,
        ).reshape(GC, GK, ROWS)
        shifted = logits - jnp.max(logits, 1, keepdims=True)
        code_log = shifted - jnp.log(jnp.sum(jnp.exp(shifted), 1, keepdims=True))
        code = jnp.exp(code_log)
        spread = jnp.sum(code * code_log, 1, keepdims=True)
        code_kl = jnp.sum(jnp.sum(code * (code_log + math.log(GK)), 1), 0, keepdims=True)
        flat = jnp.concatenate(
            [code.reshape(GCODE, ROWS), jnp.zeros((ROWS - GCODE, ROWS), F32)], 0
        )
        self.soft_turned[...] = flat[0:GCODE].astype(BF)
        soft = flat.T[:, 0:GCODE].astype(BF)
        matmul_into(self.dec_normed, soft, self.goal_in)
        hidden_rows(self.dec_normed, self.dec_inverse, goal_gain, self.dec_hidden)
        turn_into(self.dec_left, self.dec_hidden)

        def one(j, total):
            lanes = pl.ds(pl.multiple_of(j * TILE, TILE), TILE)
            err = product(self.dec_hidden[...], self.goal_out[:, lanes]) - self.deter[:, lanes]
            grad = scale * err * (1.0 / H)
            self.grad_deter[:, lanes] -= grad
            self.recon_low[:, lanes] = grad.astype(BF)
            return total + jnp.sum(err * err, -1, keepdims=True)

        squares = lax.fori_loop(0, H // TILE, one, jnp.zeros((ROWS, 1), F32))
        self.loss[...] += jnp.sum(scale * (0.5 / H) * squares, 0, keepdims=True) + jnp.sum(
            scale_row * code_kl, 1, keepdims=True
        )
        matmul_into(self.wide_512, self.recon_low[...], self.goal_out, turned=True)
        total = hidden_rows_back(
            lambda rows: self.wide_512[rows, :],
            self.dec_normed, self.dec_inverse, goal_gain, self.dec_pre,
        )
        put_vector(self.small, GOAL_G, total)
        spread_lanes(self.dec_pre, self.dec_pair, 0, 0)
        grad_code = lax.dot_general(
            self.goal_in[...], self.dec_pre[...], (((1,), (1,)), ((), ())),
            preferred_element_type=F32,
        ).reshape(GC, GK, ROWS)
        grad_logits = code * (grad_code - jnp.sum(code * grad_code, 1, keepdims=True))
        grad_logits = grad_logits + scale_row[None] * code * (code_log - spread)
        grad_turned = grad_logits.reshape(GCODE, ROWS)
        grad_low = jnp.concatenate(
            [grad_turned, jnp.zeros((ROWS - GCODE, ROWS), F32)], 0
        ).T[:, 0:GCODE].astype(BF)
        put_table(
            self.small, ENC_T, product(grad_turned.astype(BF), self.hid_512[...]), GCODE
        )
        matmul_into(self.wide_512, grad_low, self.enc_out)
        total = hidden_rows_back(
            lambda rows: self.wide_512[rows, :],
            self.pre_512, self.inverse, gain, self.back_512,
        )
        put_vector(self.small, ENC_G, total)
        spread_lanes(self.back_512, self.me_right, ROWS, 1)
        self.add_back(self.back_512, self.enc_in)

    def prior(self):
        matmul_into(self.prior_normed, self.deter_low[...], self.prior_in)
        hidden_rows(
            self.prior_normed, self.prior_inverse, self.gain(PRIOR_G, H), self.prior_hidden
        )
        turn_into(self.prior_out_left, self.prior_hidden)

    def post(self):
        def one(j, carry):
            lanes = pl.ds(pl.multiple_of(j * TILE, TILE), TILE)
            value = product(self.deter_low[...], self.post_in[0:H, lanes])
            self.post_normed[:, lanes] = value + product(
                self.embed[...], self.post_in[H : H + E, lanes]
            )
            return carry

        lax.fori_loop(0, H // TILE, one, 0)
        hidden_rows(self.post_normed, self.post_inverse, self.gain(POST_G, H), self.post_hidden)
        turn_into(self.post_out_left, self.post_hidden)

    def logits(self, hidden_ref, weight_ref, turned_ref):
        matmul_into(self.wide, hidden_ref[...], weight_ref)
        turn_into(turned_ref, self.wide)

    def state_kl(self):
        scale_row = self.meta_turned[33:34, :] * (1.0 / ROWS)

        def log_part(value):
            shifted = value - jnp.max(value, 0, keepdims=True)
            return shifted - jnp.log(jnp.sum(jnp.exp(shifted), 0, keepdims=True))

        def one(rows, total):
            post_log = log_part(self.post_turned[rows, :])
            prior_log = log_part(self.prior_turned[rows, :])
            post = jnp.exp(post_log)
            gap = post_log - prior_log
            kl = jnp.sum(post * gap, 0, keepdims=True)
            self.post_turned[rows, :] = scale_row * post * (gap - kl)
            self.prior_turned[rows, :] = scale_row * (jnp.exp(prior_log) - post)
            return total + kl

        total = by_rows(Z, ZK, one, jnp.zeros((1, ROWS), F32))
        self.loss[...] += jnp.sum(scale_row * total, 1, keepdims=True)
        for turned, low in (
            (self.post_turned, self.post_out_right), (self.prior_turned, self.prior_out_right),
        ):
            for j in range(Z // LANES):
                lanes = slice(j * LANES, (j + 1) * LANES)
                low[:, lanes] = turned[lanes, :].T.astype(BF)

    def prior_back(self):
        matmul_into(self.wide, self.prior_out_right[...], self.prior_out, turned=True)
        total = hidden_rows_back(
            lambda rows: self.wide[rows, :],
            self.prior_normed, self.prior_inverse, self.gain(PRIOR_G, H), self.prior_right,
        )
        put_vector(self.small, PRIOR_G, total)
        self.add_back(self.prior_right, self.prior_in)

    def post_back(self):
        matmul_into(self.wide, self.post_out_right[...], self.post_out, turned=True)
        total = hidden_rows_back(
            lambda rows: self.wide[rows, :],
            self.post_normed, self.post_inverse, self.gain(POST_G, H), self.post_right,
        )
        put_vector(self.small, POST_G, total)
        self.add_back(self.post_right, self.post_in)
        matmul_into(self.embed_grad, self.post_right[...], self.post_in, turned=True, low=H)
        for y in range(2):
            for c in range(2):
                self.small[c, y, LOSS : LOSS + 1, :] = jnp.broadcast_to(
                    self.loss[...], (1, LANES)
                )


class Places:
    def __init__(self):
        dp, rep = (lax.axis_index("dp"), lax.axis_index("rep"))
        self.dp, self.rep = (dp, rep)
        self.x, self.z, self.w = (lax.rem(dp, 2), lax.rem(dp // 2, 2), dp // 4)
        self.y, self.c = (rep // 2, lax.rem(rep, 2))
        self.to_x = (dp + 1 - 2 * self.x, rep)
        self.to_z = (dp + 2 - 4 * self.z, rep)
        self.to_w = (dp + 4 - 8 * self.w, rep)
        self.to_y = (dp, rep + 2 - 4 * self.y)
        self.to_c = (dp, rep + 1 - 2 * self.c)
        self.to_d = (dp, 3 - rep)

    def around(self, offset):
        return lax.rem(self.dp + offset, 8)


def greet(devices):
    barrier = pltpu.get_barrier_semaphore()
    for device in devices:
        pl.semaphore_signal(barrier, inc=1, device_id=device, device_id_type=MESH)
    return lambda: pl.semaphore_wait(barrier, len(devices))


def send_to(source, target, send_sem, recv_sem, device):
    return pltpu.make_async_remote_copy(
        src_ref=source,
        dst_ref=target,
        send_sem=send_sem,
        recv_sem=recv_sem,
        device_id=device,
        device_id_type=MESH,
    )


def regroup_start(places, outgoing, incoming, send_sem, recv_sem):
    count = ROWS // 8
    mine = pl.ds(pl.multiple_of(places.dp * count, 16), count)
    copies = []
    for offset in range(1, 8):
        there = places.around(offset)
        copy = send_to(
            outgoing.at[pl.ds(pl.multiple_of(there * count, 16), count)],
            incoming.at[mine],
            send_sem.at[offset],
            recv_sem.at[offset],
            (there, places.rep),
        )
        copy.start()
        copies.append(copy)
    incoming[mine, :] = outgoing[mine, :]
    return copies


def diagonal_split(u, columns):
    tiles = columns // LANES
    shares = [tiles // 3 + (1 if (i - u) % 3 < tiles % 3 else 0) for i in range(3)]
    return tuple(share * LANES for share in shares)


OWN, Y_A, Y_B, X_A, Z_A, X_B, Z_B, RELAY = range(8)


class Gather:
    def __init__(self, places, units, send_sem, recv_sem, load_sem):
        self.places, self.units = (places, units)
        self.send_sem, self.recv_sem, self.load_sem = (send_sem, recv_sem, load_sem)
        self.far = places.rep + 2 - 4 * places.y
        self.mine = places.x * 2 + places.z
        self.across = 3 - self.mine
        self.from_x = (1 - places.x) * 2 + places.z
        self.from_z = places.x * 2 + 1 - places.z
        self.copies = {}
        self.loads = {}

    def remote(self, u, kind, source, target, device):
        copy = send_to(
            source, target, self.send_sem.at[u, kind], self.recv_sem.at[u, kind], device
        )
        copy.start()
        self.copies[u, kind] = copy

    def rows(self, u, share, piece, low, number):
        extent = self.units[u][0].shape[0]
        start = share * extent + piece * (extent // 4) + low
        return pl.ds(pl.multiple_of(start, 16), number)

    def part(self, u, rows, whole=True, first=0, columns=None):
        share, all_rows, low, count = self.units[u]
        lanes = pl.ds(low + first, count if columns is None else columns)
        return (all_rows if whole else share).at[rows, lanes]

    def diagonal(self, u, share, piece, over, whole=True):
        split = diagonal_split(u, self.units[u][3])
        return self.part(
            u, self.rows(u, share, piece, 0, self.extent(u) // 4), whole, sum(split[:over]),
            split[over],
        )

    def extent(self, u):
        return self.units[u][0].shape[0]

    def load(self, u):
        everything = self.rows(u, 0, 0, 0, self.extent(u))
        copy = pltpu.make_async_copy(
            self.part(u, everything, False),
            self.part(u, self.rows(u, self.places.rep, 0, 0, self.extent(u))),
            self.load_sem.at[u],
        )
        copy.start()
        self.loads[u] = copy

    def over_y(self, u):
        if u >= len(self.units):
            return
        rep, quarter = (self.places.rep, self.extent(u) // 4)
        self.remote(
            u, Y_A,
            self.part(u, self.rows(u, 0, self.mine, 0, quarter), False),
            self.part(u, self.rows(u, rep, self.mine, 0, quarter)),
            self.places.to_y,
        )

    def over_y_more(self, u):
        if u >= len(self.units):
            return
        rep = self.places.rep
        if diagonal_split(u, self.units[u][3])[0]:
            self.remote(
                u, Y_B, self.diagonal(u, 0, self.across, 0, False),
                self.diagonal(u, rep, self.across, 0), self.places.to_y,
            )
        everything = self.rows(u, 0, 0, 0, self.extent(u))
        self.remote(
            u, OWN,
            self.part(u, everything, False),
            self.part(u, self.rows(u, rep, 0, 0, self.extent(u))),
            self.places.to_c,
        )

    def stage_1(self, u):
        self.copies[u, Y_A].wait_recv()
        piece = self.part(u, self.rows(u, self.far, self.mine, 0, self.extent(u) // 4))
        self.remote(u, X_A, piece, piece, self.places.to_x)
        self.remote(u, Z_A, piece, piece, self.places.to_z)

    def stage_2(self, u):
        _, second, third = diagonal_split(u, self.units[u][3])
        self.copies[u, Z_A].wait_recv()
        if second:
            piece = self.diagonal(u, self.far, self.from_z, 1)
            self.remote(u, X_B, piece, piece, self.places.to_x)
        self.copies[u, X_A].wait_recv()
        if third:
            piece = self.diagonal(u, self.far, self.from_x, 2)
            self.remote(u, Z_B, piece, piece, self.places.to_z)

    def stage_3(self, u):
        for kind in (Y_B, X_B, Z_B):
            if (u, kind) in self.copies:
                self.copies[u, kind].wait_recv()
        share = self.part(u, self.rows(u, self.far, 0, 0, self.extent(u)))
        self.remote(u, RELAY, share, share, self.places.to_c)

    def open(self):
        for u in range(AHEAD):
            self.over_y(u)
            if u < MORE:
                self.over_y_more(u)

    def pump(self, t):
        count = len(self.units)
        if t < count:
            self.stage_1(t)
            self.over_y(t + AHEAD)
        if 0 <= t < count:
            self.over_y_more(t + MORE)
        if 0 <= t - LAG_2 < count:
            self.stage_2(t - LAG_2)
        if 0 <= t - LAG_3 < count:
            self.stage_3(t - LAG_3)

    def complete(self, u):
        self.loads[u].wait()
        self.copies[u, OWN].wait_recv()
        self.copies[u, RELAY].wait_recv()

    def drain(self):
        for copy in self.copies.values():
            copy.wait_send()


AHEAD, MORE, LAG_2, LAG_3, DONE = (8, 4, 2, 4, 5)


def frames_kernel(f):
    places = Places()
    units = [(f.img_stoch_share, f.img_stoch, 0, H)]
    units += [(f.gru_weight_share, f.gru_weight, i * H, H) for i in range(3)]
    units += [
        (f.manager_in_share, f.manager_in, 0, U),
        (f.enc_in_share, f.enc_in, 0, U),
        (f.goal_out_share, f.goal_out, 0, H),
        (f.prior_in_share, f.prior_in, 0, H),
        (f.post_in_share, f.post_in, 0, U),
        (f.post_in_share, f.post_in, U, U),
        (f.prior_out_share, f.prior_out, 0, Z),
        (f.post_out_share, f.post_out, 0, Z),
        (f.actor_in_share, f.actor_in, 0, 256),
        (f.actor_in_share, f.actor_in, 256, 256),
        (f.critic_in_share, f.critic_in, 0, 256),
        (f.critic_in_share, f.critic_in, 256, 128),
        (f.critic_in_share, f.critic_in, 384, 128),
    ]
    met = greet(
        [(places.around(o), places.rep) for o in range(1, 8)]
        + [places.to_c, places.to_y, places.to_d]
    )
    gather = Gather(places, units, f.piece_send, f.piece_recv, f.load_done)
    for u in range(len(units)):
        gather.load(u)
    f.pack()
    f.start()
    met()
    packs = []
    for i, (share, whole) in enumerate(((f.vector_share, f.vectors), (f.table_share, f.tables))):
        for k, device in enumerate((places.to_c, places.to_y, places.to_d)):
            copy = send_to(
                share, whole.at[places.rep], f.small_send.at[i, k], f.small_recv.at[i, k], device
            )
            copy.start()
            packs.append(copy)
    gather.open()
    f.vectors[places.rep] = f.vector_share[...]
    f.tables[places.rep] = f.table_share[...]
    saves = []

    def save(k, source, target):
        copy = pltpu.make_async_copy(source, target, f.save_done.at[k])
        copy.start()
        saves.append(copy)

    def pump(t):
        gather.pump(t)

    pump(0)
    f.turns()
    states = []

    def first():
        for copy in packs:
            copy.wait()
        f.unpack()
        f.img()

    def state():
        f.gru(2)
        save(0, f.gru_weight, f.gru_weight_out)
        f.state()
        f.picked()
        states.extend(
            regroup_start(places, f.outgoing, f.incoming, f.state_send, f.state_recv)
        )

    def encoder():
        save(1, f.goal_out, f.goal_out_out)
        f.encoder()

    def posterior():
        f.logits(f.post_hidden, f.post_out, f.post_turned)
        f.state_kl()

    def arrived():
        for copy in states:
            copy.wait()
        f.start_state[...] = f.incoming[...]

    work = {
        0: first, 1: lambda: f.gru(0), 2: lambda: f.gru(1), 3: state, 4: f.manager, 6: encoder,
        7: f.prior, 9: f.post,
        10: lambda: f.logits(f.prior_hidden, f.prior_out, f.prior_turned),
        11: posterior, 12: f.prior_back, 13: f.post_back, 14: arrived,
    }
    count = len(units)
    for t in range(1, count + DONE):
        pump(t)
        if 0 <= t - DONE:
            gather.complete(t - DONE)
            work.get(t - DONE, lambda: None)()
    save(2, f.actor_in, f.actor_in_out)
    save(3, f.critic_in, f.critic_in_out)
    for copy in saves:
        copy.wait()
    gather.drain()


class Source(NamedTuple):
    rows: int
    parts: Any
    columns: int

    @property
    def depth(self):
        return sum(self.parts)


SOURCE_POST = Source((H + E) // 4, (ROWS,), H)
SOURCE_1024 = Source(H // 4, (ROWS,), H)
SOURCE_MAN_ENC = Source(H // 4, (2 * ROWS,), 2 * U)
SOURCE_GRU = Source(H // 2, (ROWS,), 3 * H)
SOURCE_GOAL_OUT = Source(U // 4, (ROWS, ROWS), H)
SOURCE_GOAL_IN = Source(GCODE // 4, (ROWS, ROWS), 2 * U)
WORKER_SHARE = (768, 1024)
ALONG_X, ALONG_Z, ALONG_W, ALONG_Y = range(4)
Y_FIRST = (ALONG_Y, ALONG_X, ALONG_Z, ALONG_W)
X_FIRST = (ALONG_X, ALONG_Y, ALONG_Z, ALONG_W)
Z_FIRST = (ALONG_Z, ALONG_Y, ALONG_X, ALONG_W)
X_ONLY = (ALONG_X, ALONG_Z, ALONG_W)
Z_ONLY = (ALONG_Z, ALONG_X, ALONG_W)


def side_by_side(left, right_ref, lanes):
    right = jnp.concatenate([right_ref[:, lane] for lane in lanes], 1)
    wide = product(left, right)
    return [wide[:, i * LANES : (i + 1) * LANES] for i in range(len(lanes))]


class Exchange:
    def __init__(self, places, source, left_2, right_2, send_sem, recv_sem, local_sem, first):
        self.places, self.source = (places, source)
        self.left_2, self.right_2 = (left_2, right_2)
        self.sems, self.first = ((send_sem, recv_sem, local_sem), first)
        self.copies = []

    def move(self, part, j, mine, target, theirs, place):
        send_sem, recv_sem, local_sem = (sem.at[self.first + part, j] for sem in self.sems)
        remote = send_to(theirs, place, send_sem, recv_sem, self.places.to_c)
        local = pltpu.make_async_copy(mine, target, local_sem)
        remote.start()
        local.start()
        self.copies += [remote, local]

    def lows(self, part):
        low = sum(self.source.parts[:part])
        depth = self.source.parts[part]
        return (pl.ds(low, depth), pl.ds(self.source.depth + low, depth))

    def start_left(self, part, left):
        low, high = self.lows(part)
        for y in range(2):
            ours, theirs = (
                pl.ds(pl.multiple_of((2 * y + core) * self.source.rows, 16), self.source.rows)
                for core in (self.places.c, 1 - self.places.c)
            )
            self.move(
                part, y, left.at[ours], self.left_2.at[y, :, low],
                left.at[theirs], self.left_2.at[y, :, high],
            )

    def start_right(self, part, right):
        low, high = self.lows(part)
        self.move(part, 2, right, self.right_2.at[low], right, self.right_2.at[high])

    def start(self, part, left, right):
        self.start_right(part, right)
        self.start_left(part, left)

    def ready(self, first, offset):
        while self.copies:
            self.copies.pop(0).wait()

    def terms(self, y, rows, lanes):
        return side_by_side(self.left_2[y, rows, :], self.right_2, lanes)


class Wide:
    def __init__(self, places, rows, depth, left_4, right_4, send_sem, recv_sem, local_sem):
        self.places, self.rows, self.depth = (places, rows, depth)
        self.left_4, self.right_4 = (left_4, right_4)
        self.send_sem, self.recv_sem, self.local_sem = (send_sem, recv_sem, local_sem)
        self.copies = {}
        self.from_y = {}

    def part(self, i):
        return pl.ds(i * self.depth, self.depth)

    def remote(self, k, source, target, device):
        copy = send_to(source, target, self.send_sem.at[k], self.recv_sem.at[k], device)
        copy.start()
        return copy

    def local(self, k, source, target):
        copy = pltpu.make_async_copy(source, target, self.local_sem.at[k])
        copy.start()
        return copy

    def start_left(self, left):
        rep, places = (self.places.rep, self.places)
        copies = []
        for i, device in enumerate((places.to_c, places.to_y, places.to_d)):
            rows = pl.ds(pl.multiple_of(device[1] * self.rows, 16), self.rows)
            copies.append(
                self.remote(i, left.at[rows], self.left_4.at[:, self.part(1 + i)], device)
            )
        rows = pl.ds(pl.multiple_of(rep * self.rows, 16), self.rows)
        copies.append(self.local(0, left.at[rows], self.left_4.at[:, self.part(0)]))
        self.copies[-1] = copies

    def start_right(self, right, third):
        lanes = pl.ds(third * H, H)
        source, k = (right.at[:, lanes], 3 + 3 * third)
        self.from_y[third] = self.remote(
            k, source, self.right_4.at[self.part(2), lanes], self.places.to_y
        )
        self.copies[third] = [
            self.remote(k + 1, source, self.right_4.at[self.part(1), lanes], self.places.to_c),
            self.local(1 + third, source, self.right_4.at[self.part(0), lanes]),
        ]

    def relay(self, third):
        self.from_y[third].wait()
        lanes = pl.ds(third * H, H)
        self.copies[third].append(
            self.remote(
                5 + 3 * third, self.right_4.at[self.part(2), lanes],
                self.right_4.at[self.part(3), lanes], self.places.to_c,
            )
        )

    def ready(self, first, offset):
        for part in (-1, offset // H):
            for copy in self.copies.pop(part, ()):
                copy.wait()

    def terms(self, y, rows, lanes):
        return side_by_side(self.left_4[rows, :], self.right_4, lanes)


class Addition:
    def __init__(self, own, sibling, done):
        self.own, self.sibling, self.done = (own, sibling, done)
        self.copies = {}

    def start(self, own, sibling, part):
        half = self.own.shape[1] // 2
        rows, copies = (pl.ds(part * half, half), [])
        for i, (source, target) in enumerate(((own, self.own), (sibling, self.sibling))):
            copies.append(
                pltpu.make_async_copy(
                    source.at[:, rows], target.at[:, rows], self.done.at[part, i]
                )
            )
            copies[i].start()
        self.copies[part] = copies

    def ready(self, first, offset):
        for copy in self.copies.pop(first // (self.own.shape[1] // 2), ()):
            copy.wait()

    def terms(self, y, rows, lanes):
        return [
            self.own[y, rows, lane].astype(F32) + self.sibling[y, rows, lane].astype(F32)
            for lane in lanes
        ]


class Halving:
    def __init__(self, places, units, outbox, inbox, send_sem, recv_sem, outs, groups):
        self.units, self.groups = (units, groups)
        self.outbox, self.inbox, self.outs = (outbox, inbox, outs)
        self.send_sem, self.recv_sem = (send_sem, recv_sem)
        self.bits = (places.x, places.z, places.w, places.y)
        self.peers = (places.to_x, places.to_z, places.to_w, places.to_y)
        self.copies = {}

    def blocks(self, u, k):
        source, stride, offset, order, first, count = self.units[u]
        free = order[k + 1 :]
        place = {ALONG_Y: self.bits[ALONG_Y]}
        for i, along in enumerate(order[: k + 1]):
            place[along] = self.bits[along] if i < k else 1 - self.bits[along]
        choices = [
            {along: (j >> (len(free) - 1 - i)) & 1 for i, along in enumerate(free)}
            for j in range(1 << len(free))
        ]
        results = [None] * len(choices)
        for y in (0, 1) if ALONG_Y in free else (None,):
            chosen = [j for j, choice in enumerate(choices) if choice.get(ALONG_Y) == y]
            lanes = []
            for j in chosen:
                bits = place | choices[j]
                device = bits[ALONG_W] * 4 + bits[ALONG_Z] * 2 + bits[ALONG_X]
                start = device * stride + offset
                if not isinstance(start, int):
                    start = pl.multiple_of(start, LANES)
                lanes.append(pl.ds(start, LANES))
            terms = source.terms(place[ALONG_Y] if y is None else y, pl.ds(first, count), lanes)
            for j, total in zip(chosen, terms):
                bits = place | choices[j]
                for i in range(k):
                    index = 0
                    for along in order[i + 1 :]:
                        index = index * 2 + bits[along]
                    total = total + self.inbox[u][i][index].astype(F32)
                results[j] = total
        return results

    def step(self, u, k):
        if k == 0:
            self.units[u][0].ready(self.units[u][4], self.units[u][2])
        else:
            self.copies[u, k - 1].wait_recv()
        if k == len(self.units[u][3]):
            self.outs[u][...] = self.blocks(u, k)[0]
            return
        for j, block in enumerate(self.blocks(u, k)):
            self.outbox[u][k][j] = block.astype(BF)
        copy = send_to(
            self.outbox[u][k], self.inbox[u][k], self.send_sem.at[u, k], self.recv_sem.at[u, k],
            self.peers[self.units[u][3][k]],
        )
        copy.start()
        self.copies[u, k] = copy

    def slot(self, t, lag=1):
        for k in range(5):
            if 0 <= t - lag * k < len(self.groups):
                for u in self.groups[t - lag * k]:
                    if k <= len(self.units[u][3]):
                        self.step(u, k)

    def drain(self):
        for copy in self.copies.values():
            copy.wait_send()


def boxes(units):
    return tuple(
        tuple(kept(1 << k, unit[-1], LANES) for k in reversed(range(len(unit[3]))))
        for unit in units
    )


HEAD_POST, HEAD_PRIOR, HEAD_POST_OUT, HEAD_PRIOR_OUT, HEAD_MAN_ENC = range(5)
HEAD_SOURCES = (SOURCE_POST, SOURCE_1024, SOURCE_1024, SOURCE_1024, SOURCE_MAN_ENC)
HEAD_UNITS = (
    (HEAD_POST, 128, 0, Y_FIRST, 0, 128),
    (HEAD_PRIOR, 128, 0, X_FIRST, 0, 128),
    (HEAD_POST_OUT, 128, 0, Z_FIRST, 0, 128),
    (HEAD_POST, 128, 0, Y_FIRST, 128, 128),
    (HEAD_PRIOR, 128, 0, X_FIRST, 128, 128),
    (HEAD_POST_OUT, 128, 0, Z_FIRST, 128, 128),
    (HEAD_POST, 128, 0, Y_FIRST, 256, 128),
    (HEAD_MAN_ENC, 128, 0, X_FIRST, 0, 128),
    (HEAD_PRIOR_OUT, 128, 0, Z_FIRST, 0, 128),
    (HEAD_POST, 128, 0, Y_FIRST, 384, 128),
    (HEAD_MAN_ENC, 128, 0, X_FIRST, 128, 128),
    (HEAD_PRIOR_OUT, 128, 0, Z_FIRST, 128, 128),
    (HEAD_POST, 128, 0, X_FIRST, 512, 128),
)
HEAD_GROUPS = ((0, 1, 2), (3, 4, 5), (6, 7, 8), (9, 10, 11), (12,))
HEAD_TIMES = (0, 2, 4, 7, 9, 11, 13, 15, 17)
HEAD_LAG = 1
FORWARD_ROWS, BACK_ROWS = (128, 128)
LAST_WORKER, LAST_GOAL_OUT, LAST_GOAL_IN, LAST_IMG, LAST_GRU = range(5)
LAST_SOURCES = (None, SOURCE_GOAL_OUT, SOURCE_GOAL_IN, SOURCE_1024)
LAST_UNITS = (
    (LAST_WORKER, 128, 0, X_FIRST, 384, 128),
    (LAST_WORKER, 128, 0, Z_FIRST, 640, 128),
    (LAST_WORKER, 128, 0, X_FIRST, 512, 128),
    (LAST_GOAL_OUT, 128, 0, Z_FIRST, 0, 128),
    (LAST_GOAL_IN, 128, 0, Z_FIRST, 0, 16),
    (LAST_IMG, 128, 0, X_FIRST, 0, 128),
    (LAST_GRU, 128, 0, X_ONLY, 0, 256),
    (LAST_GRU, 128, 0, Z_ONLY, 256, 256),
    (LAST_WORKER, 128, 0, Y_FIRST, 0, 128),
    (LAST_GRU, 128, H, X_ONLY, 0, 256),
    (LAST_GRU, 128, H, Z_ONLY, 256, 256),
    (LAST_WORKER, 128, 0, Y_FIRST, 128, 128),
    (LAST_GRU, 128, 2 * H, X_ONLY, 0, 256),
    (LAST_GRU, 128, 2 * H, Z_ONLY, 384, 128),
    (LAST_WORKER, 128, 0, Y_FIRST, 256, 128),
    (LAST_IMG, 128, 0, Y_FIRST, 128, 128),
    (LAST_GRU, 128, 2 * H, X_ONLY, 256, 128),
)
LAST_GROUPS = ((0, 1), (2, 3, 4), (5, 6, 7), (8, 9, 10), (11, 12, 13), (14, 15, 16))


class Worker(NamedTuple):
    goal_codes: Any = taken(GC, ROWS, dtype=jnp.int32)
    actions: Any = taken(HOR, ROWS, dtype=jnp.int32)
    samples: Any = taken(HOR, ZG, ROWS, dtype=jnp.int32)
    vectors: Any = taken(4, VECTOR_TILES, LANES, dtype=F32)
    tables: Any = taken(4, TABLES, LANES)
    start_state: Any = taken(ROWS, H + LANES)
    goal_out: Any = taken(U, H)
    actor_in: Any = taken(3 * H, U)
    critic_in: Any = taken(3 * H, U)
    post_left: Any = taken(H + E, ROWS, here=False)
    post_out_left: Any = taken(H, ROWS, here=False)
    prior_out_left: Any = taken(H, ROWS, here=False)
    me_left: Any = taken(H, 2 * ROWS, here=False)
    post_right: Any = taken(ROWS, H, here=False)
    prior_right: Any = taken(ROWS, H, here=False)
    post_out_right: Any = taken(ROWS, Z, here=False)
    prior_out_right: Any = taken(ROWS, Z, here=False)
    me_right: Any = taken(2 * ROWS, 2 * U, here=False)
    worker_own: Any = given(2, *WORKER_SHARE, here=False)
    worker_sibling: Any = given(2, *WORKER_SHARE, here=False)
    returned: Any = given(ROWS, H)
    goal_left: Any = given(U, ROWS)
    code_turned: Any = given(GCODE, ROWS)
    goal_right: Any = given(ROWS, H)
    goal_pair: Any = given(ROWS, 2 * U)
    small: Any = given(2, 2, SMALL_TILES, LANES, dtype=F32)
    sums: Any = tuple(given(unit[-1], LANES, dtype=F32) for unit in HEAD_UNITS)
    worker_left: Any = kept(3 * H, 2 * U)
    act_out: Any = kept(32, U)
    goal_in: Any = kept(GCODE, U)
    action_columns: Any = kept(ROWS, LANES, dtype=F32)
    goal_normed: Any = kept(ROWS, U, dtype=F32)
    goal_inverse: Any = kept(ROWS, 1, dtype=F32)
    goal_hidden: Any = kept(ROWS, U)
    goal_pre: Any = kept(ROWS, U)
    goal_low: Any = kept(ROWS, H)
    turned: Any = kept(2 * H, ROWS)
    slot_part: Any = kept(2, ROWS, U, dtype=F32)
    hot: Any = kept(2 * ROWS, Z)
    pre: Any = kept(2 * ROWS, U, dtype=F32)
    hidden: Any = kept(2 * ROWS, U)
    normed: Any = kept(2, HOR * ROWS, U, dtype=F32)
    inverse: Any = kept(2, HOR * ROWS, 1, dtype=F32)
    hot_turned: Any = kept(Z, HOR * ROWS)
    log_chance: Any = kept(HOR * ROWS, 32, dtype=F32)
    chosen: Any = kept(ROWS, LANES, dtype=F32)
    value: Any = kept(ROWS, LANES, dtype=F32)
    returns: Any = kept(ROWS, LANES, dtype=F32)
    pre_pair: Any = kept(HOR * ROWS, 2 * U)
    summed: Any = kept(2, ROWS, U, dtype=F32)
    sum_low: Any = kept(2, ROWS, U)
    sum_pair: Any = kept(ROWS, 2 * U)
    low_512: Any = kept(ROWS, U)
    grad_column: Any = kept(ROWS, 1, dtype=F32)
    to_state: Any = kept(ROWS, H)
    incoming: Any = kept(ROWS, H)
    wide_512: Any = kept(ROWS, U, dtype=F32)
    top: Any = kept(2, 8, LANES, dtype=F32)
    top_in: Any = kept(10, 8, LANES, dtype=F32)
    left_2: Any = tuple(kept(2, s.rows, 2 * s.depth) for s in HEAD_SOURCES)
    right_2: Any = tuple(kept(2 * s.depth, s.columns) for s in HEAD_SOURCES)
    outbox: Any = boxes(HEAD_UNITS)
    inbox: Any = boxes(HEAD_UNITS)
    add_send: Any = signal(2, 2)
    add_recv: Any = signal(2, 2)
    add_local: Any = signal(2, 2)
    top_send: Any = signal(10)
    top_recv: Any = signal(10)
    state_send: Any = signal(8)
    state_recv: Any = signal(8)
    pair_send: Any = signal(len(HEAD_SOURCES), 3)
    pair_recv: Any = signal(len(HEAD_SOURCES), 3)
    pair_local: Any = signal(len(HEAD_SOURCES), 3)
    half_send: Any = signal(len(HEAD_UNITS), 4)
    half_recv: Any = signal(len(HEAD_UNITS), 4)

    def gain(self, low, size):
        return vector_of(self.vectors, low, size // (4 * LANES))

    def goal(self):
        self.small[...] = jnp.zeros(self.small.shape, F32)
        for r in range(4):
            self.act_out[:, r * LANES : (r + 1) * LANES] = self.tables[
                r, TAB_ACT : TAB_ACT + 32, :
            ]
            for i in range(4):
                self.goal_in[16 * r : 16 * (r + 1), i * LANES : (i + 1) * LANES] = self.tables[
                    r, TAB_GOAL + 16 * i : TAB_GOAL + 16 * (i + 1), :
                ]
        self.action_columns[...] = columns_of(self.actions[...].astype(F32))
        hot = hot_rows(columns_of(self.goal_codes[...].astype(F32)), GK, GC, LANES)
        self.code_turned[...] = hot.T[0:GCODE].astype(BF)
        matmul_into(self.goal_normed, hot[:, 0:GCODE].astype(BF), self.goal_in)
        hidden_rows(
            self.goal_normed, self.goal_inverse, self.gain(GOAL_G, U), self.goal_hidden
        )
        turn_into(self.goal_left, self.goal_hidden)

        def one(j, totals):
            lanes = pl.ds(pl.multiple_of(j * TILE, TILE), TILE)
            goal = product(self.goal_hidden[...], self.goal_out[:, lanes])
            state = self.start_state[:, lanes].astype(F32)
            self.goal_low[:, lanes] = goal.astype(BF)
            terms = (goal * state, goal * goal, state * state)
            return tuple(
                t + jnp.sum(term, -1, keepdims=True) for t, term in zip(totals, terms)
            )

        zero = jnp.zeros((ROWS, 1), F32)
        aligned, goal_square, state_square = lax.fori_loop(0, H // TILE, one, (zero,) * 3)
        turn_into(self.turned, self.start_state.at[:, 0:H])
        turn_into(self.turned, self.goal_low, H)
        return aligned / (jnp.maximum(goal_square, state_square) + small_floor)

    def slots(self):
        for which, weight in enumerate((self.actor_in, self.critic_in)):
            def one(j, carry):
                lanes = pl.ds(pl.multiple_of(j * TILE, TILE), TILE)
                self.slot_part[which, :, lanes] = product(
                    self.start_state[:, 0:H], weight[0:H, lanes]
                ) + product(self.goal_low[...], weight[2 * H : 3 * H, lanes])
                return carry

            lax.fori_loop(0, U // TILE, one, 0)

    def forward(self, first, last):
        gains = (self.gain(ACT_G, U), self.gain(CRI_G, U))
        head = self.gain(CRI_O, U)
        spread = class_spread(ZG, ZK, ZG, Z)
        lane = lax.broadcasted_iota(jnp.int32, (1, Z), 1)
        lane_class = jnp.bitwise_and(lane, ZK - 1).astype(F32)
        group = lax.broadcasted_iota(jnp.int32, (Z, ZG), 1)
        place = lax.broadcasted_iota(jnp.int32, (Z, ZG), 0)
        inside = (place >= group * ZK) & (place < group * ZK + ZK)
        spread_turned = jnp.where(inside, 1.0, 0.0).astype(BF)
        place_class = jnp.bitwise_and(
            lax.broadcasted_iota(jnp.int32, (Z, 1), 0), ZK - 1
        ).astype(F32)
        act_lane = lax.broadcasted_iota(jnp.int32, (1, 32), 1)
        step_lane = lax.broadcasted_iota(jnp.int32, (1, LANES), 1)

        def pair(i, carry):
            start = pl.multiple_of(i * 2 * ROWS, 2 * ROWS)
            for half in range(2):
                k = 2 * i + half
                rows = pl.ds(pl.multiple_of(start + half * ROWS, ROWS), ROWS)
                ids = self.samples[k].astype(F32)
                self.hot[half * ROWS : (half + 1) * ROWS, :] = jnp.where(
                    product(columns_of(ids)[:, 0:ZG].astype(BF), spread) == lane_class, 1.0, 0.0
                ).astype(BF)
                self.hot_turned[:, rows] = jnp.where(
                    product(spread_turned, ids.astype(BF)) == place_class, 1.0, 0.0
                ).astype(BF)
            for which, weight in enumerate((self.actor_in, self.critic_in)):
                self.pre[...] = product(self.hot[...], weight[H : 2 * H, :])
                for low in range(0, 2 * ROWS, FORWARD_ROWS):
                    rows = pl.ds(pl.multiple_of(start + low, FORWARD_ROWS), FORWARD_ROWS)
                    slot = pl.ds(low % ROWS, FORWARD_ROWS)
                    pre = self.pre[low : low + FORWARD_ROWS, :] + self.slot_part[which, slot, :]
                    normed, inverse = normalize(pre)
                    self.normed[which, rows, :] = normed
                    self.inverse[which, rows, :] = inverse
                    hidden = elu_of(normed * gains[which]).astype(BF)
                    if which == 0:
                        self.hidden[low : low + FORWARD_ROWS, :] = hidden
                    else:
                        value = jnp.sum(hidden.astype(F32) * head, -1, keepdims=True)
                        here = step_lane == 2 * i + low // ROWS
                        self.value[slot, :] = jnp.where(here, value, self.value[slot, :])
            logits = lax.dot_general(
                self.hidden[...], self.act_out[...], (((1,), (1,)), ((), ())),
                preferred_element_type=F32,
            )
            logits = jnp.where(act_lane < NA, logits, -1e30)
            shifted = logits - jnp.max(logits, -1, keepdims=True)
            total = jnp.sum(jnp.exp(shifted), -1, keepdims=True)
            self.log_chance[pl.ds(start, 2 * ROWS), :] = shifted - jnp.log(total)
            return carry

        lax.fori_loop(first, last, pair, 0)

    def action_here(self, k):
        action = self.at_step(self.action_columns, k)
        return action == lax.broadcasted_iota(jnp.int32, (1, 32), 1).astype(F32)

    def at_step(self, ref, k):
        lane = lax.broadcasted_iota(jnp.int32, (ROWS, LANES), 1)
        return jnp.sum(jnp.where(lane == k, ref[...], 0.0), -1, keepdims=True)

    def targets(self, reward):
        weight = self.start_state[:, H : H + 1].astype(F32)
        lane = lax.broadcasted_iota(jnp.int32, (ROWS, LANES), 1)
        later = self.value[:, HOR - 1 : HOR]
        result = later
        returns = jnp.where(lane == HOR - 1, result, 0.0)
        for k in range(HOR - 2, -1, -1):
            blended = (1.0 - return_mix) * later + return_mix * result
            result = reward + discount * blended
            returns = jnp.where(lane == k, result, returns)
            later = self.value[:, k : k + 1]
        self.returns[...] = returns
        gaps = jnp.where(lane < HOR, jnp.abs(returns - self.value[...]), 0.0)
        top = jnp.max(weight * gaps, 0, keepdims=True)
        self.top[0] = jnp.broadcast_to(jnp.max(top, 1, keepdims=True), (8, LANES))

    def critic_back(self, first, last, total):
        gain, head = (self.gain(CRI_G, U), self.gain(CRI_O, U))
        weight = self.start_state[:, H : H + 1].astype(F32)

        def step(k, totals):
            rows = pl.ds(pl.multiple_of(k * ROWS, ROWS), ROWS)
            misfit = self.at_step(self.value, k) - self.at_step(self.returns, k)
            grad = weight * misfit * (1.0 / (ROWS * HOR))
            self.grad_column[...] = grad
            gain_total = totals[0] + hidden_rows_back(
                lambda r: self.grad_column[r, :] * head,
                self.normed.at[1, rows], self.inverse.at[1, rows], gain, self.low_512, BACK_ROWS,
                self.hidden,
            )
            head_total = totals[1] + jnp.sum(
                self.hidden[0:ROWS, :].astype(F32) * grad, 0, keepdims=True
            )
            for j in range(4):
                tile = self.low_512[:, j * LANES : (j + 1) * LANES].astype(F32)
                self.summed[1, :, j * LANES : (j + 1) * LANES] += tile
                turned = pltpu.roll(tile, 64, 1)
                self.pre_pair[rows, 2 * j * LANES : (2 * j + 1) * LANES] = turned.astype(BF)
                self.pre_pair[rows, (2 * j + 1) * LANES : (2 * j + 2) * LANES] = tile.astype(BF)
            return (gain_total, head_total)

        return lax.fori_loop(first, last, step, total)

    def pair(self, first, second, out_ref, rows):
        lane = lax.broadcasted_iota(jnp.int32, (ROWS, LANES), 1)
        for j in range(4):
            lanes = slice(j * LANES, (j + 1) * LANES)
            even = slice(2 * j * LANES, (2 * j + 1) * LANES)
            odd = slice((2 * j + 1) * LANES, (2 * j + 2) * LANES)
            a = first[:, lanes].astype(F32)
            if second is None:
                b_even, b_odd = (out_ref[rows, even].astype(F32), out_ref[rows, odd].astype(F32))
            else:
                b_odd = second[:, lanes].astype(F32)
                b_even = pltpu.roll(b_odd, 64, 1)
            out_ref[rows, even] = jnp.where(lane < 64, a, b_even).astype(BF)
            out_ref[rows, odd] = jnp.where(lane < 64, pltpu.roll(a, 64, 1), b_odd).astype(BF)

    def actor_back(self, first, last, totals):
        gain = self.gain(ACT_G, U)
        weight = self.start_state[:, H : H + 1].astype(F32)
        scale = self.top[1, 0:1, 0:1] + small_floor

        def step(k, totals):
            rows = pl.ds(pl.multiple_of(k * ROWS, ROWS), ROWS)
            advantage = self.at_step(self.returns, k) - self.at_step(self.value, k)
            gained = weight * advantage / scale
            here = self.action_here(k)
            log_chance = self.log_chance[rows, :]
            chance = jnp.exp(log_chance)
            grad = (gained * (-1.0 / (ROWS * HOR))) * (jnp.where(here, 1.0, 0.0) - chance)
            grad_turned = jnp.concatenate(
                [grad, jnp.zeros((ROWS, LANES - 32), F32)], 1
            ).T[0:32].astype(BF)
            self.wide_512[...] = product(grad.astype(BF), self.act_out[...])
            gain_total = totals[0] + hidden_rows_back(
                lambda r: self.wide_512[r, :],
                self.normed.at[0, rows], self.inverse.at[0, rows], gain, self.low_512, BACK_ROWS,
                self.hidden,
            )
            out_total = totals[1] + product(grad_turned, self.hidden[0:ROWS, :])
            self.summed[0] += self.low_512[...].astype(F32)
            self.pair(self.low_512, None, self.pre_pair, rows)
            chosen = jnp.sum(jnp.where(here, log_chance, 0.0), -1, keepdims=True)
            loss = totals[2] + jnp.sum(chosen * gained, 0, keepdims=True)
            return (gain_total, out_total, loss)

        return lax.fori_loop(first, last, step, totals)

    def inputs_back(self, low, out_ref):
        def one(j, carry):
            rows = pl.ds(pl.multiple_of(low + j * TILE, TILE), TILE)
            total = 0.0
            for which, weight in enumerate((self.actor_in, self.critic_in)):
                total = total + lax.dot_general(
                    self.sum_low[which], weight[rows, :], (((1,), (1,)), ((), ())),
                    preferred_element_type=F32,
                )
            out_ref[:, pl.ds(pl.multiple_of(j * TILE, TILE), TILE)] = total.astype(BF)
            return carry

        lax.fori_loop(0, H // TILE, one, 0)

    def goal_back(self):
        matmul_into(self.wide_512, self.goal_right[...], self.goal_out, turned=True)
        total = hidden_rows_back(
            lambda rows: self.wide_512[rows, :],
            self.goal_normed, self.goal_inverse, self.gain(GOAL_G, U), self.goal_pre,
        )
        put_vector(self.small, GOAL_G, total)
        spread_lanes(self.goal_pre, self.goal_pair, 0, 0)

    def weights(self, tile):
        size = 2 * U // 2
        for low in range(tile * size, (tile + 1) * size, TILE):
            lanes = slice(low, low + TILE)
            self.worker_left[H : 2 * H, lanes] = product(
                self.hot_turned[...], self.pre_pair[:, lanes]
            ).astype(BF)
            pair = self.sum_pair[:, lanes]
            self.worker_left[0:H, lanes] = product(self.turned[0:H], pair).astype(BF)
            self.worker_left[2 * H : 3 * H, lanes] = product(
                self.turned[H : 2 * H], pair
            ).astype(BF)

    def hand_over(self, places, tile):
        size, rows = (2 * U // 2, WORKER_SHARE[0])
        lanes, copies = (pl.ds(tile * size, size), [])
        for y in range(2):
            ours, theirs = (
                pl.ds(pl.multiple_of((2 * y + core) * rows, 16), rows)
                for core in (places.c, 1 - places.c)
            )
            copies.append(
                send_to(
                    self.worker_left.at[theirs, lanes], self.worker_sibling.at[y, :, lanes],
                    self.add_send.at[tile, y], self.add_recv.at[tile, y], places.to_c,
                )
            )
            copies.append(
                pltpu.make_async_copy(
                    self.worker_left.at[ours, lanes], self.worker_own.at[y, :, lanes],
                    self.add_local.at[tile, y],
                )
            )
        for copy in copies:
            copy.start()
        return copies


def worker_kernel(f):
    places = Places()
    met = greet(
        [(places.around(o), places.rep) for o in range(1, 8)]
        + [places.to_c, places.to_y, places.to_d]
    )
    reward = f.goal()
    met()
    heads = []
    lefts = (f.post_left, f.post_left, f.post_out_left, f.prior_out_left, f.me_left)
    rights = (f.post_right, f.prior_right, f.post_out_right, f.prior_out_right, f.me_right)
    for i, source in enumerate(HEAD_SOURCES):
        heads.append(
            Exchange(
                places, source, f.left_2[i], f.right_2[i], f.pair_send, f.pair_recv,
                f.pair_local, i,
            )
        )
    for i in (HEAD_POST, HEAD_PRIOR, HEAD_POST_OUT):
        heads[i].start(0, lefts[i], rights[i])
    halving = Halving(
        places, [(heads[unit[0]],) + unit[1:] for unit in HEAD_UNITS], f.outbox, f.inbox,
        f.half_send, f.half_recv, f.sums, HEAD_GROUPS,
    )
    events = iter(range(24))

    def beside():
        event = next(events)
        for t, place in enumerate(HEAD_TIMES):
            if place == event:
                halving.slot(t, HEAD_LAG)

    f.slots()
    beside()
    for i in (HEAD_MAN_ENC, HEAD_PRIOR_OUT):
        heads[i].start(0, lefts[i], rights[i])
    f.value[...] = jnp.zeros(f.value.shape, F32)
    f.summed[...] = jnp.zeros(f.summed.shape, F32)
    beside()
    for i in range(4):
        f.forward(2 * i, 2 * i + 2)
        beside()
    f.targets(reward)
    totals = (jnp.zeros((1, U), F32), jnp.zeros((1, U), F32))
    steps = (0, 3, 6, 9, 12, HOR)

    def send_top(which, first, devices):
        copies = []
        for i, device in enumerate(devices):
            k = first + i
            copies.append(
                send_to(f.top.at[which], f.top_in.at[k], f.top_send.at[k], f.top_recv.at[k], device)
            )
            copies[i].start()
        return copies

    def largest(which, first, copies):
        top = f.top[which]
        for i, copy in enumerate(copies):
            copy.wait()
            top = jnp.maximum(top, f.top_in[first + i])
        f.top[1] = top

    tops = send_top(0, 0, [(places.around(o), places.rep) for o in range(1, 8)])
    for k in range(5):
        if k == 3:
            largest(0, 0, tops)
            tops = send_top(1, 7, [places.to_c, places.to_y, places.to_d])
        totals = f.critic_back(steps[k], steps[k + 1], totals)
        beside()
    largest(1, 7, tops)
    put_vector(f.small, CRI_G, totals[0])
    put_vector(f.small, CRI_O, totals[1])
    totals = (jnp.zeros((1, U), F32), jnp.zeros((32, U), F32), jnp.zeros((1, 1), F32))
    for i in range(4):
        totals = f.actor_back(4 * i, 4 * i + 4, totals)
        beside()
    actor_gain, actor_out, chosen = totals
    put_vector(f.small, ACT_G, actor_gain)
    put_table(f.small, ACT_T, actor_out, 24)
    for which in range(2):
        f.sum_low[which] = f.summed[which].astype(BF)
    f.inputs_back(0, f.to_state)
    states = regroup_start(places, f.to_state, f.incoming, f.state_send, f.state_recv)
    f.pair(f.sum_low.at[0], f.sum_low.at[1], f.sum_pair, slice(0, ROWS))
    beside()
    f.weights(0)
    halves = f.hand_over(places, 0)
    f.weights(1)
    halves += f.hand_over(places, 1)
    beside()
    f.inputs_back(2 * H, f.goal_right)
    f.goal_back()
    beside()
    weight = f.start_state[:, H : H + 1].astype(F32)
    misfit = f.value[...] - f.returns[...]
    squares = jnp.sum(jnp.sum(weight * misfit * misfit, -1, keepdims=True), 0, keepdims=True)
    loss = (0.5 * squares - chosen) * (1.0 / (ROWS * HOR))
    for y in range(2):
        for c in range(2):
            f.small[c, y, LOSS : LOSS + 1, :] = jnp.broadcast_to(loss, (1, LANES))
    for copy in states + halves:
        copy.wait()
    f.returned[...] = f.incoming[...]
    halving.drain()


class Last(NamedTuple):
    meta_turned: Any = taken(LANES, ROWS, dtype=F32)
    prev: Any = taken(ROWS, H)
    vectors: Any = taken(4, VECTOR_TILES, LANES, dtype=F32)
    returned: Any = taken(ROWS, H)
    grad_partial: Any = taken(ROWS, H, dtype=F32)
    gru_normed: Any = taken(ROWS, 3 * H, dtype=F32)
    gru_inverse: Any = taken(ROWS, 1, dtype=F32)
    img_normed: Any = taken(ROWS, H, dtype=F32)
    img_inverse: Any = taken(ROWS, 1, dtype=F32)
    small_1: Any = taken(2, 2, SMALL_TILES, LANES, dtype=F32)
    small_2: Any = taken(2, 2, SMALL_TILES, LANES, dtype=F32)
    gru_share: Any = taken(2 * H, 3 * H, here=False)
    worker_own_in: Any = taken(2, *WORKER_SHARE, here=False)
    worker_sibling_in: Any = taken(2, *WORKER_SHARE, here=False)
    goal_left: Any = taken(U, ROWS, here=False)
    dec_left: Any = taken(U, ROWS, here=False)
    code_turned: Any = taken(GCODE, ROWS, here=False)
    soft_turned: Any = taken(GCODE, ROWS, here=False)
    gru_left: Any = taken(2 * H, ROWS, here=False)
    img_left: Any = taken(Z, ROWS, here=False)
    goal_right: Any = taken(ROWS, H, here=False)
    recon_low: Any = taken(ROWS, H, here=False)
    goal_pair: Any = taken(ROWS, 2 * U, here=False)
    dec_pair: Any = taken(ROWS, 2 * U, here=False)
    deter_grad: Any = given(ROWS, H, dtype=F32)
    small_sum: Any = given(SMALL_TILES, LANES, dtype=F32)
    sums: Any = tuple(given(unit[-1], LANES, dtype=F32) for unit in LAST_UNITS)
    gru_weight: Any = kept(2 * H, 3 * H)
    gru_right: Any = kept(ROWS, 3 * H)
    gru_thirds: Any = kept(ROWS, 3 * H)
    img_right: Any = kept(ROWS, H)
    grad: Any = kept(ROWS, H, dtype=F32)
    wide: Any = kept(ROWS, 2 * H, dtype=F32)
    small: Any = kept(2, 2, SMALL_TILES, LANES, dtype=F32)
    small_pair: Any = kept(2, SMALL_TILES, LANES, dtype=F32)
    small_in: Any = kept(4, SMALL_TILES, LANES, dtype=F32)
    worker_own: Any = kept(2, *WORKER_SHARE)
    worker_sibling: Any = kept(2, *WORKER_SHARE)
    gru_left_4: Any = kept(H // 2, 4 * ROWS)
    gru_right_4: Any = kept(4 * ROWS, 3 * H)
    left_2: Any = tuple(kept(2, s.rows, 2 * s.depth) for s in LAST_SOURCES[1:])
    right_2: Any = tuple(kept(2 * s.depth, s.columns) for s in LAST_SOURCES[1:])
    outbox: Any = boxes(LAST_UNITS)
    inbox: Any = boxes(LAST_UNITS)
    load_done: Any = signal(1)
    add_done: Any = signal(2, 2)
    wide_send: Any = signal(12)
    wide_recv: Any = signal(12)
    wide_local: Any = signal(4)
    pair_send: Any = signal(5, 3)
    pair_recv: Any = signal(5, 3)
    pair_local: Any = signal(5, 3)
    half_send: Any = signal(len(LAST_UNITS), 4)
    half_recv: Any = signal(len(LAST_UNITS), 4)
    small_send: Any = signal(5)
    small_recv: Any = signal(5)

    def state_back(self):
        gain = vector_of(self.vectors, GRU_G, 6)
        frame = lax.broadcasted_iota(jnp.int32, (ROWS, ROWS), 0).astype(F32)
        place = jnp.where(self.meta_turned[37:38, :] == frame, 1.0, 0.0).astype(BF)

        def add(j, carry):
            lanes = pl.ds(pl.multiple_of(j * TILE, TILE), TILE)
            self.grad[:, lanes] = self.grad_partial[:, lanes] + product(
                place, self.returned[:, lanes]
            )
            return carry

        lax.fori_loop(0, H // TILE, add, 0)

        def one(rows, total):
            normed = self.gru_normed[rows, :]
            parts = normed * gain
            inner = parts[:, H : 2 * H]
            reset = 1.0 / (1.0 + jnp.exp(-parts[:, :H]))
            candidate = jnp.tanh(reset * inner)
            update = 1.0 / (1.0 + jnp.exp(1.0 - parts[:, 2 * H :]))
            grad = self.grad[rows, :]
            prev = self.prev[rows, :].astype(F32)
            grad_inner = grad * update * (1.0 - candidate * candidate)
            grad_parts = jnp.concatenate(
                [
                    grad_inner * inner * reset * (1.0 - reset),
                    grad_inner * reset,
                    grad * (candidate - prev) * update * (1.0 - update),
                ],
                1,
            )
            self.deter_grad[rows, :] = grad * (1.0 - update)
            total = total + jnp.sum(grad_parts * normed, 0, keepdims=True)
            back = normalize_back(grad_parts * gain, normed, self.gru_inverse[rows, :])
            self.gru_right[rows, :] = back.astype(BF)
            for j in range(24):
                low = (j % 3 * 8 + j // 3) * LANES
                self.gru_thirds[rows, low : low + LANES] = back[
                    :, j * LANES : (j + 1) * LANES
                ].astype(BF)
            return total

        put_vector(self.small, GRU_G, by_rows(ROWS, 16, one, jnp.zeros((1, 3 * H), F32)))

    def input_back(self):
        matmul_into(self.wide, self.gru_right[...], self.gru_weight, turned=True)
        self.deter_grad[...] += self.wide[:, H : 2 * H]
        total = hidden_rows_back(
            lambda rows: self.wide[rows, 0:H],
            self.img_normed, self.img_inverse, vector_of(self.vectors, IMG_G, 2), self.img_right,
        )
        put_vector(self.small, IMG_G, total)

    def action_back(self):
        place = lax.broadcasted_iota(jnp.int32, (24, ROWS), 0).astype(F32)
        hot = jnp.where(self.meta_turned[32:33, :] == place, 1.0, 0.0).astype(BF)
        for r in range(4):
            for i in range(2):
                start = (2 * r + i) * LANES
                low = IMG_T + 24 * i
                self.small[r % 2, r // 2, low : low + 24, :] = product(
                    hot, self.img_right[:, start : start + LANES]
                )


class SmallSum:
    def __init__(self, places, f):
        self.places, self.f = (places, f)
        self.copies = []

    def step(self, k):
        f, places = (self.f, self.places)
        if k > 0:
            self.copies[k - 1].wait()
        if k == 0:
            source, target, device = (f.small.at[1 - places.c], f.small_pair, places.to_c)
        elif k == 1:
            f.small_pair[...] = f.small_pair[...] + f.small[places.c]
            source, target, device = (
                f.small_pair.at[1 - places.y], f.small_in.at[0], places.to_y,
            )
        else:
            if k == 2:
                f.small_sum[...] = f.small_pair[places.y] + f.small_in[0]
            else:
                f.small_sum[...] = f.small_sum[...] + f.small_in[k - 2]
            if k == 5:
                return
            device = (places.to_x, places.to_z, places.to_w)[k - 2]
            source, target = (f.small_sum, f.small_in.at[k - 1])
        copy = send_to(source, target, f.small_send.at[k], f.small_recv.at[k], device)
        copy.start()
        self.copies.append(copy)


def last_kernel(f):
    places = Places()
    load = pltpu.make_async_copy(f.gru_share, f.gru_weight, f.load_done.at[0])
    load.start()
    worker = Addition(f.worker_own, f.worker_sibling, f.add_done)
    for part in (1, 0):
        worker.start(f.worker_own_in, f.worker_sibling_in, part)
    met = greet(
        (places.to_c, places.to_y, places.to_d, places.to_x, places.to_z, places.to_w)
    )
    f.small[...] = f.small_1[...] + f.small_2[...]
    f.state_back()
    met()
    sources, part = ([worker], 0)
    for i, source in enumerate(LAST_SOURCES[1:]):
        sources.append(
            Exchange(
                places, source, f.left_2[i], f.right_2[i], f.pair_send, f.pair_recv,
                f.pair_local, part,
            )
        )
        part += len(source.parts)
    gru = Wide(
        places, H // 2, ROWS, f.gru_left_4, f.gru_right_4, f.wide_send, f.wide_recv, f.wide_local
    )
    sources.append(gru)
    for third in range(3):
        gru.start_right(f.gru_thirds, third)
        if third == 0:
            gru.start_left(f.gru_left)
    sources[LAST_GOAL_OUT].start(0, f.goal_left, f.goal_right)
    sources[LAST_GOAL_OUT].start(1, f.dec_left, f.recon_low)
    sources[LAST_GOAL_IN].start(0, f.code_turned, f.goal_pair)
    sources[LAST_GOAL_IN].start(1, f.soft_turned, f.dec_pair)
    sources[LAST_IMG].start_left(0, f.img_left)
    halving = Halving(
        places, [(sources[unit[0]],) + unit[1:] for unit in LAST_UNITS], f.outbox, f.inbox,
        f.half_send, f.half_recv, f.sums, LAST_GROUPS,
    )
    halving.slot(0)
    load.wait()
    f.input_back()
    sources[LAST_IMG].start_right(0, f.img_right)
    halving.slot(1)
    f.action_back()
    small = SmallSum(places, f)
    small.step(0)
    for t in range(2, len(LAST_GROUPS) + 4):
        if t < 5:
            gru.relay(t - 2)
        halving.slot(t)
        if t < 7:
            small.step(t - 1)
    halving.drain()


class Unpack(NamedTuple):
    heads: Any = tuple(taken(unit[-1], LANES, dtype=F32) for unit in HEAD_UNITS)
    last: Any = tuple(taken(unit[-1], LANES, dtype=F32) for unit in LAST_UNITS)
    small: Any = taken(SMALL_TILES, LANES, dtype=F32)
    deter: Any = taken(ROWS, H, dtype=F32)
    embed: Any = taken(ROWS, E, dtype=F32)
    loss: Any = given(1, LANES, dtype=F32)
    deter_grad: Any = given(ROWS, H, dtype=F32)
    embed_grad: Any = given(ROWS, E, dtype=F32)
    obs_gain: Any = given(H // 4, dtype=F32)
    manager_in: Any = given(U // 8, H // 4, dtype=F32)
    manager_gain: Any = given(U // 4, dtype=F32)
    manager_out: Any = given(U // 4, dtype=F32)
    goal_in: Any = given(GCODE // 4, U // 8, dtype=F32)
    goal_gain: Any = given(U // 4, dtype=F32)
    goal_out: Any = given(U // 4, H // 8, dtype=F32)
    actor_in: Any = given(U // 8, 3 * H // 4, dtype=F32)
    actor_gain: Any = given(U // 4, dtype=F32)
    actor_out: Any = given(NA, U // 4, dtype=F32)
    critic_in: Any = given(U // 8, 3 * H // 4, dtype=F32)
    critic_gain: Any = given(U // 4, dtype=F32)
    critic_out: Any = given(U // 4, dtype=F32)
    img_stoch: Any = given(Z // 4, H // 8, dtype=F32)
    img_action: Any = given(NA, H // 4, dtype=F32)
    img_gain: Any = given(H // 4, dtype=F32)
    gru_weight: Any = given(H // 2, 3 * H // 8, dtype=F32)
    gru_gain: Any = given(3 * H // 4, dtype=F32)
    post_in: Any = given((H + E) // 4, H // 8, dtype=F32)
    post_gain: Any = given(H // 4, dtype=F32)
    post_out: Any = given(H // 4, Z // 8, dtype=F32)
    prior_in: Any = given(H // 4, H // 8, dtype=F32)
    prior_gain: Any = given(H // 4, dtype=F32)
    prior_out: Any = given(H // 4, Z // 8, dtype=F32)
    enc_in: Any = given(U // 8, H // 4, dtype=F32)
    enc_gain: Any = given(U // 4, dtype=F32)
    enc_out: Any = given(GCODE, U // 4, dtype=F32)


def unpack_kernel(f):
    f.loss[...] = f.small[LOSS : LOSS + 1, :]
    f.deter_grad[...] = f.deter[...]
    f.embed_grad[...] = f.embed[...]
    for low, vector in (
        (OBS, f.obs_gain), (MAN_G, f.manager_gain), (MAN_O, f.manager_out),
        (GOAL_G, f.goal_gain), (ACT_G, f.actor_gain), (CRI_G, f.critic_gain),
        (CRI_O, f.critic_out), (IMG_G, f.img_gain), (GRU_G, f.gru_gain), (POST_G, f.post_gain),
        (PRIOR_G, f.prior_gain), (ENC_G, f.enc_gain),
    ):
        for i in range(vector.shape[0] // LANES):
            vector[pl.ds(i * LANES, LANES)] = f.small[low + i, :]
    f.actor_out[...] = f.small[ACT_T : ACT_T + NA, :]
    f.enc_out[...] = f.small[ENC_T : ENC_T + GCODE, :]
    for i in range(2):
        f.img_action[:, i * LANES : (i + 1) * LANES] = f.small[
            IMG_T + 24 * i : IMG_T + 24 * i + NA, :
        ]

    def halves(value, rows, first, second):
        for low in range(0, value.shape[0], LANES):
            turned = value[low : low + LANES, :].T
            places = slice(rows.start + low, rows.start + low + LANES)
            first[:, places] = turned[0:64]
            second[:, places] = turned[64:LANES]

    whole = {
        HEAD_POST: f.post_in, HEAD_PRIOR: f.prior_in, HEAD_POST_OUT: f.post_out,
        HEAD_PRIOR_OUT: f.prior_out,
    }
    for unit, value in zip(HEAD_UNITS, f.heads):
        rows = slice(unit[4], unit[4] + unit[5])
        if unit[0] == HEAD_MAN_ENC:
            halves(value, rows, f.manager_in, f.enc_in)
        else:
            whole[unit[0]][rows, :] = value[...]
    whole = {LAST_GOAL_OUT: f.goal_out, LAST_IMG: f.img_stoch}
    for unit, value in zip(LAST_UNITS, f.last):
        rows = slice(unit[4], unit[4] + unit[5])
        if unit[0] == LAST_WORKER:
            halves(value, rows, f.actor_in, f.critic_in)
        elif unit[0] == LAST_GOAL_IN:
            f.goal_in[...] = value[:, 0:64]
        elif unit[0] == LAST_GRU:
            low = unit[2] // H * LANES
            f.gru_weight[rows, low : low + LANES] = value[...]
        else:
            whole[unit[0]][rows, :] = value[...]


class Weights(NamedTuple):
    obs_gain: Any = None
    manager_in: Any = None
    manager_gain: Any = None
    manager_out: Any = None
    goal_in: Any = None
    goal_gain: Any = None
    goal_out: Any = None
    actor_in: Any = None
    actor_gain: Any = None
    actor_out: Any = None
    critic_in: Any = None
    critic_gain: Any = None
    critic_out: Any = None
    img_stoch: Any = None
    img_action: Any = None
    img_gain: Any = None
    gru_weight: Any = None
    gru_gain: Any = None
    post_in: Any = None
    post_gain: Any = None
    post_out: Any = None
    prior_in: Any = None
    prior_gain: Any = None
    prior_out: Any = None
    enc_in: Any = None
    enc_gain: Any = None
    enc_out: Any = None


class Data(NamedTuple):
    deter_states: Any
    embed: Any
    lengths: Any
    resets: Any
    terminal: Any
    rewards: Any
    prev_stoch: Any
    prev_action: Any
    regroup: Any
    goal_codes: Any
    samples: Any
    actions: Any


def step_in_kernels(data, w):
    prev = data.deter_states.reshape(ROWS, H)
    f = run_kernel(
        frames_kernel, Frames(),
        (
            data.lengths, data.resets, data.terminal, data.rewards,
            data.prev_stoch.transpose(0, 2, 1), data.prev_action, data.regroup, prev,
            data.embed.reshape(ROWS, E), w.obs_gain, w.manager_gain, w.manager_out, w.goal_gain,
            w.actor_gain, w.critic_gain, w.critic_out, w.img_gain, w.gru_gain, w.post_gain,
            w.prior_gain, w.enc_gain, w.actor_out.T, w.enc_out.T, w.img_action, w.goal_in,
            w.img_stoch, w.gru_weight, w.manager_in, w.enc_in, w.goal_out, w.prior_in, w.post_in,
            w.prior_out, w.post_out, w.actor_in, w.critic_in,
        ),
        "frames", 0,
    )
    s = run_kernel(
        worker_kernel, Worker(),
        (
            data.goal_codes.T, data.actions.T, data.samples.transpose(1, 2, 0), f.vectors,
            f.tables, f.start_state, f.goal_out_out, f.actor_in_out, f.critic_in_out, f.post_left,
            f.post_out_left, f.prior_out_left, f.me_left, f.post_right, f.prior_right,
            f.post_out_right, f.prior_out_right, f.me_right,
        ),
        "worker", 1,
    )
    b = run_kernel(
        last_kernel, Last(),
        (
            f.meta_turned, prev, f.vectors, s.returned, f.grad_deter, f.gru_normed, f.gru_inverse,
            f.img_normed, f.img_inverse, f.small, s.small, f.gru_weight_out, s.worker_own,
            s.worker_sibling, s.goal_left, f.dec_left, s.code_turned, f.soft_turned, f.gru_left, f.img_left,
            s.goal_right, f.recon_low, s.goal_pair, f.dec_pair,
        ),
        "last", 2,
    )
    u = run_kernel(
        unpack_kernel, Unpack(),
        tuple(s.sums) + tuple(b.sums) + (b.small_sum, b.deter_grad, f.embed_grad),
        "unpack",
    )
    first = len(Unpack._fields) - len(Weights._fields)
    grads = Weights(*tuple(u)[first:])
    grads = grads._replace(
        manager_in=grads.manager_in.T, actor_in=grads.actor_in.T, critic_in=grads.critic_in.T,
        enc_in=grads.enc_in.T, actor_out=grads.actor_out.T, enc_out=grads.enc_out.T,
    )
    return (
        u.loss[0, 0],
        u.deter_grad.reshape(SEQ_DEV, LEN, H),
        u.embed_grad.reshape(SEQ_DEV, LEN, E),
    ) + tuple(grads)


DP, REP = ("dp", "rep")
IMG_ACTION = 14
LARGE = Weights(**dict.fromkeys(Weights._fields, False))._replace(
    manager_in=True,
    goal_in=True,
    goal_out=True,
    actor_in=True,
    critic_in=True,
    img_stoch=True,
    gru_weight=True,
    post_in=True,
    post_out=True,
    prior_in=True,
    prior_out=True,
    enc_in=True,
)


def hidden_forward(pre_act, scaling):
    normed, inverse = normalize(pre_act)
    scaled = normed * scaling
    return ((normed, inverse, scaled), jax.nn.elu(scaled).astype(jnp.bfloat16))


def hidden_backward(grad_hidden, cache, scaling):
    normed, inverse, scaled = cache
    grad_scaled = grad_hidden * jnp.where(scaled > 0, 1.0, jnp.exp(jnp.minimum(scaled, 0.0)))
    grad_gain = jnp.sum(grad_scaled * normed, tuple(range(scaled.ndim - 1)))
    return (normalize_back(grad_scaled * scaling, normed, inverse).astype(jnp.bfloat16), grad_gain)


def input_backward(grad_pre, input_low, weight):
    grad_weight = jnp.einsum("nk,nu->ku", input_low, grad_pre, preferred_element_type=jnp.float32)
    to_input = jnp.einsum("nu,ku->nk", grad_pre, weight, preferred_element_type=jnp.float32)
    return (grad_weight, to_input)


def head_backward(grad_head, hidden_low, head, cache, scaling):
    grad_weight = jnp.einsum("nu,nk->uk", hidden_low, grad_head, preferred_element_type=jnp.float32)
    grad_hidden = jnp.einsum("nk,uk->nu", grad_head, head, preferred_element_type=jnp.float32)
    grad_pre, grad_gain = hidden_backward(grad_hidden, cache, scaling)
    return (grad_weight, grad_pre, grad_gain)


def group_softmax(flat_logits, groups):
    log_part = jax.nn.log_softmax(flat_logits.reshape(flat_logits.shape[0], groups, -1), axis=-1)
    return (log_part, jnp.exp(log_part))


def chain_returns(values_now, rewards_now, linked, carried):

    def back_step(carry_pair, inputs):
        later_return, later_value = carry_pair
        current, reward_now, link_now, carry_now = inputs
        blended = (1.0 - return_mix) * later_value + return_mix * later_return
        result = jnp.where(link_now, reward_now + discount * carry_now * blended, current)
        return ((result, current), result)

    zero_start = jnp.zeros(values_now.shape[:1], jnp.float32)
    _, stacked = lax.scan(
        back_step,
        (zero_start, zero_start),
        (values_now.T, rewards_now.T, linked.T, carried.T),
        reverse=True,
    )
    return stacked.T


def worker_forward(start_state, goal_low, stoch_hot, first_layer, scaling):
    slot_part = product(start_state, first_layer[:H]) + product(goal_low, first_layer[H + Z :])
    varying = product(stoch_hot, first_layer[H : H + Z]).reshape(start_state.shape[0], HOR, U)
    return hidden_forward(slot_part[:, None, :] + varying, scaling)


def worker_backward(grad_pre, start_state, goal_low, stoch_hot, first_layer):
    slot_count = grad_pre.shape[0]
    grad_stoch = jnp.einsum(
        "nz,nu->zu",
        stoch_hot,
        grad_pre.reshape(slot_count * HOR, U),
        preferred_element_type=jnp.float32,
    )
    summed = jnp.sum(grad_pre, 1, dtype=jnp.float32).astype(jnp.bfloat16)
    grad_state_rows, to_state = input_backward(summed, start_state, first_layer[:H])
    grad_goal_rows, to_goal = input_backward(summed, goal_low, first_layer[H + Z :])
    return (jnp.concatenate([grad_state_rows, grad_stoch, grad_goal_rows], 0), to_state, to_goal)


def step_plain(data, shares):
    (deter_states, embed, lengths, resets, terminal, rewards, prev_stoch, prev_action, regroup, goal_codes, samples, actions) = data
    full = [
        lax.all_gather(share, REP, axis=1 if i == IMG_ACTION else 0, tiled=True)
        for i, share in enumerate(shares)
    ]
    (obs_gain, manager_in, manager_gain, manager_out, goal_in, goal_gain, goal_out, actor_in, actor_gain, actor_out, critic_in, critic_gain, critic_out, img_stoch, img_action, img_gain, gru_weight, gru_gain, post_in, post_gain, post_out, prior_in, prior_gain, prior_out, enc_in, enc_gain, enc_out) = full
    prev_low = deter_states.reshape(ROWS, H)
    prev_float = prev_low.astype(jnp.float32)
    embed_low = embed.reshape(ROWS, E)
    positions = lax.broadcasted_iota(jnp.int32, (SEQ_DEV, LEN), 1)
    is_valid = positions < lengths[:, None]
    next_valid = jnp.concatenate([is_valid[:, 1:], jnp.zeros((SEQ_DEV, 1), jnp.bool_)], 1)
    next_reset = jnp.concatenate([resets[:, 1:], jnp.ones((SEQ_DEV, 1), jnp.int32)], 1)
    linked = next_valid & (next_reset == 0)
    carried = 1.0 - terminal.astype(jnp.float32)
    valid_rows = is_valid.astype(jnp.float32).reshape(ROWS)
    frame_scale = valid_rows / ROWS
    stoch_prev_hot = (
        (prev_stoch[..., None] == lax.broadcasted_iota(jnp.int32, (1, 1, 1, ZK), 3))
        .astype(jnp.bfloat16)
        .reshape(ROWS, Z)
    )
    action_prev_hot = (
        prev_action.reshape(ROWS)[:, None] == lax.broadcasted_iota(jnp.int32, (1, NA), 1)
    ).astype(jnp.bfloat16)
    img_cache, img_hidden = hidden_forward(
        product(stoch_prev_hot, img_stoch) + product(action_prev_hot, img_action), img_gain
    )
    gru_input = jnp.concatenate([img_hidden, prev_low], 1)
    gru_normed, gru_inverse = normalize(product(gru_input, gru_weight))
    gru_parts = gru_normed * gru_gain
    reset_gate = jax.nn.sigmoid(gru_parts[:, :H])
    candidate_in = gru_parts[:, H : 2 * H]
    candidate = jnp.tanh(reset_gate * candidate_in)
    update_gate = jax.nn.sigmoid(gru_parts[:, 2 * H :] - 1.0)
    deter_state = update_gate * candidate + (1.0 - update_gate) * prev_float
    deter_low = deter_state.astype(jnp.bfloat16)
    obs_normed, obs_inverse = normalize(deter_state)
    feature = (obs_normed * obs_gain).astype(jnp.bfloat16)
    man_cache, man_hidden = hidden_forward(product(feature, manager_in), manager_gain)
    manager_value = product(man_hidden, manager_out).reshape(SEQ_DEV, LEN)
    manager_return = chain_returns(manager_value, rewards, linked, carried)
    manager_misfit = (manager_value - manager_return).reshape(ROWS)
    post_input = jnp.concatenate([deter_low, embed_low], 1)
    post_cache, post_hidden = hidden_forward(product(post_input, post_in), post_gain)
    post_log, post_prob = group_softmax(product(post_hidden, post_out), ZG)
    prior_cache, prior_hidden = hidden_forward(product(deter_low, prior_in), prior_gain)
    prior_log, prior_prob = group_softmax(product(prior_hidden, prior_out), ZG)
    log_gap = post_log - prior_log
    group_kl = jnp.sum(post_prob * log_gap, -1, keepdims=True)
    enc_cache, enc_hidden = hidden_forward(product(deter_low, enc_in), enc_gain)
    code_log, code_prob = group_softmax(product(enc_hidden, enc_out), GC)
    code_kl = jnp.sum(code_prob * (code_log + math.log(GK)), (1, 2))
    code_spread = jnp.sum(code_prob * code_log, -1, keepdims=True)
    soft_code = code_prob.reshape(ROWS, GCODE).astype(jnp.bfloat16)
    dec_cache, dec_hidden = hidden_forward(product(soft_code, goal_in), goal_gain)
    recon_err = product(dec_hidden, goal_out) - deter_state
    frame_terms = (
        jnp.sum(post_prob * log_gap, (1, 2)) + code_kl + 0.5 * jnp.mean(recon_err * recon_err, -1)
    )
    frame_loss = jnp.sum(valid_rows * (0.5 * manager_misfit * manager_misfit + frame_terms)) / ROWS
    send_order = regroup[0]
    start_state, slot_flag = (
        lax.all_to_all(deter_low[send_order], DP, split_axis=0, concat_axis=0, tiled=True),
        lax.all_to_all(
            valid_rows[send_order].astype(jnp.bfloat16),
            DP,
            split_axis=0,
            concat_axis=0,
            tiled=True,
        ),
    )
    slot_weight = slot_flag.astype(jnp.float32)
    code_hot = (
        (goal_codes[:, :, None] == lax.broadcasted_iota(jnp.int32, (1, 1, GK), 2))
        .astype(jnp.bfloat16)
        .reshape(ROWS, GCODE)
    )
    goal_cache, goal_hidden = hidden_forward(product(code_hot, goal_in), goal_gain)
    goal_vector = product(goal_hidden, goal_out)
    goal_low = goal_vector.astype(jnp.bfloat16)
    state_float = start_state.astype(jnp.float32)
    alignment = jnp.sum(goal_vector * state_float, -1)
    largest_square = (
        jnp.maximum(jnp.sum(goal_vector * goal_vector, -1), jnp.sum(state_float * state_float, -1))
        + small_floor
    )
    reward_slot = alignment / largest_square
    stoch_hot = (
        (samples[..., None] == lax.broadcasted_iota(jnp.int32, (1, 1, 1, ZK), 3))
        .astype(jnp.bfloat16)
        .reshape(ROWS * HOR, Z)
    )
    action_hot = (actions[..., None] == lax.broadcasted_iota(jnp.int32, (1, 1, NA), 2)).astype(
        jnp.float32
    )
    actor_cache, actor_hidden = worker_forward(
        start_state, goal_low, stoch_hot, actor_in, actor_gain
    )
    logits = jnp.einsum("rku,ua->rka", actor_hidden, actor_out, preferred_element_type=jnp.float32)
    log_chance = jax.nn.log_softmax(logits, axis=-1)
    chosen = jnp.sum(log_chance * action_hot, -1)
    critic_cache, critic_hidden = worker_forward(
        start_state, goal_low, stoch_hot, critic_in, critic_gain
    )
    worker_value = jnp.einsum(
        "rku,u->rk", critic_hidden, critic_out, preferred_element_type=jnp.float32
    )
    step_link = lax.broadcasted_iota(jnp.int32, (ROWS, HOR), 1) < HOR - 1
    worker_return = chain_returns(
        worker_value,
        jnp.broadcast_to(reward_slot[:, None], (ROWS, HOR)),
        step_link,
        jnp.ones((ROWS, HOR), jnp.float32),
    )
    advantage = worker_return - worker_value
    local_top = jnp.max(slot_weight[:, None] * jnp.abs(advantage))
    return_scale = lax.pmax(local_top, (DP, REP)) + small_floor
    step_total = ROWS * HOR
    value_misfit = worker_value - worker_return
    critic_part = 0.5 * jnp.sum(slot_weight[:, None] * value_misfit * value_misfit)
    actor_part = jnp.sum(slot_weight[:, None] * chosen * advantage) / return_scale
    local_loss = frame_loss + (critic_part - actor_part) / step_total
    grad_value = slot_weight[:, None] * value_misfit / step_total
    grad_chosen = -slot_weight[:, None] * advantage / return_scale / step_total
    grad_logits = (grad_chosen[..., None] * (action_hot - jnp.exp(log_chance))).astype(jnp.bfloat16)
    grad_actor_out = jnp.einsum(
        "rku,rka->ua", actor_hidden, grad_logits, preferred_element_type=jnp.float32
    )
    grad_actor_hidden = jnp.einsum(
        "rka,ua->rku", grad_logits, actor_out, preferred_element_type=jnp.float32
    )
    actor_pre, grad_actor_gain = hidden_backward(grad_actor_hidden, actor_cache, actor_gain)
    grad_critic_out = jnp.einsum("rku,rk->u", critic_hidden, grad_value, precision=highest)
    critic_pre, grad_critic_gain = hidden_backward(
        grad_value[..., None] * critic_out, critic_cache, critic_gain
    )
    grad_actor_in, actor_to_state, actor_to_goal = worker_backward(
        actor_pre, start_state, goal_low, stoch_hot, actor_in
    )
    grad_critic_in, critic_to_state, critic_to_goal = worker_backward(
        critic_pre, start_state, goal_low, stoch_hot, critic_in
    )
    grad_goal_low = (actor_to_goal + critic_to_goal).astype(jnp.bfloat16)
    worker_goal_out, goal_pre, worker_goal_gain = head_backward(
        grad_goal_low, goal_hidden, goal_out, goal_cache, goal_gain
    )
    worker_goal_in = jnp.einsum("ng,nu->gu", code_hot, goal_pre, preferred_element_type=jnp.float32)
    returned = lax.all_to_all(
        (actor_to_state + critic_to_state).astype(jnp.bfloat16),
        DP,
        split_axis=0,
        concat_axis=0,
        tiled=True,
    )
    grad_manager_value = frame_scale * manager_misfit
    grad_manager_out = jnp.dot(grad_manager_value, man_hidden, precision=highest)
    manager_pre, grad_manager_gain = hidden_backward(
        grad_manager_value[:, None] * manager_out, man_cache, manager_gain
    )
    grad_manager_in, grad_feature = input_backward(manager_pre, feature, manager_in)
    grad_obs_gain = jnp.sum(grad_feature * obs_normed, 0)
    obs_back = normalize_back(grad_feature * obs_gain, obs_normed, obs_inverse)
    weight_cube = frame_scale[:, None, None]
    post_grad_logits = (
        (weight_cube * post_prob * (log_gap - group_kl)).reshape(ROWS, Z).astype(jnp.bfloat16)
    )
    prior_grad_logits = (
        (weight_cube * (prior_prob - post_prob)).reshape(ROWS, Z).astype(jnp.bfloat16)
    )
    grad_post_out, post_pre, grad_post_gain = head_backward(
        post_grad_logits, post_hidden, post_out, post_cache, post_gain
    )
    grad_post_in, post_back = input_backward(post_pre, post_input, post_in)
    grad_prior_out, prior_pre, grad_prior_gain = head_backward(
        prior_grad_logits, prior_hidden, prior_out, prior_cache, prior_gain
    )
    grad_prior_in, prior_back = input_backward(prior_pre, deter_low, prior_in)
    recon_grad = frame_scale[:, None] * recon_err / H
    dec_goal_out, dec_pre, dec_goal_gain = head_backward(
        recon_grad.astype(jnp.bfloat16), dec_hidden, goal_out, dec_cache, goal_gain
    )
    dec_goal_in, grad_code = input_backward(dec_pre, soft_code, goal_in)
    grad_code = grad_code.reshape(ROWS, GC, GK)
    code_grad_logits = code_prob * (
        grad_code - jnp.sum(code_prob * grad_code, -1, keepdims=True)
    ) + weight_cube * code_prob * (code_log - code_spread)
    grad_enc_out, enc_pre, grad_enc_gain = head_backward(
        code_grad_logits.reshape(ROWS, GCODE).astype(jnp.bfloat16),
        enc_hidden,
        enc_out,
        enc_cache,
        enc_gain,
    )
    grad_enc_in, enc_back = input_backward(enc_pre, deter_low, enc_in)
    grad_goal_out = worker_goal_out + dec_goal_out
    grad_goal_in = worker_goal_in + dec_goal_in
    grad_goal_gain = worker_goal_gain + dec_goal_gain
    scattered = jnp.zeros((ROWS, H), jnp.float32).at[send_order].add(returned.astype(jnp.float32))
    grad_deter = obs_back + post_back[:, :H] + prior_back + enc_back + scattered - recon_grad
    grad_inner = grad_deter * update_gate * (1.0 - candidate * candidate)
    grad_parts = jnp.concatenate(
        [
            grad_inner * candidate_in * reset_gate * (1.0 - reset_gate),
            grad_inner * reset_gate,
            grad_deter * (candidate - prev_float) * update_gate * (1.0 - update_gate),
        ],
        1,
    )
    grad_gru_gain = jnp.sum(grad_parts * gru_normed, 0)
    gru_pre = normalize_back(grad_parts * gru_gain, gru_normed, gru_inverse).astype(jnp.bfloat16)
    grad_gru_weight, gru_back = input_backward(gru_pre, gru_input, gru_weight)
    img_pre, grad_img_gain = hidden_backward(gru_back[:, :H], img_cache, img_gain)
    grad_img_stoch = jnp.einsum(
        "nz,nh->zh", stoch_prev_hot, img_pre, preferred_element_type=jnp.float32
    )
    grad_img_action = jnp.einsum(
        "na,nh->ah", action_prev_hot, img_pre, preferred_element_type=jnp.float32
    )
    grad_prev = grad_deter * (1.0 - update_gate) + gru_back[:, H:]
    embed_grad = post_back[:, H:]
    count = lax.axis_size(REP)
    loss_share = lax.psum_scatter(
        jnp.full((count,), local_loss), REP, scatter_dimension=0, tiled=True
    )
    grads = Weights(
        obs_gain=grad_obs_gain,
        manager_in=grad_manager_in,
        manager_gain=grad_manager_gain,
        manager_out=grad_manager_out,
        goal_in=grad_goal_in,
        goal_gain=grad_goal_gain,
        goal_out=grad_goal_out,
        actor_in=grad_actor_in,
        actor_gain=grad_actor_gain,
        actor_out=grad_actor_out,
        critic_in=grad_critic_in,
        critic_gain=grad_critic_gain,
        critic_out=grad_critic_out,
        img_stoch=grad_img_stoch,
        img_action=grad_img_action,
        img_gain=grad_img_gain,
        gru_weight=grad_gru_weight,
        gru_gain=grad_gru_gain,
        post_in=grad_post_in,
        post_gain=grad_post_gain,
        post_out=grad_post_out,
        prior_in=grad_prior_in,
        prior_gain=grad_prior_gain,
        prior_out=grad_prior_out,
        enc_in=grad_enc_in,
        enc_gain=grad_enc_gain,
        enc_out=grad_enc_out,
    )
    shares = []
    for i, (grad, by_column) in enumerate(zip(grads, LARGE)):
        grad = lax.psum_scatter(
            grad, REP, scatter_dimension=1 if i == IMG_ACTION else 0, tiled=True
        )
        if by_column:
            shares.append(lax.psum_scatter(grad, DP, scatter_dimension=1, tiled=True))
        else:
            shares.append(lax.psum(grad, DP))
    return (
        lax.psum(loss_share, DP)[0],
        grad_prev.reshape(SEQ_DEV, LEN, H),
        embed_grad.reshape(SEQ_DEV, LEN, E),
    ) + tuple(shares)


def solution(mesh):
    split, over_rep = (P((DP, REP)), P(REP))
    in_kernels = mesh.shape[DP] == 8 and mesh.shape[REP] == 4

    def per_device(*arguments):
        data, shares = (Data(*arguments[:12]), Weights(*arguments[12:]))
        return (step_in_kernels if in_kernels else step_plain)(data, shares)

    in_specs, out_specs = ((split,) * 12, (P(), split, split))
    for i, by_column in enumerate(LARGE):
        spec = P(None, REP) if i == IMG_ACTION else over_rep
        in_specs += (spec,)
        out_specs += (P(REP, DP) if by_column else spec,)
    return jax.shard_map(
        per_device, mesh=mesh, in_specs=in_specs, out_specs=out_specs, check_vma=False
    )
```

```python
import math
from typing import Any, NamedTuple

import jax
import jax.numpy as jnp
from jax import lax
from jax.experimental import pallas as pl
from jax.experimental.pallas import tpu as pltpu
from jax.sharding import PartitionSpec as P

H = 1024
ZG = 32
ZK = 32
U = 512
GC = 8
GK = 8
NA = 17
E = 1536
LEN = 64
HOR = 16
SEQ_DEV = 2
Z = 1024
GCODE = 64
ROWS = 128


discount = 0.99
return_mix = 0.95
epsilon = 1e-05
small_floor = 1e-06
highest = lax.Precision.HIGHEST


MESH = pl.DeviceIdType.MESH
BF = jnp.bfloat16
F32 = jnp.float32
LANES = 128
VMEM_BYTES = 62 * 2**20
TILE = 512


class Arg(NamedTuple):
    kind: Any
    shape: Any
    dtype: Any
    here: bool = True


TAKEN, GIVEN, KEPT, SIGNAL = range(4)


def taken(*shape, dtype=BF, here=True):
    return Arg(TAKEN, shape, dtype, here)


def given(*shape, dtype=BF, here=True):
    return Arg(GIVEN, shape, dtype, here)


def kept(*shape, dtype=BF):
    return Arg(KEPT, shape, dtype)


def signal(*shape):
    return Arg(SIGNAL, shape, None)


def run_kernel(body, layout, inputs, name, collective=None):
    leaves, tree = jax.tree.flatten(layout, is_leaf=lambda a: isinstance(a, Arg))

    def kernel(*refs):
        body(jax.tree.unflatten(tree, refs))

    def place(arg):
        return pl.BlockSpec(memory_space=pltpu.VMEM if arg.here else pl.ANY)

    outs = [a for a in leaves if a.kind == GIVEN]
    more = {} if collective is None else dict(collective_id=collective, has_side_effects=True)
    results = pl.pallas_call(
        kernel,
        out_shape=[jax.ShapeDtypeStruct(a.shape, a.dtype) for a in outs],
        in_specs=[place(a) for a in leaves if a.kind == TAKEN],
        out_specs=[place(a) for a in outs],
        scratch_shapes=[
            pltpu.VMEM(a.shape, a.dtype) if a.kind == KEPT else pltpu.SemaphoreType.DMA(a.shape)
            for a in leaves
            if a.kind >= KEPT
        ],
        compiler_params=pltpu.CompilerParams(vmem_limit_bytes=VMEM_BYTES, **more),
        name=name,
    )(*inputs)
    results = iter(results)
    return jax.tree.unflatten(
        tree, [next(results) if a.kind == GIVEN else None for a in leaves]
    )


def product(left, right):
    return jnp.dot(left, right, preferred_element_type=jnp.float32)


def normalize(values_in):
    row_mean = jnp.mean(values_in, -1, keepdims=True)
    centred = values_in - row_mean
    inverse = lax.rsqrt(jnp.mean(centred * centred, -1, keepdims=True) + epsilon)
    return (centred * inverse, inverse)


def normalize_back(grad_normed, normed, inverse):
    return inverse * (
        grad_normed
        - jnp.mean(grad_normed, -1, keepdims=True)
        - normed * jnp.mean(grad_normed * normed, -1, keepdims=True)
    )


def matmul_into(out_ref, left, weight_ref, turned=False, tile=TILE, low=0, extra=None):
    total = out_ref.shape[-1]

    def one(j, carry):
        start = pl.multiple_of(j * tile, tile)
        if turned:
            value = lax.dot_general(
                left,
                weight_ref[pl.ds(pl.multiple_of(low + j * tile, tile), tile), :],
                (((1,), (1,)), ((), ())),
                preferred_element_type=F32,
            )
        else:
            value = product(left, weight_ref[:, pl.ds(start, tile)])
        if extra is not None:
            value = value + extra(start, tile)
        out_ref[:, pl.ds(start, tile)] = value
        return carry

    lax.fori_loop(0, total // tile, one, 0)


def by_rows(count, size, body, carry=0):
    def one(i, carry):
        return body(pl.ds(pl.multiple_of(i * size, size), size), carry)

    return lax.fori_loop(0, count // size, one, carry)


def elu_of(value):
    return jnp.where(value > 0, value, jnp.exp(jnp.minimum(value, 0.0)) - 1.0)


def normalize_rows(ref, inverse_ref, size):
    def one(rows, carry):
        normed, inverse = normalize(ref[rows, :])
        ref[rows, :] = normed
        inverse_ref[rows, :] = inverse
        return carry

    by_rows(ref.shape[0], size, one)


def hidden_rows(ref, inverse_ref, gain, hidden_ref, size=128):
    def one(rows, carry):
        normed, inverse = normalize(ref[rows, :])
        ref[rows, :] = normed
        inverse_ref[rows, :] = inverse
        hidden_ref[rows, :] = elu_of(normed * gain).astype(BF)
        return carry

    by_rows(ref.shape[0], size, one)


def hidden_rows_back(grad_of, ref, inverse_ref, gain, pre_ref, size=128, hidden_ref=None):
    def one(rows, total):
        normed = ref[rows, :]
        scaled = normed * gain
        power = jnp.exp(jnp.minimum(scaled, 0.0))
        if hidden_ref is not None:
            hidden_ref[rows, :] = jnp.where(scaled > 0, scaled, power - 1.0).astype(BF)
        grad_scaled = grad_of(rows) * jnp.where(scaled > 0, 1.0, power)
        total = total + jnp.sum(grad_scaled * normed, 0, keepdims=True)
        back = normalize_back(grad_scaled * gain, normed, inverse_ref[rows, :])
        pre_ref[rows, :] = back.astype(pre_ref.dtype)
        return total

    return by_rows(ref.shape[0], size, one, jnp.zeros((1, ref.shape[1]), F32))


def turn_into(out_ref, value_ref, low=0):
    for j in range(value_ref.shape[1] // LANES):
        tile = value_ref[:, j * LANES : (j + 1) * LANES].astype(F32).T
        out_ref[low + j * LANES : low + (j + 1) * LANES, :] = tile.astype(out_ref.dtype)


def class_spread(groups, classes, rows, width):
    group = lax.broadcasted_iota(jnp.int32, (rows, width), 0)
    lane = lax.broadcasted_iota(jnp.int32, (rows, width), 1)
    inside = (lane >= group * classes) & (lane < group * classes + classes) & (group < groups)
    return jnp.where(inside, 1.0, 0.0).astype(BF)


def hot_rows(ids, classes, groups, width):
    here = product(ids.astype(BF), class_spread(groups, classes, ids.shape[1], width))
    lane = lax.broadcasted_iota(jnp.int32, (1, width), 1)
    same = here == jnp.bitwise_and(lane, classes - 1).astype(F32)
    return jnp.where(same & (lane < groups * classes), 1.0, 0.0)


def columns_of(rows):
    count = rows.shape[0]
    return jnp.concatenate([rows, jnp.zeros((LANES - count, rows.shape[1]), F32)], 0).T


def vector_of(packed, low, tiles):
    return jnp.concatenate(
        [packed[r, low + i : low + i + 1, :] for r in range(4) for i in range(tiles)], 1
    )


def put_vector(small_ref, low, value):
    tiles = value.shape[1] // (4 * LANES)
    for r in range(4):
        for i in range(tiles):
            start = (r * tiles + i) * LANES
            small_ref[r % 2, r // 2, low + i : low + i + 1, :] = value[:, start : start + LANES]


def put_table(small_ref, low, value, rows):
    for r in range(4):
        small_ref[r % 2, r // 2, low : low + rows, :] = value[
            0:rows, r * LANES : (r + 1) * LANES
        ]


OBS, MAN_G, MAN_O, GOAL_G, ACT_G, CRI_G, CRI_O, IMG_G, GRU_G, POST_G, PRIOR_G, ENC_G, LOSS = (
    0, 2, 3, 4, 5, 6, 7, 8, 10, 16, 18, 20, 21,
)
ACT_T, ENC_T, IMG_T, SMALL_TILES = (24, 48, 112, 160)
TAB_ACT, TAB_ENC, TAB_IMG, TAB_GOAL, TABLES = (0, 32, 96, 160, 224)
VECTOR_TILES = 24


def spread_lanes(low_ref, out_ref, first_row, which):
    lane = lax.broadcasted_iota(jnp.int32, (ROWS, LANES), 1)
    keep = (lane < 64) if which == 0 else (lane >= 64)
    for j in range(4):
        tile = low_ref[:, j * LANES : (j + 1) * LANES].astype(F32)
        turned = pltpu.roll(tile, 64, 1)
        for x in range(2):
            source = tile if x == which else turned
            lanes = slice((2 * j + x) * LANES, (2 * j + x + 1) * LANES)
            out_ref[first_row : first_row + ROWS, lanes] = jnp.where(keep, source, 0.0).astype(BF)


def column(meta, k):
    return meta[:, k : k + 1]


class Frames(NamedTuple):
    lengths: Any = taken(SEQ_DEV, dtype=jnp.int32)
    resets: Any = taken(SEQ_DEV, LEN, dtype=jnp.int32)
    terminal: Any = taken(SEQ_DEV, LEN, dtype=jnp.int32)
    rewards: Any = taken(SEQ_DEV, LEN, dtype=F32)
    prev_stoch: Any = taken(SEQ_DEV, ZG, LEN, dtype=jnp.int32)
    prev_action: Any = taken(SEQ_DEV, LEN, dtype=jnp.int32)
    regroup: Any = taken(1, ROWS, dtype=jnp.int32)
    prev: Any = taken(ROWS, H)
    embed: Any = taken(ROWS, E)
    obs_gain: Any = taken(H // 4)
    manager_gain: Any = taken(U // 4)
    manager_head: Any = taken(U // 4)
    goal_gain: Any = taken(U // 4)
    actor_gain: Any = taken(U // 4)
    critic_gain: Any = taken(U // 4)
    critic_head: Any = taken(U // 4)
    img_gain: Any = taken(H // 4)
    gru_gain: Any = taken(3 * H // 4)
    post_gain: Any = taken(H // 4)
    prior_gain: Any = taken(H // 4)
    enc_gain: Any = taken(U // 4)
    actor_head: Any = taken(NA, U // 4)
    enc_head: Any = taken(GCODE, U // 4)
    img_action_share: Any = taken(NA, H // 4)
    goal_in_share: Any = taken(GCODE // 4, U)
    img_stoch_share: Any = taken(Z // 4, H, here=False)
    gru_weight_share: Any = taken(H // 2, 3 * H, here=False)
    manager_in_share: Any = taken(H // 4, U, here=False)
    enc_in_share: Any = taken(H // 4, U, here=False)
    goal_out_share: Any = taken(U // 4, H, here=False)
    prior_in_share: Any = taken(H // 4, H, here=False)
    post_in_share: Any = taken((H + E) // 4, H, here=False)
    prior_out_share: Any = taken(H // 4, Z, here=False)
    post_out_share: Any = taken(H // 4, Z, here=False)
    actor_in_share: Any = taken(768, U, here=False)
    critic_in_share: Any = taken(768, U, here=False)
    gru_weight_out: Any = given(2 * H, 3 * H, here=False)
    goal_out_out: Any = given(U, H, here=False)
    actor_in_out: Any = given(3 * H, U, here=False)
    critic_in_out: Any = given(3 * H, U, here=False)
    vectors: Any = given(4, VECTOR_TILES, LANES, dtype=F32)
    tables: Any = given(4, TABLES, LANES)
    meta_turned: Any = given(LANES, ROWS, dtype=F32)
    start_state: Any = given(ROWS, H + LANES)
    gru_left: Any = given(2 * H, ROWS)
    post_left: Any = given(H + E, ROWS)
    post_out_left: Any = given(H, ROWS)
    prior_out_left: Any = given(H, ROWS)
    img_left: Any = given(Z, ROWS)
    me_left: Any = given(H, 2 * ROWS)
    dec_left: Any = given(U, ROWS)
    soft_turned: Any = given(GCODE, ROWS)
    post_right: Any = given(ROWS, H)
    prior_right: Any = given(ROWS, H)
    post_out_right: Any = given(ROWS, Z)
    prior_out_right: Any = given(ROWS, Z)
    me_right: Any = given(2 * ROWS, 2 * U)
    recon_low: Any = given(ROWS, H)
    dec_pair: Any = given(ROWS, 2 * U)
    gru_normed: Any = given(ROWS, 3 * H, dtype=F32)
    gru_inverse: Any = given(ROWS, 1, dtype=F32)
    img_normed: Any = given(ROWS, H, dtype=F32)
    img_inverse: Any = given(ROWS, 1, dtype=F32)
    grad_deter: Any = given(ROWS, H, dtype=F32)
    embed_grad: Any = given(ROWS, E, dtype=F32)
    small: Any = given(2, 2, SMALL_TILES, LANES, dtype=F32)
    img_stoch: Any = kept(Z, H)
    gru_weight: Any = kept(2 * H, 3 * H)
    manager_in: Any = kept(H, U)
    enc_in: Any = kept(H, U)
    goal_out: Any = kept(U, H)
    prior_in: Any = kept(H, H)
    post_in: Any = kept(H + E, H)
    prior_out: Any = kept(H, Z)
    post_out: Any = kept(H, Z)
    actor_in: Any = kept(3 * H, U)
    critic_in: Any = kept(3 * H, U)
    img_action: Any = kept(32, H)
    enc_out: Any = kept(GCODE, U)
    goal_in: Any = kept(GCODE, U)
    vector_share: Any = kept(VECTOR_TILES, LANES, dtype=F32)
    table_share: Any = kept(TABLES, LANES)
    meta: Any = kept(ROWS, LANES, dtype=F32)
    hot: Any = kept(ROWS, Z)
    img_hidden: Any = kept(ROWS, H)
    deter: Any = kept(ROWS, H, dtype=F32)
    deter_low: Any = kept(ROWS, H)
    feature: Any = kept(ROWS, H)
    obs_normed: Any = kept(ROWS, H, dtype=F32)
    obs_inverse: Any = kept(ROWS, 1, dtype=F32)
    outgoing: Any = kept(ROWS, H + LANES)
    incoming: Any = kept(ROWS, H + LANES)
    pre_512: Any = kept(ROWS, U, dtype=F32)
    hid_512: Any = kept(ROWS, U)
    back_512: Any = kept(ROWS, U)
    wide_512: Any = kept(ROWS, U, dtype=F32)
    inverse: Any = kept(ROWS, 1, dtype=F32)
    grad_value: Any = kept(ROWS, 1, dtype=F32)
    dec_normed: Any = kept(ROWS, U, dtype=F32)
    dec_inverse: Any = kept(ROWS, 1, dtype=F32)
    dec_hidden: Any = kept(ROWS, U)
    dec_pre: Any = kept(ROWS, U)
    wide: Any = kept(ROWS, H, dtype=F32)
    prior_normed: Any = kept(ROWS, H, dtype=F32)
    prior_inverse: Any = kept(ROWS, 1, dtype=F32)
    prior_hidden: Any = kept(ROWS, H)
    post_normed: Any = kept(ROWS, H, dtype=F32)
    post_inverse: Any = kept(ROWS, 1, dtype=F32)
    post_hidden: Any = kept(ROWS, H)
    post_turned: Any = kept(Z, ROWS, dtype=F32)
    prior_turned: Any = kept(Z, ROWS, dtype=F32)
    loss: Any = kept(1, 1, dtype=F32)
    piece_send: Any = signal(17, 8)
    piece_recv: Any = signal(17, 8)
    load_done: Any = signal(17)
    save_done: Any = signal(4)
    small_send: Any = signal(2, 3)
    small_recv: Any = signal(2, 3)
    state_send: Any = signal(8)
    state_recv: Any = signal(8)

    def pack(self):
        vectors = (
            self.obs_gain, self.manager_gain, self.manager_head, self.goal_gain, self.actor_gain,
            self.critic_gain, self.critic_head, self.img_gain, self.gru_gain, self.post_gain,
            self.prior_gain, self.enc_gain,
        )
        low = 0
        for vector in vectors:
            for i in range(vector.shape[0] // LANES):
                self.vector_share[low, :] = vector[pl.ds(i * LANES, LANES)].astype(F32)
                low += 1
        self.vector_share[low:, :] = jnp.zeros((VECTOR_TILES - low, LANES), F32)
        self.table_share[...] = jnp.zeros(self.table_share.shape, BF)
        self.table_share[TAB_ACT : TAB_ACT + NA, :] = self.actor_head[...]
        self.table_share[TAB_ENC : TAB_ENC + GCODE, :] = self.enc_head[...]
        for i in range(2):
            low = TAB_IMG + 32 * i
            lanes = slice(i * LANES, (i + 1) * LANES)
            self.table_share[low : low + NA, :] = self.img_action_share[:, lanes]
        for i in range(4):
            low = TAB_GOAL + 16 * i
            lanes = slice(i * LANES, (i + 1) * LANES)
            self.table_share[low : low + 16, :] = self.goal_in_share[:, lanes]

    def start(self):
        def row(ref):
            value = ref[...].astype(F32)
            return jnp.concatenate([value[0:1], value[1:2]], 1)

        position = lax.broadcasted_iota(jnp.int32, (SEQ_DEV, LEN), 1)
        length = self.lengths[...].reshape(SEQ_DEV, 1)
        later = jnp.where((position + 1 < length) & (position + 1 < LEN), 1.0, 0.0)
        kinds = (
            row(self.prev_action),
            row(jnp.where(position < length, 1.0, 0.0)),
            row(later) * (1.0 - jnp.minimum(pltpu.roll(row(self.resets), ROWS - 1, 1), 1.0)),
            1.0 - row(self.terminal),
            row(self.rewards),
            self.regroup[...].astype(F32),
        )
        self.meta_turned[...] = jnp.zeros(self.meta_turned.shape, F32)
        for i, kind in enumerate(kinds):
            self.meta_turned[32 + i : 33 + i, :] = kind
        self.meta[...] = self.meta_turned[...].T
        ids = jnp.concatenate([self.prev_stoch[0], self.prev_stoch[1]], 1).astype(F32)
        self.hot[...] = hot_rows(columns_of(ids)[:, 0:ZG], ZK, ZG, Z).astype(BF)

    def turns(self):
        turn_into(self.img_left, self.hot)
        turn_into(self.gru_left, self.prev, H)
        turn_into(self.post_left, self.embed, H)
        self.small[...] = jnp.zeros(self.small.shape, F32)

    def unpack(self):
        for r in range(4):
            for i in range(2):
                self.img_action[:, (2 * r + i) * LANES : (2 * r + i + 1) * LANES] = self.tables[
                    r, TAB_IMG + 32 * i : TAB_IMG + 32 * (i + 1), :
                ]
            self.enc_out[:, r * LANES : (r + 1) * LANES] = self.tables[
                r, TAB_ENC : TAB_ENC + 64, :
            ]
            for i in range(4):
                self.goal_in[16 * r : 16 * (r + 1), i * LANES : (i + 1) * LANES] = self.tables[
                    r, TAB_GOAL + 16 * i : TAB_GOAL + 16 * (i + 1), :
                ]

    def gain(self, low, size):
        return vector_of(self.vectors, low, size // (4 * LANES))

    def img(self):
        meta = self.meta[...]
        lane = lax.broadcasted_iota(jnp.int32, (ROWS, 32), 1).astype(F32)
        action = jnp.where(column(meta, 32) == lane, 1.0, 0.0).astype(BF)
        matmul_into(
            self.img_normed, self.hot[...], self.img_stoch,
            extra=lambda start, tile: product(action, self.img_action[:, pl.ds(start, tile)]),
        )
        hidden_rows(self.img_normed, self.img_inverse, self.gain(IMG_G, H), self.img_hidden)
        turn_into(self.gru_left, self.img_hidden)

    def gru(self, third):
        low = third * H
        out = self.gru_normed.at[:, low : low + H]

        def one(j, carry):
            start = pl.multiple_of(low + j * TILE, TILE)
            value = product(self.img_hidden[...], self.gru_weight[0:H, pl.ds(start, TILE)])
            value = value + product(
                self.prev[...], self.gru_weight[H : 2 * H, pl.ds(start, TILE)]
            )
            self.gru_normed[:, pl.ds(start, TILE)] = value
            return carry

        lax.fori_loop(0, H // TILE, one, 0)

    def state(self):
        gain = self.gain(GRU_G, 3 * H)
        obs_gain = self.gain(OBS, H)

        def one(rows, carry):
            normed, inverse = normalize(self.gru_normed[rows, :])
            self.gru_normed[rows, :] = normed
            self.gru_inverse[rows, :] = inverse
            parts = normed * gain
            reset = 1.0 / (1.0 + jnp.exp(-parts[:, :H]))
            candidate = jnp.tanh(reset * parts[:, H : 2 * H])
            update = 1.0 / (1.0 + jnp.exp(1.0 - parts[:, 2 * H :]))
            state = update * candidate + (1.0 - update) * self.prev[rows, :].astype(F32)
            self.deter[rows, :] = state
            self.deter_low[rows, :] = state.astype(BF)
            obs, obs_inverse = normalize(state)
            self.obs_normed[rows, :] = obs
            self.obs_inverse[rows, :] = obs_inverse
            self.feature[rows, :] = (obs * obs_gain).astype(BF)
            return carry

        by_rows(ROWS, 16, one)
        turn_into(self.post_left, self.deter_low)

    def picked(self):
        meta = self.meta[...]
        lane = lax.broadcasted_iota(jnp.int32, (ROWS, ROWS), 1).astype(F32)
        pick = jnp.where(column(meta, 37) == lane, 1.0, 0.0).astype(BF)

        def one(j, carry):
            lanes = pl.ds(pl.multiple_of(j * TILE, TILE), TILE)
            self.outgoing[:, lanes] = product(pick, self.deter_low[:, lanes]).astype(BF)
            return carry

        lax.fori_loop(0, H // TILE, one, 0)
        valid = jnp.broadcast_to(column(meta, 33), (ROWS, LANES)).astype(BF)
        self.outgoing[:, H:] = product(pick, valid).astype(BF)

    def manager(self):
        meta = self.meta[...]
        gain, head = (self.gain(MAN_G, U), self.gain(MAN_O, U))
        for j in range(H // LANES):
            lanes = slice(j * LANES, (j + 1) * LANES)
            self.me_left[lanes, 0:ROWS] = self.feature[:, lanes].astype(F32).T.astype(BF)
            self.me_left[lanes, ROWS:] = self.deter_low[:, lanes].astype(F32).T.astype(BF)
        matmul_into(self.pre_512, self.feature[...], self.manager_in)
        hidden_rows(self.pre_512, self.inverse, gain, self.hid_512)
        value = jnp.sum(self.hid_512[...].astype(F32) * head, -1, keepdims=True)
        valid, linked, carried, rewards = (column(meta, 33 + i) for i in range(4))
        later = pltpu.roll(jnp.broadcast_to(value, (ROWS, LANES)), ROWS - 1, 0)
        base = jnp.where(
            linked > 0, rewards + discount * carried * ((1.0 - return_mix) * later), value
        )
        slope = jnp.broadcast_to(linked * (discount * return_mix) * carried, (ROWS, LANES))
        step = 1
        while step < LEN:
            base = base + slope * pltpu.roll(base, ROWS - step, 0)
            slope = slope * pltpu.roll(slope, ROWS - step, 0)
            step *= 2
        misfit = value - base[:, 0:1]
        scale = valid * (1.0 / ROWS)
        self.loss[...] = 0.5 * jnp.sum(scale * misfit * misfit, 0, keepdims=True)
        grad_value = scale * misfit
        put_vector(
            self.small, MAN_O,
            jnp.sum(self.hid_512[...].astype(F32) * grad_value, 0, keepdims=True),
        )
        self.grad_value[...] = grad_value
        total = hidden_rows_back(
            lambda rows: self.grad_value[rows, :] * head,
            self.pre_512, self.inverse, gain, self.back_512,
        )
        put_vector(self.small, MAN_G, total)
        spread_lanes(self.back_512, self.me_right, 0, 0)
        self.feature_back()

    def feature_back(self):
        obs_gain = self.gain(OBS, H)
        matmul_into(self.wide, self.back_512[...], self.manager_in, turned=True)

        def one(rows, total):
            grad = self.wide[rows, :]
            normed = self.obs_normed[rows, :]
            total = total + jnp.sum(grad * normed, 0, keepdims=True)
            self.grad_deter[rows, :] = normalize_back(
                grad * obs_gain, normed, self.obs_inverse[rows, :]
            )
            return total

        put_vector(self.small, OBS, by_rows(ROWS, 32, one, jnp.zeros((1, H), F32)))

    def add_back(self, left_ref, weight_ref):
        def one(j, carry):
            lanes = pl.ds(pl.multiple_of(j * TILE, TILE), TILE)
            self.grad_deter[:, lanes] += lax.dot_general(
                left_ref[...], weight_ref[lanes, :], (((1,), (1,)), ((), ())),
                preferred_element_type=F32,
            )
            return carry

        lax.fori_loop(0, H // TILE, one, 0)

    def encoder(self):
        gain, goal_gain = (self.gain(ENC_G, U), self.gain(GOAL_G, U))
        valid_row = self.meta_turned[33:34, :]
        scale_row = valid_row * (1.0 / ROWS)
        scale = column(self.meta[...], 33) * (1.0 / ROWS)
        matmul_into(self.pre_512, self.deter_low[...], self.enc_in)
        hidden_rows(self.pre_512, self.inverse, gain, self.hid_512)
        logits = lax.dot_general(
            self.enc_out[...], self.hid_512[...], (((1,), (1,)), ((), ())),
            preferred_element_type=F32,
        ).reshape(GC, GK, ROWS)
        shifted = logits - jnp.max(logits, 1, keepdims=True)
        code_log = shifted - jnp.log(jnp.sum(jnp.exp(shifted), 1, keepdims=True))
        code = jnp.exp(code_log)
        spread = jnp.sum(code * code_log, 1, keepdims=True)
        code_kl = jnp.sum(jnp.sum(code * (code_log + math.log(GK)), 1), 0, keepdims=True)
        flat = jnp.concatenate(
            [code.reshape(GCODE, ROWS), jnp.zeros((ROWS - GCODE, ROWS), F32)], 0
        )
        self.soft_turned[...] = flat[0:GCODE].astype(BF)
        soft = flat.T[:, 0:GCODE].astype(BF)
        matmul_into(self.dec_normed, soft, self.goal_in)
        hidden_rows(self.dec_normed, self.dec_inverse, goal_gain, self.dec_hidden)
        turn_into(self.dec_left, self.dec_hidden)

        def one(j, total):
            lanes = pl.ds(pl.multiple_of(j * TILE, TILE), TILE)
            err = product(self.dec_hidden[...], self.goal_out[:, lanes]) - self.deter[:, lanes]
            grad = scale * err * (1.0 / H)
            self.grad_deter[:, lanes] -= grad
            self.recon_low[:, lanes] = grad.astype(BF)
            return total + jnp.sum(err * err, -1, keepdims=True)

        squares = lax.fori_loop(0, H // TILE, one, jnp.zeros((ROWS, 1), F32))
        self.loss[...] += jnp.sum(scale * (0.5 / H) * squares, 0, keepdims=True) + jnp.sum(
            scale_row * code_kl, 1, keepdims=True
        )
        matmul_into(self.wide_512, self.recon_low[...], self.goal_out, turned=True)
        total = hidden_rows_back(
            lambda rows: self.wide_512[rows, :],
            self.dec_normed, self.dec_inverse, goal_gain, self.dec_pre,
        )
        put_vector(self.small, GOAL_G, total)
        spread_lanes(self.dec_pre, self.dec_pair, 0, 0)
        grad_code = lax.dot_general(
            self.goal_in[...], self.dec_pre[...], (((1,), (1,)), ((), ())),
            preferred_element_type=F32,
        ).reshape(GC, GK, ROWS)
        grad_logits = code * (grad_code - jnp.sum(code * grad_code, 1, keepdims=True))
        grad_logits = grad_logits + scale_row[None] * code * (code_log - spread)
        grad_turned = grad_logits.reshape(GCODE, ROWS)
        grad_low = jnp.concatenate(
            [grad_turned, jnp.zeros((ROWS - GCODE, ROWS), F32)], 0
        ).T[:, 0:GCODE].astype(BF)
        put_table(
            self.small, ENC_T, product(grad_turned.astype(BF), self.hid_512[...]), GCODE
        )
        matmul_into(self.wide_512, grad_low, self.enc_out)
        total = hidden_rows_back(
            lambda rows: self.wide_512[rows, :],
            self.pre_512, self.inverse, gain, self.back_512,
        )
        put_vector(self.small, ENC_G, total)
        spread_lanes(self.back_512, self.me_right, ROWS, 1)
        self.add_back(self.back_512, self.enc_in)

    def prior(self):
        matmul_into(self.prior_normed, self.deter_low[...], self.prior_in)
        hidden_rows(
            self.prior_normed, self.prior_inverse, self.gain(PRIOR_G, H), self.prior_hidden
        )
        turn_into(self.prior_out_left, self.prior_hidden)

    def post(self):
        def one(j, carry):
            lanes = pl.ds(pl.multiple_of(j * TILE, TILE), TILE)
            value = product(self.deter_low[...], self.post_in[0:H, lanes])
            self.post_normed[:, lanes] = value + product(
                self.embed[...], self.post_in[H : H + E, lanes]
            )
            return carry

        lax.fori_loop(0, H // TILE, one, 0)
        hidden_rows(self.post_normed, self.post_inverse, self.gain(POST_G, H), self.post_hidden)
        turn_into(self.post_out_left, self.post_hidden)

    def logits(self, hidden_ref, weight_ref, turned_ref):
        matmul_into(self.wide, hidden_ref[...], weight_ref)
        turn_into(turned_ref, self.wide)

    def state_kl(self):
        scale_row = self.meta_turned[33:34, :] * (1.0 / ROWS)

        def log_part(value):
            shifted = value - jnp.max(value, 0, keepdims=True)
            return shifted - jnp.log(jnp.sum(jnp.exp(shifted), 0, keepdims=True))

        def one(rows, total):
            post_log = log_part(self.post_turned[rows, :])
            prior_log = log_part(self.prior_turned[rows, :])
            post = jnp.exp(post_log)
            gap = post_log - prior_log
            kl = jnp.sum(post * gap, 0, keepdims=True)
            self.post_turned[rows, :] = scale_row * post * (gap - kl)
            self.prior_turned[rows, :] = scale_row * (jnp.exp(prior_log) - post)
            return total + kl

        total = by_rows(Z, ZK, one, jnp.zeros((1, ROWS), F32))
        self.loss[...] += jnp.sum(scale_row * total, 1, keepdims=True)
        for turned, low in (
            (self.post_turned, self.post_out_right), (self.prior_turned, self.prior_out_right),
        ):
            for j in range(Z // LANES):
                lanes = slice(j * LANES, (j + 1) * LANES)
                low[:, lanes] = turned[lanes, :].T.astype(BF)

    def prior_back(self):
        matmul_into(self.wide, self.prior_out_right[...], self.prior_out, turned=True)
        total = hidden_rows_back(
            lambda rows: self.wide[rows, :],
            self.prior_normed, self.prior_inverse, self.gain(PRIOR_G, H), self.prior_right,
        )
        put_vector(self.small, PRIOR_G, total)
        self.add_back(self.prior_right, self.prior_in)

    def post_back(self):
        matmul_into(self.wide, self.post_out_right[...], self.post_out, turned=True)
        total = hidden_rows_back(
            lambda rows: self.wide[rows, :],
            self.post_normed, self.post_inverse, self.gain(POST_G, H), self.post_right,
        )
        put_vector(self.small, POST_G, total)
        self.add_back(self.post_right, self.post_in)
        matmul_into(self.embed_grad, self.post_right[...], self.post_in, turned=True, low=H)
        for y in range(2):
            for c in range(2):
                self.small[c, y, LOSS : LOSS + 1, :] = jnp.broadcast_to(
                    self.loss[...], (1, LANES)
                )


class Places:
    def __init__(self):
        dp, rep = (lax.axis_index("dp"), lax.axis_index("rep"))
        self.dp, self.rep = (dp, rep)
        self.x, self.z, self.w = (lax.rem(dp, 2), lax.rem(dp // 2, 2), dp // 4)
        self.y, self.c = (rep // 2, lax.rem(rep, 2))
        self.to_x = (dp + 1 - 2 * self.x, rep)
        self.to_z = (dp + 2 - 4 * self.z, rep)
        self.to_w = (dp + 4 - 8 * self.w, rep)
        self.to_y = (dp, rep + 2 - 4 * self.y)
        self.to_c = (dp, rep + 1 - 2 * self.c)
        self.to_d = (dp, 3 - rep)

    def around(self, offset):
        return lax.rem(self.dp + offset, 8)


def greet(devices):
    barrier = pltpu.get_barrier_semaphore()
    for device in devices:
        pl.semaphore_signal(barrier, inc=1, device_id=device, device_id_type=MESH)
    return lambda: pl.semaphore_wait(barrier, len(devices))


def send_to(source, target, send_sem, recv_sem, device):
    return pltpu.make_async_remote_copy(
        src_ref=source,
        dst_ref=target,
        send_sem=send_sem,
        recv_sem=recv_sem,
        device_id=device,
        device_id_type=MESH,
    )


def regroup_start(places, outgoing, incoming, send_sem, recv_sem):
    count = ROWS // 8
    mine = pl.ds(pl.multiple_of(places.dp * count, 16), count)
    copies = []
    for offset in range(1, 8):
        there = places.around(offset)
        copy = send_to(
            outgoing.at[pl.ds(pl.multiple_of(there * count, 16), count)],
            incoming.at[mine],
            send_sem.at[offset],
            recv_sem.at[offset],
            (there, places.rep),
        )
        copy.start()
        copies.append(copy)
    incoming[mine, :] = outgoing[mine, :]
    return copies


def diagonal_split(u, columns):
    tiles = columns // LANES
    shares = [tiles // 3 + (1 if (i - u) % 3 < tiles % 3 else 0) for i in range(3)]
    return tuple(share * LANES for share in shares)


OWN, Y_A, Y_B, X_A, Z_A, X_B, Z_B, RELAY = range(8)


class Gather:
    def __init__(self, places, units, send_sem, recv_sem, load_sem):
        self.places, self.units = (places, units)
        self.send_sem, self.recv_sem, self.load_sem = (send_sem, recv_sem, load_sem)
        self.far = places.rep + 2 - 4 * places.y
        self.mine = places.x * 2 + places.z
        self.across = 3 - self.mine
        self.from_x = (1 - places.x) * 2 + places.z
        self.from_z = places.x * 2 + 1 - places.z
        self.copies = {}
        self.loads = {}

    def remote(self, u, kind, source, target, device):
        copy = send_to(
            source, target, self.send_sem.at[u, kind], self.recv_sem.at[u, kind], device
        )
        copy.start()
        self.copies[u, kind] = copy

    def rows(self, u, share, piece, low, number):
        extent = self.units[u][0].shape[0]
        start = share * extent + piece * (extent // 4) + low
        return pl.ds(pl.multiple_of(start, 16), number)

    def part(self, u, rows, whole=True, first=0, columns=None):
        share, all_rows, low, count = self.units[u]
        lanes = pl.ds(low + first, count if columns is None else columns)
        return (all_rows if whole else share).at[rows, lanes]

    def diagonal(self, u, share, piece, over, whole=True):
        split = diagonal_split(u, self.units[u][3])
        return self.part(
            u, self.rows(u, share, piece, 0, self.extent(u) // 4), whole, sum(split[:over]),
            split[over],
        )

    def extent(self, u):
        return self.units[u][0].shape[0]

    def load(self, u):
        everything = self.rows(u, 0, 0, 0, self.extent(u))
        copy = pltpu.make_async_copy(
            self.part(u, everything, False),
            self.part(u, self.rows(u, self.places.rep, 0, 0, self.extent(u))),
            self.load_sem.at[u],
        )
        copy.start()
        self.loads[u] = copy

    def over_y(self, u):
        if u >= len(self.units):
            return
        rep, quarter = (self.places.rep, self.extent(u) // 4)
        self.remote(
            u, Y_A,
            self.part(u, self.rows(u, 0, self.mine, 0, quarter), False),
            self.part(u, self.rows(u, rep, self.mine, 0, quarter)),
            self.places.to_y,
        )

    def over_y_more(self, u):
        if u >= len(self.units):
            return
        rep = self.places.rep
        if diagonal_split(u, self.units[u][3])[0]:
            self.remote(
                u, Y_B, self.diagonal(u, 0, self.across, 0, False),
                self.diagonal(u, rep, self.across, 0), self.places.to_y,
            )
        everything = self.rows(u, 0, 0, 0, self.extent(u))
        self.remote(
            u, OWN,
            self.part(u, everything, False),
            self.part(u, self.rows(u, rep, 0, 0, self.extent(u))),
            self.places.to_c,
        )

    def stage_1(self, u):
        self.copies[u, Y_A].wait_recv()
        piece = self.part(u, self.rows(u, self.far, self.mine, 0, self.extent(u) // 4))
        self.remote(u, X_A, piece, piece, self.places.to_x)
        self.remote(u, Z_A, piece, piece, self.places.to_z)

    def stage_2(self, u):
        _, second, third = diagonal_split(u, self.units[u][3])
        self.copies[u, Z_A].wait_recv()
        if second:
            piece = self.diagonal(u, self.far, self.from_z, 1)
            self.remote(u, X_B, piece, piece, self.places.to_x)
        self.copies[u, X_A].wait_recv()
        if third:
            piece = self.diagonal(u, self.far, self.from_x, 2)
            self.remote(u, Z_B, piece, piece, self.places.to_z)

    def stage_3(self, u):
        for kind in (Y_B, X_B, Z_B):
            if (u, kind) in self.copies:
                self.copies[u, kind].wait_recv()
        share = self.part(u, self.rows(u, self.far, 0, 0, self.extent(u)))
        self.remote(u, RELAY, share, share, self.places.to_c)

    def open(self):
        for u in range(AHEAD):
            self.over_y(u)
            if u < MORE:
                self.over_y_more(u)

    def pump(self, t):
        count = len(self.units)
        if t < count:
            self.stage_1(t)
            self.over_y(t + AHEAD)
        if 0 <= t < count:
            self.over_y_more(t + MORE)
        if 0 <= t - LAG_2 < count:
            self.stage_2(t - LAG_2)
        if 0 <= t - LAG_3 < count:
            self.stage_3(t - LAG_3)

    def complete(self, u):
        self.loads[u].wait()
        self.copies[u, OWN].wait_recv()
        self.copies[u, RELAY].wait_recv()

    def drain(self):
        for copy in self.copies.values():
            copy.wait_send()


AHEAD, MORE, LAG_2, LAG_3, DONE = (10, 6, 2, 4, 5)


def frames_kernel(f):
    places = Places()
    units = [(f.img_stoch_share, f.img_stoch, 0, H)]
    units += [(f.gru_weight_share, f.gru_weight, i * H, H) for i in range(3)]
    units += [
        (f.manager_in_share, f.manager_in, 0, U),
        (f.enc_in_share, f.enc_in, 0, U),
        (f.goal_out_share, f.goal_out, 0, H),
        (f.prior_in_share, f.prior_in, 0, H),
        (f.post_in_share, f.post_in, 0, U),
        (f.post_in_share, f.post_in, U, U),
        (f.prior_out_share, f.prior_out, 0, Z),
        (f.post_out_share, f.post_out, 0, Z),
        (f.actor_in_share, f.actor_in, 0, 256),
        (f.actor_in_share, f.actor_in, 256, 256),
        (f.critic_in_share, f.critic_in, 0, 256),
        (f.critic_in_share, f.critic_in, 256, 128),
        (f.critic_in_share, f.critic_in, 384, 128),
    ]
    met = greet(
        [(places.around(o), places.rep) for o in range(1, 8)]
        + [places.to_c, places.to_y, places.to_d]
    )
    gather = Gather(places, units, f.piece_send, f.piece_recv, f.load_done)
    for u in range(len(units)):
        gather.load(u)
    f.pack()
    f.start()
    met()
    packs = []
    for i, (share, whole) in enumerate(((f.vector_share, f.vectors), (f.table_share, f.tables))):
        for k, device in enumerate((places.to_c, places.to_y, places.to_d)):
            copy = send_to(
                share, whole.at[places.rep], f.small_send.at[i, k], f.small_recv.at[i, k], device
            )
            copy.start()
            packs.append(copy)
    gather.open()
    f.vectors[places.rep] = f.vector_share[...]
    f.tables[places.rep] = f.table_share[...]
    saves = []

    def save(k, source, target):
        copy = pltpu.make_async_copy(source, target, f.save_done.at[k])
        copy.start()
        saves.append(copy)

    def pump(t):
        gather.pump(t)

    pump(0)
    f.turns()
    states = []

    def first():
        for copy in packs:
            copy.wait()
        f.unpack()
        f.img()

    def state():
        f.gru(2)
        save(0, f.gru_weight, f.gru_weight_out)
        f.state()
        f.picked()
        states.extend(
            regroup_start(places, f.outgoing, f.incoming, f.state_send, f.state_recv)
        )

    def encoder():
        save(1, f.goal_out, f.goal_out_out)
        f.encoder()

    def posterior():
        f.logits(f.post_hidden, f.post_out, f.post_turned)
        f.state_kl()

    def arrived():
        save(2, f.actor_in, f.actor_in_out)
        for copy in states:
            copy.wait()
        f.start_state[...] = f.incoming[...]

    work = {
        0: first, 1: lambda: f.gru(0), 2: lambda: f.gru(1), 3: state, 4: f.manager, 6: encoder,
        7: f.prior, 9: f.post,
        10: lambda: f.logits(f.prior_hidden, f.prior_out, f.prior_turned),
        11: posterior, 12: f.prior_back, 13: f.post_back, 14: arrived,
    }
    count = len(units)
    for t in range(1, count + DONE):
        pump(t)
        if 0 <= t - DONE:
            gather.complete(t - DONE)
            work.get(t - DONE, lambda: None)()
    save(3, f.critic_in, f.critic_in_out)
    for copy in saves:
        copy.wait()
    gather.drain()


class Source(NamedTuple):
    rows: int
    parts: Any
    columns: int

    @property
    def depth(self):
        return sum(self.parts)


SOURCE_POST = Source((H + E) // 4, (ROWS,), H)
SOURCE_1024 = Source(H // 4, (ROWS,), H)
SOURCE_MAN_ENC = Source(H // 4, (2 * ROWS,), 2 * U)
SOURCE_GRU = Source(H // 2, (ROWS,), 3 * H)
SOURCE_GOAL_OUT = Source(U // 4, (ROWS, ROWS), H)
SOURCE_GOAL_IN = Source(GCODE // 4, (ROWS, ROWS), 2 * U)
WORKER_SHARE = (768, 1024)
ALONG_X, ALONG_Z, ALONG_W, ALONG_Y = range(4)
Y_FIRST = (ALONG_Y, ALONG_X, ALONG_Z, ALONG_W)
X_FIRST = (ALONG_X, ALONG_Y, ALONG_Z, ALONG_W)
Z_FIRST = (ALONG_Z, ALONG_Y, ALONG_X, ALONG_W)
X_ONLY = (ALONG_X, ALONG_Z, ALONG_W)
Z_ONLY = (ALONG_Z, ALONG_X, ALONG_W)


def side_by_side(left, right_ref, lanes):
    right = jnp.concatenate([right_ref[:, lane] for lane in lanes], 1)
    wide = product(left, right)
    return [wide[:, i * LANES : (i + 1) * LANES] for i in range(len(lanes))]


class Exchange:
    def __init__(self, places, source, left_2, right_2, send_sem, recv_sem, local_sem, first):
        self.places, self.source = (places, source)
        self.left_2, self.right_2 = (left_2, right_2)
        self.sems, self.first = ((send_sem, recv_sem, local_sem), first)
        self.copies = []

    def move(self, part, j, mine, target, theirs, place):
        send_sem, recv_sem, local_sem = (sem.at[self.first + part, j] for sem in self.sems)
        remote = send_to(theirs, place, send_sem, recv_sem, self.places.to_c)
        local = pltpu.make_async_copy(mine, target, local_sem)
        remote.start()
        local.start()
        self.copies += [remote, local]

    def lows(self, part):
        low = sum(self.source.parts[:part])
        depth = self.source.parts[part]
        return (pl.ds(low, depth), pl.ds(self.source.depth + low, depth))

    def start_left(self, part, left):
        low, high = self.lows(part)
        for y in range(2):
            ours, theirs = (
                pl.ds(pl.multiple_of((2 * y + core) * self.source.rows, 16), self.source.rows)
                for core in (self.places.c, 1 - self.places.c)
            )
            self.move(
                part, y, left.at[ours], self.left_2.at[y, :, low],
                left.at[theirs], self.left_2.at[y, :, high],
            )

    def start_right(self, part, right):
        low, high = self.lows(part)
        self.move(part, 2, right, self.right_2.at[low], right, self.right_2.at[high])

    def start(self, part, left, right):
        self.start_right(part, right)
        self.start_left(part, left)

    def ready(self, first, offset):
        while self.copies:
            self.copies.pop(0).wait()

    def terms(self, y, rows, lanes):
        return side_by_side(self.left_2[y, rows, :], self.right_2, lanes)


class Wide:
    def __init__(self, places, rows, depth, left_4, right_4, send_sem, recv_sem, local_sem):
        self.places, self.rows, self.depth = (places, rows, depth)
        self.left_4, self.right_4 = (left_4, right_4)
        self.send_sem, self.recv_sem, self.local_sem = (send_sem, recv_sem, local_sem)
        self.copies = {}
        self.from_y = {}

    def part(self, i):
        return pl.ds(i * self.depth, self.depth)

    def remote(self, k, source, target, device):
        copy = send_to(source, target, self.send_sem.at[k], self.recv_sem.at[k], device)
        copy.start()
        return copy

    def local(self, k, source, target):
        copy = pltpu.make_async_copy(source, target, self.local_sem.at[k])
        copy.start()
        return copy

    def start_left(self, left):
        rep, places = (self.places.rep, self.places)
        copies = []
        for i, device in enumerate((places.to_c, places.to_y, places.to_d)):
            rows = pl.ds(pl.multiple_of(device[1] * self.rows, 16), self.rows)
            copies.append(
                self.remote(i, left.at[rows], self.left_4.at[:, self.part(1 + i)], device)
            )
        rows = pl.ds(pl.multiple_of(rep * self.rows, 16), self.rows)
        copies.append(self.local(0, left.at[rows], self.left_4.at[:, self.part(0)]))
        self.copies[-1] = copies

    def start_right(self, right, third):
        lanes = pl.ds(third * H, H)
        source, k = (right.at[:, lanes], 3 + 3 * third)
        self.from_y[third] = self.remote(
            k, source, self.right_4.at[self.part(2), lanes], self.places.to_y
        )
        self.copies[third] = [
            self.remote(k + 1, source, self.right_4.at[self.part(1), lanes], self.places.to_c),
            self.local(1 + third, source, self.right_4.at[self.part(0), lanes]),
        ]

    def relay(self, third):
        self.from_y[third].wait()
        lanes = pl.ds(third * H, H)
        self.copies[third].append(
            self.remote(
                5 + 3 * third, self.right_4.at[self.part(2), lanes],
                self.right_4.at[self.part(3), lanes], self.places.to_c,
            )
        )

    def ready(self, first, offset):
        for part in (-1, offset // H):
            for copy in self.copies.pop(part, ()):
                copy.wait()

    def terms(self, y, rows, lanes):
        return side_by_side(self.left_4[rows, :], self.right_4, lanes)


class Addition:
    def __init__(self, own, sibling, done):
        self.own, self.sibling, self.done = (own, sibling, done)
        self.copies = {}

    def start(self, own, sibling, part):
        half = self.own.shape[1] // 2
        rows, copies = (pl.ds(part * half, half), [])
        for i, (source, target) in enumerate(((own, self.own), (sibling, self.sibling))):
            copies.append(
                pltpu.make_async_copy(
                    source.at[:, rows], target.at[:, rows], self.done.at[part, i]
                )
            )
            copies[i].start()
        self.copies[part] = copies

    def ready(self, first, offset):
        for copy in self.copies.pop(first // (self.own.shape[1] // 2), ()):
            copy.wait()

    def terms(self, y, rows, lanes):
        return [
            self.own[y, rows, lane].astype(F32) + self.sibling[y, rows, lane].astype(F32)
            for lane in lanes
        ]


class Halving:
    def __init__(self, places, units, outbox, inbox, send_sem, recv_sem, outs, groups):
        self.units, self.groups = (units, groups)
        self.outbox, self.inbox, self.outs = (outbox, inbox, outs)
        self.send_sem, self.recv_sem = (send_sem, recv_sem)
        self.bits = (places.x, places.z, places.w, places.y)
        self.peers = (places.to_x, places.to_z, places.to_w, places.to_y)
        self.copies = {}

    def blocks(self, u, k):
        source, stride, offset, order, first, count = self.units[u]
        free = order[k + 1 :]
        place = {ALONG_Y: self.bits[ALONG_Y]}
        for i, along in enumerate(order[: k + 1]):
            place[along] = self.bits[along] if i < k else 1 - self.bits[along]
        choices = [
            {along: (j >> (len(free) - 1 - i)) & 1 for i, along in enumerate(free)}
            for j in range(1 << len(free))
        ]
        results = [None] * len(choices)
        for y in (0, 1) if ALONG_Y in free else (None,):
            chosen = [j for j, choice in enumerate(choices) if choice.get(ALONG_Y) == y]
            lanes = []
            for j in chosen:
                bits = place | choices[j]
                device = bits[ALONG_W] * 4 + bits[ALONG_Z] * 2 + bits[ALONG_X]
                start = device * stride + offset
                if not isinstance(start, int):
                    start = pl.multiple_of(start, LANES)
                lanes.append(pl.ds(start, LANES))
            terms = source.terms(place[ALONG_Y] if y is None else y, pl.ds(first, count), lanes)
            for j, total in zip(chosen, terms):
                bits = place | choices[j]
                for i in range(k):
                    index = 0
                    for along in order[i + 1 :]:
                        index = index * 2 + bits[along]
                    total = total + self.inbox[u][i][index].astype(F32)
                results[j] = total
        return results

    def step(self, u, k):
        if k == 0:
            self.units[u][0].ready(self.units[u][4], self.units[u][2])
        else:
            self.copies[u, k - 1].wait_recv()
        if k == len(self.units[u][3]):
            self.outs[u][...] = self.blocks(u, k)[0]
            return
        for j, block in enumerate(self.blocks(u, k)):
            self.outbox[u][k][j] = block.astype(BF)
        copy = send_to(
            self.outbox[u][k], self.inbox[u][k], self.send_sem.at[u, k], self.recv_sem.at[u, k],
            self.peers[self.units[u][3][k]],
        )
        copy.start()
        self.copies[u, k] = copy

    def slot(self, t, lag=1):
        for k in range(5):
            if 0 <= t - lag * k < len(self.groups):
                for u in self.groups[t - lag * k]:
                    if k <= len(self.units[u][3]):
                        self.step(u, k)

    def drain(self):
        for copy in self.copies.values():
            copy.wait_send()


def boxes(units):
    return tuple(
        tuple(kept(1 << k, unit[-1], LANES) for k in reversed(range(len(unit[3]))))
        for unit in units
    )


HEAD_POST, HEAD_PRIOR, HEAD_POST_OUT, HEAD_PRIOR_OUT, HEAD_MAN_ENC = range(5)
HEAD_SOURCES = (SOURCE_POST, SOURCE_1024, SOURCE_1024, SOURCE_1024, SOURCE_MAN_ENC)
HEAD_UNITS = (
    (HEAD_POST, 128, 0, Y_FIRST, 0, 128),
    (HEAD_PRIOR, 128, 0, X_FIRST, 0, 128),
    (HEAD_POST_OUT, 128, 0, Z_FIRST, 0, 128),
    (HEAD_POST, 128, 0, Y_FIRST, 128, 128),
    (HEAD_PRIOR, 128, 0, X_FIRST, 128, 128),
    (HEAD_POST_OUT, 128, 0, Z_FIRST, 128, 128),
    (HEAD_POST, 128, 0, Y_FIRST, 256, 128),
    (HEAD_MAN_ENC, 128, 0, X_FIRST, 0, 128),
    (HEAD_PRIOR_OUT, 128, 0, Z_FIRST, 0, 128),
    (HEAD_POST, 128, 0, Y_FIRST, 384, 128),
    (HEAD_MAN_ENC, 128, 0, X_FIRST, 128, 128),
    (HEAD_PRIOR_OUT, 128, 0, Z_FIRST, 128, 128),
    (HEAD_POST, 128, 0, X_FIRST, 512, 128),
)
HEAD_GROUPS = ((0, 1, 2), (3, 4, 5), (6, 7, 8), (9, 10, 11), (12,))
HEAD_TIMES = (0, 2, 4, 7, 9, 11, 13, 15, 17)
HEAD_LAG = 1
FORWARD_ROWS, BACK_ROWS = (128, 128)
LAST_WORKER, LAST_GOAL_OUT, LAST_GOAL_IN, LAST_IMG, LAST_GRU = range(5)
LAST_SOURCES = (None, SOURCE_GOAL_OUT, SOURCE_GOAL_IN, SOURCE_1024)
LAST_UNITS = (
    (LAST_WORKER, 128, 0, X_FIRST, 384, 128),
    (LAST_WORKER, 128, 0, Z_FIRST, 640, 128),
    (LAST_WORKER, 128, 0, X_FIRST, 512, 128),
    (LAST_GOAL_OUT, 128, 0, Z_FIRST, 0, 128),
    (LAST_GOAL_IN, 128, 0, Z_FIRST, 0, 16),
    (LAST_IMG, 128, 0, X_FIRST, 0, 128),
    (LAST_GRU, 128, 0, X_ONLY, 0, 256),
    (LAST_GRU, 128, 0, Z_ONLY, 256, 256),
    (LAST_WORKER, 128, 0, Y_FIRST, 0, 128),
    (LAST_GRU, 128, H, X_ONLY, 0, 256),
    (LAST_GRU, 128, H, Z_ONLY, 256, 256),
    (LAST_WORKER, 128, 0, Y_FIRST, 128, 128),
    (LAST_GRU, 128, 2 * H, X_ONLY, 0, 256),
    (LAST_GRU, 128, 2 * H, Z_ONLY, 384, 128),
    (LAST_WORKER, 128, 0, Y_FIRST, 256, 128),
    (LAST_IMG, 128, 0, Y_FIRST, 128, 128),
    (LAST_GRU, 128, 2 * H, X_ONLY, 256, 128),
)
LAST_GROUPS = ((0, 1), (2, 3, 4), (5, 6, 7), (8, 9, 10), (11, 12, 13), (14, 15, 16))


class Worker(NamedTuple):
    goal_codes: Any = taken(GC, ROWS, dtype=jnp.int32)
    actions: Any = taken(HOR, ROWS, dtype=jnp.int32)
    samples: Any = taken(HOR, ZG, ROWS, dtype=jnp.int32)
    vectors: Any = taken(4, VECTOR_TILES, LANES, dtype=F32)
    tables: Any = taken(4, TABLES, LANES)
    start_state: Any = taken(ROWS, H + LANES)
    goal_out: Any = taken(U, H)
    actor_in_whole: Any = taken(3 * H, U, here=False)
    critic_in_whole: Any = taken(3 * H, U, here=False)
    post_left: Any = taken(H + E, ROWS, here=False)
    post_out_left: Any = taken(H, ROWS, here=False)
    prior_out_left: Any = taken(H, ROWS, here=False)
    me_left: Any = taken(H, 2 * ROWS, here=False)
    post_right: Any = taken(ROWS, H, here=False)
    prior_right: Any = taken(ROWS, H, here=False)
    post_out_right: Any = taken(ROWS, Z, here=False)
    prior_out_right: Any = taken(ROWS, Z, here=False)
    me_right: Any = taken(2 * ROWS, 2 * U, here=False)
    worker_own: Any = given(2, *WORKER_SHARE, here=False)
    worker_sibling: Any = given(2, *WORKER_SHARE, here=False)
    returned: Any = given(ROWS, H)
    goal_left: Any = given(U, ROWS)
    code_turned: Any = given(GCODE, ROWS)
    goal_right: Any = given(ROWS, H)
    goal_pair: Any = given(ROWS, 2 * U)
    small: Any = given(2, 2, SMALL_TILES, LANES, dtype=F32)
    sums: Any = tuple(given(unit[-1], LANES, dtype=F32) for unit in HEAD_UNITS)
    actor_in: Any = kept(3 * H, U)
    critic_in: Any = kept(3 * H, U)
    worker_left: Any = kept(3 * H, 2 * U)
    act_out: Any = kept(32, U)
    goal_in: Any = kept(GCODE, U)
    action_columns: Any = kept(ROWS, LANES, dtype=F32)
    goal_normed: Any = kept(ROWS, U, dtype=F32)
    goal_inverse: Any = kept(ROWS, 1, dtype=F32)
    goal_hidden: Any = kept(ROWS, U)
    goal_pre: Any = kept(ROWS, U)
    goal_low: Any = kept(ROWS, H)
    turned: Any = kept(2 * H, ROWS)
    slot_part: Any = kept(2, ROWS, U, dtype=F32)
    hot: Any = kept(2 * ROWS, Z)
    pre: Any = kept(2 * ROWS, U, dtype=F32)
    hidden: Any = kept(2 * ROWS, U)
    normed: Any = kept(2, HOR * ROWS, U, dtype=F32)
    inverse: Any = kept(2, HOR * ROWS, 1, dtype=F32)
    hot_turned: Any = kept(Z, HOR * ROWS)
    log_chance: Any = kept(HOR * ROWS, 32, dtype=F32)
    chosen: Any = kept(ROWS, LANES, dtype=F32)
    value: Any = kept(ROWS, LANES, dtype=F32)
    returns: Any = kept(ROWS, LANES, dtype=F32)
    pre_pair: Any = kept(HOR * ROWS, 2 * U)
    summed: Any = kept(2, ROWS, U, dtype=F32)
    sum_low: Any = kept(2, ROWS, U)
    sum_pair: Any = kept(ROWS, 2 * U)
    low_512: Any = kept(ROWS, U)
    grad_column: Any = kept(ROWS, 1, dtype=F32)
    to_state: Any = kept(ROWS, H)
    incoming: Any = kept(ROWS, H)
    wide_512: Any = kept(ROWS, U, dtype=F32)
    top: Any = kept(2, 8, LANES, dtype=F32)
    top_in: Any = kept(10, 8, LANES, dtype=F32)
    left_2: Any = tuple(kept(2, s.rows, 2 * s.depth) for s in HEAD_SOURCES)
    right_2: Any = tuple(kept(2 * s.depth, s.columns) for s in HEAD_SOURCES)
    outbox: Any = boxes(HEAD_UNITS)
    inbox: Any = boxes(HEAD_UNITS)
    load_done: Any = signal(2)
    add_send: Any = signal(2, 2)
    add_recv: Any = signal(2, 2)
    add_local: Any = signal(2, 2)
    top_send: Any = signal(10)
    top_recv: Any = signal(10)
    state_send: Any = signal(8)
    state_recv: Any = signal(8)
    pair_send: Any = signal(len(HEAD_SOURCES), 3)
    pair_recv: Any = signal(len(HEAD_SOURCES), 3)
    pair_local: Any = signal(len(HEAD_SOURCES), 3)
    half_send: Any = signal(len(HEAD_UNITS), 4)
    half_recv: Any = signal(len(HEAD_UNITS), 4)

    def gain(self, low, size):
        return vector_of(self.vectors, low, size // (4 * LANES))

    def goal(self):
        self.small[...] = jnp.zeros(self.small.shape, F32)
        for r in range(4):
            self.act_out[:, r * LANES : (r + 1) * LANES] = self.tables[
                r, TAB_ACT : TAB_ACT + 32, :
            ]
            for i in range(4):
                self.goal_in[16 * r : 16 * (r + 1), i * LANES : (i + 1) * LANES] = self.tables[
                    r, TAB_GOAL + 16 * i : TAB_GOAL + 16 * (i + 1), :
                ]
        self.action_columns[...] = columns_of(self.actions[...].astype(F32))
        hot = hot_rows(columns_of(self.goal_codes[...].astype(F32)), GK, GC, LANES)
        self.code_turned[...] = hot.T[0:GCODE].astype(BF)
        matmul_into(self.goal_normed, hot[:, 0:GCODE].astype(BF), self.goal_in)
        hidden_rows(
            self.goal_normed, self.goal_inverse, self.gain(GOAL_G, U), self.goal_hidden
        )
        turn_into(self.goal_left, self.goal_hidden)

        def one(j, totals):
            lanes = pl.ds(pl.multiple_of(j * TILE, TILE), TILE)
            goal = product(self.goal_hidden[...], self.goal_out[:, lanes])
            state = self.start_state[:, lanes].astype(F32)
            self.goal_low[:, lanes] = goal.astype(BF)
            terms = (goal * state, goal * goal, state * state)
            return tuple(
                t + jnp.sum(term, -1, keepdims=True) for t, term in zip(totals, terms)
            )

        zero = jnp.zeros((ROWS, 1), F32)
        aligned, goal_square, state_square = lax.fori_loop(0, H // TILE, one, (zero,) * 3)
        turn_into(self.turned, self.start_state.at[:, 0:H])
        turn_into(self.turned, self.goal_low, H)
        return aligned / (jnp.maximum(goal_square, state_square) + small_floor)

    def slots(self):
        for which, weight in enumerate((self.actor_in, self.critic_in)):
            def one(j, carry):
                lanes = pl.ds(pl.multiple_of(j * TILE, TILE), TILE)
                self.slot_part[which, :, lanes] = product(
                    self.start_state[:, 0:H], weight[0:H, lanes]
                ) + product(self.goal_low[...], weight[2 * H : 3 * H, lanes])
                return carry

            lax.fori_loop(0, U // TILE, one, 0)

    def forward(self, first, last):
        gains = (self.gain(ACT_G, U), self.gain(CRI_G, U))
        head = self.gain(CRI_O, U)
        spread = class_spread(ZG, ZK, ZG, Z)
        lane = lax.broadcasted_iota(jnp.int32, (1, Z), 1)
        lane_class = jnp.bitwise_and(lane, ZK - 1).astype(F32)
        group = lax.broadcasted_iota(jnp.int32, (Z, ZG), 1)
        place = lax.broadcasted_iota(jnp.int32, (Z, ZG), 0)
        inside = (place >= group * ZK) & (place < group * ZK + ZK)
        spread_turned = jnp.where(inside, 1.0, 0.0).astype(BF)
        place_class = jnp.bitwise_and(
            lax.broadcasted_iota(jnp.int32, (Z, 1), 0), ZK - 1
        ).astype(F32)
        act_lane = lax.broadcasted_iota(jnp.int32, (1, 32), 1)
        step_lane = lax.broadcasted_iota(jnp.int32, (1, LANES), 1)

        def pair(i, carry):
            start = pl.multiple_of(i * 2 * ROWS, 2 * ROWS)
            for half in range(2):
                k = 2 * i + half
                rows = pl.ds(pl.multiple_of(start + half * ROWS, ROWS), ROWS)
                ids = self.samples[k].astype(F32)
                self.hot[half * ROWS : (half + 1) * ROWS, :] = jnp.where(
                    product(columns_of(ids)[:, 0:ZG].astype(BF), spread) == lane_class, 1.0, 0.0
                ).astype(BF)
                self.hot_turned[:, rows] = jnp.where(
                    product(spread_turned, ids.astype(BF)) == place_class, 1.0, 0.0
                ).astype(BF)
            for which, weight in enumerate((self.actor_in, self.critic_in)):
                self.pre[...] = product(self.hot[...], weight[H : 2 * H, :])
                for low in range(0, 2 * ROWS, FORWARD_ROWS):
                    rows = pl.ds(pl.multiple_of(start + low, FORWARD_ROWS), FORWARD_ROWS)
                    slot = pl.ds(low % ROWS, FORWARD_ROWS)
                    pre = self.pre[low : low + FORWARD_ROWS, :] + self.slot_part[which, slot, :]
                    normed, inverse = normalize(pre)
                    self.normed[which, rows, :] = normed
                    self.inverse[which, rows, :] = inverse
                    hidden = elu_of(normed * gains[which]).astype(BF)
                    if which == 0:
                        self.hidden[low : low + FORWARD_ROWS, :] = hidden
                    else:
                        value = jnp.sum(hidden.astype(F32) * head, -1, keepdims=True)
                        here = step_lane == 2 * i + low // ROWS
                        self.value[slot, :] = jnp.where(here, value, self.value[slot, :])
            logits = lax.dot_general(
                self.hidden[...], self.act_out[...], (((1,), (1,)), ((), ())),
                preferred_element_type=F32,
            )
            logits = jnp.where(act_lane < NA, logits, -1e30)
            shifted = logits - jnp.max(logits, -1, keepdims=True)
            total = jnp.sum(jnp.exp(shifted), -1, keepdims=True)
            self.log_chance[pl.ds(start, 2 * ROWS), :] = shifted - jnp.log(total)
            return carry

        lax.fori_loop(first, last, pair, 0)

    def action_here(self, k):
        action = self.at_step(self.action_columns, k)
        return action == lax.broadcasted_iota(jnp.int32, (1, 32), 1).astype(F32)

    def at_step(self, ref, k):
        lane = lax.broadcasted_iota(jnp.int32, (ROWS, LANES), 1)
        return jnp.sum(jnp.where(lane == k, ref[...], 0.0), -1, keepdims=True)

    def targets(self, reward):
        weight = self.start_state[:, H : H + 1].astype(F32)
        lane = lax.broadcasted_iota(jnp.int32, (ROWS, LANES), 1)
        later = self.value[:, HOR - 1 : HOR]
        result = later
        returns = jnp.where(lane == HOR - 1, result, 0.0)
        for k in range(HOR - 2, -1, -1):
            blended = (1.0 - return_mix) * later + return_mix * result
            result = reward + discount * blended
            returns = jnp.where(lane == k, result, returns)
            later = self.value[:, k : k + 1]
        self.returns[...] = returns
        gaps = jnp.where(lane < HOR, jnp.abs(returns - self.value[...]), 0.0)
        top = jnp.max(weight * gaps, 0, keepdims=True)
        self.top[0] = jnp.broadcast_to(jnp.max(top, 1, keepdims=True), (8, LANES))

    def critic_back(self, first, last, total):
        gain, head = (self.gain(CRI_G, U), self.gain(CRI_O, U))
        weight = self.start_state[:, H : H + 1].astype(F32)

        def step(k, totals):
            rows = pl.ds(pl.multiple_of(k * ROWS, ROWS), ROWS)
            misfit = self.at_step(self.value, k) - self.at_step(self.returns, k)
            grad = weight * misfit * (1.0 / (ROWS * HOR))
            self.grad_column[...] = grad
            gain_total = totals[0] + hidden_rows_back(
                lambda r: self.grad_column[r, :] * head,
                self.normed.at[1, rows], self.inverse.at[1, rows], gain, self.low_512, BACK_ROWS,
                self.hidden,
            )
            head_total = totals[1] + jnp.sum(
                self.hidden[0:ROWS, :].astype(F32) * grad, 0, keepdims=True
            )
            for j in range(4):
                tile = self.low_512[:, j * LANES : (j + 1) * LANES].astype(F32)
                self.summed[1, :, j * LANES : (j + 1) * LANES] += tile
                turned = pltpu.roll(tile, 64, 1)
                self.pre_pair[rows, 2 * j * LANES : (2 * j + 1) * LANES] = turned.astype(BF)
                self.pre_pair[rows, (2 * j + 1) * LANES : (2 * j + 2) * LANES] = tile.astype(BF)
            return (gain_total, head_total)

        return lax.fori_loop(first, last, step, total)

    def pair(self, first, second, out_ref, rows):
        lane = lax.broadcasted_iota(jnp.int32, (ROWS, LANES), 1)
        for j in range(4):
            lanes = slice(j * LANES, (j + 1) * LANES)
            even = slice(2 * j * LANES, (2 * j + 1) * LANES)
            odd = slice((2 * j + 1) * LANES, (2 * j + 2) * LANES)
            a = first[:, lanes].astype(F32)
            if second is None:
                b_even, b_odd = (out_ref[rows, even].astype(F32), out_ref[rows, odd].astype(F32))
            else:
                b_odd = second[:, lanes].astype(F32)
                b_even = pltpu.roll(b_odd, 64, 1)
            out_ref[rows, even] = jnp.where(lane < 64, a, b_even).astype(BF)
            out_ref[rows, odd] = jnp.where(lane < 64, pltpu.roll(a, 64, 1), b_odd).astype(BF)

    def actor_back(self, first, last, totals):
        gain = self.gain(ACT_G, U)
        weight = self.start_state[:, H : H + 1].astype(F32)
        scale = self.top[1, 0:1, 0:1] + small_floor

        def step(k, totals):
            rows = pl.ds(pl.multiple_of(k * ROWS, ROWS), ROWS)
            advantage = self.at_step(self.returns, k) - self.at_step(self.value, k)
            gained = weight * advantage / scale
            here = self.action_here(k)
            log_chance = self.log_chance[rows, :]
            chance = jnp.exp(log_chance)
            grad = (gained * (-1.0 / (ROWS * HOR))) * (jnp.where(here, 1.0, 0.0) - chance)
            grad_turned = jnp.concatenate(
                [grad, jnp.zeros((ROWS, LANES - 32), F32)], 1
            ).T[0:32].astype(BF)
            self.wide_512[...] = product(grad.astype(BF), self.act_out[...])
            gain_total = totals[0] + hidden_rows_back(
                lambda r: self.wide_512[r, :],
                self.normed.at[0, rows], self.inverse.at[0, rows], gain, self.low_512, BACK_ROWS,
                self.hidden,
            )
            out_total = totals[1] + product(grad_turned, self.hidden[0:ROWS, :])
            self.summed[0] += self.low_512[...].astype(F32)
            self.pair(self.low_512, None, self.pre_pair, rows)
            chosen = jnp.sum(jnp.where(here, log_chance, 0.0), -1, keepdims=True)
            loss = totals[2] + jnp.sum(chosen * gained, 0, keepdims=True)
            return (gain_total, out_total, loss)

        return lax.fori_loop(first, last, step, totals)

    def inputs_back(self, low, out_ref):
        def one(j, carry):
            rows = pl.ds(pl.multiple_of(low + j * TILE, TILE), TILE)
            total = 0.0
            for which, weight in enumerate((self.actor_in, self.critic_in)):
                total = total + lax.dot_general(
                    self.sum_low[which], weight[rows, :], (((1,), (1,)), ((), ())),
                    preferred_element_type=F32,
                )
            out_ref[:, pl.ds(pl.multiple_of(j * TILE, TILE), TILE)] = total.astype(BF)
            return carry

        lax.fori_loop(0, H // TILE, one, 0)

    def goal_back(self):
        matmul_into(self.wide_512, self.goal_right[...], self.goal_out, turned=True)
        total = hidden_rows_back(
            lambda rows: self.wide_512[rows, :],
            self.goal_normed, self.goal_inverse, self.gain(GOAL_G, U), self.goal_pre,
        )
        put_vector(self.small, GOAL_G, total)
        spread_lanes(self.goal_pre, self.goal_pair, 0, 0)

    def weights(self, tile):
        size = 2 * U // 2
        for low in range(tile * size, (tile + 1) * size, TILE):
            lanes = slice(low, low + TILE)
            self.worker_left[H : 2 * H, lanes] = product(
                self.hot_turned[...], self.pre_pair[:, lanes]
            ).astype(BF)
            pair = self.sum_pair[:, lanes]
            self.worker_left[0:H, lanes] = product(self.turned[0:H], pair).astype(BF)
            self.worker_left[2 * H : 3 * H, lanes] = product(
                self.turned[H : 2 * H], pair
            ).astype(BF)

    def hand_over(self, places, tile):
        size, rows = (2 * U // 2, WORKER_SHARE[0])
        lanes, copies = (pl.ds(tile * size, size), [])
        for y in range(2):
            ours, theirs = (
                pl.ds(pl.multiple_of((2 * y + core) * rows, 16), rows)
                for core in (places.c, 1 - places.c)
            )
            copies.append(
                send_to(
                    self.worker_left.at[theirs, lanes], self.worker_sibling.at[y, :, lanes],
                    self.add_send.at[tile, y], self.add_recv.at[tile, y], places.to_c,
                )
            )
            copies.append(
                pltpu.make_async_copy(
                    self.worker_left.at[ours, lanes], self.worker_own.at[y, :, lanes],
                    self.add_local.at[tile, y],
                )
            )
        for copy in copies:
            copy.start()
        return copies


def worker_kernel(f):
    places = Places()
    met = greet(
        [(places.around(o), places.rep) for o in range(1, 8)]
        + [places.to_c, places.to_y, places.to_d]
    )
    loads = (
        pltpu.make_async_copy(f.actor_in_whole, f.actor_in, f.load_done.at[0]),
        pltpu.make_async_copy(f.critic_in_whole, f.critic_in, f.load_done.at[1]),
    )
    for load in loads:
        load.start()
    reward = f.goal()
    met()
    heads = []
    lefts = (f.post_left, f.post_left, f.post_out_left, f.prior_out_left, f.me_left)
    rights = (f.post_right, f.prior_right, f.post_out_right, f.prior_out_right, f.me_right)
    for i, source in enumerate(HEAD_SOURCES):
        heads.append(
            Exchange(
                places, source, f.left_2[i], f.right_2[i], f.pair_send, f.pair_recv,
                f.pair_local, i,
            )
        )
    for i in (HEAD_POST, HEAD_PRIOR, HEAD_POST_OUT):
        heads[i].start(0, lefts[i], rights[i])
    halving = Halving(
        places, [(heads[unit[0]],) + unit[1:] for unit in HEAD_UNITS], f.outbox, f.inbox,
        f.half_send, f.half_recv, f.sums, HEAD_GROUPS,
    )
    events = iter(range(24))

    def beside():
        event = next(events)
        for t, place in enumerate(HEAD_TIMES):
            if place == event:
                halving.slot(t, HEAD_LAG)

    for load in loads:
        load.wait()
    f.slots()
    beside()
    for i in (HEAD_MAN_ENC, HEAD_PRIOR_OUT):
        heads[i].start(0, lefts[i], rights[i])
    f.value[...] = jnp.zeros(f.value.shape, F32)
    f.summed[...] = jnp.zeros(f.summed.shape, F32)
    beside()
    for i in range(4):
        f.forward(2 * i, 2 * i + 2)
        beside()
    f.targets(reward)
    totals = (jnp.zeros((1, U), F32), jnp.zeros((1, U), F32))
    steps = (0, 3, 6, 9, 12, HOR)

    def send_top(which, first, devices):
        copies = []
        for i, device in enumerate(devices):
            k = first + i
            copies.append(
                send_to(f.top.at[which], f.top_in.at[k], f.top_send.at[k], f.top_recv.at[k], device)
            )
            copies[i].start()
        return copies

    def largest(which, first, copies):
        top = f.top[which]
        for i, copy in enumerate(copies):
            copy.wait()
            top = jnp.maximum(top, f.top_in[first + i])
        f.top[1] = top

    tops = send_top(0, 0, [(places.around(o), places.rep) for o in range(1, 8)])
    for k in range(5):
        if k == 3:
            largest(0, 0, tops)
            tops = send_top(1, 7, [places.to_c, places.to_y, places.to_d])
        totals = f.critic_back(steps[k], steps[k + 1], totals)
        beside()
    largest(1, 7, tops)
    put_vector(f.small, CRI_G, totals[0])
    put_vector(f.small, CRI_O, totals[1])
    totals = (jnp.zeros((1, U), F32), jnp.zeros((32, U), F32), jnp.zeros((1, 1), F32))
    for i in range(4):
        totals = f.actor_back(4 * i, 4 * i + 4, totals)
        beside()
    actor_gain, actor_out, chosen = totals
    put_vector(f.small, ACT_G, actor_gain)
    put_table(f.small, ACT_T, actor_out, 24)
    for which in range(2):
        f.sum_low[which] = f.summed[which].astype(BF)
    f.inputs_back(0, f.to_state)
    states = regroup_start(places, f.to_state, f.incoming, f.state_send, f.state_recv)
    f.pair(f.sum_low.at[0], f.sum_low.at[1], f.sum_pair, slice(0, ROWS))
    beside()
    f.weights(0)
    halves = f.hand_over(places, 0)
    f.weights(1)
    halves += f.hand_over(places, 1)
    beside()
    f.inputs_back(2 * H, f.goal_right)
    f.goal_back()
    beside()
    weight = f.start_state[:, H : H + 1].astype(F32)
    misfit = f.value[...] - f.returns[...]
    squares = jnp.sum(jnp.sum(weight * misfit * misfit, -1, keepdims=True), 0, keepdims=True)
    loss = (0.5 * squares - chosen) * (1.0 / (ROWS * HOR))
    for y in range(2):
        for c in range(2):
            f.small[c, y, LOSS : LOSS + 1, :] = jnp.broadcast_to(loss, (1, LANES))
    for copy in states + halves:
        copy.wait()
    f.returned[...] = f.incoming[...]
    halving.drain()


class Last(NamedTuple):
    meta_turned: Any = taken(LANES, ROWS, dtype=F32)
    prev: Any = taken(ROWS, H)
    vectors: Any = taken(4, VECTOR_TILES, LANES, dtype=F32)
    returned: Any = taken(ROWS, H)
    grad_partial: Any = taken(ROWS, H, dtype=F32)
    gru_normed: Any = taken(ROWS, 3 * H, dtype=F32)
    gru_inverse: Any = taken(ROWS, 1, dtype=F32)
    img_normed: Any = taken(ROWS, H, dtype=F32)
    img_inverse: Any = taken(ROWS, 1, dtype=F32)
    small_1: Any = taken(2, 2, SMALL_TILES, LANES, dtype=F32)
    small_2: Any = taken(2, 2, SMALL_TILES, LANES, dtype=F32)
    gru_share: Any = taken(2 * H, 3 * H, here=False)
    worker_own_in: Any = taken(2, *WORKER_SHARE, here=False)
    worker_sibling_in: Any = taken(2, *WORKER_SHARE, here=False)
    goal_left: Any = taken(U, ROWS, here=False)
    dec_left: Any = taken(U, ROWS, here=False)
    code_turned: Any = taken(GCODE, ROWS, here=False)
    soft_turned: Any = taken(GCODE, ROWS, here=False)
    gru_left: Any = taken(2 * H, ROWS, here=False)
    img_left: Any = taken(Z, ROWS, here=False)
    goal_right: Any = taken(ROWS, H, here=False)
    recon_low: Any = taken(ROWS, H, here=False)
    goal_pair: Any = taken(ROWS, 2 * U, here=False)
    dec_pair: Any = taken(ROWS, 2 * U, here=False)
    deter_grad: Any = given(ROWS, H, dtype=F32)
    small_sum: Any = given(SMALL_TILES, LANES, dtype=F32)
    sums: Any = tuple(given(unit[-1], LANES, dtype=F32) for unit in LAST_UNITS)
    gru_weight: Any = kept(2 * H, 3 * H)
    gru_right: Any = kept(ROWS, 3 * H)
    gru_thirds: Any = kept(ROWS, 3 * H)
    img_right: Any = kept(ROWS, H)
    grad: Any = kept(ROWS, H, dtype=F32)
    wide: Any = kept(ROWS, 2 * H, dtype=F32)
    small: Any = kept(2, 2, SMALL_TILES, LANES, dtype=F32)
    small_pair: Any = kept(2, SMALL_TILES, LANES, dtype=F32)
    small_in: Any = kept(4, SMALL_TILES, LANES, dtype=F32)
    worker_own: Any = kept(2, *WORKER_SHARE)
    worker_sibling: Any = kept(2, *WORKER_SHARE)
    gru_left_4: Any = kept(H // 2, 4 * ROWS)
    gru_right_4: Any = kept(4 * ROWS, 3 * H)
    left_2: Any = tuple(kept(2, s.rows, 2 * s.depth) for s in LAST_SOURCES[1:])
    right_2: Any = tuple(kept(2 * s.depth, s.columns) for s in LAST_SOURCES[1:])
    outbox: Any = boxes(LAST_UNITS)
    inbox: Any = boxes(LAST_UNITS)
    load_done: Any = signal(1)
    add_done: Any = signal(2, 2)
    wide_send: Any = signal(12)
    wide_recv: Any = signal(12)
    wide_local: Any = signal(4)
    pair_send: Any = signal(5, 3)
    pair_recv: Any = signal(5, 3)
    pair_local: Any = signal(5, 3)
    half_send: Any = signal(len(LAST_UNITS), 4)
    half_recv: Any = signal(len(LAST_UNITS), 4)
    small_send: Any = signal(5)
    small_recv: Any = signal(5)

    def state_back(self):
        gain = vector_of(self.vectors, GRU_G, 6)
        frame = lax.broadcasted_iota(jnp.int32, (ROWS, ROWS), 0).astype(F32)
        place = jnp.where(self.meta_turned[37:38, :] == frame, 1.0, 0.0).astype(BF)

        def add(j, carry):
            lanes = pl.ds(pl.multiple_of(j * TILE, TILE), TILE)
            self.grad[:, lanes] = self.grad_partial[:, lanes] + product(
                place, self.returned[:, lanes]
            )
            return carry

        lax.fori_loop(0, H // TILE, add, 0)

        def one(rows, total):
            normed = self.gru_normed[rows, :]
            parts = normed * gain
            inner = parts[:, H : 2 * H]
            reset = 1.0 / (1.0 + jnp.exp(-parts[:, :H]))
            candidate = jnp.tanh(reset * inner)
            update = 1.0 / (1.0 + jnp.exp(1.0 - parts[:, 2 * H :]))
            grad = self.grad[rows, :]
            prev = self.prev[rows, :].astype(F32)
            grad_inner = grad * update * (1.0 - candidate * candidate)
            grad_parts = jnp.concatenate(
                [
                    grad_inner * inner * reset * (1.0 - reset),
                    grad_inner * reset,
                    grad * (candidate - prev) * update * (1.0 - update),
                ],
                1,
            )
            self.deter_grad[rows, :] = grad * (1.0 - update)
            total = total + jnp.sum(grad_parts * normed, 0, keepdims=True)
            back = normalize_back(grad_parts * gain, normed, self.gru_inverse[rows, :])
            self.gru_right[rows, :] = back.astype(BF)
            for j in range(24):
                low = (j % 3 * 8 + j // 3) * LANES
                self.gru_thirds[rows, low : low + LANES] = back[
                    :, j * LANES : (j + 1) * LANES
                ].astype(BF)
            return total

        put_vector(self.small, GRU_G, by_rows(ROWS, 16, one, jnp.zeros((1, 3 * H), F32)))

    def input_back(self):
        matmul_into(self.wide, self.gru_right[...], self.gru_weight, turned=True)
        self.deter_grad[...] += self.wide[:, H : 2 * H]
        total = hidden_rows_back(
            lambda rows: self.wide[rows, 0:H],
            self.img_normed, self.img_inverse, vector_of(self.vectors, IMG_G, 2), self.img_right,
        )
        put_vector(self.small, IMG_G, total)

    def action_back(self):
        place = lax.broadcasted_iota(jnp.int32, (24, ROWS), 0).astype(F32)
        hot = jnp.where(self.meta_turned[32:33, :] == place, 1.0, 0.0).astype(BF)
        for r in range(4):
            for i in range(2):
                start = (2 * r + i) * LANES
                low = IMG_T + 24 * i
                self.small[r % 2, r // 2, low : low + 24, :] = product(
                    hot, self.img_right[:, start : start + LANES]
                )


class SmallSum:
    def __init__(self, places, f):
        self.places, self.f = (places, f)
        self.copies = []

    def step(self, k):
        f, places = (self.f, self.places)
        if k > 0:
            self.copies[k - 1].wait()
        if k == 0:
            source, target, device = (f.small.at[1 - places.c], f.small_pair, places.to_c)
        elif k == 1:
            f.small_pair[...] = f.small_pair[...] + f.small[places.c]
            source, target, device = (
                f.small_pair.at[1 - places.y], f.small_in.at[0], places.to_y,
            )
        else:
            if k == 2:
                f.small_sum[...] = f.small_pair[places.y] + f.small_in[0]
            else:
                f.small_sum[...] = f.small_sum[...] + f.small_in[k - 2]
            if k == 5:
                return
            device = (places.to_x, places.to_z, places.to_w)[k - 2]
            source, target = (f.small_sum, f.small_in.at[k - 1])
        copy = send_to(source, target, f.small_send.at[k], f.small_recv.at[k], device)
        copy.start()
        self.copies.append(copy)


def last_kernel(f):
    places = Places()
    load = pltpu.make_async_copy(f.gru_share, f.gru_weight, f.load_done.at[0])
    load.start()
    worker = Addition(f.worker_own, f.worker_sibling, f.add_done)
    for part in (1, 0):
        worker.start(f.worker_own_in, f.worker_sibling_in, part)
    met = greet(
        (places.to_c, places.to_y, places.to_d, places.to_x, places.to_z, places.to_w)
    )
    f.small[...] = f.small_1[...] + f.small_2[...]
    f.state_back()
    met()
    sources, part = ([worker], 0)
    for i, source in enumerate(LAST_SOURCES[1:]):
        sources.append(
            Exchange(
                places, source, f.left_2[i], f.right_2[i], f.pair_send, f.pair_recv,
                f.pair_local, part,
            )
        )
        part += len(source.parts)
    gru = Wide(
        places, H // 2, ROWS, f.gru_left_4, f.gru_right_4, f.wide_send, f.wide_recv, f.wide_local
    )
    sources.append(gru)
    for third in range(3):
        gru.start_right(f.gru_thirds, third)
        if third == 0:
            gru.start_left(f.gru_left)
    sources[LAST_GOAL_OUT].start(0, f.goal_left, f.goal_right)
    sources[LAST_GOAL_OUT].start(1, f.dec_left, f.recon_low)
    sources[LAST_GOAL_IN].start(0, f.code_turned, f.goal_pair)
    sources[LAST_GOAL_IN].start(1, f.soft_turned, f.dec_pair)
    sources[LAST_IMG].start_left(0, f.img_left)
    halving = Halving(
        places, [(sources[unit[0]],) + unit[1:] for unit in LAST_UNITS], f.outbox, f.inbox,
        f.half_send, f.half_recv, f.sums, LAST_GROUPS,
    )
    halving.slot(0)
    load.wait()
    f.input_back()
    sources[LAST_IMG].start_right(0, f.img_right)
    halving.slot(1)
    f.action_back()
    small = SmallSum(places, f)
    small.step(0)
    for t in range(2, len(LAST_GROUPS) + 4):
        if t < 5:
            gru.relay(t - 2)
        halving.slot(t)
        if t < 7:
            small.step(t - 1)
    halving.drain()


class Unpack(NamedTuple):
    heads: Any = tuple(taken(unit[-1], LANES, dtype=F32) for unit in HEAD_UNITS)
    last: Any = tuple(taken(unit[-1], LANES, dtype=F32) for unit in LAST_UNITS)
    small: Any = taken(SMALL_TILES, LANES, dtype=F32)
    deter: Any = taken(ROWS, H, dtype=F32)
    embed: Any = taken(ROWS, E, dtype=F32)
    loss: Any = given(1, LANES, dtype=F32)
    deter_grad: Any = given(ROWS, H, dtype=F32)
    embed_grad: Any = given(ROWS, E, dtype=F32)
    obs_gain: Any = given(H // 4, dtype=F32)
    manager_in: Any = given(U // 8, H // 4, dtype=F32)
    manager_gain: Any = given(U // 4, dtype=F32)
    manager_out: Any = given(U // 4, dtype=F32)
    goal_in: Any = given(GCODE // 4, U // 8, dtype=F32)
    goal_gain: Any = given(U // 4, dtype=F32)
    goal_out: Any = given(U // 4, H // 8, dtype=F32)
    actor_in: Any = given(U // 8, 3 * H // 4, dtype=F32)
    actor_gain: Any = given(U // 4, dtype=F32)
    actor_out: Any = given(NA, U // 4, dtype=F32)
    critic_in: Any = given(U // 8, 3 * H // 4, dtype=F32)
    critic_gain: Any = given(U // 4, dtype=F32)
    critic_out: Any = given(U // 4, dtype=F32)
    img_stoch: Any = given(Z // 4, H // 8, dtype=F32)
    img_action: Any = given(NA, H // 4, dtype=F32)
    img_gain: Any = given(H // 4, dtype=F32)
    gru_weight: Any = given(H // 2, 3 * H // 8, dtype=F32)
    gru_gain: Any = given(3 * H // 4, dtype=F32)
    post_in: Any = given((H + E) // 4, H // 8, dtype=F32)
    post_gain: Any = given(H // 4, dtype=F32)
    post_out: Any = given(H // 4, Z // 8, dtype=F32)
    prior_in: Any = given(H // 4, H // 8, dtype=F32)
    prior_gain: Any = given(H // 4, dtype=F32)
    prior_out: Any = given(H // 4, Z // 8, dtype=F32)
    enc_in: Any = given(U // 8, H // 4, dtype=F32)
    enc_gain: Any = given(U // 4, dtype=F32)
    enc_out: Any = given(GCODE, U // 4, dtype=F32)


def unpack_kernel(f):
    f.loss[...] = f.small[LOSS : LOSS + 1, :]
    f.deter_grad[...] = f.deter[...]
    f.embed_grad[...] = f.embed[...]
    for low, vector in (
        (OBS, f.obs_gain), (MAN_G, f.manager_gain), (MAN_O, f.manager_out),
        (GOAL_G, f.goal_gain), (ACT_G, f.actor_gain), (CRI_G, f.critic_gain),
        (CRI_O, f.critic_out), (IMG_G, f.img_gain), (GRU_G, f.gru_gain), (POST_G, f.post_gain),
        (PRIOR_G, f.prior_gain), (ENC_G, f.enc_gain),
    ):
        for i in range(vector.shape[0] // LANES):
            vector[pl.ds(i * LANES, LANES)] = f.small[low + i, :]
    f.actor_out[...] = f.small[ACT_T : ACT_T + NA, :]
    f.enc_out[...] = f.small[ENC_T : ENC_T + GCODE, :]
    for i in range(2):
        f.img_action[:, i * LANES : (i + 1) * LANES] = f.small[
            IMG_T + 24 * i : IMG_T + 24 * i + NA, :
        ]

    def halves(value, rows, first, second):
        for low in range(0, value.shape[0], LANES):
            turned = value[low : low + LANES, :].T
            places = slice(rows.start + low, rows.start + low + LANES)
            first[:, places] = turned[0:64]
            second[:, places] = turned[64:LANES]

    whole = {
        HEAD_POST: f.post_in, HEAD_PRIOR: f.prior_in, HEAD_POST_OUT: f.post_out,
        HEAD_PRIOR_OUT: f.prior_out,
    }
    for unit, value in zip(HEAD_UNITS, f.heads):
        rows = slice(unit[4], unit[4] + unit[5])
        if unit[0] == HEAD_MAN_ENC:
            halves(value, rows, f.manager_in, f.enc_in)
        else:
            whole[unit[0]][rows, :] = value[...]
    whole = {LAST_GOAL_OUT: f.goal_out, LAST_IMG: f.img_stoch}
    for unit, value in zip(LAST_UNITS, f.last):
        rows = slice(unit[4], unit[4] + unit[5])
        if unit[0] == LAST_WORKER:
            halves(value, rows, f.actor_in, f.critic_in)
        elif unit[0] == LAST_GOAL_IN:
            f.goal_in[...] = value[:, 0:64]
        elif unit[0] == LAST_GRU:
            low = unit[2] // H * LANES
            f.gru_weight[rows, low : low + LANES] = value[...]
        else:
            whole[unit[0]][rows, :] = value[...]


class Weights(NamedTuple):
    obs_gain: Any = None
    manager_in: Any = None
    manager_gain: Any = None
    manager_out: Any = None
    goal_in: Any = None
    goal_gain: Any = None
    goal_out: Any = None
    actor_in: Any = None
    actor_gain: Any = None
    actor_out: Any = None
    critic_in: Any = None
    critic_gain: Any = None
    critic_out: Any = None
    img_stoch: Any = None
    img_action: Any = None
    img_gain: Any = None
    gru_weight: Any = None
    gru_gain: Any = None
    post_in: Any = None
    post_gain: Any = None
    post_out: Any = None
    prior_in: Any = None
    prior_gain: Any = None
    prior_out: Any = None
    enc_in: Any = None
    enc_gain: Any = None
    enc_out: Any = None


class Data(NamedTuple):
    deter_states: Any
    embed: Any
    lengths: Any
    resets: Any
    terminal: Any
    rewards: Any
    prev_stoch: Any
    prev_action: Any
    regroup: Any
    goal_codes: Any
    samples: Any
    actions: Any


def step_in_kernels(data, w):
    prev = data.deter_states.reshape(ROWS, H)
    f = run_kernel(
        frames_kernel, Frames(),
        (
            data.lengths, data.resets, data.terminal, data.rewards,
            data.prev_stoch.transpose(0, 2, 1), data.prev_action, data.regroup, prev,
            data.embed.reshape(ROWS, E), w.obs_gain, w.manager_gain, w.manager_out, w.goal_gain,
            w.actor_gain, w.critic_gain, w.critic_out, w.img_gain, w.gru_gain, w.post_gain,
            w.prior_gain, w.enc_gain, w.actor_out.T, w.enc_out.T, w.img_action, w.goal_in,
            w.img_stoch, w.gru_weight, w.manager_in, w.enc_in, w.goal_out, w.prior_in, w.post_in,
            w.prior_out, w.post_out, w.actor_in, w.critic_in,
        ),
        "frames", 0,
    )
    s = run_kernel(
        worker_kernel, Worker(),
        (
            data.goal_codes.T, data.actions.T, data.samples.transpose(1, 2, 0), f.vectors,
            f.tables, f.start_state, f.goal_out_out, f.actor_in_out, f.critic_in_out, f.post_left,
            f.post_out_left, f.prior_out_left, f.me_left, f.post_right, f.prior_right,
            f.post_out_right, f.prior_out_right, f.me_right,
        ),
        "worker", 1,
    )
    b = run_kernel(
        last_kernel, Last(),
        (
            f.meta_turned, prev, f.vectors, s.returned, f.grad_deter, f.gru_normed, f.gru_inverse,
            f.img_normed, f.img_inverse, f.small, s.small, f.gru_weight_out, s.worker_own,
            s.worker_sibling, s.goal_left, f.dec_left, s.code_turned, f.soft_turned, f.gru_left, f.img_left,
            s.goal_right, f.recon_low, s.goal_pair, f.dec_pair,
        ),
        "last", 2,
    )
    u = run_kernel(
        unpack_kernel, Unpack(),
        tuple(s.sums) + tuple(b.sums) + (b.small_sum, b.deter_grad, f.embed_grad),
        "unpack",
    )
    first = len(Unpack._fields) - len(Weights._fields)
    grads = Weights(*tuple(u)[first:])
    grads = grads._replace(
        manager_in=grads.manager_in.T, actor_in=grads.actor_in.T, critic_in=grads.critic_in.T,
        enc_in=grads.enc_in.T, actor_out=grads.actor_out.T, enc_out=grads.enc_out.T,
    )
    return (
        u.loss[0, 0],
        u.deter_grad.reshape(SEQ_DEV, LEN, H),
        u.embed_grad.reshape(SEQ_DEV, LEN, E),
    ) + tuple(grads)


DP, REP = ("dp", "rep")
IMG_ACTION = 14
LARGE = Weights(**dict.fromkeys(Weights._fields, False))._replace(
    manager_in=True,
    goal_in=True,
    goal_out=True,
    actor_in=True,
    critic_in=True,
    img_stoch=True,
    gru_weight=True,
    post_in=True,
    post_out=True,
    prior_in=True,
    prior_out=True,
    enc_in=True,
)


def hidden_forward(pre_act, scaling):
    normed, inverse = normalize(pre_act)
    scaled = normed * scaling
    return ((normed, inverse, scaled), jax.nn.elu(scaled).astype(jnp.bfloat16))


def hidden_backward(grad_hidden, cache, scaling):
    normed, inverse, scaled = cache
    grad_scaled = grad_hidden * jnp.where(scaled > 0, 1.0, jnp.exp(jnp.minimum(scaled, 0.0)))
    grad_gain = jnp.sum(grad_scaled * normed, tuple(range(scaled.ndim - 1)))
    return (normalize_back(grad_scaled * scaling, normed, inverse).astype(jnp.bfloat16), grad_gain)


def input_backward(grad_pre, input_low, weight):
    grad_weight = jnp.einsum("nk,nu->ku", input_low, grad_pre, preferred_element_type=jnp.float32)
    to_input = jnp.einsum("nu,ku->nk", grad_pre, weight, preferred_element_type=jnp.float32)
    return (grad_weight, to_input)


def head_backward(grad_head, hidden_low, head, cache, scaling):
    grad_weight = jnp.einsum("nu,nk->uk", hidden_low, grad_head, preferred_element_type=jnp.float32)
    grad_hidden = jnp.einsum("nk,uk->nu", grad_head, head, preferred_element_type=jnp.float32)
    grad_pre, grad_gain = hidden_backward(grad_hidden, cache, scaling)
    return (grad_weight, grad_pre, grad_gain)


def group_softmax(flat_logits, groups):
    log_part = jax.nn.log_softmax(flat_logits.reshape(flat_logits.shape[0], groups, -1), axis=-1)
    return (log_part, jnp.exp(log_part))


def chain_returns(values_now, rewards_now, linked, carried):

    def back_step(carry_pair, inputs):
        later_return, later_value = carry_pair
        current, reward_now, link_now, carry_now = inputs
        blended = (1.0 - return_mix) * later_value + return_mix * later_return
        result = jnp.where(link_now, reward_now + discount * carry_now * blended, current)
        return ((result, current), result)

    zero_start = jnp.zeros(values_now.shape[:1], jnp.float32)
    _, stacked = lax.scan(
        back_step,
        (zero_start, zero_start),
        (values_now.T, rewards_now.T, linked.T, carried.T),
        reverse=True,
    )
    return stacked.T


def worker_forward(start_state, goal_low, stoch_hot, first_layer, scaling):
    slot_part = product(start_state, first_layer[:H]) + product(goal_low, first_layer[H + Z :])
    varying = product(stoch_hot, first_layer[H : H + Z]).reshape(start_state.shape[0], HOR, U)
    return hidden_forward(slot_part[:, None, :] + varying, scaling)


def worker_backward(grad_pre, start_state, goal_low, stoch_hot, first_layer):
    slot_count = grad_pre.shape[0]
    grad_stoch = jnp.einsum(
        "nz,nu->zu",
        stoch_hot,
        grad_pre.reshape(slot_count * HOR, U),
        preferred_element_type=jnp.float32,
    )
    summed = jnp.sum(grad_pre, 1, dtype=jnp.float32).astype(jnp.bfloat16)
    grad_state_rows, to_state = input_backward(summed, start_state, first_layer[:H])
    grad_goal_rows, to_goal = input_backward(summed, goal_low, first_layer[H + Z :])
    return (jnp.concatenate([grad_state_rows, grad_stoch, grad_goal_rows], 0), to_state, to_goal)


def step_plain(data, shares):
    (deter_states, embed, lengths, resets, terminal, rewards, prev_stoch, prev_action, regroup, goal_codes, samples, actions) = data
    full = [
        lax.all_gather(share, REP, axis=1 if i == IMG_ACTION else 0, tiled=True)
        for i, share in enumerate(shares)
    ]
    (obs_gain, manager_in, manager_gain, manager_out, goal_in, goal_gain, goal_out, actor_in, actor_gain, actor_out, critic_in, critic_gain, critic_out, img_stoch, img_action, img_gain, gru_weight, gru_gain, post_in, post_gain, post_out, prior_in, prior_gain, prior_out, enc_in, enc_gain, enc_out) = full
    prev_low = deter_states.reshape(ROWS, H)
    prev_float = prev_low.astype(jnp.float32)
    embed_low = embed.reshape(ROWS, E)
    positions = lax.broadcasted_iota(jnp.int32, (SEQ_DEV, LEN), 1)
    is_valid = positions < lengths[:, None]
    next_valid = jnp.concatenate([is_valid[:, 1:], jnp.zeros((SEQ_DEV, 1), jnp.bool_)], 1)
    next_reset = jnp.concatenate([resets[:, 1:], jnp.ones((SEQ_DEV, 1), jnp.int32)], 1)
    linked = next_valid & (next_reset == 0)
    carried = 1.0 - terminal.astype(jnp.float32)
    valid_rows = is_valid.astype(jnp.float32).reshape(ROWS)
    frame_scale = valid_rows / ROWS
    stoch_prev_hot = (
        (prev_stoch[..., None] == lax.broadcasted_iota(jnp.int32, (1, 1, 1, ZK), 3))
        .astype(jnp.bfloat16)
        .reshape(ROWS, Z)
    )
    action_prev_hot = (
        prev_action.reshape(ROWS)[:, None] == lax.broadcasted_iota(jnp.int32, (1, NA), 1)
    ).astype(jnp.bfloat16)
    img_cache, img_hidden = hidden_forward(
        product(stoch_prev_hot, img_stoch) + product(action_prev_hot, img_action), img_gain
    )
    gru_input = jnp.concatenate([img_hidden, prev_low], 1)
    gru_normed, gru_inverse = normalize(product(gru_input, gru_weight))
    gru_parts = gru_normed * gru_gain
    reset_gate = jax.nn.sigmoid(gru_parts[:, :H])
    candidate_in = gru_parts[:, H : 2 * H]
    candidate = jnp.tanh(reset_gate * candidate_in)
    update_gate = jax.nn.sigmoid(gru_parts[:, 2 * H :] - 1.0)
    deter_state = update_gate * candidate + (1.0 - update_gate) * prev_float
    deter_low = deter_state.astype(jnp.bfloat16)
    obs_normed, obs_inverse = normalize(deter_state)
    feature = (obs_normed * obs_gain).astype(jnp.bfloat16)
    man_cache, man_hidden = hidden_forward(product(feature, manager_in), manager_gain)
    manager_value = product(man_hidden, manager_out).reshape(SEQ_DEV, LEN)
    manager_return = chain_returns(manager_value, rewards, linked, carried)
    manager_misfit = (manager_value - manager_return).reshape(ROWS)
    post_input = jnp.concatenate([deter_low, embed_low], 1)
    post_cache, post_hidden = hidden_forward(product(post_input, post_in), post_gain)
    post_log, post_prob = group_softmax(product(post_hidden, post_out), ZG)
    prior_cache, prior_hidden = hidden_forward(product(deter_low, prior_in), prior_gain)
    prior_log, prior_prob = group_softmax(product(prior_hidden, prior_out), ZG)
    log_gap = post_log - prior_log
    group_kl = jnp.sum(post_prob * log_gap, -1, keepdims=True)
    enc_cache, enc_hidden = hidden_forward(product(deter_low, enc_in), enc_gain)
    code_log, code_prob = group_softmax(product(enc_hidden, enc_out), GC)
    code_kl = jnp.sum(code_prob * (code_log + math.log(GK)), (1, 2))
    code_spread = jnp.sum(code_prob * code_log, -1, keepdims=True)
    soft_code = code_prob.reshape(ROWS, GCODE).astype(jnp.bfloat16)
    dec_cache, dec_hidden = hidden_forward(product(soft_code, goal_in), goal_gain)
    recon_err = product(dec_hidden, goal_out) - deter_state
    frame_terms = (
        jnp.sum(post_prob * log_gap, (1, 2)) + code_kl + 0.5 * jnp.mean(recon_err * recon_err, -1)
    )
    frame_loss = jnp.sum(valid_rows * (0.5 * manager_misfit * manager_misfit + frame_terms)) / ROWS
    send_order = regroup[0]
    start_state, slot_flag = (
        lax.all_to_all(deter_low[send_order], DP, split_axis=0, concat_axis=0, tiled=True),
        lax.all_to_all(
            valid_rows[send_order].astype(jnp.bfloat16),
            DP,
            split_axis=0,
            concat_axis=0,
            tiled=True,
        ),
    )
    slot_weight = slot_flag.astype(jnp.float32)
    code_hot = (
        (goal_codes[:, :, None] == lax.broadcasted_iota(jnp.int32, (1, 1, GK), 2))
        .astype(jnp.bfloat16)
        .reshape(ROWS, GCODE)
    )
    goal_cache, goal_hidden = hidden_forward(product(code_hot, goal_in), goal_gain)
    goal_vector = product(goal_hidden, goal_out)
    goal_low = goal_vector.astype(jnp.bfloat16)
    state_float = start_state.astype(jnp.float32)
    alignment = jnp.sum(goal_vector * state_float, -1)
    largest_square = (
        jnp.maximum(jnp.sum(goal_vector * goal_vector, -1), jnp.sum(state_float * state_float, -1))
        + small_floor
    )
    reward_slot = alignment / largest_square
    stoch_hot = (
        (samples[..., None] == lax.broadcasted_iota(jnp.int32, (1, 1, 1, ZK), 3))
        .astype(jnp.bfloat16)
        .reshape(ROWS * HOR, Z)
    )
    action_hot = (actions[..., None] == lax.broadcasted_iota(jnp.int32, (1, 1, NA), 2)).astype(
        jnp.float32
    )
    actor_cache, actor_hidden = worker_forward(
        start_state, goal_low, stoch_hot, actor_in, actor_gain
    )
    logits = jnp.einsum("rku,ua->rka", actor_hidden, actor_out, preferred_element_type=jnp.float32)
    log_chance = jax.nn.log_softmax(logits, axis=-1)
    chosen = jnp.sum(log_chance * action_hot, -1)
    critic_cache, critic_hidden = worker_forward(
        start_state, goal_low, stoch_hot, critic_in, critic_gain
    )
    worker_value = jnp.einsum(
        "rku,u->rk", critic_hidden, critic_out, preferred_element_type=jnp.float32
    )
    step_link = lax.broadcasted_iota(jnp.int32, (ROWS, HOR), 1) < HOR - 1
    worker_return = chain_returns(
        worker_value,
        jnp.broadcast_to(reward_slot[:, None], (ROWS, HOR)),
        step_link,
        jnp.ones((ROWS, HOR), jnp.float32),
    )
    advantage = worker_return - worker_value
    local_top = jnp.max(slot_weight[:, None] * jnp.abs(advantage))
    return_scale = lax.pmax(local_top, (DP, REP)) + small_floor
    step_total = ROWS * HOR
    value_misfit = worker_value - worker_return
    critic_part = 0.5 * jnp.sum(slot_weight[:, None] * value_misfit * value_misfit)
    actor_part = jnp.sum(slot_weight[:, None] * chosen * advantage) / return_scale
    local_loss = frame_loss + (critic_part - actor_part) / step_total
    grad_value = slot_weight[:, None] * value_misfit / step_total
    grad_chosen = -slot_weight[:, None] * advantage / return_scale / step_total
    grad_logits = (grad_chosen[..., None] * (action_hot - jnp.exp(log_chance))).astype(jnp.bfloat16)
    grad_actor_out = jnp.einsum(
        "rku,rka->ua", actor_hidden, grad_logits, preferred_element_type=jnp.float32
    )
    grad_actor_hidden = jnp.einsum(
        "rka,ua->rku", grad_logits, actor_out, preferred_element_type=jnp.float32
    )
    actor_pre, grad_actor_gain = hidden_backward(grad_actor_hidden, actor_cache, actor_gain)
    grad_critic_out = jnp.einsum("rku,rk->u", critic_hidden, grad_value, precision=highest)
    critic_pre, grad_critic_gain = hidden_backward(
        grad_value[..., None] * critic_out, critic_cache, critic_gain
    )
    grad_actor_in, actor_to_state, actor_to_goal = worker_backward(
        actor_pre, start_state, goal_low, stoch_hot, actor_in
    )
    grad_critic_in, critic_to_state, critic_to_goal = worker_backward(
        critic_pre, start_state, goal_low, stoch_hot, critic_in
    )
    grad_goal_low = (actor_to_goal + critic_to_goal).astype(jnp.bfloat16)
    worker_goal_out, goal_pre, worker_goal_gain = head_backward(
        grad_goal_low, goal_hidden, goal_out, goal_cache, goal_gain
    )
    worker_goal_in = jnp.einsum("ng,nu->gu", code_hot, goal_pre, preferred_element_type=jnp.float32)
    returned = lax.all_to_all(
        (actor_to_state + critic_to_state).astype(jnp.bfloat16),
        DP,
        split_axis=0,
        concat_axis=0,
        tiled=True,
    )
    grad_manager_value = frame_scale * manager_misfit
    grad_manager_out = jnp.dot(grad_manager_value, man_hidden, precision=highest)
    manager_pre, grad_manager_gain = hidden_backward(
        grad_manager_value[:, None] * manager_out, man_cache, manager_gain
    )
    grad_manager_in, grad_feature = input_backward(manager_pre, feature, manager_in)
    grad_obs_gain = jnp.sum(grad_feature * obs_normed, 0)
    obs_back = normalize_back(grad_feature * obs_gain, obs_normed, obs_inverse)
    weight_cube = frame_scale[:, None, None]
    post_grad_logits = (
        (weight_cube * post_prob * (log_gap - group_kl)).reshape(ROWS, Z).astype(jnp.bfloat16)
    )
    prior_grad_logits = (
        (weight_cube * (prior_prob - post_prob)).reshape(ROWS, Z).astype(jnp.bfloat16)
    )
    grad_post_out, post_pre, grad_post_gain = head_backward(
        post_grad_logits, post_hidden, post_out, post_cache, post_gain
    )
    grad_post_in, post_back = input_backward(post_pre, post_input, post_in)
    grad_prior_out, prior_pre, grad_prior_gain = head_backward(
        prior_grad_logits, prior_hidden, prior_out, prior_cache, prior_gain
    )
    grad_prior_in, prior_back = input_backward(prior_pre, deter_low, prior_in)
    recon_grad = frame_scale[:, None] * recon_err / H
    dec_goal_out, dec_pre, dec_goal_gain = head_backward(
        recon_grad.astype(jnp.bfloat16), dec_hidden, goal_out, dec_cache, goal_gain
    )
    dec_goal_in, grad_code = input_backward(dec_pre, soft_code, goal_in)
    grad_code = grad_code.reshape(ROWS, GC, GK)
    code_grad_logits = code_prob * (
        grad_code - jnp.sum(code_prob * grad_code, -1, keepdims=True)
    ) + weight_cube * code_prob * (code_log - code_spread)
    grad_enc_out, enc_pre, grad_enc_gain = head_backward(
        code_grad_logits.reshape(ROWS, GCODE).astype(jnp.bfloat16),
        enc_hidden,
        enc_out,
        enc_cache,
        enc_gain,
    )
    grad_enc_in, enc_back = input_backward(enc_pre, deter_low, enc_in)
    grad_goal_out = worker_goal_out + dec_goal_out
    grad_goal_in = worker_goal_in + dec_goal_in
    grad_goal_gain = worker_goal_gain + dec_goal_gain
    scattered = jnp.zeros((ROWS, H), jnp.float32).at[send_order].add(returned.astype(jnp.float32))
    grad_deter = obs_back + post_back[:, :H] + prior_back + enc_back + scattered - recon_grad
    grad_inner = grad_deter * update_gate * (1.0 - candidate * candidate)
    grad_parts = jnp.concatenate(
        [
            grad_inner * candidate_in * reset_gate * (1.0 - reset_gate),
            grad_inner * reset_gate,
            grad_deter * (candidate - prev_float) * update_gate * (1.0 - update_gate),
        ],
        1,
    )
    grad_gru_gain = jnp.sum(grad_parts * gru_normed, 0)
    gru_pre = normalize_back(grad_parts * gru_gain, gru_normed, gru_inverse).astype(jnp.bfloat16)
    grad_gru_weight, gru_back = input_backward(gru_pre, gru_input, gru_weight)
    img_pre, grad_img_gain = hidden_backward(gru_back[:, :H], img_cache, img_gain)
    grad_img_stoch = jnp.einsum(
        "nz,nh->zh", stoch_prev_hot, img_pre, preferred_element_type=jnp.float32
    )
    grad_img_action = jnp.einsum(
        "na,nh->ah", action_prev_hot, img_pre, preferred_element_type=jnp.float32
    )
    grad_prev = grad_deter * (1.0 - update_gate) + gru_back[:, H:]
    embed_grad = post_back[:, H:]
    count = lax.axis_size(REP)
    loss_share = lax.psum_scatter(
        jnp.full((count,), local_loss), REP, scatter_dimension=0, tiled=True
    )
    grads = Weights(
        obs_gain=grad_obs_gain,
        manager_in=grad_manager_in,
        manager_gain=grad_manager_gain,
        manager_out=grad_manager_out,
        goal_in=grad_goal_in,
        goal_gain=grad_goal_gain,
        goal_out=grad_goal_out,
        actor_in=grad_actor_in,
        actor_gain=grad_actor_gain,
        actor_out=grad_actor_out,
        critic_in=grad_critic_in,
        critic_gain=grad_critic_gain,
        critic_out=grad_critic_out,
        img_stoch=grad_img_stoch,
        img_action=grad_img_action,
        img_gain=grad_img_gain,
        gru_weight=grad_gru_weight,
        gru_gain=grad_gru_gain,
        post_in=grad_post_in,
        post_gain=grad_post_gain,
        post_out=grad_post_out,
        prior_in=grad_prior_in,
        prior_gain=grad_prior_gain,
        prior_out=grad_prior_out,
        enc_in=grad_enc_in,
        enc_gain=grad_enc_gain,
        enc_out=grad_enc_out,
    )
    shares = []
    for i, (grad, by_column) in enumerate(zip(grads, LARGE)):
        grad = lax.psum_scatter(
            grad, REP, scatter_dimension=1 if i == IMG_ACTION else 0, tiled=True
        )
        if by_column:
            shares.append(lax.psum_scatter(grad, DP, scatter_dimension=1, tiled=True))
        else:
            shares.append(lax.psum(grad, DP))
    return (
        lax.psum(loss_share, DP)[0],
        grad_prev.reshape(SEQ_DEV, LEN, H),
        embed_grad.reshape(SEQ_DEV, LEN, E),
    ) + tuple(shares)


def solution(mesh):
    split, over_rep = (P((DP, REP)), P(REP))
    in_kernels = mesh.shape[DP] == 8 and mesh.shape[REP] == 4

    def per_device(*arguments):
        data, shares = (Data(*arguments[:12]), Weights(*arguments[12:]))
        return (step_in_kernels if in_kernels else step_plain)(data, shares)

    in_specs, out_specs = ((split,) * 12, (P(), split, split))
    for i, by_column in enumerate(LARGE):
        spec = P(None, REP) if i == IMG_ACTION else over_rep
        in_specs += (spec,)
        out_specs += (P(REP, DP) if by_column else spec,)
    return jax.shard_map(
        per_device, mesh=mesh, in_specs=in_specs, out_specs=out_specs, check_vma=False
    )
```
